32 devices in a mesh: gx: 8 (over y, x, core), gy: 4 (over z).
Axes of the slice: x: 2, y: 2, z: 4, core: 2. Of those that a mesh axis runs over, the one named last changes fastest.
Arguments:
- tokens: bfloat16 [16384, 1024], P(('gx', 'gy')), may hold values from -6 to 6
- expert_ids: int32 [16384, 2], P(('gx', 'gy')), may hold values from 0 to 15, as said below
- gain_attn: bfloat16 [1024], P('gx'), may hold values from 0.099609375 to 1.8984375
- w_qkv: bfloat16 [3, 1024, 1024], P(None, 'gx', 'gy'), may hold values from -0.1875 to 0.1875
- w_out: bfloat16 [1024, 1024], P('gy', 'gx'), may hold values from -1.796875 to 1.796875
- rel_bias: bfloat16 [32, 16], P('gx', 'gy'), may hold values from -4 to 4
- gain_ffn: bfloat16 [1024], P('gx'), may hold values from 0.099609375 to 1.8984375
- router: bfloat16 [1024, 16], P('gx'), may hold values from -0.125 to 0.125
- w_in: bfloat16 [16, 1024, 5632], P('gy', 'gx'), may hold values from -0.1875 to 0.1875
- w_down: bfloat16 [16, 2816, 1024], P('gy', None, 'gx'), may hold values from -0.8984375 to 0.8984375
- cotangent: bfloat16 [16384, 1024], P(('gx', 'gy')), may hold values from -6 to 6
Outputs:
- mixed: bfloat16 [16384, 1024], P(('gx', 'gy'))
- loss: float32 [], replicated
- router_load: float32 [2, 16], replicated
- grad_tokens: float32 [16384, 1024], P(('gx', 'gy'))
- grad_gain_attn: float32 [1024], P('gx')
- grad_w_qkv: float32 [3, 1024, 1024], P(None, 'gx', 'gy')
- grad_w_out: float32 [1024, 1024], P('gy', 'gx')
- grad_rel_bias: float32 [32, 16], P('gx', 'gy')
- grad_gain_ffn: float32 [1024], P('gx')
- grad_router: float32 [1024, 16], P('gx')
- grad_w_in: float32 [16, 1024, 5632], P('gy', 'gx')
- grad_w_down: float32 [16, 2816, 1024], P('gy', None, 'gx')
The draws below stay inside these ranges and needn't reach their ends.
Inputs may be any that keep to these rules, and one draw needn't show every extreme that they name: `expert_ids`: each row names 2 different experts; every expert is named by some row.
All inputs are finite; a program needn't handle non-finite values.
Results may differ from the reference program's by a relative error of at most 0.029.
Values may be sent and summed in bfloat16 or wider, within the bound.
A program may use at most 320 MiB of HBM per device.

```python
import math
import jax
import jax.numpy as jnp
from jax import lax

D = 1024
H = 16
DH = 64
FF = 2816
E = 16
TOP = 2
NB = 32
LEN = 1024
BLK = 256
TOK_DEV = 512
CAP = 80
TOKENS = 16384
N_GY = 4
DEVICES = 32


def draw_expert_ids(key, part):
    key = jax.random.fold_in(key, 7)
    key_favour, key_other, key_second = jax.random.split(key, 3)
    position = jnp.arange(TOKENS, dtype=jnp.int32)
    device_number = position // TOK_DEV
    favoured = device_number * E // (TOKENS // TOK_DEV)
    favour = (jax.random.randint(key_favour, (TOKENS,), 0, 8) < 3) | (position % TOK_DEV == 0)
    other_pick = jax.random.randint(key_other, (TOKENS,), 0, E)
    first_pick = jnp.where(favour, favoured, other_pick).astype(jnp.int32)
    second_pick = ((first_pick + jax.random.randint(key_second, (TOKENS,), 1, E)) % E).astype(jnp.int32)
    return jnp.stack([first_pick, second_pick], axis=1).astype(jnp.int32)


def levels(key, dims, shards, least, high):
    factor_of, own = 1.0, jax.random.fold_in(key, 6)
    for dim, parts in shards:
        steps = jnp.exp(jax.random.uniform(jax.random.fold_in(own, dim), (parts,), jnp.float32, least / len(shards), high / len(shards)))
        factor_of = factor_of * jnp.repeat(steps, dims[dim] // parts).reshape([-1 if axis == dim else 1 for axis in range(len(dims))])
    return factor_of


def noise(rng, shape, scale, bound, cuts=(), kind=jnp.bfloat16):
    values = scale * jax.random.normal(rng, shape, jnp.float32)
    if cuts:
        values = values * levels(rng, shape, cuts, -0.22, 0.18)
    return jnp.clip(values, -bound, bound).astype(kind)


def setup_inputs(seed: int = 0) -> dict:
    keys = jax.random.split(jax.random.key(seed), 12)
    return {
        "tokens": noise(keys[0], (TOKENS, D), 1.0, 6.0, ((0, 32),)),
        "expert_ids": draw_expert_ids(jax.random.fold_in(keys[11], 71), 0),
        "gain_attn": jnp.clip(1.0 + 0.18 * jax.random.normal(keys[2], (D,), jnp.float32), 0.099609375, 1.8984375).astype(jnp.bfloat16),
        "w_qkv": noise(keys[3], (3, D, H * DH), D ** -0.5, 0.1875, ((1, 8), (2, 4))),
        "w_out": noise(keys[4], (H * DH, D), 0.3, 1.796875, ((0, 4), (1, 8))),
        "rel_bias": noise(keys[5], (NB, H), 1.0, 4.0, ((0, 8), (1, 4))),
        "gain_ffn": jnp.clip(1.0 + 0.18 * jax.random.normal(keys[6], (D,), jnp.float32), 0.099609375, 1.8984375).astype(jnp.bfloat16),
        "router": noise(keys[7], (D, E), (2 * D) ** -0.5, 0.125, ((0, 8),)),
        "w_in": noise(keys[8], (E, D, 2 * FF), D ** -0.5, 0.1875, ((0, 4), (1, 8))),
        "w_down": noise(keys[9], (E, FF, D), 0.15, 0.8984375, ((0, 4), (2, 8))),
        "cotangent": noise(keys[10], (TOKENS, D), 1.0, 6.0, ((0, 32),)),
    }


@jax.custom_vjp
def low(v):
    return lax.optimization_barrier(v.astype(jnp.bfloat16)).astype(jnp.float32)

@jax.custom_vjp
def low_back(v):
    return v

def low_keep(v):
    return (low(v), None)

def low_pass(kept, grad):
    return (grad,)

def back_keep(v):
    return (v, None)

def back_low(kept, grad):
    return (low(grad),)
low.defvjp(low_keep, low_pass)
low_back.defvjp(back_keep, back_low)
bucket_edges = (12, 16, 23, 32, 46, 64, 91)
epsilon = 1e-06
loss_weight = 0.01
masked_score = -1e+30

def bucket_of(offset):
    magnitude = jnp.abs(offset)
    far_bucket = 8 + sum(((magnitude >= edge_value).astype(jnp.int32) for edge_value in bucket_edges))
    return jnp.where(magnitude < 8, magnitude, far_bucket) + 16 * (offset > 0).astype(jnp.int32)

def highest(left_side, right_side):
    return jnp.dot(left_side, right_side, precision=lax.Precision.HIGHEST)

def rms_norm(values, gain_vector):
    return values * lax.rsqrt(lax.optimization_barrier(jnp.mean(values * values, axis=-1, keepdims=True)) + epsilon) * gain_vector

def attend_sequence(pieces, table):
    query_rows, key_rows, value_rows = pieces
    position = jnp.arange(LEN, dtype=jnp.int32)
    offset = position[None, :] - position[:, None]
    bias_grid = jnp.transpose(table[bucket_of(offset)], (2, 0, 1))
    scores = jnp.einsum('qhd,khd->hqk', query_rows, key_rows, precision=lax.Precision.HIGHEST) / math.sqrt(DH) + bias_grid
    allowed = position[None, :] // BLK <= position[:, None] // BLK
    scores = low_back(jnp.where(allowed[None], scores, masked_score))
    row_max = lax.optimization_barrier(jnp.max(scores, axis=-1, keepdims=True))
    weights = jnp.exp(scores - row_max)
    weights = low(weights / lax.optimization_barrier(jnp.sum(weights, axis=-1, keepdims=True)))
    mixed_rows = jnp.einsum('hqk,khd->qhd', weights, value_rows, precision=lax.Precision.HIGHEST)
    return mixed_rows.reshape(LEN, H * DH)

def run_expert(pieces):
    expert_rows, inner_weight, outer_weight = pieces
    upper = low_back(highest(expert_rows, inner_weight))
    half_width = upper.shape[-1] // 2
    hidden_rows = low(jax.nn.gelu(upper[:, :half_width], approximate=True) * upper[:, half_width:])
    return low(low_back(highest(hidden_rows, outer_weight)))

def forward(tokens, gain_attn, w_qkv, w_out, rel_bias, gain_ffn, router, w_in, w_down, expert_ids):
    normed_one = low(rms_norm(tokens, gain_attn))
    projected = low(low_back(jnp.einsum('td,cdf->ctf', normed_one, w_qkv, precision=lax.Precision.HIGHEST)))
    projected = projected.reshape(3, TOKENS // LEN, LEN, H, DH)
    attended = lax.map(jax.checkpoint(lambda pieces: attend_sequence(pieces, rel_bias)), (projected[0], projected[1], projected[2]))
    attended = low(low_back(attended.reshape(TOKENS, H * DH)))
    group_width = H * DH // N_GY
    summed = jnp.zeros((TOKENS, D), jnp.float32)
    for group_index in range(N_GY):
        part_sum = highest(attended[:, group_index * group_width:(group_index + 1) * group_width], w_out[group_index * group_width:(group_index + 1) * group_width])
        summed = summed + low(low_back(part_sum))
    hidden_state = tokens + summed
    normed_two = low(rms_norm(hidden_state, gain_ffn))
    logits = low_back(highest(normed_two, router))
    route = jax.nn.softmax(logits, axis=-1)
    owner_ids = expert_ids.reshape(DEVICES, TOK_DEV * TOP)
    chosen = (owner_ids[:, :, None] == jnp.arange(E, dtype=jnp.int32)).astype(jnp.int32)
    earlier = jnp.cumsum(chosen, axis=1) - chosen
    slot = lax.optimization_barrier(jnp.sum(earlier * chosen, axis=-1)).reshape(TOKENS, TOP)
    kept = (slot < CAP).astype(jnp.float32)
    counts = lax.optimization_barrier(jnp.sum(chosen, axis=(0, 1))).astype(jnp.float32)
    route_sums = lax.optimization_barrier(jnp.sum(route, axis=0))
    loss = E * jnp.sum(counts / (TOKENS * TOP) * (route_sums / TOKENS))
    router_load = jnp.stack([E * counts / (TOKENS * TOP), E * route_sums / TOKENS], axis=0)
    device_index = (jnp.arange(TOKENS, dtype=jnp.int32) // TOK_DEV)[:, None]
    place = (expert_ids * DEVICES + device_index) * CAP + jnp.minimum(slot, CAP - 1)
    copies = low_back(jnp.broadcast_to(normed_two[:, None, :], (TOKENS, TOP, D)))
    buffer_rows = jnp.zeros((E * DEVICES * CAP, D), jnp.float32).at[place.reshape(-1)].add((copies * kept[:, :, None]).reshape(-1, D))
    results = lax.map(jax.checkpoint(run_expert), (buffer_rows.reshape(E, DEVICES * CAP, D), w_in, w_down))
    results = results.reshape(E * DEVICES * CAP, D)
    gate_value = jnp.take_along_axis(route, expert_ids, axis=1) * kept
    mixed = hidden_state + lax.optimization_barrier(jnp.sum(results[place] * gate_value[:, :, None], axis=1))
    return ((mixed, loss), router_load)

def reference(tokens, expert_ids, gain_attn, w_qkv, w_out, rel_bias, gain_ffn, router, w_in, w_down, cotangent):
    floats = tuple((array_in.astype(jnp.float32) for array_in in (tokens, gain_attn, w_qkv, w_out, rel_bias, gain_ffn, router, w_in, w_down)))

    def objective(*values):
        return forward(*values, expert_ids)
    (mixed, loss), pull_back, router_load = jax.vjp(objective, *floats, has_aux=True)
    grads = pull_back((cotangent.astype(jnp.float32), jnp.float32(loss_weight)))
    return (mixed.astype(jnp.bfloat16), loss, router_load, grads[0], grads[1], grads[2], grads[3], grads[4], grads[5], grads[6], grads[7], grads[8])
```

```python
import functools
import math

import jax
import jax.numpy as jnp
from jax import lax
from jax.experimental import pallas as pl
from jax.experimental.pallas import tpu as pltpu
from jax.sharding import PartitionSpec as P

LEN = 1024
BLK = 256
CAP = 80


bucket_edges = (12, 16, 23, 32, 46, 64, 91)
epsilon = 1e-06
loss_weight = 0.01
masked_score = -1e30


def bucket_of(offset):
    magnitude = jnp.abs(offset)
    far_bucket = 8 + sum(
        ((magnitude >= edge_value).astype(jnp.int32) for edge_value in bucket_edges)
    )
    return jnp.where(magnitude < 8, magnitude, far_bucket) + 16 * (offset > 0).astype(jnp.int32)


def normalize(values):
    row_scale = lax.rsqrt(jnp.mean(values * values, axis=-1, keepdims=True) + epsilon)
    return (values * row_scale, row_scale)


def norm_back(grad_out, normed, row_scale, gain_vector):
    grad_normed = grad_out * gain_vector
    grad_gain = jnp.sum(grad_out * normed, axis=0)
    grad_input = row_scale * (
        grad_normed - normed * jnp.mean(grad_normed * normed, axis=-1, keepdims=True)
    )
    return (grad_input, grad_gain)


def spread_offsets(along_offsets, row_count):
    head_count, span_width = along_offsets.shape
    key_count = span_width - row_count + 1
    tiled_rows = jnp.broadcast_to(
        along_offsets[:, None, :], (head_count, row_count, span_width)
    ).reshape(head_count, row_count * span_width)
    padded = jnp.pad(tiled_rows, ((0, 0), (0, row_count)))
    shaped = padded.reshape(head_count, row_count, span_width + 1)[:, :, :key_count]
    return shaped[:, :, ::-1]


def gather_offsets(score_grid, row_count):
    head_count = score_grid.shape[0]
    key_count = score_grid.shape[2]
    span_width = key_count + row_count - 1
    padded = jnp.pad(score_grid[:, :, ::-1], ((0, 0), (0, 0), (0, row_count)))
    flat_rows = padded.reshape(head_count, row_count * (key_count + row_count))[
        :, : row_count * span_width
    ]
    return jnp.sum(flat_rows.reshape(head_count, row_count, span_width), axis=1)


def offset_table(q_start, row_count, key_count, bucket_count):
    spot_index = jnp.arange(key_count + row_count - 1, dtype=jnp.int32)
    offsets = key_count - 1 - spot_index - q_start
    return (
        bucket_of(offsets)[:, None] == jnp.arange(bucket_count, dtype=jnp.int32)[None, :]
    ).astype(jnp.float32)


def block_scores(query_rows, key_rows, table_float, q_start):
    row_count = query_rows.shape[0]
    depth = query_rows.shape[2]
    key_count = key_rows.shape[0]
    picks_table = offset_table(q_start, row_count, key_count, table_float.shape[0])
    along_offsets = jnp.dot(picks_table, table_float, precision=lax.Precision.HIGHEST).T
    bias_grid = spread_offsets(along_offsets, row_count)
    scores = (
        jnp.einsum("qhd,khd->hqk", query_rows, key_rows, preferred_element_type=jnp.float32)
        / math.sqrt(depth)
        + bias_grid
    )
    query_pos = q_start + jnp.arange(row_count, dtype=jnp.int32)
    key_pos = jnp.arange(key_count, dtype=jnp.int32)
    allowed = key_pos[None, :] // BLK <= query_pos[:, None] // BLK
    return (jnp.where(allowed[None], scores, masked_score), picks_table)


def general_device(
    tokens, expert_ids, gain_attn, w_qkv, w_out, rel_bias, gain_ffn, router, w_in, w_down, cotangent
):
    shard_list = (gain_attn, w_qkv, w_out, rel_bias, gain_ffn, router, w_in, w_down)
    (
        gain_first,
        qkv_weight,
        out_weight,
        bias_table,
        gain_second,
        route_weight,
        inner_weight,
        outer_weight,
    ) = (
        lax.all_gather(shard_list[0], "gx", axis=0, tiled=True),
        lax.all_gather(shard_list[1], "gx", axis=1, tiled=True),
        lax.all_gather(shard_list[2], "gx", axis=1, tiled=True),
        lax.all_gather(shard_list[3], "gx", axis=0, tiled=True),
        lax.all_gather(shard_list[4], "gx", axis=0, tiled=True),
        lax.all_gather(shard_list[5], "gx", axis=0, tiled=True),
        lax.all_gather(shard_list[6], "gx", axis=1, tiled=True),
        lax.all_gather(shard_list[7], "gx", axis=2, tiled=True),
    )
    tok_dev = tokens.shape[0]
    count_x = lax.axis_size("gx")
    count_y = lax.axis_size("gy")
    total_tokens = tok_dev * count_x * count_y
    model_width = tokens.shape[1]
    expert_count = route_weight.shape[1]
    top_count = expert_ids.shape[1]
    local_experts = inner_weight.shape[0]
    head_count = bias_table.shape[1]
    head_width = qkv_weight.shape[2]
    depth = head_width // head_count
    q_rows = min(512, LEN)
    per_seq = LEN // q_rows
    inputs_float = tokens.astype(jnp.float32)
    normed_one, scale_one = normalize(inputs_float)
    first_norm = (normed_one * gain_first.astype(jnp.float32)).astype(jnp.bfloat16)
    group_rows = lax.all_gather(first_norm, "gy", axis=0, tiled=True)
    tok_group = group_rows.shape[0]
    seq_count = tok_group // LEN
    projected = jnp.einsum(
        "td,cdf->tcf", group_rows, qkv_weight, preferred_element_type=jnp.float32
    ).astype(jnp.bfloat16)
    projected = projected.reshape(tok_group, 3, head_count, depth)
    table_float = bias_table.astype(jnp.float32)

    def forward_block(item_index):
        seq_index = item_index // per_seq
        q_start = item_index % per_seq * q_rows
        query_rows = lax.dynamic_slice_in_dim(projected, seq_index * LEN + q_start, q_rows, 0)[:, 0]
        seq_rows = lax.dynamic_slice_in_dim(projected, seq_index * LEN, LEN, 0)
        scores, unused_picks = block_scores(query_rows, seq_rows[:, 1], table_float, q_start)
        row_max = jnp.max(scores, axis=-1, keepdims=True)
        expo_scores = jnp.exp(scores - row_max)
        row_total = jnp.sum(expo_scores, axis=-1, keepdims=True)
        soft_weights = (expo_scores / row_total).astype(jnp.bfloat16)
        block_out = jnp.einsum(
            "hqk,khd->qhd", soft_weights, seq_rows[:, 2], preferred_element_type=jnp.float32
        ).astype(jnp.bfloat16)
        return (block_out.reshape(q_rows, head_width), (row_max + jnp.log(row_total))[:, :, 0])

    attended, log_totals = lax.map(forward_block, jnp.arange(seq_count * per_seq, dtype=jnp.int32))
    attended = attended.reshape(tok_group, head_width)
    attn_sum = lax.psum_scatter(
        jnp.dot(attended, out_weight, preferred_element_type=jnp.float32).astype(jnp.bfloat16),
        "gy",
        scatter_dimension=0,
        tiled=True,
    ).astype(jnp.float32)
    hidden_state = inputs_float + attn_sum
    normed_two, scale_two = normalize(hidden_state)
    second_norm = (normed_two * gain_second.astype(jnp.float32)).astype(jnp.bfloat16)
    logits = jnp.dot(second_norm, route_weight, preferred_element_type=jnp.float32)
    route = jax.nn.softmax(logits, axis=-1)
    chosen = (
        expert_ids.reshape(-1)[:, None] == jnp.arange(expert_count, dtype=jnp.int32)[None, :]
    ).astype(jnp.int32)
    earlier = jnp.cumsum(chosen, axis=0) - chosen
    slot = jnp.sum(earlier * chosen, axis=-1).reshape(tok_dev, top_count)
    kept = (slot < CAP).astype(jnp.float32)
    counts, prob_sums = lax.psum(
        (jnp.sum(chosen, axis=0).astype(jnp.float32), jnp.sum(route, axis=0)), ("gx", "gy")
    )
    loss = expert_count * jnp.sum(counts / (total_tokens * top_count) * (prob_sums / total_tokens))
    router_load = jnp.stack(
        [
            expert_count * counts / (total_tokens * top_count),
            expert_count * prob_sums / total_tokens,
        ],
        axis=0,
    )
    slot_place = expert_ids * CAP + jnp.minimum(slot, CAP - 1)
    buffer_index = jnp.arange(expert_count * CAP, dtype=jnp.int32)[:, None, None]
    hit_table = (buffer_index == slot_place[None]).astype(jnp.float32) * kept[None]
    dispatch_matrix = jnp.sum(hit_table, axis=-1).astype(jnp.bfloat16)
    send_rows = jnp.dot(dispatch_matrix, second_norm, preferred_element_type=jnp.float32).astype(
        jnp.bfloat16
    )
    send_rows = send_rows.reshape(count_y, local_experts, CAP, model_width)
    received = lax.all_to_all(send_rows, "gy", split_axis=0, concat_axis=0, tiled=True)
    upper = jnp.einsum("slcd,ldf->slcf", received, inner_weight, preferred_element_type=jnp.float32)
    half_width = upper.shape[-1] // 2
    hidden_rows = (
        jax.nn.gelu(upper[..., :half_width], approximate=True) * upper[..., half_width:]
    ).astype(jnp.bfloat16)
    expert_out = jnp.einsum(
        "slcf,lfd->slcd", hidden_rows, outer_weight, preferred_element_type=jnp.float32
    ).astype(jnp.bfloat16)
    expert_out, upper, received = (expert_out, upper, received)
    returned = lax.all_to_all(expert_out, "gy", split_axis=0, concat_axis=0, tiled=True).reshape(
        expert_count * CAP, model_width
    )
    picked_rows = jnp.take(returned, slot_place, axis=0).astype(jnp.float32)
    gate_value = jnp.take_along_axis(route, expert_ids, axis=1) * kept
    mixed = hidden_state + jnp.sum(picked_rows * gate_value[:, :, None], axis=1)
    (
        gain_first,
        qkv_weight,
        out_weight,
        bias_table,
        gain_second,
        route_weight,
        inner_weight,
        outer_weight,
    ) = (
        lax.all_gather(shard_list[0], "gx", axis=0, tiled=True),
        lax.all_gather(shard_list[1], "gx", axis=1, tiled=True),
        lax.all_gather(shard_list[2], "gx", axis=1, tiled=True),
        lax.all_gather(shard_list[3], "gx", axis=0, tiled=True),
        lax.all_gather(shard_list[4], "gx", axis=0, tiled=True),
        lax.all_gather(shard_list[5], "gx", axis=0, tiled=True),
        lax.all_gather(shard_list[6], "gx", axis=1, tiled=True),
        lax.all_gather(shard_list[7], "gx", axis=2, tiled=True),
    )
    table_float = bias_table.astype(jnp.float32)
    grad_mixed = cotangent.astype(jnp.float32)
    grad_gate = kept * jnp.sum(grad_mixed[:, None, :] * picked_rows, axis=-1)
    gate_matrix = jnp.sum(hit_table * gate_value[None], axis=-1)
    grad_buffer = jnp.dot(gate_matrix, grad_mixed, precision=lax.Precision.HIGHEST).astype(
        jnp.bfloat16
    )
    grad_expert = lax.all_to_all(
        grad_buffer.reshape(count_y, local_experts, CAP, model_width),
        "gy",
        split_axis=0,
        concat_axis=0,
        tiled=True,
    )
    half_width = upper.shape[-1] // 2
    activated, pull_gelu = jax.vjp(
        lambda gate_part, up_part: jax.nn.gelu(gate_part, approximate=True) * up_part,
        upper[..., :half_width],
        upper[..., half_width:],
    )
    hidden_rows = activated.astype(jnp.bfloat16)
    grad_hidden = jnp.einsum(
        "slcd,lfd->slcf", grad_expert, outer_weight, preferred_element_type=jnp.float32
    )
    grad_outer = jnp.einsum(
        "slcf,slcd->lfd", hidden_rows, grad_expert, preferred_element_type=jnp.float32
    )
    grad_gate_part, grad_up_part = pull_gelu(grad_hidden)
    grad_upper = jnp.concatenate([grad_gate_part, grad_up_part], axis=-1).astype(jnp.bfloat16)
    grad_inner = jnp.einsum(
        "slcd,slcf->ldf", received, grad_upper, preferred_element_type=jnp.float32
    )
    grad_received = jnp.einsum(
        "slcf,ldf->slcd", grad_upper, inner_weight, preferred_element_type=jnp.float32
    ).astype(jnp.bfloat16)
    grad_copies = lax.all_to_all(
        grad_received, "gy", split_axis=0, concat_axis=0, tiled=True
    ).reshape(expert_count * CAP, model_width)
    grad_second = jnp.sum(
        jnp.take(grad_copies, slot_place, axis=0).astype(jnp.float32) * kept[:, :, None], axis=1
    )
    expert_hits = (expert_ids[:, :, None] == jnp.arange(expert_count, dtype=jnp.int32)).astype(
        jnp.float32
    )
    grad_route = (
        jnp.sum(grad_gate[:, :, None] * expert_hits, axis=1)
        + loss_weight * expert_count * (counts / (total_tokens * top_count)) / total_tokens
    )
    grad_logits = (
        route * (grad_route - jnp.sum(route * grad_route, axis=-1, keepdims=True))
    ).astype(jnp.bfloat16)
    grad_router = jnp.dot(second_norm.T, grad_logits, preferred_element_type=jnp.float32)
    grad_second = grad_second + jnp.dot(
        grad_logits, route_weight.T, preferred_element_type=jnp.float32
    )
    grad_hidden_state, grad_gain_second = norm_back(
        grad_second, normed_two, scale_two, gain_second.astype(jnp.float32)
    )
    grad_hidden_state = grad_mixed + grad_hidden_state
    piece_rows = lax.all_gather(grad_hidden_state.astype(jnp.bfloat16), "gy", axis=0, tiled=True)
    grad_out_weight = jnp.einsum(
        "tf,td->fd", attended, piece_rows, preferred_element_type=jnp.float32
    )
    update_rows = jnp.dot(piece_rows, out_weight.T, preferred_element_type=jnp.float32).astype(
        jnp.bfloat16
    )
    grad_out_weight, grad_attended = (grad_out_weight, update_rows)

    def backward_sequence(seq_index):
        seq_rows = lax.dynamic_slice_in_dim(projected, seq_index * LEN, LEN, 0)
        key_rows = seq_rows[:, 1]
        value_rows = seq_rows[:, 2]
        grad_keys = jnp.zeros((LEN, head_count, depth), jnp.float32)
        grad_values = jnp.zeros((LEN, head_count, depth), jnp.float32)
        grad_table = jnp.zeros(table_float.shape, jnp.float32)
        grad_queries = []
        for block_index in range(per_seq):
            q_start = block_index * q_rows
            query_rows = seq_rows[q_start : q_start + q_rows, 0]
            grad_out = lax.dynamic_slice_in_dim(
                grad_attended, seq_index * LEN + q_start, q_rows, 0
            ).reshape(q_rows, head_count, depth)
            scores, picks_table = block_scores(query_rows, key_rows, table_float, q_start)
            block_lse = log_totals[seq_index * per_seq + block_index]
            soft_probs = jnp.exp(scores - block_lse[:, :, None])
            grad_probs = jnp.einsum(
                "qhd,khd->hqk", grad_out, value_rows, preferred_element_type=jnp.float32
            )
            grad_scores = (
                soft_probs * (grad_probs - jnp.sum(soft_probs * grad_probs, axis=-1, keepdims=True))
            ).astype(jnp.bfloat16)
            grad_queries.append(
                jnp.einsum(
                    "hqk,khd->qhd", grad_scores, key_rows, preferred_element_type=jnp.float32
                )
                / math.sqrt(depth)
            )
            grad_keys = grad_keys + jnp.einsum(
                "hqk,qhd->khd", grad_scores, query_rows, preferred_element_type=jnp.float32
            ) / math.sqrt(depth)
            grad_values = grad_values + jnp.einsum(
                "hqk,qhd->khd",
                soft_probs.astype(jnp.bfloat16),
                grad_out,
                preferred_element_type=jnp.float32,
            )
            along_grads = gather_offsets(grad_scores.astype(jnp.float32), q_rows)
            grad_table = grad_table + jnp.dot(
                picks_table.T, along_grads.T, precision=lax.Precision.HIGHEST
            )
        stacked = jnp.stack(
            [jnp.concatenate(grad_queries, axis=0), grad_keys, grad_values], axis=1
        ).astype(jnp.bfloat16)
        return (stacked, grad_table)

    grad_projected, table_parts = lax.map(backward_sequence, jnp.arange(seq_count, dtype=jnp.int32))
    grad_projected = grad_projected.reshape(tok_group, 3, head_width)
    grad_bias_table = jnp.sum(table_parts, axis=0)
    grad_qkv_weight = jnp.einsum(
        "td,tcf->cdf", group_rows, grad_projected, preferred_element_type=jnp.float32
    )
    grad_slice = lax.slice_in_dim(grad_projected, 0, tok_dev * lax.axis_size("gy"), axis=0)
    grad_first = lax.psum_scatter(
        jnp.einsum(
            "tcf,cdf->td", grad_slice, qkv_weight, preferred_element_type=jnp.float32
        ).astype(jnp.bfloat16),
        "gy",
        scatter_dimension=0,
        tiled=True,
    ).astype(jnp.float32)
    grad_inputs, grad_gain_first = norm_back(
        grad_first, normed_one, scale_one, gain_first.astype(jnp.float32)
    )
    grad_tokens = grad_hidden_state + grad_inputs
    grad_gain_first, grad_gain_second, grad_router = (
        lax.psum(grad_gain_first.astype(jnp.bfloat16), "gy").astype(jnp.float32),
        lax.psum(grad_gain_second.astype(jnp.bfloat16), "gy").astype(jnp.float32),
        lax.psum(grad_router.astype(jnp.bfloat16), "gy").astype(jnp.float32),
    )
    summed_grads = (
        lax.psum_scatter(
            grad_gain_first.astype(jnp.bfloat16), "gx", scatter_dimension=0, tiled=True
        ).astype(jnp.float32),
        lax.psum_scatter(
            grad_qkv_weight.astype(jnp.bfloat16), "gx", scatter_dimension=1, tiled=True
        ).astype(jnp.float32),
        lax.psum_scatter(
            grad_out_weight.astype(jnp.bfloat16), "gx", scatter_dimension=1, tiled=True
        ).astype(jnp.float32),
        lax.psum_scatter(
            grad_bias_table.astype(jnp.bfloat16), "gx", scatter_dimension=0, tiled=True
        ).astype(jnp.float32),
        lax.psum_scatter(
            grad_gain_second.astype(jnp.bfloat16), "gx", scatter_dimension=0, tiled=True
        ).astype(jnp.float32),
        lax.psum_scatter(
            grad_router.astype(jnp.bfloat16), "gx", scatter_dimension=0, tiled=True
        ).astype(jnp.float32),
        lax.psum_scatter(
            grad_inner.astype(jnp.bfloat16), "gx", scatter_dimension=1, tiled=True
        ).astype(jnp.float32),
        lax.psum_scatter(
            grad_outer.astype(jnp.bfloat16), "gx", scatter_dimension=2, tiled=True
        ).astype(jnp.float32),
    )
    return (
        mixed.astype(jnp.bfloat16),
        loss,
        router_load,
        grad_tokens,
        summed_grads[0],
        summed_grads[1],
        summed_grads[2],
        summed_grads[3],
        summed_grads[4],
        summed_grads[5],
        summed_grads[6],
        summed_grads[7],
    )


def dot_nn(a, b):
    return lax.dot_general(a, b, (((1,), (0,)), ((), ())), preferred_element_type=jnp.float32)

def dot_nt(a, b):
    return lax.dot_general(a, b, (((1,), (1,)), ((), ())), preferred_element_type=jnp.float32)

def span_buckets():
    k = jnp.arange(2 * BLK, dtype=jnp.int32)
    return jnp.stack([bucket_of(BLK - k - BLK * d) for d in range(2)])

def attend_fwd_kernel(proj_ref, span_ref, out_ref, lse_ref, tile_ref):
    length = proj_ref.shape[1]
    blocks = length // BLK
    depth = 64
    lane = lax.broadcasted_iota(jnp.int32, (1, 2 * depth), 1)
    for h in range(2):
        for d in range(2):
            row = span_ref[h, d:d + 1, :]
            wide = jnp.broadcast_to(row, (BLK, 2 * BLK))
            turned = pltpu.roll(wide, 0, 1, stride=1, stride_axis=0)
            tile_ref[h, d] = turned[:, BLK:]
    far = [span_ref[h, 1:2, 2 * BLK - 1:2 * BLK] for h in range(2)]
    keys = proj_ref[1]
    values_t = proj_ref[2].T
    for block in range(blocks):
        rows = pl.ds(block * BLK, BLK)
        query = proj_ref[0, rows, :] * jnp.bfloat16(0.125)
        key_count = (block + 1) * BLK
        outs = []
        for h in range(2):
            picked = jnp.where((lane // depth) == h, query, jnp.bfloat16(0))
            scores = dot_nt(keys[:key_count], picked)
            parts = []
            for kb in range(block + 1):
                part = scores[kb * BLK:(kb + 1) * BLK]
                d = block - kb
                parts.append(part + (tile_ref[h, d] if d < 2 else far[h]))
            top = functools.reduce(jnp.maximum, [jnp.max(p, axis=0, keepdims=True) for p in parts])
            parts = [jnp.exp(p - top) for p in parts]
            total = functools.reduce(jnp.add, [jnp.sum(p, axis=0, keepdims=True) for p in parts])
            scale = 1.0 / total
            weights = jnp.concatenate([(p * scale).astype(jnp.bfloat16) for p in parts], axis=0)
            outs.append(dot_nn(values_t[h * depth:(h + 1) * depth, :key_count], weights))
            lse_ref[0, h:h + 1, rows] = top + jnp.log(total)
        out_ref[rows, :] = jnp.concatenate(outs, axis=0).T.astype(jnp.bfloat16)

def attend_fwd(proj, spans):
    _, length, width = proj.shape
    pairs = width // 128
    return pl.pallas_call(
        attend_fwd_kernel,
        grid=(pairs,),
        out_shape=(
            jax.ShapeDtypeStruct((length, width), jnp.bfloat16),
            jax.ShapeDtypeStruct((pairs, 2, length), jnp.float32),
            jax.ShapeDtypeStruct((2 * pairs, 2, BLK, BLK), jnp.float32),
        ),
        in_specs=[
            pl.BlockSpec((3, length, 128), lambda p: (0, 0, p)),
            pl.BlockSpec((2, 2, 2 * BLK), lambda p: (p, 0, 0)),
        ],
        out_specs=(
            pl.BlockSpec((length, 128), lambda p: (0, p)),
            pl.BlockSpec((1, 2, length), lambda p: (p, 0, 0)),
            pl.BlockSpec((2, 2, BLK, BLK), lambda p: (p, 0, 0, 0)),
        ),
        compiler_params=pltpu.CompilerParams(vmem_limit_bytes=48 * 2**20),
        name="attend_forward",
    )(proj, spans)

def attend_bwd_kernel(proj_ref, dout_ref, lse_ref, tile_ref, far_ref, dproj_ref, span_ref, dk_ref, dv_ref, near_ref):
    length = proj_ref.shape[1]
    blocks = length // BLK
    depth = 64
    lane = lax.broadcasted_iota(jnp.int32, (1, 2 * depth), 1)
    keys = proj_ref[1]
    values = proj_ref[2]
    keys_t = keys.T
    dk_ref[...] = jnp.zeros_like(dk_ref)
    dv_ref[...] = jnp.zeros_like(dv_ref)
    near_ref[...] = jnp.zeros_like(near_ref)
    far_sum = [jnp.zeros((1, BLK), jnp.float32) for h in range(2)]
    for block in range(blocks):
        rows = pl.ds(block * BLK, BLK)
        key_count = (block + 1) * BLK
        query = proj_ref[0, rows, :] * jnp.bfloat16(0.125)
        grad = dout_ref[rows, :]
        dq_parts = []
        dk_sum = None
        dv_sum = None
        for h in range(2):
            own = (lane // depth) == h
            query_h = jnp.where(own, query, jnp.bfloat16(0))
            grad_h = jnp.where(own, grad, jnp.bfloat16(0))
            scores = dot_nt(keys[:key_count], query_h)
            grad_p = dot_nt(values[:key_count], grad_h)
            lse = lse_ref[0, h:h + 1, rows]
            far = far_ref[0, h:h + 1, 0:1]
            probs = []
            delta = None
            for kb in range(block + 1):
                d = block - kb
                part = scores[kb * BLK:(kb + 1) * BLK]
                part = jnp.exp(part + ((tile_ref[h, d] - lse) if d < 2 else (far - lse)))
                probs.append(part)
                term = jnp.sum(part * grad_p[kb * BLK:(kb + 1) * BLK], axis=0, keepdims=True)
                delta = term if delta is None else delta + term
            ds = []
            for kb in range(block + 1):
                d = block - kb
                part = probs[kb] * (grad_p[kb * BLK:(kb + 1) * BLK] - delta)
                if d < 2:
                    near_ref[h, d] += part
                else:
                    far_sum[h] = far_sum[h] + jnp.sum(part, axis=0, keepdims=True)
                ds.append(part.astype(jnp.bfloat16))
            ds = jnp.concatenate(ds, axis=0)
            weights = jnp.concatenate([p.astype(jnp.bfloat16) for p in probs], axis=0)
            dv_h = dot_nn(weights, grad_h)
            dk_h = dot_nn(ds, query_h)
            dv_sum = dv_h if dv_sum is None else dv_sum + dv_h
            dk_sum = dk_h if dk_sum is None else dk_sum + dk_h
            dq_parts.append(dot_nn(keys_t[h * depth:(h + 1) * depth, :key_count], ds))
        dk_ref[:key_count] += dk_sum
        dv_ref[:key_count] += dv_sum
        dproj_ref[0, rows, :] = (jnp.concatenate(dq_parts, axis=0).T * 0.125).astype(jnp.bfloat16)
    dproj_ref[1] = dk_ref[...].astype(jnp.bfloat16)
    dproj_ref[2] = dv_ref[...].astype(jnp.bfloat16)
    flip = (
        lax.broadcasted_iota(jnp.int32, (BLK, BLK), 0) + lax.broadcasted_iota(jnp.int32, (BLK, BLK), 1) == BLK - 1
    ).astype(jnp.bfloat16)
    for h in range(2):
        for d in range(2):
            near = near_ref[h, d]
            near_high = near.astype(jnp.bfloat16)
            near_low = (near - near_high.astype(jnp.float32)).astype(jnp.bfloat16)
            flipped = dot_nn(flip, near_high) + dot_nn(flip, near_low)
            wide = jnp.concatenate([flipped, jnp.zeros((BLK, BLK), jnp.float32)], axis=1)
            turned = pltpu.roll(wide, 1, 1, stride=1, stride_axis=0)
            span_ref[h, d:d + 1, :] = jnp.sum(turned, axis=0, keepdims=True)
        lanes = lax.broadcasted_iota(jnp.int32, (1, 2 * BLK), 1)
        total = jnp.sum(far_sum[h], axis=1, keepdims=True)
        span_ref[h, 1:2, :] += jnp.where(lanes == 2 * BLK - 1, total, 0.0)

def attend_bwd(proj, dout, lse, tiles, far):
    _, length, width = proj.shape
    pairs = width // 128
    return pl.pallas_call(
        attend_bwd_kernel,
        grid=(pairs,),
        out_shape=(
            jax.ShapeDtypeStruct((3, length, width), jnp.bfloat16),
            jax.ShapeDtypeStruct((2 * pairs, 2, 2 * BLK), jnp.float32),
        ),
        in_specs=[
            pl.BlockSpec((3, length, 128), lambda p: (0, 0, p)),
            pl.BlockSpec((length, 128), lambda p: (0, p)),
            pl.BlockSpec((1, 2, length), lambda p: (p, 0, 0)),
            pl.BlockSpec((2, 2, BLK, BLK), lambda p: (p, 0, 0, 0)),
            pl.BlockSpec((1, 2, 128), lambda p: (p, 0, 0)),
        ],
        out_specs=(
            pl.BlockSpec((3, length, 128), lambda p: (0, 0, p)),
            pl.BlockSpec((2, 2, 2 * BLK), lambda p: (p, 0, 0)),
        ),
        scratch_shapes=[
            pltpu.VMEM((length, 128), jnp.float32),
            pltpu.VMEM((length, 128), jnp.float32),
            pltpu.VMEM((2, 2, BLK, BLK), jnp.float32),
        ],
        compiler_params=pltpu.CompilerParams(vmem_limit_bytes=48 * 2**20),
        name="attend_backward",
    )(proj, dout, lse, tiles, far)


AXES = ("gx", "gy")
MESH_ID = pl.DeviceIdType.MESH


def fits_fast(mesh):
    return mesh.shape["gx"] == 8 and mesh.shape["gy"] == 4


def places():
    x = lax.axis_index("gx")
    z = lax.axis_index("gy")
    core = x % 2
    chip = x // 2
    along_z = (z + 1 - 2 * (z % 2), (z + 2) % 4, 3 - z)
    chips = (chip + 1 - 2 * (chip % 2), (chip + 2) % 4, 3 - chip)
    return x, z, along_z, tuple(2 * other + core for other in chips), x + 1 - 2 * core


def gather_kernel(
    tok_ref, wq_ref, wo_ref, small_ref, seq_ref, wqs_ref, wos_ref, smalls_ref, send_sem, recv_sem, local_sem
):
    x, z, along_z, across, sibling = places()
    peers = [(x, other) for other in along_z] + [(other, z) for other in across] + [(sibling, z)]
    barrier = pltpu.get_barrier_semaphore()
    for peer in peers:
        pl.semaphore_signal(barrier, inc=1, device_id=peer, device_id_type=MESH_ID)
    pl.semaphore_wait(barrier, len(peers))
    started = []

    def send(source, target, device):
        index = len(started)
        copy = pltpu.make_async_remote_copy(
            src_ref=source,
            dst_ref=target,
            send_sem=send_sem.at[index],
            recv_sem=recv_sem.at[index],
            device_id=device,
            device_id_type=MESH_ID,
        )
        copy.start()
        started.append(copy)
        return copy

    depth = wq_ref.shape[1]
    width = wq_ref.shape[2]
    rows_out = wo_ref.shape[0]

    def qkv_part(owner, slot):
        return wqs_ref.at[:, pl.ds(pl.multiple_of(owner * depth, depth), depth), pl.ds(slot * width, width)]

    def out_part(owner, slot, slots):
        return wos_ref.at[
            pl.ds(slot * rows_out, slots * rows_out), pl.ds(pl.multiple_of(owner * depth, depth), depth)
        ]

    out_slots = (2, 1, 3)
    locals_started = []

    def keep(source, target):
        copy = pltpu.make_async_copy(source, target, local_sem.at[len(locals_started)])
        copy.start()
        locals_started.append(copy)
        return copy

    half = z % 2
    kept_wq = keep(wq_ref, qkv_part(x, 0))
    kept_wo = keep(wo_ref, out_part(x, 0, 1))
    kept_small = keep(small_ref, smalls_ref.at[0, x])
    keep(tok_ref, seq_ref.at[half])
    small_z = [send(small_ref, smalls_ref.at[j + 1, x], (x, along_z[j])) for j in range(3)]
    wq_z = send(wq_ref, qkv_part(x, 1), (x, along_z[1]))
    wo_z = [send(wo_ref, out_part(x, out_slots[j], 1), (x, along_z[j])) for j in range(3)]
    wq_first = [send(wq_ref, qkv_part(x, 0), (other, z)) for other in across + (sibling,)]
    send(tok_ref, seq_ref.at[half], (x, along_z[0]))
    kept_small.wait()
    for copy in small_z:
        copy.wait_recv()
    small_x = [send(smalls_ref.at[:, x], smalls_ref.at[:, x], (other, z)) for other in across + (sibling,)]
    wq_z.wait_recv()
    wq_second = [send(qkv_part(x, 1), qkv_part(x, 1), (other, z)) for other in across + (sibling,)]
    kept_wo.wait()
    for copy in wo_z:
        copy.wait_recv()
    wo_x = [send(out_part(x, 0, 4), out_part(x, 0, 4), (other, z)) for other in across + (sibling,)]
    waited = small_z + [wq_z] + wo_z
    for j in range(3):
        owner = across[j]
        small_x[j].wait_recv()
        send(smalls_ref.at[:, owner], smalls_ref.at[:, owner], (sibling, z))
        wq_first[j].wait_recv()
        send(qkv_part(owner, 0), qkv_part(owner, 0), (sibling, z))
        waited += [small_x[j], wq_first[j]]
    for j in range(3):
        owner = across[j]
        wq_second[j].wait_recv()
        send(qkv_part(owner, 1), qkv_part(owner, 1), (sibling, z))
        wo_x[j].wait_recv()
        send(out_part(owner, 0, 4), out_part(owner, 0, 4), (sibling, z))
        waited += [wq_second[j], wo_x[j]]
    for copy in started:
        if not any(copy is other for other in waited):
            copy.wait_recv()
    for copy in started:
        copy.wait_send()
    kept_wq.wait()
    locals_started[3].wait()


def gather_params(tokens, w_qkv, w_out, small):
    tok_dev, model_width = tokens.shape
    copies = 3 + 1 + 3 + 4 + 1 + 4 + 4 + 4 + 12
    anywhere = pl.BlockSpec(memory_space=pl.ANY)
    return pl.pallas_call(
        gather_kernel,
        out_shape=(
            jax.ShapeDtypeStruct((2, tok_dev, model_width), jnp.bfloat16),
            jax.ShapeDtypeStruct((3, model_width, 2 * w_qkv.shape[2]), jnp.bfloat16),
            jax.ShapeDtypeStruct((4 * w_out.shape[0], model_width), jnp.bfloat16),
            jax.ShapeDtypeStruct((4, 8) + small.shape, jnp.bfloat16),
        ),
        in_specs=[anywhere] * 4,
        out_specs=(anywhere,) * 4,
        scratch_shapes=[
            pltpu.SemaphoreType.DMA((copies,)),
            pltpu.SemaphoreType.DMA((copies,)),
            pltpu.SemaphoreType.DMA((4,)),
        ],
        compiler_params=pltpu.CompilerParams(collective_id=0, has_side_effects=True),
        name="gather_params",
    )(tokens, w_qkv, w_out, small)


def swap_z(values, step):
    return lax.ppermute(values, "gy", [(i, i ^ step) for i in range(4)])


def swap_core(values):
    return lax.ppermute(values, "gx", [(i, i ^ 1) for i in range(8)])


def exchange_slots(rows):
    groups = [[(2 * c + h) * 4 + z for c in range(4) for z in range(4)] for h in range(2)]
    return lax.all_to_all(rows, AXES, 0, 0, axis_index_groups=groups, tiled=True)


def geglu(gate_part, up_part):
    return jax.nn.gelu(gate_part, approximate=True) * up_part


def fast_device(
    tokens, expert_ids, gain_attn, w_qkv, w_out, rel_bias, gain_ffn, router, w_in, w_down, cotangent
):
    f32, bf16 = jnp.float32, jnp.bfloat16
    z = lax.axis_index("gy")
    half = z % 2
    tok_dev, model_width = tokens.shape
    total_tokens = tok_dev * 32
    expert_count = router.shape[1]
    top_count = expert_ids.shape[1]
    shard = model_width // 8
    local_experts, _, upper_width = w_in.shape
    quarter = upper_width // 4
    bucket_count = rel_bias.shape[0] * 8
    group_heads = rel_bias.shape[1]

    expert_row = jnp.arange(expert_count, dtype=jnp.int32)
    hits = [(expert_ids[:, c][:, None] == expert_row[None]) for c in range(top_count)]
    both = sum(hit.astype(bf16) for hit in hits)
    steps = jnp.arange(tok_dev, dtype=jnp.int32)
    lower = (steps[None, :] < steps[:, None]).astype(bf16)
    before = jnp.dot(lower, both, preferred_element_type=f32)
    slots = [jnp.sum(jnp.where(hit, before, 0.0), axis=1).astype(jnp.int32) for hit in hits]
    kept = [slot < CAP for slot in slots]
    local_counts = jnp.sum(both.astype(f32), axis=0)
    count_high = jnp.floor(local_counts / 32.0)
    count_low = local_counts - 32.0 * count_high

    def lanes(rows):
        return jnp.pad(rows.astype(bf16), ((0, 0), (0, shard - rows.shape[1])))

    small = jnp.concatenate(
        [
            router.T,
            gain_attn[None],
            gain_ffn[None],
            lanes(rel_bias),
            lanes(count_high[None]),
            lanes(count_low[None]),
            jnp.zeros((8, shard), bf16),
        ],
        axis=0,
    )
    seq_tokens, qkv_weight, out_weight, smalls = gather_params(tokens, w_qkv, w_out, small)

    inner_sent = (
        w_in.reshape(local_experts, shard, 2, 2, quarter).transpose(0, 3, 1, 2, 4).reshape(8, shard, 2 * quarter)
    )
    outer_sent = w_down.reshape(8, quarter, shard)
    outer_own = lax.all_to_all(outer_sent, "gx", 0, 0, tiled=True)
    outer_own = outer_own.transpose(1, 0, 2).reshape(quarter, model_width)
    inner_own = lax.all_to_all(inner_sent, "gx", 0, 0, tiled=True).reshape(model_width, 2 * quarter)
    outer_parts = (outer_own, swap_core(outer_own))
    inner_parts = (inner_own, swap_core(inner_own))

    own_small = smalls[0]
    router_t = own_small[:, :16].transpose(1, 0, 2).reshape(expert_count, model_width)
    gain_first = own_small[:, 16].reshape(model_width).astype(f32)
    gain_second = own_small[:, 17].reshape(model_width).astype(f32)
    bias_table = jnp.concatenate(
        [smalls[j, :, 18:22, :group_heads].reshape(bucket_count, group_heads) for j in (0, 2)], axis=1
    )
    all_counts = smalls[:, :, 22:24, :expert_count].astype(f32).sum(axis=(0, 1))
    counts = 32.0 * all_counts[0] + all_counts[1]

    seq_float = seq_tokens.reshape(2 * tok_dev, model_width).astype(f32)
    seq_normed, _ = normalize(seq_float)
    first_norm = (seq_normed * gain_first).astype(bf16)
    projected = jnp.einsum("td,cdf->ctf", first_norm, qkv_weight, preferred_element_type=f32).astype(bf16)
    picks = (span_buckets().reshape(-1)[:, None] == jnp.arange(bucket_count, dtype=jnp.int32)).astype(bf16)
    spans = jnp.einsum("kb,bh->hk", picks, bias_table, preferred_element_type=f32)
    head_count = spans.shape[0]
    spans = spans.reshape(head_count, 2, 2 * BLK)
    attended, log_totals, bias_tiles = attend_fwd(projected, spans)
    attended = attended.reshape(2, tok_dev, -1)
    attended_other = swap_z(lax.dynamic_index_in_dim(attended, 1 - half, 0, keepdims=False), 1)
    attended = jnp.concatenate(
        [lax.dynamic_index_in_dim(attended, half, 0, keepdims=False), attended_other], axis=1
    )
    inputs_float = tokens.astype(f32)
    hidden_state = inputs_float + jnp.dot(attended, out_weight, preferred_element_type=f32)
    normed_two, scale_two = normalize(hidden_state)
    second_norm = (normed_two * gain_second).astype(bf16)
    logits = lax.dot_general(second_norm, router_t, (((1,), (1,)), ((), ())), preferred_element_type=f32)
    route = jax.nn.softmax(logits, axis=-1)

    gates = [
        jnp.where(keep, jnp.sum(jnp.where(hit, route, 0.0), axis=1), 0.0) for hit, keep in zip(hits, kept)
    ]
    spots = [
        jnp.where(keep, ((expert_ids[:, c] % 4) * 4 + expert_ids[:, c] // 4) * CAP + slots[c], -1)
        for c, keep in enumerate(kept)
    ]
    buffer_rows = jnp.arange(expert_count * CAP, dtype=jnp.int32)
    marks = [buffer_rows[:, None] == spot[None] for spot in spots]
    dispatch = (marks[0] | marks[1]).astype(bf16)
    gate_rows = jnp.sum(
        jnp.where(marks[0], gates[0][None], 0.0) + jnp.where(marks[1], gates[1][None], 0.0), axis=1
    )
    send_rows = jnp.dot(dispatch, second_norm, preferred_element_type=f32).astype(bf16)
    received = exchange_slots(send_rows.reshape(expert_count, CAP, model_width)).reshape(-1, model_width)
    grad_rows = (jnp.dot(dispatch, cotangent, preferred_element_type=f32) * gate_rows[:, None]).astype(bf16)
    grad_expert = exchange_slots(grad_rows.reshape(expert_count, CAP, model_width)).reshape(-1, model_width)

    uppers = [jnp.dot(received, part, preferred_element_type=f32) for part in inner_parts]
    hiddens = [geglu(upper[:, :quarter], upper[:, quarter:]).astype(bf16) for upper in uppers]
    expert_out = sum(
        jnp.dot(hidden, part, preferred_element_type=f32) for hidden, part in zip(hiddens, outer_parts)
    ).astype(bf16)
    returned = exchange_slots(expert_out.reshape(expert_count, CAP, model_width)).reshape(-1, model_width)

    grad_uppers = []
    for upper, part in zip(uppers, outer_parts):
        grad_hidden = lax.dot_general(grad_expert, part, (((1,), (1,)), ((), ())), preferred_element_type=f32)
        _, pull_back = jax.vjp(geglu, upper[:, :quarter], upper[:, quarter:])
        grad_uppers.append(jnp.concatenate(pull_back(grad_hidden), axis=1).astype(bf16))
    grad_received = sum(
        lax.dot_general(grad_upper, part, (((1,), (1,)), ((), ())), preferred_element_type=f32)
        for grad_upper, part in zip(grad_uppers, inner_parts)
    ).astype(bf16)
    grad_copies = exchange_slots(grad_received.reshape(expert_count, CAP, model_width)).reshape(-1, model_width)

    def over_rows(left, right):
        return lax.dot_general(left, right, (((0,), (0,)), ((), ())), preferred_element_type=f32)

    grad_inner_other = swap_core(over_rows(received, grad_uppers[1]).astype(bf16))
    grad_outer_other = swap_core(over_rows(hiddens[1], grad_expert).astype(bf16))
    grad_inner = (over_rows(received, grad_uppers[0]) + grad_inner_other.astype(f32)).astype(bf16)
    grad_outer = (over_rows(hiddens[0], grad_expert) + grad_outer_other.astype(f32)).astype(bf16)
    grad_inner = lax.all_to_all(grad_inner.reshape(8, shard, 2 * quarter), "gx", 0, 0, tiled=True)
    grad_inner = (
        grad_inner.reshape(local_experts, 2, shard, 2, quarter)
        .transpose(0, 2, 3, 1, 4)
        .reshape(local_experts, shard, upper_width)
        .astype(f32)
    )
    grad_outer = lax.all_to_all(
        grad_outer.reshape(quarter, 8, shard).transpose(1, 0, 2), "gx", 0, 0, tiled=True
    )
    grad_outer = grad_outer.reshape(local_experts, 2 * quarter, shard).astype(f32)

    picked = [
        lax.dot_general(mark.astype(bf16), returned, (((0,), (0,)), ((), ())), preferred_element_type=f32)
        for mark in marks
    ]
    mixed = hidden_state + (picked[0] * gates[0][:, None] + picked[1] * gates[1][:, None])
    grad_mixed = cotangent.astype(f32)
    grad_gates = [jnp.sum(grad_mixed * rows, axis=1) for rows in picked]
    grad_second = over_rows(dispatch, grad_copies)
    grad_route = sum(
        jnp.where(hit, grad_gate[:, None], 0.0) for hit, grad_gate in zip(hits, grad_gates)
    ) + loss_weight * expert_count * (counts / (total_tokens * top_count)) / total_tokens
    grad_logits = (
        route * (grad_route - jnp.sum(route * grad_route, axis=-1, keepdims=True))
    ).astype(bf16)
    grad_router_t = over_rows(grad_logits, second_norm)
    grad_second = grad_second + jnp.dot(grad_logits, router_t, preferred_element_type=f32)
    grad_hidden_state, grad_gain_second = norm_back(grad_second, normed_two, scale_two, gain_second)
    grad_hidden_state = grad_mixed + grad_hidden_state

    grad_part = grad_hidden_state.astype(bf16)
    grad_attended = lax.dot_general(
        grad_part, out_weight, (((1,), (1,)), ((), ())), preferred_element_type=f32
    ).astype(bf16)
    own_width = grad_attended.shape[1] // 2
    grad_own = grad_attended[:, :own_width]
    grad_other = swap_z(grad_attended[:, own_width:], 1)
    grad_seq = jnp.where(
        half == 0,
        jnp.concatenate([grad_own, grad_other], axis=0),
        jnp.concatenate([grad_other, grad_own], axis=0),
    )
    far_bias = jnp.broadcast_to(
        spans[:, 1, 2 * BLK - 1].reshape(head_count // 2, 2, 1), (head_count // 2, 2, 128)
    )
    grad_projected, grad_spans = attend_bwd(projected, grad_seq, log_totals, bias_tiles, far_bias)
    grad_out_weight = over_rows(attended, grad_part).astype(bf16)
    grad_out_weight = lax.psum_scatter(grad_out_weight, "gx", scatter_dimension=1, tiled=True)
    grad_out_weight = grad_out_weight.reshape(4, w_out.shape[0], shard)
    order = jnp.arange(4, dtype=jnp.int32) ^ z
    order = jnp.where(order == 1, 2, jnp.where(order == 2, 1, order))
    grad_out_weight = jnp.take(grad_out_weight, order, axis=0)
    grad_out_weight = lax.psum_scatter(grad_out_weight, "gy", scatter_dimension=0, tiled=True)[0].astype(f32)

    group_width = w_qkv.shape[2]
    grad_qkv = jnp.einsum("td,ctf->cdf", first_norm, grad_projected, preferred_element_type=f32).astype(bf16)
    grad_qkv = lax.psum_scatter(grad_qkv, "gx", scatter_dimension=1, tiled=True)
    grad_qkv = grad_qkv[:, :, :group_width].astype(f32) + swap_z(grad_qkv[:, :, group_width:], 2).astype(f32)

    grad_first = jnp.einsum("ctf,cdf->td", grad_projected, qkv_weight, preferred_element_type=f32)
    grad_first = grad_first.reshape(2, tok_dev, model_width)
    sent_first = lax.dynamic_index_in_dim(grad_first, 1 - half, 0, keepdims=False).astype(bf16)
    grad_first = lax.dynamic_index_in_dim(grad_first, half, 0, keepdims=False) + swap_z(sent_first, 1).astype(f32)
    normed_one, scale_one = normalize(inputs_float)
    grad_inputs, grad_gain_first = norm_back(grad_first, normed_one, scale_one, gain_first)
    grad_tokens = grad_hidden_state + grad_inputs

    grad_table = jnp.einsum(
        "hk,kb->bh", grad_spans.reshape(head_count, -1), picks.astype(f32), precision=lax.Precision.HIGHEST
    )
    grad_heads = jnp.zeros((bucket_count, 4, group_heads), f32)
    grad_heads = lax.dynamic_update_slice(grad_heads, grad_table[:, None, :group_heads], (0, z, 0))
    grad_heads = lax.dynamic_update_slice(grad_heads, grad_table[:, None, group_heads:], (0, z ^ 2, 0))
    grad_heads = grad_heads.reshape(8, bucket_count // 8, 4 * group_heads)
    route_sums = jnp.broadcast_to(jnp.sum(route, axis=0), (8, 1, expert_count))

    def wide(rows):
        return jnp.pad(rows, ((0, 0), (0, 0), (0, shard - rows.shape[2])))

    sums = jnp.concatenate(
        [
            grad_gain_first.reshape(8, 1, shard),
            grad_gain_second.reshape(8, 1, shard),
            grad_router_t.reshape(expert_count, 8, shard).transpose(1, 0, 2),
            wide(grad_heads),
            wide(route_sums),
            jnp.zeros((8, 1, shard), f32),
        ],
        axis=1,
    )
    sums = lax.psum_scatter(sums, "gx", scatter_dimension=0, tiled=True)
    sums = lax.psum(sums, "gy")[0]
    prob_sums = sums[22, :expert_count]
    loss = expert_count * jnp.sum(counts / (total_tokens * top_count) * (prob_sums / total_tokens))
    router_load = jnp.stack(
        [
            expert_count * counts / (total_tokens * top_count),
            expert_count * prob_sums / total_tokens,
        ],
        axis=0,
    )
    grad_rel_bias = lax.dynamic_slice(sums, (18, z * group_heads), (bucket_count // 8, group_heads))
    return (
        mixed.astype(bf16),
        loss,
        router_load,
        grad_tokens,
        sums[0],
        grad_qkv,
        grad_out_weight,
        grad_rel_bias,
        sums[1],
        sums[2:18].T,
        grad_inner,
        grad_outer,
    )


def solution(mesh):
    in_specs = (
        P(("gx", "gy"), None),
        P(("gx", "gy"), None),
        P("gx"),
        P(None, "gx", "gy"),
        P("gy", "gx"),
        P("gx", "gy"),
        P("gx"),
        P("gx", None),
        P("gy", "gx", None),
        P("gy", None, "gx"),
        P(("gx", "gy"), None),
    )
    out_specs = (
        P(("gx", "gy"), None),
        P(),
        P(),
        P(("gx", "gy"), None),
        P("gx"),
        P(None, "gx", "gy"),
        P("gy", "gx"),
        P("gx", "gy"),
        P("gx"),
        P("gx", None),
        P("gy", "gx", None),
        P("gy", None, "gx"),
    )
    return jax.shard_map(
        fast_device if fits_fast(mesh) else general_device, mesh=mesh, in_specs=in_specs, out_specs=out_specs, check_vma=False
    )
```

```python
import functools
import math

import jax
import jax.numpy as jnp
from jax import lax
from jax.experimental import pallas as pl
from jax.experimental.pallas import tpu as pltpu
from jax.sharding import PartitionSpec as P

LEN = 1024
BLK = 256
CAP = 80


bucket_edges = (12, 16, 23, 32, 46, 64, 91)
epsilon = 1e-06
loss_weight = 0.01
masked_score = -1e30


def bucket_of(offset):
    magnitude = jnp.abs(offset)
    far_bucket = 8 + sum(
        ((magnitude >= edge_value).astype(jnp.int32) for edge_value in bucket_edges)
    )
    return jnp.where(magnitude < 8, magnitude, far_bucket) + 16 * (offset > 0).astype(jnp.int32)


def normalize(values):
    row_scale = lax.rsqrt(jnp.mean(values * values, axis=-1, keepdims=True) + epsilon)
    return (values * row_scale, row_scale)


def norm_back(grad_out, normed, row_scale, gain_vector):
    grad_normed = grad_out * gain_vector
    grad_gain = jnp.sum(grad_out * normed, axis=0)
    grad_input = row_scale * (
        grad_normed - normed * jnp.mean(grad_normed * normed, axis=-1, keepdims=True)
    )
    return (grad_input, grad_gain)


def spread_offsets(along_offsets, row_count):
    head_count, span_width = along_offsets.shape
    key_count = span_width - row_count + 1
    tiled_rows = jnp.broadcast_to(
        along_offsets[:, None, :], (head_count, row_count, span_width)
    ).reshape(head_count, row_count * span_width)
    padded = jnp.pad(tiled_rows, ((0, 0), (0, row_count)))
    shaped = padded.reshape(head_count, row_count, span_width + 1)[:, :, :key_count]
    return shaped[:, :, ::-1]


def gather_offsets(score_grid, row_count):
    head_count = score_grid.shape[0]
    key_count = score_grid.shape[2]
    span_width = key_count + row_count - 1
    padded = jnp.pad(score_grid[:, :, ::-1], ((0, 0), (0, 0), (0, row_count)))
    flat_rows = padded.reshape(head_count, row_count * (key_count + row_count))[
        :, : row_count * span_width
    ]
    return jnp.sum(flat_rows.reshape(head_count, row_count, span_width), axis=1)


def offset_table(q_start, row_count, key_count, bucket_count):
    spot_index = jnp.arange(key_count + row_count - 1, dtype=jnp.int32)
    offsets = key_count - 1 - spot_index - q_start
    return (
        bucket_of(offsets)[:, None] == jnp.arange(bucket_count, dtype=jnp.int32)[None, :]
    ).astype(jnp.float32)


def block_scores(query_rows, key_rows, table_float, q_start):
    row_count = query_rows.shape[0]
    depth = query_rows.shape[2]
    key_count = key_rows.shape[0]
    picks_table = offset_table(q_start, row_count, key_count, table_float.shape[0])
    along_offsets = jnp.dot(picks_table, table_float, precision=lax.Precision.HIGHEST).T
    bias_grid = spread_offsets(along_offsets, row_count)
    scores = (
        jnp.einsum("qhd,khd->hqk", query_rows, key_rows, preferred_element_type=jnp.float32)
        / math.sqrt(depth)
        + bias_grid
    )
    query_pos = q_start + jnp.arange(row_count, dtype=jnp.int32)
    key_pos = jnp.arange(key_count, dtype=jnp.int32)
    allowed = key_pos[None, :] // BLK <= query_pos[:, None] // BLK
    return (jnp.where(allowed[None], scores, masked_score), picks_table)


def general_device(
    tokens, expert_ids, gain_attn, w_qkv, w_out, rel_bias, gain_ffn, router, w_in, w_down, cotangent
):
    shard_list = (gain_attn, w_qkv, w_out, rel_bias, gain_ffn, router, w_in, w_down)
    (
        gain_first,
        qkv_weight,
        out_weight,
        bias_table,
        gain_second,
        route_weight,
        inner_weight,
        outer_weight,
    ) = (
        lax.all_gather(shard_list[0], "gx", axis=0, tiled=True),
        lax.all_gather(shard_list[1], "gx", axis=1, tiled=True),
        lax.all_gather(shard_list[2], "gx", axis=1, tiled=True),
        lax.all_gather(shard_list[3], "gx", axis=0, tiled=True),
        lax.all_gather(shard_list[4], "gx", axis=0, tiled=True),
        lax.all_gather(shard_list[5], "gx", axis=0, tiled=True),
        lax.all_gather(shard_list[6], "gx", axis=1, tiled=True),
        lax.all_gather(shard_list[7], "gx", axis=2, tiled=True),
    )
    tok_dev = tokens.shape[0]
    count_x = lax.axis_size("gx")
    count_y = lax.axis_size("gy")
    total_tokens = tok_dev * count_x * count_y
    model_width = tokens.shape[1]
    expert_count = route_weight.shape[1]
    top_count = expert_ids.shape[1]
    local_experts = inner_weight.shape[0]
    head_count = bias_table.shape[1]
    head_width = qkv_weight.shape[2]
    depth = head_width // head_count
    q_rows = min(512, LEN)
    per_seq = LEN // q_rows
    inputs_float = tokens.astype(jnp.float32)
    normed_one, scale_one = normalize(inputs_float)
    first_norm = (normed_one * gain_first.astype(jnp.float32)).astype(jnp.bfloat16)
    group_rows = lax.all_gather(first_norm, "gy", axis=0, tiled=True)
    tok_group = group_rows.shape[0]
    seq_count = tok_group // LEN
    projected = jnp.einsum(
        "td,cdf->tcf", group_rows, qkv_weight, preferred_element_type=jnp.float32
    ).astype(jnp.bfloat16)
    projected = projected.reshape(tok_group, 3, head_count, depth)
    table_float = bias_table.astype(jnp.float32)

    def forward_block(item_index):
        seq_index = item_index // per_seq
        q_start = item_index % per_seq * q_rows
        query_rows = lax.dynamic_slice_in_dim(projected, seq_index * LEN + q_start, q_rows, 0)[:, 0]
        seq_rows = lax.dynamic_slice_in_dim(projected, seq_index * LEN, LEN, 0)
        scores, unused_picks = block_scores(query_rows, seq_rows[:, 1], table_float, q_start)
        row_max = jnp.max(scores, axis=-1, keepdims=True)
        expo_scores = jnp.exp(scores - row_max)
        row_total = jnp.sum(expo_scores, axis=-1, keepdims=True)
        soft_weights = (expo_scores / row_total).astype(jnp.bfloat16)
        block_out = jnp.einsum(
            "hqk,khd->qhd", soft_weights, seq_rows[:, 2], preferred_element_type=jnp.float32
        ).astype(jnp.bfloat16)
        return (block_out.reshape(q_rows, head_width), (row_max + jnp.log(row_total))[:, :, 0])

    attended, log_totals = lax.map(forward_block, jnp.arange(seq_count * per_seq, dtype=jnp.int32))
    attended = attended.reshape(tok_group, head_width)
    attn_sum = lax.psum_scatter(
        jnp.dot(attended, out_weight, preferred_element_type=jnp.float32).astype(jnp.bfloat16),
        "gy",
        scatter_dimension=0,
        tiled=True,
    ).astype(jnp.float32)
    hidden_state = inputs_float + attn_sum
    normed_two, scale_two = normalize(hidden_state)
    second_norm = (normed_two * gain_second.astype(jnp.float32)).astype(jnp.bfloat16)
    logits = jnp.dot(second_norm, route_weight, preferred_element_type=jnp.float32)
    route = jax.nn.softmax(logits, axis=-1)
    chosen = (
        expert_ids.reshape(-1)[:, None] == jnp.arange(expert_count, dtype=jnp.int32)[None, :]
    ).astype(jnp.int32)
    earlier = jnp.cumsum(chosen, axis=0) - chosen
    slot = jnp.sum(earlier * chosen, axis=-1).reshape(tok_dev, top_count)
    kept = (slot < CAP).astype(jnp.float32)
    counts, prob_sums = lax.psum(
        (jnp.sum(chosen, axis=0).astype(jnp.float32), jnp.sum(route, axis=0)), ("gx", "gy")
    )
    loss = expert_count * jnp.sum(counts / (total_tokens * top_count) * (prob_sums / total_tokens))
    router_load = jnp.stack(
        [
            expert_count * counts / (total_tokens * top_count),
            expert_count * prob_sums / total_tokens,
        ],
        axis=0,
    )
    slot_place = expert_ids * CAP + jnp.minimum(slot, CAP - 1)
    buffer_index = jnp.arange(expert_count * CAP, dtype=jnp.int32)[:, None, None]
    hit_table = (buffer_index == slot_place[None]).astype(jnp.float32) * kept[None]
    dispatch_matrix = jnp.sum(hit_table, axis=-1).astype(jnp.bfloat16)
    send_rows = jnp.dot(dispatch_matrix, second_norm, preferred_element_type=jnp.float32).astype(
        jnp.bfloat16
    )
    send_rows = send_rows.reshape(count_y, local_experts, CAP, model_width)
    received = lax.all_to_all(send_rows, "gy", split_axis=0, concat_axis=0, tiled=True)
    upper = jnp.einsum("slcd,ldf->slcf", received, inner_weight, preferred_element_type=jnp.float32)
    half_width = upper.shape[-1] // 2
    hidden_rows = (
        jax.nn.gelu(upper[..., :half_width], approximate=True) * upper[..., half_width:]
    ).astype(jnp.bfloat16)
    expert_out = jnp.einsum(
        "slcf,lfd->slcd", hidden_rows, outer_weight, preferred_element_type=jnp.float32
    ).astype(jnp.bfloat16)
    expert_out, upper, received = (expert_out, upper, received)
    returned = lax.all_to_all(expert_out, "gy", split_axis=0, concat_axis=0, tiled=True).reshape(
        expert_count * CAP, model_width
    )
    picked_rows = jnp.take(returned, slot_place, axis=0).astype(jnp.float32)
    gate_value = jnp.take_along_axis(route, expert_ids, axis=1) * kept
    mixed = hidden_state + jnp.sum(picked_rows * gate_value[:, :, None], axis=1)
    (
        gain_first,
        qkv_weight,
        out_weight,
        bias_table,
        gain_second,
        route_weight,
        inner_weight,
        outer_weight,
    ) = (
        lax.all_gather(shard_list[0], "gx", axis=0, tiled=True),
        lax.all_gather(shard_list[1], "gx", axis=1, tiled=True),
        lax.all_gather(shard_list[2], "gx", axis=1, tiled=True),
        lax.all_gather(shard_list[3], "gx", axis=0, tiled=True),
        lax.all_gather(shard_list[4], "gx", axis=0, tiled=True),
        lax.all_gather(shard_list[5], "gx", axis=0, tiled=True),
        lax.all_gather(shard_list[6], "gx", axis=1, tiled=True),
        lax.all_gather(shard_list[7], "gx", axis=2, tiled=True),
    )
    table_float = bias_table.astype(jnp.float32)
    grad_mixed = cotangent.astype(jnp.float32)
    grad_gate = kept * jnp.sum(grad_mixed[:, None, :] * picked_rows, axis=-1)
    gate_matrix = jnp.sum(hit_table * gate_value[None], axis=-1)
    grad_buffer = jnp.dot(gate_matrix, grad_mixed, precision=lax.Precision.HIGHEST).astype(
        jnp.bfloat16
    )
    grad_expert = lax.all_to_all(
        grad_buffer.reshape(count_y, local_experts, CAP, model_width),
        "gy",
        split_axis=0,
        concat_axis=0,
        tiled=True,
    )
    half_width = upper.shape[-1] // 2
    activated, pull_gelu = jax.vjp(
        lambda gate_part, up_part: jax.nn.gelu(gate_part, approximate=True) * up_part,
        upper[..., :half_width],
        upper[..., half_width:],
    )
    hidden_rows = activated.astype(jnp.bfloat16)
    grad_hidden = jnp.einsum(
        "slcd,lfd->slcf", grad_expert, outer_weight, preferred_element_type=jnp.float32
    )
    grad_outer = jnp.einsum(
        "slcf,slcd->lfd", hidden_rows, grad_expert, preferred_element_type=jnp.float32
    )
    grad_gate_part, grad_up_part = pull_gelu(grad_hidden)
    grad_upper = jnp.concatenate([grad_gate_part, grad_up_part], axis=-1).astype(jnp.bfloat16)
    grad_inner = jnp.einsum(
        "slcd,slcf->ldf", received, grad_upper, preferred_element_type=jnp.float32
    )
    grad_received = jnp.einsum(
        "slcf,ldf->slcd", grad_upper, inner_weight, preferred_element_type=jnp.float32
    ).astype(jnp.bfloat16)
    grad_copies = lax.all_to_all(
        grad_received, "gy", split_axis=0, concat_axis=0, tiled=True
    ).reshape(expert_count * CAP, model_width)
    grad_second = jnp.sum(
        jnp.take(grad_copies, slot_place, axis=0).astype(jnp.float32) * kept[:, :, None], axis=1
    )
    expert_hits = (expert_ids[:, :, None] == jnp.arange(expert_count, dtype=jnp.int32)).astype(
        jnp.float32
    )
    grad_route = (
        jnp.sum(grad_gate[:, :, None] * expert_hits, axis=1)
        + loss_weight * expert_count * (counts / (total_tokens * top_count)) / total_tokens
    )
    grad_logits = (
        route * (grad_route - jnp.sum(route * grad_route, axis=-1, keepdims=True))
    ).astype(jnp.bfloat16)
    grad_router = jnp.dot(second_norm.T, grad_logits, preferred_element_type=jnp.float32)
    grad_second = grad_second + jnp.dot(
        grad_logits, route_weight.T, preferred_element_type=jnp.float32
    )
    grad_hidden_state, grad_gain_second = norm_back(
        grad_second, normed_two, scale_two, gain_second.astype(jnp.float32)
    )
    grad_hidden_state = grad_mixed + grad_hidden_state
    piece_rows = lax.all_gather(grad_hidden_state.astype(jnp.bfloat16), "gy", axis=0, tiled=True)
    grad_out_weight = jnp.einsum(
        "tf,td->fd", attended, piece_rows, preferred_element_type=jnp.float32
    )
    update_rows = jnp.dot(piece_rows, out_weight.T, preferred_element_type=jnp.float32).astype(
        jnp.bfloat16
    )
    grad_out_weight, grad_attended = (grad_out_weight, update_rows)

    def backward_sequence(seq_index):
        seq_rows = lax.dynamic_slice_in_dim(projected, seq_index * LEN, LEN, 0)
        key_rows = seq_rows[:, 1]
        value_rows = seq_rows[:, 2]
        grad_keys = jnp.zeros((LEN, head_count, depth), jnp.float32)
        grad_values = jnp.zeros((LEN, head_count, depth), jnp.float32)
        grad_table = jnp.zeros(table_float.shape, jnp.float32)
        grad_queries = []
        for block_index in range(per_seq):
            q_start = block_index * q_rows
            query_rows = seq_rows[q_start : q_start + q_rows, 0]
            grad_out = lax.dynamic_slice_in_dim(
                grad_attended, seq_index * LEN + q_start, q_rows, 0
            ).reshape(q_rows, head_count, depth)
            scores, picks_table = block_scores(query_rows, key_rows, table_float, q_start)
            block_lse = log_totals[seq_index * per_seq + block_index]
            soft_probs = jnp.exp(scores - block_lse[:, :, None])
            grad_probs = jnp.einsum(
                "qhd,khd->hqk", grad_out, value_rows, preferred_element_type=jnp.float32
            )
            grad_scores = (
                soft_probs * (grad_probs - jnp.sum(soft_probs * grad_probs, axis=-1, keepdims=True))
            ).astype(jnp.bfloat16)
            grad_queries.append(
                jnp.einsum(
                    "hqk,khd->qhd", grad_scores, key_rows, preferred_element_type=jnp.float32
                )
                / math.sqrt(depth)
            )
            grad_keys = grad_keys + jnp.einsum(
                "hqk,qhd->khd", grad_scores, query_rows, preferred_element_type=jnp.float32
            ) / math.sqrt(depth)
            grad_values = grad_values + jnp.einsum(
                "hqk,qhd->khd",
                soft_probs.astype(jnp.bfloat16),
                grad_out,
                preferred_element_type=jnp.float32,
            )
            along_grads = gather_offsets(grad_scores.astype(jnp.float32), q_rows)
            grad_table = grad_table + jnp.dot(
                picks_table.T, along_grads.T, precision=lax.Precision.HIGHEST
            )
        stacked = jnp.stack(
            [jnp.concatenate(grad_queries, axis=0), grad_keys, grad_values], axis=1
        ).astype(jnp.bfloat16)
        return (stacked, grad_table)

    grad_projected, table_parts = lax.map(backward_sequence, jnp.arange(seq_count, dtype=jnp.int32))
    grad_projected = grad_projected.reshape(tok_group, 3, head_width)
    grad_bias_table = jnp.sum(table_parts, axis=0)
    grad_qkv_weight = jnp.einsum(
        "td,tcf->cdf", group_rows, grad_projected, preferred_element_type=jnp.float32
    )
    grad_slice = lax.slice_in_dim(grad_projected, 0, tok_dev * lax.axis_size("gy"), axis=0)
    grad_first = lax.psum_scatter(
        jnp.einsum(
            "tcf,cdf->td", grad_slice, qkv_weight, preferred_element_type=jnp.float32
        ).astype(jnp.bfloat16),
        "gy",
        scatter_dimension=0,
        tiled=True,
    ).astype(jnp.float32)
    grad_inputs, grad_gain_first = norm_back(
        grad_first, normed_one, scale_one, gain_first.astype(jnp.float32)
    )
    grad_tokens = grad_hidden_state + grad_inputs
    grad_gain_first, grad_gain_second, grad_router = (
        lax.psum(grad_gain_first.astype(jnp.bfloat16), "gy").astype(jnp.float32),
        lax.psum(grad_gain_second.astype(jnp.bfloat16), "gy").astype(jnp.float32),
        lax.psum(grad_router.astype(jnp.bfloat16), "gy").astype(jnp.float32),
    )
    summed_grads = (
        lax.psum_scatter(
            grad_gain_first.astype(jnp.bfloat16), "gx", scatter_dimension=0, tiled=True
        ).astype(jnp.float32),
        lax.psum_scatter(
            grad_qkv_weight.astype(jnp.bfloat16), "gx", scatter_dimension=1, tiled=True
        ).astype(jnp.float32),
        lax.psum_scatter(
            grad_out_weight.astype(jnp.bfloat16), "gx", scatter_dimension=1, tiled=True
        ).astype(jnp.float32),
        lax.psum_scatter(
            grad_bias_table.astype(jnp.bfloat16), "gx", scatter_dimension=0, tiled=True
        ).astype(jnp.float32),
        lax.psum_scatter(
            grad_gain_second.astype(jnp.bfloat16), "gx", scatter_dimension=0, tiled=True
        ).astype(jnp.float32),
        lax.psum_scatter(
            grad_router.astype(jnp.bfloat16), "gx", scatter_dimension=0, tiled=True
        ).astype(jnp.float32),
        lax.psum_scatter(
            grad_inner.astype(jnp.bfloat16), "gx", scatter_dimension=1, tiled=True
        ).astype(jnp.float32),
        lax.psum_scatter(
            grad_outer.astype(jnp.bfloat16), "gx", scatter_dimension=2, tiled=True
        ).astype(jnp.float32),
    )
    return (
        mixed.astype(jnp.bfloat16),
        loss,
        router_load,
        grad_tokens,
        summed_grads[0],
        summed_grads[1],
        summed_grads[2],
        summed_grads[3],
        summed_grads[4],
        summed_grads[5],
        summed_grads[6],
        summed_grads[7],
    )


def dot_nn(a, b):
    return lax.dot_general(a, b, (((1,), (0,)), ((), ())), preferred_element_type=jnp.float32)

def dot_nt(a, b):
    return lax.dot_general(a, b, (((1,), (1,)), ((), ())), preferred_element_type=jnp.float32)

def span_buckets():
    k = jnp.arange(2 * BLK, dtype=jnp.int32)
    return jnp.stack([bucket_of(BLK - k - BLK * d) for d in range(2)])

def attend_fwd_kernel(proj_ref, span_ref, out_ref, lse_ref, tile_ref):
    length = proj_ref.shape[1]
    blocks = length // BLK
    depth = 64
    lane = lax.broadcasted_iota(jnp.int32, (1, 2 * depth), 1)
    for h in range(2):
        for d in range(2):
            row = span_ref[h, d:d + 1, :]
            wide = jnp.broadcast_to(row, (BLK, 2 * BLK))
            turned = pltpu.roll(wide, 0, 1, stride=1, stride_axis=0)
            tile_ref[h, d] = turned[:, BLK:]
    far = [span_ref[h, 1:2, 2 * BLK - 1:2 * BLK] for h in range(2)]
    keys = proj_ref[1]
    values_t = proj_ref[2].T
    for block in range(blocks):
        rows = pl.ds(block * BLK, BLK)
        query = proj_ref[0, rows, :] * jnp.bfloat16(0.125)
        key_count = (block + 1) * BLK
        outs = []
        for h in range(2):
            picked = jnp.where((lane // depth) == h, query, jnp.bfloat16(0))
            scores = dot_nt(keys[:key_count], picked)
            parts = []
            for kb in range(block + 1):
                part = scores[kb * BLK:(kb + 1) * BLK]
                d = block - kb
                parts.append(part + (tile_ref[h, d] if d < 2 else far[h]))
            top = functools.reduce(jnp.maximum, [jnp.max(p, axis=0, keepdims=True) for p in parts])
            parts = [jnp.exp(p - top) for p in parts]
            total = functools.reduce(jnp.add, [jnp.sum(p, axis=0, keepdims=True) for p in parts])
            scale = 1.0 / total
            weights = jnp.concatenate([(p * scale).astype(jnp.bfloat16) for p in parts], axis=0)
            outs.append(dot_nn(values_t[h * depth:(h + 1) * depth, :key_count], weights))
            lse_ref[0, h:h + 1, rows] = top + jnp.log(total)
        out_ref[rows, :] = jnp.concatenate(outs, axis=0).T.astype(jnp.bfloat16)

def attend_fwd(proj, spans):
    _, length, width = proj.shape
    pairs = width // 128
    return pl.pallas_call(
        attend_fwd_kernel,
        grid=(pairs,),
        out_shape=(
            jax.ShapeDtypeStruct((length, width), jnp.bfloat16),
            jax.ShapeDtypeStruct((pairs, 2, length), jnp.float32),
            jax.ShapeDtypeStruct((2 * pairs, 2, BLK, BLK), jnp.float32),
        ),
        in_specs=[
            pl.BlockSpec((3, length, 128), lambda p: (0, 0, p)),
            pl.BlockSpec((2, 2, 2 * BLK), lambda p: (p, 0, 0)),
        ],
        out_specs=(
            pl.BlockSpec((length, 128), lambda p: (0, p)),
            pl.BlockSpec((1, 2, length), lambda p: (p, 0, 0)),
            pl.BlockSpec((2, 2, BLK, BLK), lambda p: (p, 0, 0, 0)),
        ),
        compiler_params=pltpu.CompilerParams(vmem_limit_bytes=48 * 2**20),
        name="attend_forward",
    )(proj, spans)

def attend_bwd_kernel(proj_ref, dout_ref, lse_ref, tile_ref, far_ref, dproj_ref, span_ref, dk_ref, dv_ref, near_ref):
    length = proj_ref.shape[1]
    blocks = length // BLK
    depth = 64
    lane = lax.broadcasted_iota(jnp.int32, (1, 2 * depth), 1)
    keys = proj_ref[1]
    values = proj_ref[2]
    keys_t = keys.T
    dk_ref[...] = jnp.zeros_like(dk_ref)
    dv_ref[...] = jnp.zeros_like(dv_ref)
    near_ref[...] = jnp.zeros_like(near_ref)
    far_sum = [jnp.zeros((1, BLK), jnp.float32) for h in range(2)]
    for block in range(blocks):
        rows = pl.ds(block * BLK, BLK)
        key_count = (block + 1) * BLK
        query = proj_ref[0, rows, :] * jnp.bfloat16(0.125)
        grad = dout_ref[rows, :]
        dq_parts = []
        dk_sum = None
        dv_sum = None
        for h in range(2):
            own = (lane // depth) == h
            query_h = jnp.where(own, query, jnp.bfloat16(0))
            grad_h = jnp.where(own, grad, jnp.bfloat16(0))
            scores = dot_nt(keys[:key_count], query_h)
            grad_p = dot_nt(values[:key_count], grad_h)
            lse = lse_ref[0, h:h + 1, rows]
            far = far_ref[0, h:h + 1, 0:1]
            probs = []
            delta = None
            for kb in range(block + 1):
                d = block - kb
                part = scores[kb * BLK:(kb + 1) * BLK]
                part = jnp.exp(part + ((tile_ref[h, d] - lse) if d < 2 else (far - lse)))
                probs.append(part)
                term = jnp.sum(part * grad_p[kb * BLK:(kb + 1) * BLK], axis=0, keepdims=True)
                delta = term if delta is None else delta + term
            ds = []
            for kb in range(block + 1):
                d = block - kb
                part = probs[kb] * (grad_p[kb * BLK:(kb + 1) * BLK] - delta)
                if d < 2:
                    near_ref[h, d] += part
                else:
                    far_sum[h] = far_sum[h] + jnp.sum(part, axis=0, keepdims=True)
                ds.append(part.astype(jnp.bfloat16))
            ds = jnp.concatenate(ds, axis=0)
            weights = jnp.concatenate([p.astype(jnp.bfloat16) for p in probs], axis=0)
            dv_h = dot_nn(weights, grad_h)
            dk_h = dot_nn(ds, query_h)
            dv_sum = dv_h if dv_sum is None else dv_sum + dv_h
            dk_sum = dk_h if dk_sum is None else dk_sum + dk_h
            dq_parts.append(dot_nn(keys_t[h * depth:(h + 1) * depth, :key_count], ds))
        dk_ref[:key_count] += dk_sum
        dv_ref[:key_count] += dv_sum
        dproj_ref[0, rows, :] = (jnp.concatenate(dq_parts, axis=0).T * 0.125).astype(jnp.bfloat16)
    dproj_ref[1] = dk_ref[...].astype(jnp.bfloat16)
    dproj_ref[2] = dv_ref[...].astype(jnp.bfloat16)
    flip = (
        lax.broadcasted_iota(jnp.int32, (BLK, BLK), 0) + lax.broadcasted_iota(jnp.int32, (BLK, BLK), 1) == BLK - 1
    ).astype(jnp.bfloat16)
    for h in range(2):
        for d in range(2):
            near = near_ref[h, d]
            near_high = near.astype(jnp.bfloat16)
            near_low = (near - near_high.astype(jnp.float32)).astype(jnp.bfloat16)
            flipped = dot_nn(flip, near_high) + dot_nn(flip, near_low)
            wide = jnp.concatenate([flipped, jnp.zeros((BLK, BLK), jnp.float32)], axis=1)
            turned = pltpu.roll(wide, 1, 1, stride=1, stride_axis=0)
            span_ref[h, d:d + 1, :] = jnp.sum(turned, axis=0, keepdims=True)
        lanes = lax.broadcasted_iota(jnp.int32, (1, 2 * BLK), 1)
        total = jnp.sum(far_sum[h], axis=1, keepdims=True)
        span_ref[h, 1:2, :] += jnp.where(lanes == 2 * BLK - 1, total, 0.0)

def attend_bwd(proj, dout, lse, tiles, far):
    _, length, width = proj.shape
    pairs = width // 128
    return pl.pallas_call(
        attend_bwd_kernel,
        grid=(pairs,),
        out_shape=(
            jax.ShapeDtypeStruct((3, length, width), jnp.bfloat16),
            jax.ShapeDtypeStruct((2 * pairs, 2, 2 * BLK), jnp.float32),
        ),
        in_specs=[
            pl.BlockSpec((3, length, 128), lambda p: (0, 0, p)),
            pl.BlockSpec((length, 128), lambda p: (0, p)),
            pl.BlockSpec((1, 2, length), lambda p: (p, 0, 0)),
            pl.BlockSpec((2, 2, BLK, BLK), lambda p: (p, 0, 0, 0)),
            pl.BlockSpec((1, 2, 128), lambda p: (p, 0, 0)),
        ],
        out_specs=(
            pl.BlockSpec((3, length, 128), lambda p: (0, 0, p)),
            pl.BlockSpec((2, 2, 2 * BLK), lambda p: (p, 0, 0)),
        ),
        scratch_shapes=[
            pltpu.VMEM((length, 128), jnp.float32),
            pltpu.VMEM((length, 128), jnp.float32),
            pltpu.VMEM((2, 2, BLK, BLK), jnp.float32),
        ],
        compiler_params=pltpu.CompilerParams(vmem_limit_bytes=48 * 2**20),
        name="attend_backward",
    )(proj, dout, lse, tiles, far)


AXES = ("gx", "gy")
MESH_ID = pl.DeviceIdType.MESH


def fits_fast(mesh):
    return mesh.shape["gx"] == 8 and mesh.shape["gy"] == 4


def places():
    x = lax.axis_index("gx")
    z = lax.axis_index("gy")
    core = x % 2
    chip = x // 2
    along_z = (z + 1 - 2 * (z % 2), (z + 2) % 4, 3 - z)
    chips = (chip + 1 - 2 * (chip % 2), (chip + 2) % 4, 3 - chip)
    return x, z, along_z, tuple(2 * other + core for other in chips), x + 1 - 2 * core


def gather_kernel(
    tok_ref, wq_ref, wo_ref, small_ref, seq_ref, wqs_ref, wos_ref, smalls_ref, send_sem, recv_sem, local_sem
):
    x, z, along_z, across, sibling = places()
    peers = [(x, other) for other in along_z] + [(other, z) for other in across] + [(sibling, z)]
    barrier = pltpu.get_barrier_semaphore()
    for peer in peers:
        pl.semaphore_signal(barrier, inc=1, device_id=peer, device_id_type=MESH_ID)
    pl.semaphore_wait(barrier, len(peers))
    started = []

    def send(source, target, device):
        index = len(started)
        copy = pltpu.make_async_remote_copy(
            src_ref=source,
            dst_ref=target,
            send_sem=send_sem.at[index],
            recv_sem=recv_sem.at[index],
            device_id=device,
            device_id_type=MESH_ID,
        )
        copy.start()
        started.append(copy)
        return copy

    depth = wq_ref.shape[1]
    width = wq_ref.shape[2]
    rows_out = wo_ref.shape[0]

    def qkv_part(owner, slot):
        return wqs_ref.at[:, pl.ds(pl.multiple_of(owner * depth, depth), depth), pl.ds(slot * width, width)]

    def out_part(owner, slot, slots):
        return wos_ref.at[
            pl.ds(slot * rows_out, slots * rows_out), pl.ds(pl.multiple_of(owner * depth, depth), depth)
        ]

    out_slots = (2, 1, 3)
    locals_started = []

    def keep(source, target):
        copy = pltpu.make_async_copy(source, target, local_sem.at[len(locals_started)])
        copy.start()
        locals_started.append(copy)
        return copy

    half = z % 2
    kept_wq = keep(wq_ref, qkv_part(x, 0))
    kept_wo = keep(wo_ref, out_part(x, 0, 1))
    kept_small = keep(small_ref, smalls_ref.at[0, x])
    keep(tok_ref, seq_ref.at[half])
    small_z = [send(small_ref, smalls_ref.at[j + 1, x], (x, along_z[j])) for j in range(3)]
    wq_z = send(wq_ref, qkv_part(x, 1), (x, along_z[1]))
    wo_z = [send(wo_ref, out_part(x, out_slots[j], 1), (x, along_z[j])) for j in range(3)]
    wq_first = [send(wq_ref, qkv_part(x, 0), (other, z)) for other in across + (sibling,)]
    send(tok_ref, seq_ref.at[half], (x, along_z[0]))
    kept_small.wait()
    for copy in small_z:
        copy.wait_recv()
    small_x = [send(smalls_ref.at[:, x], smalls_ref.at[:, x], (other, z)) for other in across + (sibling,)]
    wq_z.wait_recv()
    wq_second = [send(qkv_part(x, 1), qkv_part(x, 1), (other, z)) for other in across + (sibling,)]
    kept_wo.wait()
    for copy in wo_z:
        copy.wait_recv()
    wo_x = [send(out_part(x, 0, 4), out_part(x, 0, 4), (other, z)) for other in across + (sibling,)]
    waited = small_z + [wq_z] + wo_z
    for j in range(3):
        owner = across[j]
        small_x[j].wait_recv()
        send(smalls_ref.at[:, owner], smalls_ref.at[:, owner], (sibling, z))
        wq_first[j].wait_recv()
        send(qkv_part(owner, 0), qkv_part(owner, 0), (sibling, z))
        waited += [small_x[j], wq_first[j]]
    for j in range(3):
        owner = across[j]
        wq_second[j].wait_recv()
        send(qkv_part(owner, 1), qkv_part(owner, 1), (sibling, z))
        wo_x[j].wait_recv()
        send(out_part(owner, 0, 4), out_part(owner, 0, 4), (sibling, z))
        waited += [wq_second[j], wo_x[j]]
    for copy in started:
        if not any(copy is other for other in waited):
            copy.wait_recv()
    for copy in started:
        copy.wait_send()
    kept_wq.wait()
    locals_started[3].wait()


def gather_params(tokens, w_qkv, w_out, small):
    tok_dev, model_width = tokens.shape
    copies = 3 + 1 + 3 + 4 + 1 + 4 + 4 + 4 + 12
    anywhere = pl.BlockSpec(memory_space=pl.ANY)
    return pl.pallas_call(
        gather_kernel,
        out_shape=(
            jax.ShapeDtypeStruct((2, tok_dev, model_width), jnp.bfloat16),
            jax.ShapeDtypeStruct((3, model_width, 2 * w_qkv.shape[2]), jnp.bfloat16),
            jax.ShapeDtypeStruct((4 * w_out.shape[0], model_width), jnp.bfloat16),
            jax.ShapeDtypeStruct((4, 8) + small.shape, jnp.bfloat16),
        ),
        in_specs=[anywhere] * 4,
        out_specs=(anywhere,) * 4,
        scratch_shapes=[
            pltpu.SemaphoreType.DMA((copies,)),
            pltpu.SemaphoreType.DMA((copies,)),
            pltpu.SemaphoreType.DMA((4,)),
        ],
        compiler_params=pltpu.CompilerParams(collective_id=0, has_side_effects=True),
        name="gather_params",
    )(tokens, w_qkv, w_out, small)


def swap_z(values, step):
    return lax.ppermute(values, "gy", [(i, i ^ step) for i in range(4)])


def swap_core(values):
    return lax.ppermute(values, "gx", [(i, i ^ 1) for i in range(8)])


def exchange_chips(blocks):
    groups = [[2 * c + h for c in range(4)] for h in range(2)]
    return lax.all_to_all(blocks, "gx", 0, 0, axis_index_groups=groups, tiled=True)


def geglu(gate_part, up_part):
    return jax.nn.gelu(gate_part, approximate=True) * up_part


def expert_kernel(
    rows_ref, grads_ref, inner_ref, outer_ref,
    returned_ref, copies_ref, ginner_ref, gouter_ref, inner_in_ref, outer_in_ref, gouter_sum_ref,
    x_ref, x_t_ref, dy_ref, win_ref, wout_ref, upper_ref, total_ref, back_ref, hid_ref, dup_ref,
    stage_in_ref, stage_out_ref, add_in_ref, add_out_ref,
    row_send, row_recv, grad_send, grad_recv, out_send, out_recv, copy_send, copy_recv,
    w_send, w_recv, part_send, part_recv, gout_send, gout_recv, local_sem,
):
    x, z, _, across, sibling = places()
    core = x % 2
    chip = x // 2
    me = chip * 4 + z
    count, slots, width = x_ref.shape
    tokens = count * slots
    tiles = upper_ref.shape[0]
    half = upper_ref.shape[2] // 2
    hidden = tiles * half
    shard = width // 8
    chunk = tokens // 4
    f32, bf16 = jnp.float32, jnp.bfloat16

    spots = [lax.rem(me + k, count) for k in range(1, count)]
    peers = [(2 * (spot // 4) + core, spot % 4) for spot in spots]
    pair = (sibling, z)
    barrier = pltpu.get_barrier_semaphore()
    for peer in peers + [pair]:
        pl.semaphore_signal(barrier, inc=1, device_id=peer, device_id_type=MESH_ID)
    pl.semaphore_wait(barrier, len(peers) + 1)

    def remote(source, target, sems, index, device):
        return pltpu.make_async_remote_copy(
            src_ref=source, dst_ref=target, send_sem=sems[0].at[index], recv_sem=sems[1].at[index],
            device_id=device, device_id_type=MESH_ID,
        )

    def spread(source, target, sems):
        return [
            remote(source.at[spot], target.at[me], sems, k, peer)
            for k, (spot, peer) in enumerate(zip(spots, peers))
        ]

    def lanes_of(owner):
        return pl.ds(pl.multiple_of(owner * shard, shard), shard)

    row_copies = spread(rows_ref, x_ref, (row_send, row_recv))
    for copy in row_copies:
        copy.start()
    own_rows = pltpu.make_async_copy(rows_ref.at[me], x_ref.at[me], local_sem.at[0])
    own_rows.start()
    own_inner = pltpu.make_async_copy(inner_ref, win_ref.at[:, core], local_sem.at[1])
    own_inner.start()
    pair_inner = remote(inner_ref, win_ref.at[:, core], (w_send, w_recv), 0, pair)
    pair_inner.start()
    own_outer = pltpu.make_async_copy(outer_ref.at[chip], wout_ref.at[:, lanes_of(x)], local_sem.at[2])
    own_outer.start()
    outer_copies = [
        remote(outer_ref.at[device // 2], wout_ref.at[:, lanes_of(x)], (w_send, w_recv), 1 + j, (device, z))
        for j, device in enumerate(across)
    ]
    for copy in outer_copies:
        copy.start()
    own_grads = pltpu.make_async_copy(grads_ref.at[me], dy_ref.at[me], local_sem.at[3])
    own_grads.start()
    pair_outer = remote(outer_ref.at[chip], wout_ref.at[:, lanes_of(x)], (w_send, w_recv), 4, pair)
    pair_outer.start()
    pair_outer_more = []
    for j, device in enumerate(across):
        outer_copies[j].wait_recv()
        block = wout_ref.at[:, lanes_of(device)]
        copy = remote(block, block, (w_send, w_recv), 5 + j, pair)
        copy.start()
        pair_outer_more.append(copy)
    for copy in row_copies:
        copy.wait_send()
    grad_copies = spread(grads_ref, dy_ref, (grad_send, grad_recv))
    for copy in grad_copies:
        copy.start()
    own_rows.wait()
    own_inner.wait()
    own_outer.wait()
    pair_inner.wait()
    for copy in outer_copies:
        copy.wait_send()
    for copy in [pair_outer] + pair_outer_more:
        copy.wait()
    for copy in row_copies:
        copy.wait_recv()

    def cols(tile, part):
        return pl.ds(pl.multiple_of(part * hidden + tile * half, half), half)

    def weight(tile, part):
        return win_ref[:, :, :, cols(tile, part)].reshape(width, half)

    def outer_rows(tile):
        return wout_ref[pl.ds(pl.multiple_of(tile * half, half), half), :]

    blocks = count // 4
    total_ref[...] = jnp.zeros_like(total_ref)

    def forward(tile, carry):
        gate_weight, up_weight, down = weight(tile, 0), weight(tile, 1), outer_rows(tile)
        for m in range(4):
            here = pl.ds(m * chunk, chunk)
            rows = x_ref[m * blocks:(m + 1) * blocks].reshape(chunk, width)
            gate = dot_nn(rows, gate_weight)
            up = dot_nn(rows, up_weight)
            upper_ref[tile, here, :half] = gate.astype(bf16)
            upper_ref[tile, here, half:] = up.astype(bf16)
            total_ref[here, :] += dot_nn(geglu(gate, up).astype(bf16), down)
        return carry

    lax.fori_loop(0, tiles, forward, 0)
    for m in range(4):
        back_ref[0, m * blocks:(m + 1) * blocks] = (
            total_ref[pl.ds(m * chunk, chunk), :].astype(bf16).reshape(blocks, slots, width)
        )
    out_copies = spread(back_ref.at[0], returned_ref, (out_send, out_recv))
    for copy in out_copies:
        copy.start()
    own_out = pltpu.make_async_copy(back_ref.at[0, me], returned_ref.at[me], local_sem.at[4])
    own_out.start()
    x_t_ref[...] = x_ref[...].reshape(tokens, width).T.reshape(x_t_ref.shape)

    own_grads.wait()
    for copy in grad_copies:
        copy.wait()
    total_ref[...] = jnp.zeros_like(total_ref)

    def backward(tile, carry):
        gate_weight, up_weight, down = weight(tile, 0), weight(tile, 1), outer_rows(tile)
        for m in range(4):
            here = pl.ds(m * chunk, chunk)
            grads = dy_ref[m * blocks:(m + 1) * blocks].reshape(chunk, width)
            grad_hidden = dot_nt(grads, down)
            gate = upper_ref[tile, here, :half].astype(f32)
            up = upper_ref[tile, here, half:].astype(f32)
            inner = 0.7978845608028654 * gate * (1.0 + 0.044715 * gate * gate)
            bent = jnp.tanh(inner)
            lifted = 0.5 * (1.0 + bent)
            active = gate * lifted
            slope = lifted + 0.5 * gate * (1.0 - bent * bent) * (
                0.7978845608028654 * (1.0 + 3 * 0.044715 * gate * gate)
            )
            hid_ref[here, :] = (active * up).astype(bf16)
            grad_gate = (grad_hidden * up * slope).astype(bf16)
            grad_up = (grad_hidden * active).astype(bf16)
            dup_ref[here, :half] = grad_gate
            dup_ref[here, half:] = grad_up
            total_ref[here, :] += dot_nt(grad_gate, gate_weight) + dot_nt(grad_up, up_weight)
        grad_upper = dup_ref[...]
        other = x_t_ref[:, 1 - core].reshape(width // 2, tokens)
        part_slot = lax.rem(tile, 2)

        @pl.when(tile >= 2)
        def _():
            for copy in parts(tile - 2):
                copy.wait_send()

        stage_in_ref[part_slot] = dot_nn(other, grad_upper).astype(bf16).reshape(4, shard, 2 * half)
        grad_down = dot_nn(hid_ref[...].T, dy_ref[...].reshape(tokens, width))
        for j in range(4):
            low = grad_down[:, (2 * j) * shard:(2 * j + 1) * shard].astype(bf16)
            high = grad_down[:, (2 * j + 1) * shard:(2 * j + 2) * shard].astype(bf16)
            stage_out_ref[part_slot, :, j * shard:(j + 1) * shard] = jnp.where(core == 0, high, low)
            upper_ref[tile, pl.ds(width // 2, half), j * shard:(j + 1) * shard] = jnp.where(core == 0, low, high)
        for copy in parts(tile):
            copy.start()
        own = x_t_ref[:, core].reshape(width // 2, tokens)
        upper_ref[tile, pl.ds(0, width // 2), :] = dot_nn(own, grad_upper).astype(bf16)
        return carry

    def parts(tile):
        slot = lax.rem(tile, 2)
        return [
            remote(stage_in_ref.at[slot], inner_in_ref.at[tile], (part_send, part_recv), 2 * tile, pair),
            remote(stage_out_ref.at[slot], outer_in_ref.at[tile], (part_send, part_recv), 2 * tile + 1, pair),
        ]

    lax.fori_loop(0, tiles, backward, 0)
    for m in range(4):
        back_ref[1, m * blocks:(m + 1) * blocks] = (
            total_ref[pl.ds(m * chunk, chunk), :].astype(bf16).reshape(blocks, slots, width)
        )
    copy_copies = spread(back_ref.at[1], copies_ref, (copy_send, copy_recv))
    for copy in copy_copies:
        copy.start()
    own_copy = pltpu.make_async_copy(back_ref.at[1, me], copies_ref.at[me], local_sem.at[5])
    own_copy.start()

    for tile in (tiles - 2, tiles - 1):
        for copy in parts(tile):
            copy.wait_send()

    def join(tile, carry):
        for copy in parts(tile):
            copy.wait_recv()
        loads = [
            pltpu.make_async_copy(inner_in_ref.at[tile], add_in_ref, local_sem.at[6]),
            pltpu.make_async_copy(outer_in_ref.at[tile], add_out_ref, local_sem.at[7]),
        ]
        for copy in loads:
            copy.start()
        for copy in loads:
            copy.wait()
        own = upper_ref[tile, pl.ds(0, width // 2), :].astype(f32)
        add_in_ref[...] = (own + add_in_ref[...].reshape(width // 2, 2 * half).astype(f32)).astype(bf16).reshape(
            add_in_ref.shape
        )
        own = upper_ref[tile, pl.ds(width // 2, half), :].astype(f32)
        add_out_ref[...] = (own + add_out_ref[...].astype(f32)).astype(bf16)
        stores = [
            pltpu.make_async_copy(add_in_ref.at[:, :, pl.ds(part * half, half)], ginner_ref.at[:, :, cols(tile, part)], local_sem.at[6 + part])
            for part in range(2)
        ] + [
            pltpu.make_async_copy(
                add_out_ref, gouter_sum_ref.at[pl.ds(pl.multiple_of(tile * half, half), half), :], local_sem.at[8]
            )
        ]
        for copy in stores:
            copy.start()
        for copy in stores:
            copy.wait()
        return carry

    lax.fori_loop(0, tiles, join, 0)

    def sums_of(owner):
        return gouter_sum_ref.at[:, pl.ds(pl.multiple_of((owner // 2) * shard, shard), shard)]

    own_gout = pltpu.make_async_copy(sums_of(x), gouter_ref.at[chip], local_sem.at[9])
    own_gout.start()
    gout_copies = [
        remote(sums_of(device), gouter_ref.at[chip], (gout_send, gout_recv), j, (device, z))
        for j, device in enumerate(across)
    ]
    for copy in gout_copies:
        copy.start()
    own_out.wait()
    own_copy.wait()
    own_gout.wait()
    for copy in out_copies + copy_copies + gout_copies:
        copy.wait()


def run_experts(rows, grads, inner, outer):
    count, slots, width = rows.shape
    tokens = count * slots
    hidden = outer.shape[1]
    half = 256
    tiles = hidden // half
    shard = width // 8
    bf16 = jnp.bfloat16
    anywhere = pl.BlockSpec(memory_space=pl.ANY)
    sems = [pltpu.SemaphoreType.DMA((count,))] * 8 + [
        pltpu.SemaphoreType.DMA((8,)),
        pltpu.SemaphoreType.DMA((8,)),
        pltpu.SemaphoreType.DMA((2 * tiles,)),
        pltpu.SemaphoreType.DMA((2 * tiles,)),
        pltpu.SemaphoreType.DMA((3,)),
        pltpu.SemaphoreType.DMA((3,)),
        pltpu.SemaphoreType.DMA((10,)),
    ]
    outs = pl.pallas_call(
        expert_kernel,
        out_shape=(
            jax.ShapeDtypeStruct(rows.shape, bf16),
            jax.ShapeDtypeStruct(rows.shape, bf16),
            jax.ShapeDtypeStruct(inner.shape, bf16),
            jax.ShapeDtypeStruct(outer.shape, bf16),
            jax.ShapeDtypeStruct((tiles, 4, shard, 2 * half), bf16),
            jax.ShapeDtypeStruct((tiles, half, 4 * shard), bf16),
            jax.ShapeDtypeStruct((hidden, 4 * shard), bf16),
        ),
        in_specs=[anywhere] * 4,
        out_specs=(anywhere,) * 7,
        scratch_shapes=[
            pltpu.VMEM((count, slots, width), bf16),
            pltpu.VMEM((4, 2, shard, tokens), bf16),
            pltpu.VMEM((count, slots, width), bf16),
            pltpu.VMEM((4, 2, shard, 2 * hidden), bf16),
            pltpu.VMEM((hidden, width), bf16),
            pltpu.VMEM((tiles, tokens, 2 * half), bf16),
            pltpu.VMEM((tokens, width), jnp.float32),
            pltpu.VMEM((2, count, slots, width), bf16),
            pltpu.VMEM((tokens, half), bf16),
            pltpu.VMEM((tokens, 2 * half), bf16),
            pltpu.VMEM((2, 4, shard, 2 * half), bf16),
            pltpu.VMEM((2, half, 4 * shard), bf16),
            pltpu.VMEM((4, shard, 2 * half), bf16),
            pltpu.VMEM((half, 4 * shard), bf16),
        ] + sems,
        compiler_params=pltpu.CompilerParams(
            collective_id=1, has_side_effects=True, vmem_limit_bytes=63 * 2**20
        ),
        cost_estimate=pl.CostEstimate(
            flops=6 * 3 * tokens * width * hidden, bytes_accessed=60 * 2**20, transcendentals=tokens * hidden
        ),
        name="run_experts",
    )(rows, grads, inner, outer)
    return outs[:4]


def fast_device(
    tokens, expert_ids, gain_attn, w_qkv, w_out, rel_bias, gain_ffn, router, w_in, w_down, cotangent
):
    f32, bf16 = jnp.float32, jnp.bfloat16
    z = lax.axis_index("gy")
    half = z % 2
    tok_dev, model_width = tokens.shape
    total_tokens = tok_dev * 32
    expert_count = router.shape[1]
    top_count = expert_ids.shape[1]
    shard = model_width // 8
    bucket_count = rel_bias.shape[0] * 8
    group_heads = rel_bias.shape[1]

    expert_row = jnp.arange(expert_count, dtype=jnp.int32)
    hits = [(expert_ids[:, c][:, None] == expert_row[None]) for c in range(top_count)]
    both = sum(hit.astype(bf16) for hit in hits)
    steps = jnp.arange(tok_dev, dtype=jnp.int32)
    lower = (steps[None, :] < steps[:, None]).astype(bf16)
    before = jnp.dot(lower, both, preferred_element_type=f32)
    slots = [jnp.sum(jnp.where(hit, before, 0.0), axis=1).astype(jnp.int32) for hit in hits]
    kept = [slot < CAP for slot in slots]
    local_counts = jnp.sum(both.astype(f32), axis=0)
    count_high = jnp.floor(local_counts / 32.0)
    count_low = local_counts - 32.0 * count_high

    def lanes(rows):
        return jnp.pad(rows.astype(bf16), ((0, 0), (0, shard - rows.shape[1])))

    small = jnp.concatenate(
        [
            router.T,
            gain_attn[None],
            gain_ffn[None],
            lanes(rel_bias),
            lanes(count_high[None]),
            lanes(count_low[None]),
            jnp.zeros((8, shard), bf16),
        ],
        axis=0,
    )
    seq_tokens, qkv_weight, out_weight, smalls = gather_params(tokens, w_qkv, w_out, small)

    inner_own, seq_tokens = lax.optimization_barrier((w_in, seq_tokens))
    inner_own = exchange_chips(inner_own)

    own_small = smalls[0]
    router_t = own_small[:, :16].transpose(1, 0, 2).reshape(expert_count, model_width)
    gain_first = own_small[:, 16].reshape(model_width).astype(f32)
    gain_second = own_small[:, 17].reshape(model_width).astype(f32)
    bias_table = jnp.concatenate(
        [smalls[j, :, 18:22, :group_heads].reshape(bucket_count, group_heads) for j in (0, 2)], axis=1
    )
    all_counts = smalls[:, :, 22:24, :expert_count].astype(f32).sum(axis=(0, 1))
    counts = 32.0 * all_counts[0] + all_counts[1]

    seq_float = seq_tokens.reshape(2 * tok_dev, model_width).astype(f32)
    seq_normed, _ = normalize(seq_float)
    first_norm = (seq_normed * gain_first).astype(bf16)
    projected = jnp.einsum("td,cdf->ctf", first_norm, qkv_weight, preferred_element_type=f32).astype(bf16)
    picks = (span_buckets().reshape(-1)[:, None] == jnp.arange(bucket_count, dtype=jnp.int32)).astype(bf16)
    spans = jnp.einsum("kb,bh->hk", picks, bias_table, preferred_element_type=f32)
    head_count = spans.shape[0]
    spans = spans.reshape(head_count, 2, 2 * BLK)
    attended, log_totals, bias_tiles = attend_fwd(projected, spans)
    attended = attended.reshape(2, tok_dev, -1)
    attended_other = swap_z(lax.dynamic_index_in_dim(attended, 1 - half, 0, keepdims=False), 1)
    attended = jnp.concatenate(
        [lax.dynamic_index_in_dim(attended, half, 0, keepdims=False), attended_other], axis=1
    )
    inputs_float = tokens.astype(f32)
    hidden_state = inputs_float + jnp.dot(attended, out_weight, preferred_element_type=f32)
    normed_two, scale_two = normalize(hidden_state)
    second_norm = (normed_two * gain_second).astype(bf16)
    logits = lax.dot_general(second_norm, router_t, (((1,), (1,)), ((), ())), preferred_element_type=f32)
    route = jax.nn.softmax(logits, axis=-1)

    gates = [
        jnp.where(keep, jnp.sum(jnp.where(hit, route, 0.0), axis=1), 0.0) for hit, keep in zip(hits, kept)
    ]
    spots = [
        jnp.where(keep, ((expert_ids[:, c] % 4) * 4 + expert_ids[:, c] // 4) * CAP + slots[c], -1)
        for c, keep in enumerate(kept)
    ]
    buffer_rows = jnp.arange(expert_count * CAP, dtype=jnp.int32)
    marks = [buffer_rows[:, None] == spot[None] for spot in spots]
    dispatch = (marks[0] | marks[1]).astype(bf16)
    gate_rows = jnp.sum(
        jnp.where(marks[0], gates[0][None], 0.0) + jnp.where(marks[1], gates[1][None], 0.0), axis=1
    )
    send_rows = jnp.dot(dispatch, second_norm, preferred_element_type=f32).astype(bf16)
    grad_rows = (jnp.dot(dispatch, cotangent, preferred_element_type=f32) * gate_rows[:, None]).astype(bf16)
    returned, grad_copies, grad_inner, grad_outer = run_experts(
        send_rows.reshape(expert_count, CAP, model_width),
        grad_rows.reshape(expert_count, CAP, model_width),
        inner_own,
        w_down,
    )
    returned = returned.reshape(-1, model_width)
    grad_copies = grad_copies.reshape(-1, model_width)
    grad_inner = exchange_chips(grad_inner).astype(f32)
    grad_outer = grad_outer.astype(f32)

    def over_rows(left, right):
        return lax.dot_general(left, right, (((0,), (0,)), ((), ())), preferred_element_type=f32)

    picked = [
        lax.dot_general(mark.astype(bf16), returned, (((0,), (0,)), ((), ())), preferred_element_type=f32)
        for mark in marks
    ]
    mixed = hidden_state + (picked[0] * gates[0][:, None] + picked[1] * gates[1][:, None])
    grad_mixed = cotangent.astype(f32)
    grad_gates = [jnp.sum(grad_mixed * rows, axis=1) for rows in picked]
    grad_second = over_rows(dispatch, grad_copies)
    grad_route = sum(
        jnp.where(hit, grad_gate[:, None], 0.0) for hit, grad_gate in zip(hits, grad_gates)
    ) + loss_weight * expert_count * (counts / (total_tokens * top_count)) / total_tokens
    grad_logits = (
        route * (grad_route - jnp.sum(route * grad_route, axis=-1, keepdims=True))
    ).astype(bf16)
    grad_router_t = over_rows(grad_logits, second_norm)
    grad_second = grad_second + jnp.dot(grad_logits, router_t, preferred_element_type=f32)
    grad_hidden_state, grad_gain_second = norm_back(grad_second, normed_two, scale_two, gain_second)
    grad_hidden_state = grad_mixed + grad_hidden_state

    grad_part = grad_hidden_state.astype(bf16)
    grad_attended = lax.dot_general(
        grad_part, out_weight, (((1,), (1,)), ((), ())), preferred_element_type=f32
    ).astype(bf16)
    own_width = grad_attended.shape[1] // 2
    grad_own = grad_attended[:, :own_width]
    grad_other = swap_z(grad_attended[:, own_width:], 1)
    grad_seq = jnp.where(
        half == 0,
        jnp.concatenate([grad_own, grad_other], axis=0),
        jnp.concatenate([grad_other, grad_own], axis=0),
    )
    far_bias = jnp.broadcast_to(
        spans[:, 1, 2 * BLK - 1].reshape(head_count // 2, 2, 1), (head_count // 2, 2, 128)
    )
    grad_projected, grad_spans = attend_bwd(projected, grad_seq, log_totals, bias_tiles, far_bias)
    grad_out_weight = over_rows(attended, grad_part).astype(bf16)
    grad_out_weight = lax.psum_scatter(grad_out_weight, "gx", scatter_dimension=1, tiled=True)
    grad_out_weight = grad_out_weight.reshape(4, w_out.shape[0], shard)
    order = jnp.arange(4, dtype=jnp.int32) ^ z
    order = jnp.where(order == 1, 2, jnp.where(order == 2, 1, order))
    grad_out_weight = jnp.take(grad_out_weight, order, axis=0)
    grad_out_weight = lax.psum_scatter(grad_out_weight, "gy", scatter_dimension=0, tiled=True)[0].astype(f32)

    group_width = w_qkv.shape[2]
    grad_qkv = jnp.einsum("td,ctf->cdf", first_norm, grad_projected, preferred_element_type=f32).astype(bf16)
    grad_qkv = lax.psum_scatter(grad_qkv, "gx", scatter_dimension=1, tiled=True)
    grad_qkv = grad_qkv[:, :, :group_width].astype(f32) + swap_z(grad_qkv[:, :, group_width:], 2).astype(f32)

    grad_first = jnp.einsum("ctf,cdf->td", grad_projected, qkv_weight, preferred_element_type=f32)
    grad_first = grad_first.reshape(2, tok_dev, model_width)
    sent_first = lax.dynamic_index_in_dim(grad_first, 1 - half, 0, keepdims=False).astype(bf16)
    grad_first = lax.dynamic_index_in_dim(grad_first, half, 0, keepdims=False) + swap_z(sent_first, 1).astype(f32)
    normed_one, scale_one = normalize(inputs_float)
    grad_inputs, grad_gain_first = norm_back(grad_first, normed_one, scale_one, gain_first)
    grad_tokens = grad_hidden_state + grad_inputs

    grad_table = jnp.einsum(
        "hk,kb->bh", grad_spans.reshape(head_count, -1), picks.astype(f32), precision=lax.Precision.HIGHEST
    )
    grad_heads = jnp.zeros((bucket_count, 4, group_heads), f32)
    grad_heads = lax.dynamic_update_slice(grad_heads, grad_table[:, None, :group_heads], (0, z, 0))
    grad_heads = lax.dynamic_update_slice(grad_heads, grad_table[:, None, group_heads:], (0, z ^ 2, 0))
    grad_heads = grad_heads.reshape(8, bucket_count // 8, 4 * group_heads)
    route_sums = jnp.broadcast_to(jnp.sum(route, axis=0), (8, 1, expert_count))

    def wide(rows):
        return jnp.pad(rows, ((0, 0), (0, 0), (0, shard - rows.shape[2])))

    sums = jnp.concatenate(
        [
            grad_gain_first.reshape(8, 1, shard),
            grad_gain_second.reshape(8, 1, shard),
            grad_router_t.reshape(expert_count, 8, shard).transpose(1, 0, 2),
            wide(grad_heads),
            wide(route_sums),
            jnp.zeros((8, 1, shard), f32),
        ],
        axis=1,
    )
    sums = lax.psum_scatter(sums, "gx", scatter_dimension=0, tiled=True)
    sums = lax.psum(sums, "gy")[0]
    prob_sums = sums[22, :expert_count]
    loss = expert_count * jnp.sum(counts / (total_tokens * top_count) * (prob_sums / total_tokens))
    router_load = jnp.stack(
        [
            expert_count * counts / (total_tokens * top_count),
            expert_count * prob_sums / total_tokens,
        ],
        axis=0,
    )
    grad_rel_bias = lax.dynamic_slice(sums, (18, z * group_heads), (bucket_count // 8, group_heads))
    return (
        mixed.astype(bf16),
        loss,
        router_load,
        grad_tokens,
        sums[0],
        grad_qkv,
        grad_out_weight,
        grad_rel_bias,
        sums[1],
        sums[2:18].T,
        grad_inner,
        grad_outer,
    )


def solution(mesh):
    in_specs = (
        P(("gx", "gy"), None),
        P(("gx", "gy"), None),
        P("gx"),
        P(None, "gx", "gy"),
        P("gy", "gx"),
        P("gx", "gy"),
        P("gx"),
        P("gx", None),
        P("gy", "gx", None),
        P("gy", None, "gx"),
        P(("gx", "gy"), None),
    )
    out_specs = (
        P(("gx", "gy"), None),
        P(),
        P(),
        P(("gx", "gy"), None),
        P("gx"),
        P(None, "gx", "gy"),
        P("gy", "gx"),
        P("gx", "gy"),
        P("gx"),
        P("gx", None),
        P("gy", "gx", None),
        P("gy", None, "gx"),
    )
    return jax.shard_map(
        fast_device if fits_fast(mesh) else general_device, mesh=mesh, in_specs=in_specs, out_specs=out_specs, check_vma=False
    )
```

```python
import functools
import math

import jax
import jax.numpy as jnp
from jax import lax
from jax.experimental import pallas as pl
from jax.experimental.pallas import tpu as pltpu
from jax.sharding import PartitionSpec as P

LEN = 1024
BLK = 256
CAP = 80


bucket_edges = (12, 16, 23, 32, 46, 64, 91)
epsilon = 1e-06
loss_weight = 0.01
masked_score = -1e30


def bucket_of(offset):
    magnitude = jnp.abs(offset)
    far_bucket = 8 + sum(
        ((magnitude >= edge_value).astype(jnp.int32) for edge_value in bucket_edges)
    )
    return jnp.where(magnitude < 8, magnitude, far_bucket) + 16 * (offset > 0).astype(jnp.int32)


def normalize(values):
    row_scale = lax.rsqrt(jnp.mean(values * values, axis=-1, keepdims=True) + epsilon)
    return (values * row_scale, row_scale)


def norm_back(grad_out, normed, row_scale, gain_vector):
    grad_normed = grad_out * gain_vector
    grad_gain = jnp.sum(grad_out * normed, axis=0)
    grad_input = row_scale * (
        grad_normed - normed * jnp.mean(grad_normed * normed, axis=-1, keepdims=True)
    )
    return (grad_input, grad_gain)


def spread_offsets(along_offsets, row_count):
    head_count, span_width = along_offsets.shape
    key_count = span_width - row_count + 1
    tiled_rows = jnp.broadcast_to(
        along_offsets[:, None, :], (head_count, row_count, span_width)
    ).reshape(head_count, row_count * span_width)
    padded = jnp.pad(tiled_rows, ((0, 0), (0, row_count)))
    shaped = padded.reshape(head_count, row_count, span_width + 1)[:, :, :key_count]
    return shaped[:, :, ::-1]


def gather_offsets(score_grid, row_count):
    head_count = score_grid.shape[0]
    key_count = score_grid.shape[2]
    span_width = key_count + row_count - 1
    padded = jnp.pad(score_grid[:, :, ::-1], ((0, 0), (0, 0), (0, row_count)))
    flat_rows = padded.reshape(head_count, row_count * (key_count + row_count))[
        :, : row_count * span_width
    ]
    return jnp.sum(flat_rows.reshape(head_count, row_count, span_width), axis=1)


def offset_table(q_start, row_count, key_count, bucket_count):
    spot_index = jnp.arange(key_count + row_count - 1, dtype=jnp.int32)
    offsets = key_count - 1 - spot_index - q_start
    return (
        bucket_of(offsets)[:, None] == jnp.arange(bucket_count, dtype=jnp.int32)[None, :]
    ).astype(jnp.float32)


def block_scores(query_rows, key_rows, table_float, q_start):
    row_count = query_rows.shape[0]
    depth = query_rows.shape[2]
    key_count = key_rows.shape[0]
    picks_table = offset_table(q_start, row_count, key_count, table_float.shape[0])
    along_offsets = jnp.dot(picks_table, table_float, precision=lax.Precision.HIGHEST).T
    bias_grid = spread_offsets(along_offsets, row_count)
    scores = (
        jnp.einsum("qhd,khd->hqk", query_rows, key_rows, preferred_element_type=jnp.float32)
        / math.sqrt(depth)
        + bias_grid
    )
    query_pos = q_start + jnp.arange(row_count, dtype=jnp.int32)
    key_pos = jnp.arange(key_count, dtype=jnp.int32)
    allowed = key_pos[None, :] // BLK <= query_pos[:, None] // BLK
    return (jnp.where(allowed[None], scores, masked_score), picks_table)


def general_device(
    tokens, expert_ids, gain_attn, w_qkv, w_out, rel_bias, gain_ffn, router, w_in, w_down, cotangent
):
    shard_list = (gain_attn, w_qkv, w_out, rel_bias, gain_ffn, router, w_in, w_down)
    (
        gain_first,
        qkv_weight,
        out_weight,
        bias_table,
        gain_second,
        route_weight,
        inner_weight,
        outer_weight,
    ) = (
        lax.all_gather(shard_list[0], "gx", axis=0, tiled=True),
        lax.all_gather(shard_list[1], "gx", axis=1, tiled=True),
        lax.all_gather(shard_list[2], "gx", axis=1, tiled=True),
        lax.all_gather(shard_list[3], "gx", axis=0, tiled=True),
        lax.all_gather(shard_list[4], "gx", axis=0, tiled=True),
        lax.all_gather(shard_list[5], "gx", axis=0, tiled=True),
        lax.all_gather(shard_list[6], "gx", axis=1, tiled=True),
        lax.all_gather(shard_list[7], "gx", axis=2, tiled=True),
    )
    tok_dev = tokens.shape[0]
    count_x = lax.axis_size("gx")
    count_y = lax.axis_size("gy")
    total_tokens = tok_dev * count_x * count_y
    model_width = tokens.shape[1]
    expert_count = route_weight.shape[1]
    top_count = expert_ids.shape[1]
    local_experts = inner_weight.shape[0]
    head_count = bias_table.shape[1]
    head_width = qkv_weight.shape[2]
    depth = head_width // head_count
    q_rows = min(512, LEN)
    per_seq = LEN // q_rows
    inputs_float = tokens.astype(jnp.float32)
    normed_one, scale_one = normalize(inputs_float)
    first_norm = (normed_one * gain_first.astype(jnp.float32)).astype(jnp.bfloat16)
    group_rows = lax.all_gather(first_norm, "gy", axis=0, tiled=True)
    tok_group = group_rows.shape[0]
    seq_count = tok_group // LEN
    projected = jnp.einsum(
        "td,cdf->tcf", group_rows, qkv_weight, preferred_element_type=jnp.float32
    ).astype(jnp.bfloat16)
    projected = projected.reshape(tok_group, 3, head_count, depth)
    table_float = bias_table.astype(jnp.float32)

    def forward_block(item_index):
        seq_index = item_index // per_seq
        q_start = item_index % per_seq * q_rows
        query_rows = lax.dynamic_slice_in_dim(projected, seq_index * LEN + q_start, q_rows, 0)[:, 0]
        seq_rows = lax.dynamic_slice_in_dim(projected, seq_index * LEN, LEN, 0)
        scores, unused_picks = block_scores(query_rows, seq_rows[:, 1], table_float, q_start)
        row_max = jnp.max(scores, axis=-1, keepdims=True)
        expo_scores = jnp.exp(scores - row_max)
        row_total = jnp.sum(expo_scores, axis=-1, keepdims=True)
        soft_weights = (expo_scores / row_total).astype(jnp.bfloat16)
        block_out = jnp.einsum(
            "hqk,khd->qhd", soft_weights, seq_rows[:, 2], preferred_element_type=jnp.float32
        ).astype(jnp.bfloat16)
        return (block_out.reshape(q_rows, head_width), (row_max + jnp.log(row_total))[:, :, 0])

    attended, log_totals = lax.map(forward_block, jnp.arange(seq_count * per_seq, dtype=jnp.int32))
    attended = attended.reshape(tok_group, head_width)
    attn_sum = lax.psum_scatter(
        jnp.dot(attended, out_weight, preferred_element_type=jnp.float32).astype(jnp.bfloat16),
        "gy",
        scatter_dimension=0,
        tiled=True,
    ).astype(jnp.float32)
    hidden_state = inputs_float + attn_sum
    normed_two, scale_two = normalize(hidden_state)
    second_norm = (normed_two * gain_second.astype(jnp.float32)).astype(jnp.bfloat16)
    logits = jnp.dot(second_norm, route_weight, preferred_element_type=jnp.float32)
    route = jax.nn.softmax(logits, axis=-1)
    chosen = (
        expert_ids.reshape(-1)[:, None] == jnp.arange(expert_count, dtype=jnp.int32)[None, :]
    ).astype(jnp.int32)
    earlier = jnp.cumsum(chosen, axis=0) - chosen
    slot = jnp.sum(earlier * chosen, axis=-1).reshape(tok_dev, top_count)
    kept = (slot < CAP).astype(jnp.float32)
    counts, prob_sums = lax.psum(
        (jnp.sum(chosen, axis=0).astype(jnp.float32), jnp.sum(route, axis=0)), ("gx", "gy")
    )
    loss = expert_count * jnp.sum(counts / (total_tokens * top_count) * (prob_sums / total_tokens))
    router_load = jnp.stack(
        [
            expert_count * counts / (total_tokens * top_count),
            expert_count * prob_sums / total_tokens,
        ],
        axis=0,
    )
    slot_place = expert_ids * CAP + jnp.minimum(slot, CAP - 1)
    buffer_index = jnp.arange(expert_count * CAP, dtype=jnp.int32)[:, None, None]
    hit_table = (buffer_index == slot_place[None]).astype(jnp.float32) * kept[None]
    dispatch_matrix = jnp.sum(hit_table, axis=-1).astype(jnp.bfloat16)
    send_rows = jnp.dot(dispatch_matrix, second_norm, preferred_element_type=jnp.float32).astype(
        jnp.bfloat16
    )
    send_rows = send_rows.reshape(count_y, local_experts, CAP, model_width)
    received = lax.all_to_all(send_rows, "gy", split_axis=0, concat_axis=0, tiled=True)
    upper = jnp.einsum("slcd,ldf->slcf", received, inner_weight, preferred_element_type=jnp.float32)
    half_width = upper.shape[-1] // 2
    hidden_rows = (
        jax.nn.gelu(upper[..., :half_width], approximate=True) * upper[..., half_width:]
    ).astype(jnp.bfloat16)
    expert_out = jnp.einsum(
        "slcf,lfd->slcd", hidden_rows, outer_weight, preferred_element_type=jnp.float32
    ).astype(jnp.bfloat16)
    expert_out, upper, received = (expert_out, upper, received)
    returned = lax.all_to_all(expert_out, "gy", split_axis=0, concat_axis=0, tiled=True).reshape(
        expert_count * CAP, model_width
    )
    picked_rows = jnp.take(returned, slot_place, axis=0).astype(jnp.float32)
    gate_value = jnp.take_along_axis(route, expert_ids, axis=1) * kept
    mixed = hidden_state + jnp.sum(picked_rows * gate_value[:, :, None], axis=1)
    (
        gain_first,
        qkv_weight,
        out_weight,
        bias_table,
        gain_second,
        route_weight,
        inner_weight,
        outer_weight,
    ) = (
        lax.all_gather(shard_list[0], "gx", axis=0, tiled=True),
        lax.all_gather(shard_list[1], "gx", axis=1, tiled=True),
        lax.all_gather(shard_list[2], "gx", axis=1, tiled=True),
        lax.all_gather(shard_list[3], "gx", axis=0, tiled=True),
        lax.all_gather(shard_list[4], "gx", axis=0, tiled=True),
        lax.all_gather(shard_list[5], "gx", axis=0, tiled=True),
        lax.all_gather(shard_list[6], "gx", axis=1, tiled=True),
        lax.all_gather(shard_list[7], "gx", axis=2, tiled=True),
    )
    table_float = bias_table.astype(jnp.float32)
    grad_mixed = cotangent.astype(jnp.float32)
    grad_gate = kept * jnp.sum(grad_mixed[:, None, :] * picked_rows, axis=-1)
    gate_matrix = jnp.sum(hit_table * gate_value[None], axis=-1)
    grad_buffer = jnp.dot(gate_matrix, grad_mixed, precision=lax.Precision.HIGHEST).astype(
        jnp.bfloat16
    )
    grad_expert = lax.all_to_all(
        grad_buffer.reshape(count_y, local_experts, CAP, model_width),
        "gy",
        split_axis=0,
        concat_axis=0,
        tiled=True,
    )
    half_width = upper.shape[-1] // 2
    activated, pull_gelu = jax.vjp(
        lambda gate_part, up_part: jax.nn.gelu(gate_part, approximate=True) * up_part,
        upper[..., :half_width],
        upper[..., half_width:],
    )
    hidden_rows = activated.astype(jnp.bfloat16)
    grad_hidden = jnp.einsum(
        "slcd,lfd->slcf", grad_expert, outer_weight, preferred_element_type=jnp.float32
    )
    grad_outer = jnp.einsum(
        "slcf,slcd->lfd", hidden_rows, grad_expert, preferred_element_type=jnp.float32
    )
    grad_gate_part, grad_up_part = pull_gelu(grad_hidden)
    grad_upper = jnp.concatenate([grad_gate_part, grad_up_part], axis=-1).astype(jnp.bfloat16)
    grad_inner = jnp.einsum(
        "slcd,slcf->ldf", received, grad_upper, preferred_element_type=jnp.float32
    )
    grad_received = jnp.einsum(
        "slcf,ldf->slcd", grad_upper, inner_weight, preferred_element_type=jnp.float32
    ).astype(jnp.bfloat16)
    grad_copies = lax.all_to_all(
        grad_received, "gy", split_axis=0, concat_axis=0, tiled=True
    ).reshape(expert_count * CAP, model_width)
    grad_second = jnp.sum(
        jnp.take(grad_copies, slot_place, axis=0).astype(jnp.float32) * kept[:, :, None], axis=1
    )
    expert_hits = (expert_ids[:, :, None] == jnp.arange(expert_count, dtype=jnp.int32)).astype(
        jnp.float32
    )
    grad_route = (
        jnp.sum(grad_gate[:, :, None] * expert_hits, axis=1)
        + loss_weight * expert_count * (counts / (total_tokens * top_count)) / total_tokens
    )
    grad_logits = (
        route * (grad_route - jnp.sum(route * grad_route, axis=-1, keepdims=True))
    ).astype(jnp.bfloat16)
    grad_router = jnp.dot(second_norm.T, grad_logits, preferred_element_type=jnp.float32)
    grad_second = grad_second + jnp.dot(
        grad_logits, route_weight.T, preferred_element_type=jnp.float32
    )
    grad_hidden_state, grad_gain_second = norm_back(
        grad_second, normed_two, scale_two, gain_second.astype(jnp.float32)
    )
    grad_hidden_state = grad_mixed + grad_hidden_state
    piece_rows = lax.all_gather(grad_hidden_state.astype(jnp.bfloat16), "gy", axis=0, tiled=True)
    grad_out_weight = jnp.einsum(
        "tf,td->fd", attended, piece_rows, preferred_element_type=jnp.float32
    )
    update_rows = jnp.dot(piece_rows, out_weight.T, preferred_element_type=jnp.float32).astype(
        jnp.bfloat16
    )
    grad_out_weight, grad_attended = (grad_out_weight, update_rows)

    def backward_sequence(seq_index):
        seq_rows = lax.dynamic_slice_in_dim(projected, seq_index * LEN, LEN, 0)
        key_rows = seq_rows[:, 1]
        value_rows = seq_rows[:, 2]
        grad_keys = jnp.zeros((LEN, head_count, depth), jnp.float32)
        grad_values = jnp.zeros((LEN, head_count, depth), jnp.float32)
        grad_table = jnp.zeros(table_float.shape, jnp.float32)
        grad_queries = []
        for block_index in range(per_seq):
            q_start = block_index * q_rows
            query_rows = seq_rows[q_start : q_start + q_rows, 0]
            grad_out = lax.dynamic_slice_in_dim(
                grad_attended, seq_index * LEN + q_start, q_rows, 0
            ).reshape(q_rows, head_count, depth)
            scores, picks_table = block_scores(query_rows, key_rows, table_float, q_start)
            block_lse = log_totals[seq_index * per_seq + block_index]
            soft_probs = jnp.exp(scores - block_lse[:, :, None])
            grad_probs = jnp.einsum(
                "qhd,khd->hqk", grad_out, value_rows, preferred_element_type=jnp.float32
            )
            grad_scores = (
                soft_probs * (grad_probs - jnp.sum(soft_probs * grad_probs, axis=-1, keepdims=True))
            ).astype(jnp.bfloat16)
            grad_queries.append(
                jnp.einsum(
                    "hqk,khd->qhd", grad_scores, key_rows, preferred_element_type=jnp.float32
                )
                / math.sqrt(depth)
            )
            grad_keys = grad_keys + jnp.einsum(
                "hqk,qhd->khd", grad_scores, query_rows, preferred_element_type=jnp.float32
            ) / math.sqrt(depth)
            grad_values = grad_values + jnp.einsum(
                "hqk,qhd->khd",
                soft_probs.astype(jnp.bfloat16),
                grad_out,
                preferred_element_type=jnp.float32,
            )
            along_grads = gather_offsets(grad_scores.astype(jnp.float32), q_rows)
            grad_table = grad_table + jnp.dot(
                picks_table.T, along_grads.T, precision=lax.Precision.HIGHEST
            )
        stacked = jnp.stack(
            [jnp.concatenate(grad_queries, axis=0), grad_keys, grad_values], axis=1
        ).astype(jnp.bfloat16)
        return (stacked, grad_table)

    grad_projected, table_parts = lax.map(backward_sequence, jnp.arange(seq_count, dtype=jnp.int32))
    grad_projected = grad_projected.reshape(tok_group, 3, head_width)
    grad_bias_table = jnp.sum(table_parts, axis=0)
    grad_qkv_weight = jnp.einsum(
        "td,tcf->cdf", group_rows, grad_projected, preferred_element_type=jnp.float32
    )
    grad_slice = lax.slice_in_dim(grad_projected, 0, tok_dev * lax.axis_size("gy"), axis=0)
    grad_first = lax.psum_scatter(
        jnp.einsum(
            "tcf,cdf->td", grad_slice, qkv_weight, preferred_element_type=jnp.float32
        ).astype(jnp.bfloat16),
        "gy",
        scatter_dimension=0,
        tiled=True,
    ).astype(jnp.float32)
    grad_inputs, grad_gain_first = norm_back(
        grad_first, normed_one, scale_one, gain_first.astype(jnp.float32)
    )
    grad_tokens = grad_hidden_state + grad_inputs
    grad_gain_first, grad_gain_second, grad_router = (
        lax.psum(grad_gain_first.astype(jnp.bfloat16), "gy").astype(jnp.float32),
        lax.psum(grad_gain_second.astype(jnp.bfloat16), "gy").astype(jnp.float32),
        lax.psum(grad_router.astype(jnp.bfloat16), "gy").astype(jnp.float32),
    )
    summed_grads = (
        lax.psum_scatter(
            grad_gain_first.astype(jnp.bfloat16), "gx", scatter_dimension=0, tiled=True
        ).astype(jnp.float32),
        lax.psum_scatter(
            grad_qkv_weight.astype(jnp.bfloat16), "gx", scatter_dimension=1, tiled=True
        ).astype(jnp.float32),
        lax.psum_scatter(
            grad_out_weight.astype(jnp.bfloat16), "gx", scatter_dimension=1, tiled=True
        ).astype(jnp.float32),
        lax.psum_scatter(
            grad_bias_table.astype(jnp.bfloat16), "gx", scatter_dimension=0, tiled=True
        ).astype(jnp.float32),
        lax.psum_scatter(
            grad_gain_second.astype(jnp.bfloat16), "gx", scatter_dimension=0, tiled=True
        ).astype(jnp.float32),
        lax.psum_scatter(
            grad_router.astype(jnp.bfloat16), "gx", scatter_dimension=0, tiled=True
        ).astype(jnp.float32),
        lax.psum_scatter(
            grad_inner.astype(jnp.bfloat16), "gx", scatter_dimension=1, tiled=True
        ).astype(jnp.float32),
        lax.psum_scatter(
            grad_outer.astype(jnp.bfloat16), "gx", scatter_dimension=2, tiled=True
        ).astype(jnp.float32),
    )
    return (
        mixed.astype(jnp.bfloat16),
        loss,
        router_load,
        grad_tokens,
        summed_grads[0],
        summed_grads[1],
        summed_grads[2],
        summed_grads[3],
        summed_grads[4],
        summed_grads[5],
        summed_grads[6],
        summed_grads[7],
    )


def dot_nn(a, b):
    return lax.dot_general(a, b, (((1,), (0,)), ((), ())), preferred_element_type=jnp.float32)

def dot_nt(a, b):
    return lax.dot_general(a, b, (((1,), (1,)), ((), ())), preferred_element_type=jnp.float32)

def span_buckets():
    k = jnp.arange(2 * BLK, dtype=jnp.int32)
    return jnp.stack([bucket_of(BLK - k - BLK * d) for d in range(2)])

AXES = ("gx", "gy")
MESH_ID = pl.DeviceIdType.MESH


def fits_fast(mesh):
    return mesh.shape["gx"] == 8 and mesh.shape["gy"] == 4


def places():
    x = lax.axis_index("gx")
    z = lax.axis_index("gy")
    core = x % 2
    chip = x // 2
    along_z = (z + 1 - 2 * (z % 2), (z + 2) % 4, 3 - z)
    chips = (chip + 1 - 2 * (chip % 2), (chip + 2) % 4, 3 - chip)
    return x, z, along_z, tuple(2 * other + core for other in chips), x + 1 - 2 * core


def attend_front(pair, proj_ref, span_ref, tile_ref, attended_ref, lse_ref, kept_ref):
    length = proj_ref.shape[1]
    blocks = length // BLK
    depth = 64
    wide = 2 * depth
    here = slice(pair * wide, (pair + 1) * wide)
    lane = lax.broadcasted_iota(jnp.int32, (1, wide), 1)
    for h in range(2):
        for d in range(2):
            row = span_ref[d, 2 * pair + h:2 * pair + h + 1, :]
            spread = jnp.broadcast_to(row, (BLK, 2 * BLK))
            turned = pltpu.roll(spread, 0, 1, stride=1, stride_axis=0)
            tile_ref[h, d] = turned[:, BLK:]
            kept_ref[2 * pair + h, d] = turned[:, BLK:].astype(jnp.bfloat16)
    far = [span_ref[1, 2 * pair + h:2 * pair + h + 1, 2 * BLK - 1:2 * BLK] for h in range(2)]
    keys = proj_ref[1, :, here]
    values_t = proj_ref[2, :, here].T
    for block in range(blocks):
        rows = pl.ds(block * BLK, BLK)
        query = proj_ref[0, rows, here] * jnp.bfloat16(0.125)
        key_count = (block + 1) * BLK
        outs = []
        for h in range(2):
            picked = jnp.where((lane // depth) == h, query, jnp.bfloat16(0))
            scores = dot_nt(keys[:key_count], picked)
            parts = []
            for kb in range(block + 1):
                part = scores[kb * BLK:(kb + 1) * BLK]
                d = block - kb
                parts.append(part + (tile_ref[h, d] if d < 2 else far[h]))
            top = functools.reduce(jnp.maximum, [jnp.max(p, axis=0, keepdims=True) for p in parts])
            parts = [jnp.exp(p - top) for p in parts]
            total = functools.reduce(jnp.add, [jnp.sum(p, axis=0, keepdims=True) for p in parts])
            scale = 1.0 / total
            weights = jnp.concatenate([(p * scale).astype(jnp.bfloat16) for p in parts], axis=0)
            outs.append(dot_nn(values_t[h * depth:(h + 1) * depth, :key_count], weights))
            lse_ref[pair, h:h + 1, rows] = top + jnp.log(total)
        attended_ref[rows, here] = jnp.concatenate(outs, axis=0).T.astype(jnp.bfloat16)


def front_kernel(
    tok_ref, wq_ref, wo_ref, small_ref, inner_ref, grads_ref, picks_ref,
    seq_out, wqs_out, wos_out, smalls_out, proj_ref, att_ref, lse_ref, kept_ref, inner_a_ref, inner_b_ref, far_ref,
    seq_ref, wqs_ref, wos_ref, smalls_ref, normed_ref, attended_ref, got_ref, span_ref, tile_ref,
    send_sem, recv_sem, local_sem, out_sem,
):
    x, z, along_z, across, sibling = places()
    half = z % 2
    f32, bf16 = jnp.float32, jnp.bfloat16
    peers = [(x, other) for other in along_z] + [(other, z) for other in across] + [(sibling, z)]
    far_peers = [(device, plane) for plane in along_z[1:] for device in (x,) + across]
    peers += [peer for n, peer in enumerate(far_peers) if n % 4]
    barrier = pltpu.get_barrier_semaphore()
    for peer in peers:
        pl.semaphore_signal(barrier, inc=1, device_id=peer, device_id_type=MESH_ID)
    depth = wq_ref.shape[1]
    group = wq_ref.shape[2]
    rows_out = wo_ref.shape[0]
    rows, width = tok_ref.shape

    def qkv_part(owner, slot):
        return wqs_ref.at[:, pl.ds(pl.multiple_of(owner * depth, depth), depth), pl.ds(slot * group, group)]

    def out_part(owner, slot, slots):
        return wos_ref.at[
            pl.ds(slot * rows_out, slots * rows_out), pl.ds(pl.multiple_of(owner * depth, depth), depth)
        ]

    keeps = [
        pltpu.make_async_copy(source, target, local_sem.at[n])
        for n, (source, target) in enumerate(
            ((small_ref, smalls_ref.at[0, x]), (wo_ref, out_part(x, 0, 1)), (wq_ref, qkv_part(x, 0)),
             (tok_ref, seq_ref.at[half]))
        )
    ]
    for copy in keeps:
        copy.start()
    pl.semaphore_wait(barrier, len(peers))
    started = []

    def send(source, target, device):
        index = len(started)
        copy = pltpu.make_async_remote_copy(
            src_ref=source, dst_ref=target, send_sem=send_sem.at[index], recv_sem=recv_sem.at[index],
            device_id=device, device_id_type=MESH_ID,
        )
        copy.start()
        started.append(copy)
        return copy

    out_slots = (2, 1, 3)
    near = across + (sibling,)
    small_z = [send(small_ref, smalls_ref.at[j + 1, x], (x, along_z[j])) for j in range(3)]
    wq_z = send(wq_ref, qkv_part(x, 1), (x, along_z[1]))
    wq_first = [send(wq_ref, qkv_part(x, 0), (other, z)) for other in near]
    tok_z = send(tok_ref, seq_ref.at[half], (x, along_z[0]))
    wo_z = [send(wo_ref, out_part(x, out_slots[j], 1), (x, along_z[j])) for j in range(3)]
    keeps[0].wait()
    for copy in small_z:
        copy.wait_recv()
    small_x = [send(smalls_ref.at[:, x], smalls_ref.at[:, x], (other, z)) for other in near]
    wq_z.wait_recv()
    wq_second = [send(qkv_part(x, 1), qkv_part(x, 1), (other, z)) for other in near]
    far_copies = [
        send(grads_ref.at[(device // 2) * 4 + plane], far_ref.at[n // 4, x // 2], (device, plane))
        for n, (device, plane) in enumerate(far_peers)
    ]
    small_on = []
    first_on = []
    for j in range(3):
        owner = across[j]
        small_x[j].wait_recv()
        small_on.append(send(smalls_ref.at[:, owner], smalls_ref.at[:, owner], (sibling, z)))
        wq_first[j].wait_recv()
        first_on.append(send(qkv_part(owner, 0), qkv_part(owner, 0), (sibling, z)))
    for copy in [small_x[3], wq_first[3]] + small_on + first_on:
        copy.wait_recv()
    for copy in keeps[1:]:
        copy.wait()
    inner_copies = [
        send(inner_ref.at[device // 2], target, (device, z))
        for device, target in zip(across[:2], (inner_a_ref, inner_b_ref))
    ]

    own_smalls = [smalls_ref[0, g].astype(f32) for g in range(8)]
    gain = jnp.concatenate([part[16:17, :] for part in own_smalls], axis=1)
    heads = span_ref.shape[1] // 2
    lanes = lax.broadcasted_iota(jnp.int32, (1, depth), 1)
    table = jnp.concatenate([part[18:22, :] for part in own_smalls], axis=0)
    other_table = jnp.concatenate([smalls_ref[2, g].astype(f32)[18:22, :] for g in range(8)], axis=0)
    table = jnp.where(lanes < heads, table, pltpu.roll(other_table, heads, 1))
    table = jnp.where(lanes < 2 * heads, table, 0.0)
    table = jnp.concatenate([table, jnp.zeros((depth - table.shape[0], depth), f32)], axis=0)
    table = table.T[:2 * heads, :].astype(bf16)
    for d in range(2):
        span_ref[d] = dot_nt(table, picks_ref[d])
    step = rows // 2

    def norm(side, i):
        normed, _ = normalize(seq_ref[side, i * step:(i + 1) * step, :].astype(f32))
        here = pl.ds(pl.multiple_of(side * rows + i * step, step), step)
        normed_ref[here, :] = (normed * gain).astype(bf16)

    for i in range(2):
        norm(half, i)
    tok_z.wait_recv()
    for i in range(2):
        norm(1 - half, i)

    def project(slot):
        here = slice(slot * group, (slot + 1) * group)
        for c in range(3):
            proj_ref[c, :, here] = dot_nn(normed_ref[...], wqs_ref[c, :, here]).astype(bf16)

    def attend(pair):
        attend_front(pair, proj_ref, span_ref, tile_ref, attended_ref, lse_ref, kept_ref)

    def exchange(slot):
        here = pl.ds(slot * group, group)
        there = pl.ds(pl.multiple_of((1 - half) * rows, rows), rows)
        return send(attended_ref.at[there, here], got_ref.at[:, here], (x, along_z[0]))

    project(0)
    for copy in wo_z:
        copy.wait_recv()
    wo_x = [send(out_part(x, 0, 4), out_part(x, 0, 4), (other, z)) for other in near]
    second_on = []
    for j in range(3):
        owner = across[j]
        wq_second[j].wait_recv()
        second_on.append(send(qkv_part(owner, 1), qkv_part(owner, 1), (sibling, z)))
    attend(0)
    wo_on = []
    for j in range(3):
        owner = across[j]
        wo_x[j].wait_recv()
        wo_on.append(send(out_part(owner, 0, 4), out_part(owner, 0, 4), (sibling, z)))
    attend(1)
    got_0 = exchange(0)
    for copy in [wq_second[3]] + second_on:
        copy.wait_recv()
    project(1)
    outs = [
        pltpu.make_async_copy(source, target, out_sem.at[n])
        for n, (source, target) in enumerate(((seq_ref, seq_out), (smalls_ref, smalls_out), (wqs_ref, wqs_out)))
    ]
    for copy in outs:
        copy.start()
    attend(2)
    attend(3)
    got_1 = exchange(1)
    for copy in [wo_x[3]] + wo_on:
        copy.wait_recv()
    outs.append(pltpu.make_async_copy(wos_ref, wos_out, out_sem.at[3]))
    outs[3].start()
    own = pl.ds(pl.multiple_of(half * rows, rows), rows)
    att_ref[:, :2 * group] = attended_ref[own, :]
    for copy in (got_0, got_1):
        copy.wait_recv()
    att_ref[:, 2 * group:] = got_ref[...]
    for copy in inner_copies + far_copies:
        copy.wait_recv()
    for copy in started:
        copy.wait_send()
    for copy in outs:
        copy.wait()


def run_front(tokens, w_qkv, w_out, small, w_in, grad_rows, picks):
    rows, width = tokens.shape
    group = w_qkv.shape[2]
    f32, bf16 = jnp.float32, jnp.bfloat16
    heads = 2 * group // 64
    anywhere = pl.BlockSpec(memory_space=pl.ANY)
    inside = pl.BlockSpec(memory_space=pltpu.VMEM)
    seq = (2, rows, width)
    wqs = (3, width, 2 * group)
    wos = (width, width)
    smalls = (4, 8) + small.shape
    copies_count = 3 + 1 + 4 + 1 + 3 + 4 + 4 + 3 + 3 + 4 + 3 + 3 + 2 + 2 + 8
    return pl.pallas_call(
        front_kernel,
        out_shape=(
            jax.ShapeDtypeStruct(seq, bf16),
            jax.ShapeDtypeStruct(wqs, bf16),
            jax.ShapeDtypeStruct(wos, bf16),
            jax.ShapeDtypeStruct(smalls, bf16),
            jax.ShapeDtypeStruct((3, 2 * rows, 2 * group), bf16),
            jax.ShapeDtypeStruct((rows, width), bf16),
            jax.ShapeDtypeStruct((heads // 2, 2, 2 * rows), f32),
            jax.ShapeDtypeStruct((heads, 2, BLK, BLK), bf16),
            jax.ShapeDtypeStruct(w_in.shape[1:], bf16),
            jax.ShapeDtypeStruct(w_in.shape[1:], bf16),
            jax.ShapeDtypeStruct((2, 4) + grad_rows.shape[1:], bf16),
        ),
        in_specs=[anywhere] * 6 + [inside],
        out_specs=(anywhere,) * 4 + (inside,) * 4 + (anywhere,) * 3,
        scratch_shapes=[
            pltpu.VMEM(seq, bf16),
            pltpu.VMEM(wqs, bf16),
            pltpu.VMEM(wos, bf16),
            pltpu.VMEM(smalls, bf16),
            pltpu.VMEM((2 * rows, width), bf16),
            pltpu.VMEM((2 * rows, 2 * group), bf16),
            pltpu.VMEM((rows, 2 * group), bf16),
            pltpu.VMEM((2, heads, 2 * BLK), f32),
            pltpu.VMEM((2, 2, BLK, BLK), f32),
            pltpu.SemaphoreType.DMA((copies_count,)),
            pltpu.SemaphoreType.DMA((copies_count,)),
            pltpu.SemaphoreType.DMA((4,)),
            pltpu.SemaphoreType.DMA((4,)),
        ],
        compiler_params=pltpu.CompilerParams(
            collective_id=0, has_side_effects=True, vmem_limit_bytes=56 * 2**20
        ),
        cost_estimate=pl.CostEstimate(flops=60 * 10**9, bytes_accessed=30 * 2**20, transcendentals=0),
        name="run_front",
    )(tokens, w_qkv, w_out, small, w_in, grad_rows, picks)


def swap_z(values, step):
    return lax.ppermute(values, "gy", [(i, i ^ step) for i in range(4)])


def exchange_chips(blocks):
    groups = [[2 * c + h for c in range(4)] for h in range(2)]
    return lax.all_to_all(blocks, "gx", 0, 0, axis_index_groups=groups, tiled=True)


def expert_kernel(
    rows_ref, gates_ref, grads_ref, far_ref, inner_ref, inner_a_ref, inner_b_ref, outer_ref,
    returned_ref, copies_ref, ginner_ref, gouter_ref, inner_in_ref,
    x_ref, x_t_ref, dy_ref, gates_in_ref, win_ref, wout_ref, upper_ref, hid_ref, out_ref, back_ref,
    stage_in_ref, stage_out_ref, add_in_ref, outer_in_ref,
    row_send, row_recv, gate_send, gate_recv, out_send, out_recv, copy_send, copy_recv,
    grad_send, grad_recv, w_send, w_recv, part_send, part_recv, gout_send, gout_recv, local_sem, join_sem,
):
    x, z, along_z, across, sibling = places()
    core = x % 2
    chip = x // 2
    me = chip * 4 + z
    _, _, slots, width = x_ref.shape
    chunk = 4 * slots
    tokens = 4 * chunk
    hidden = hid_ref.shape[1]
    half = stage_out_ref.shape[2]
    tiles = hidden // half
    shard = width // 8
    f32, bf16 = jnp.float32, jnp.bfloat16
    planes = (z,) + along_z
    chips = (chip,) + tuple(device // 2 for device in across)
    pair = (sibling, z)

    peers = [(m, k) for m in range(4) for k in range(4) if m or k]
    barrier = pltpu.get_barrier_semaphore()
    for m, k in peers:
        pl.semaphore_signal(
            barrier, inc=1, device_id=(2 * chips[k] + core, planes[m]), device_id_type=MESH_ID
        )
    pl.semaphore_signal(barrier, inc=1, device_id=pair, device_id_type=MESH_ID)
    pl.semaphore_wait(barrier, len(peers) + 1)

    def remote(source, target, sems, index, device):
        return pltpu.make_async_remote_copy(
            src_ref=source, dst_ref=target, send_sem=sems[0].at[index], recv_sem=sems[1].at[index],
            device_id=device, device_id_type=MESH_ID,
        )

    def to_plane(m, source_of, target_of, sems):
        return [
            remote(
                source_of(m, chips[k]), target_of(m), sems, 4 * m + k, (2 * chips[k] + core, planes[m])
            )
            for k in range(4)
            if m or k
        ]

    def lanes_of(owner):
        return pl.ds(pl.multiple_of(owner * shard, shard), shard)

    row_copies = [
        to_plane(
            m, lambda m, c: rows_ref.at[c * 4 + planes[m]], lambda m: x_ref.at[m, chip], (row_send, row_recv)
        )
        for m in range(4)
    ]
    gate_copies = [
        to_plane(
            m, lambda m, c: gates_ref.at[c * 4 + planes[m]], lambda m: gates_in_ref.at[m, chip],
            (gate_send, gate_recv),
        )
        for m in range(4)
    ]
    keeps = [
        pltpu.make_async_copy(inner_ref.at[chip], win_ref.at[chip, core], local_sem.at[0]),
        pltpu.make_async_copy(inner_a_ref, win_ref.at[chips[1], core], local_sem.at[1]),
        pltpu.make_async_copy(inner_b_ref, win_ref.at[chips[2], core], local_sem.at[2]),
        pltpu.make_async_copy(grads_ref.at[me], dy_ref.at[0, chip], local_sem.at[3]),
        pltpu.make_async_copy(rows_ref.at[me], x_ref.at[0, chip], local_sem.at[4]),
        pltpu.make_async_copy(gates_ref.at[me], gates_in_ref.at[0, chip], local_sem.at[5]),
        pltpu.make_async_copy(outer_ref.at[chip], wout_ref.at[:, lanes_of(x)], local_sem.at[6]),
    ]
    pair_inner = [
        remote(source, win_ref.at[chips[k], core], (w_send, w_recv), k, pair)
        for k, source in enumerate((inner_ref.at[chip], inner_a_ref, inner_b_ref))
    ]
    far_inner = remote(inner_ref.at[chips[3]], win_ref.at[chip, core], (w_send, w_recv), 3, (across[2], z))
    far_block = win_ref.at[chips[3], core]
    pair_far = remote(far_block, far_block, (w_send, w_recv), 11, pair)
    outer_copies = [
        remote(outer_ref.at[device // 2], wout_ref.at[:, lanes_of(x)], (w_send, w_recv), 4 + j, (device, z))
        for j, device in enumerate(across)
    ]
    pair_outer = [remote(outer_ref.at[chip], wout_ref.at[:, lanes_of(x)], (w_send, w_recv), 7, pair)] + [
        remote(wout_ref.at[:, lanes_of(device)], wout_ref.at[:, lanes_of(device)], (w_send, w_recv), 8 + j, pair)
        for j, device in enumerate(across)
    ]
    for m in ROW_ORDER:
        for copy in row_copies[m]:
            copy.start()
    far_inner.start()
    for copy in keeps + pair_inner + outer_copies + pair_outer[:1]:
        copy.start()
    for m in range(4):
        for copy in gate_copies[m]:
            copy.start()
    grad_copies = [
        to_plane(
            m, lambda m, c: grads_ref.at[c * 4 + planes[m]], lambda m: dy_ref.at[m, chip], (grad_send, grad_recv)
        )
        for m in range(2)
    ]
    far_grads = pltpu.make_async_copy(far_ref, dy_ref.at[pl.ds(2, 2)], local_sem.at[9])
    far_grads.start()
    for copy in keeps:
        copy.wait()
    for copy in pair_inner:
        copy.wait()
    far_inner.wait_recv()
    pair_far.start()
    pair_far.wait()

    def cols(tile, part):
        return pl.ds(pl.multiple_of(part * hidden + tile * half, half), half)

    def weight(tile, part):
        return win_ref[:, :, :, cols(tile, part)].reshape(width, half)

    def block(m):
        return pl.ds(m * chunk, chunk)

    def widen(m):
        for copy in row_copies[m]:
            copy.wait_recv()
        rows = x_ref.at[m]

        def step(tile, carry):
            values = rows[...].reshape(chunk, width)
            gate = dot_nn(values, weight(tile, 0))
            up = dot_nn(values, weight(tile, 1))
            square = gate * gate
            bent = jnp.tanh(gate * (0.7978845608028654 + 0.03567740813636141 * square))
            lifted = 0.5 + 0.5 * bent
            slope = lifted + (0.5 * gate) * (1.0 - bent * bent) * (
                0.7978845608028654 + 0.10703222440908423 * square
            )
            active = gate * lifted
            upper_ref[block(m), cols(tile, 0)] = (up * slope).astype(bf16)
            upper_ref[block(m), cols(tile, 1)] = active.astype(bf16)
            hid_ref[block(m), cols(tile, 0)] = (active * up).astype(bf16)
            return carry

        lax.fori_loop(0, tiles, step, 0)

    def narrow(m):
        def step(part, carry):
            here = pl.ds(pl.multiple_of(part * 256, 256), 256)
            values = dot_nn(hid_ref[block(m), :], wout_ref[:, here])
            out_ref[m, :, :, here] = values.astype(bf16).reshape(4, slots, 256)
            return carry

        lax.fori_loop(0, width // 256, step, 0)

    out_copies = [
        to_plane(m, lambda m, c: out_ref.at[m, c], lambda m: returned_ref.at[me], (out_send, out_recv))
        for m in range(4)
    ]
    own_out = pltpu.make_async_copy(out_ref.at[0, chip], returned_ref.at[me], local_sem.at[7])
    widen(0)
    widen(1)
    for m in range(4):
        for copy in row_copies[m]:
            copy.wait_send()
    for m in range(2):
        for copy in grad_copies[m]:
            copy.start()
    for j, copy in enumerate(outer_copies):
        copy.wait_recv()
        pair_outer[1 + j].start()
    for copy in outer_copies:
        copy.wait_send()
    for copy in pair_outer:
        copy.wait()
    for m in range(4):
        if m >= 2:
            widen(m)
        narrow(m)
        for copy in out_copies[m]:
            copy.start()
    own_out.start()
    x_t_ref[...] = x_ref[...].reshape(tokens, width).T.reshape(x_t_ref.shape)

    far_grads.wait()
    for m in range(4):
        for copy in gate_copies[m] + (grad_copies[m] if m < 2 else []):
            copy.wait_recv()
        for j in range(4):
            gates = gates_in_ref[m, j].T[:slots, 0:1]
            dy_ref[m, j] = (dy_ref[m, j].astype(f32) * gates).astype(bf16)

    def outer_part(tile):
        slot = lax.rem(tile, STAGES)
        return remote(stage_out_ref.at[slot], outer_in_ref.at[tile], (part_send, part_recv), tiles + tile, pair)

    def weigh_outer(tile, carry):
        slot = lax.rem(tile, STAGES)

        @pl.when(tile >= STAGES)
        def _():
            outer_part(tile - STAGES).wait_send()

        grad_down = dot_nn(hid_ref[:, cols(tile, 0)].T, dy_ref[...].reshape(tokens, width))
        for j in range(4):
            low = grad_down[:, (2 * j) * shard:(2 * j + 1) * shard].astype(bf16)
            high = grad_down[:, (2 * j + 1) * shard:(2 * j + 2) * shard].astype(bf16)
            stage_out_ref[slot, j] = jnp.where(core == 0, high, low)
            hid_ref[pl.ds((j // 2) * half, half), pl.ds(pl.multiple_of(tile * half + (j % 2) * shard, shard), shard)] = (
                jnp.where(core == 0, low, high)
            )
        outer_part(tile).start()
        return carry

    lax.fori_loop(0, tiles, weigh_outer, 0)
    for tile in range(tiles - STAGES, tiles):
        outer_part(tile).wait_send()

    def join_outer(tile, carry):
        outer_part(tile).wait_recv()
        for j in range(4):
            own = hid_ref[pl.ds((j // 2) * half, half), pl.ds(pl.multiple_of(tile * half + (j % 2) * shard, shard), shard)]
            outer_in_ref[tile, j] = (own.astype(f32) + outer_in_ref[tile, j].astype(f32)).astype(bf16)
        return carry

    lax.fori_loop(0, tiles, join_outer, 0)
    own_gout = pltpu.make_async_copy(outer_in_ref.at[:, chip], gouter_ref.at[chip], local_sem.at[3])
    own_gout.start()
    gout_copies = [
        remote(outer_in_ref.at[:, device // 2], gouter_ref.at[chip], (gout_send, gout_recv), j, (device, z))
        for j, device in enumerate(across)
    ]
    for copy in gout_copies:
        copy.start()

    def back(first, count):
        here_rows = pl.ds(first * chunk, count * chunk)

        def step(tile, carry):
            down = wout_ref[pl.ds(pl.multiple_of(tile * half, half), half), :]
            grads = dy_ref[first:first + count].reshape(count * chunk, width)
            grad_hidden = dot_nt(grads, down)
            for part in range(2):
                slope = upper_ref[here_rows, cols(tile, part)].astype(f32)
                upper_ref[here_rows, cols(tile, part)] = (grad_hidden * slope).astype(bf16)
            return carry

        lax.fori_loop(0, tiles, step, 0)

        def gather(j, carry):
            here = pl.ds(pl.multiple_of(j * 256, 256), 256)
            weights = win_ref[j].reshape(2 * shard, 2 * hidden)
            values = dot_nt(upper_ref[here_rows, :], weights)
            back_ref[first:first + count, :, :, here] = values.astype(bf16).reshape(count, 4, slots, 256)
            return carry

        lax.fori_loop(0, 4, gather, 0)

    copy_copies = [
        to_plane(m, lambda m, c: back_ref.at[m, c], lambda m: copies_ref.at[me], (copy_send, copy_recv))
        for m in range(4)
    ]
    own_copy = pltpu.make_async_copy(back_ref.at[0, chip], copies_ref.at[me], local_sem.at[8])
    for first in range(0, 4, BACK_COUNT):
        back(first, BACK_COUNT)
        for m in range(first, first + BACK_COUNT):
            for copy in copy_copies[m]:
                copy.start()
    own_copy.start()

    def inner_part(tile):
        slot = lax.rem(tile, STAGES)
        return remote(stage_in_ref.at[slot], inner_in_ref.at[tile], (part_send, part_recv), tile, pair)

    def inner_load(tile):
        slot = lax.rem(tile, 2)
        return pltpu.make_async_copy(inner_in_ref.at[tile], add_in_ref.at[slot], join_sem.at[slot])

    def inner_stores(tile):
        slot = lax.rem(tile, 2)
        return [
            pltpu.make_async_copy(
                add_in_ref.at[slot, part], ginner_ref.at[:, :, cols(tile, part)], join_sem.at[2 + 2 * slot + part]
            )
            for part in range(2)
        ]

    def join_begin(tile):
        inner_part(tile).wait_recv()

        @pl.when(tile >= 2)
        def _():
            for copy in inner_stores(tile - 2):
                copy.wait()

        inner_load(tile).start()

    def join_end(tile):
        slot = lax.rem(tile, 2)
        inner_load(tile).wait()
        for part in range(2):
            own = upper_ref[pl.ds(0, width // 2), cols(tile, part)].astype(f32)
            other = add_in_ref[slot, part].reshape(width // 2, half).astype(f32)
            add_in_ref[slot, part] = (own + other).astype(bf16).reshape(4, shard, half)
        for copy in inner_stores(tile):
            copy.start()

    def weigh_inner(tile, carry):
        slot = lax.rem(tile, STAGES)

        @pl.when(tile >= LAG)
        def _():
            join_begin(tile - LAG)

        @pl.when(tile >= STAGES)
        def _():
            inner_part(tile - STAGES).wait_send()

        for part in range(2):
            grad_upper = upper_ref[:, cols(tile, part)]
            other = x_t_ref[:, 1 - core].reshape(width // 2, tokens)
            stage_in_ref[slot, part] = dot_nn(other, grad_upper).astype(bf16).reshape(4, shard, half)
        inner_part(tile).start()
        for part in range(2):
            grad_upper = upper_ref[:, cols(tile, part)]
            own = x_t_ref[:, core].reshape(width // 2, tokens)
            upper_ref[pl.ds(0, width // 2), cols(tile, part)] = dot_nn(own, grad_upper).astype(bf16)

        @pl.when(tile >= LAG)
        def _():
            join_end(tile - LAG)

        return carry

    lax.fori_loop(0, tiles, weigh_inner, 0)
    for tile in range(tiles - LAG, tiles):
        join_begin(tile)
        join_end(tile)
    for tile in range(tiles - STAGES, tiles):
        inner_part(tile).wait_send()
    for tile in (tiles - 2, tiles - 1):
        for copy in inner_stores(tile):
            copy.wait()
    own_out.wait()
    own_copy.wait()
    own_gout.wait()
    for m in range(4):
        for copy in (grad_copies[m] if m < 2 else []) + gate_copies[m]:
            copy.wait_send()
        for copy in out_copies[m] + copy_copies[m]:
            copy.wait()
    far_inner.wait_send()
    for copy in gout_copies:
        copy.wait()


ROW_ORDER = (0, 1, 2, 3)
BACK_COUNT = 2
STAGES = 4
LAG = 2


def run_experts(rows, gates, grads, far, inner, inner_others, outer):
    count, slots, width = rows.shape
    tokens = count * slots
    hidden = outer.shape[1]
    half = 256
    tiles = hidden // half
    shard = width // 8
    bf16 = jnp.bfloat16
    anywhere = pl.BlockSpec(memory_space=pl.ANY)
    sems = [pltpu.SemaphoreType.DMA((count,))] * 10 + [
        pltpu.SemaphoreType.DMA((12,)),
        pltpu.SemaphoreType.DMA((12,)),
        pltpu.SemaphoreType.DMA((2 * tiles,)),
        pltpu.SemaphoreType.DMA((2 * tiles,)),
        pltpu.SemaphoreType.DMA((3,)),
        pltpu.SemaphoreType.DMA((3,)),
        pltpu.SemaphoreType.DMA((10,)),
        pltpu.SemaphoreType.DMA((6,)),
    ]
    outs = pl.pallas_call(
        expert_kernel,
        out_shape=(
            jax.ShapeDtypeStruct(rows.shape, bf16),
            jax.ShapeDtypeStruct(rows.shape, bf16),
            jax.ShapeDtypeStruct(inner.shape, bf16),
            jax.ShapeDtypeStruct((4, tiles, half, shard), bf16),
            jax.ShapeDtypeStruct((tiles, 2, 4, shard, half), bf16),
        ),
        in_specs=[anywhere] * 8,
        out_specs=(anywhere,) * 5,
        scratch_shapes=[
            pltpu.VMEM((4, 4, slots, width), bf16),
            pltpu.VMEM((4, 2, shard, tokens), bf16),
            pltpu.VMEM((4, 4, slots, width), bf16),
            pltpu.VMEM((4, 4, 8, 128), jnp.float32),
            pltpu.VMEM((4, 2, shard, 2 * hidden), bf16),
            pltpu.VMEM((hidden, width), bf16),
            pltpu.VMEM((tokens, 2 * hidden), bf16),
            pltpu.VMEM((tokens, hidden), bf16),
            pltpu.VMEM((4, 4, slots, width), bf16),
            pltpu.VMEM((4, 4, slots, width), bf16),
            pltpu.VMEM((STAGES, 2, 4, shard, half), bf16),
            pltpu.VMEM((STAGES, 4, half, shard), bf16),
            pltpu.VMEM((2, 2, 4, shard, half), bf16),
            pltpu.VMEM((tiles, 4, half, shard), bf16),
        ] + sems,
        compiler_params=pltpu.CompilerParams(
            collective_id=1, has_side_effects=True, vmem_limit_bytes=63 * 2**20
        ),
        cost_estimate=pl.CostEstimate(
            flops=180 * 10**9, bytes_accessed=60 * 2**20, transcendentals=tokens * hidden
        ),
        name="run_experts",
    )(rows, gates, grads, far, inner, *inner_others, outer)
    return outs[0], outs[1], outs[2], outs[3].reshape(outer.shape)


def attend_back(pair, proj_ref, dout_ref, lse_ref, tile_ref, dproj_ref, span_ref, dk_ref, dv_ref, near_ref):
    length = proj_ref.shape[1]
    blocks = length // BLK
    depth = 64
    wide = 2 * depth
    here = slice(pair * wide, (pair + 1) * wide)
    lane = lax.broadcasted_iota(jnp.int32, (1, wide), 1)
    keys = proj_ref[1, :, here]
    values = proj_ref[2, :, here]
    keys_t = keys.T
    dk_ref[...] = jnp.zeros_like(dk_ref)
    dv_ref[...] = jnp.zeros_like(dv_ref)
    near_ref[...] = jnp.zeros_like(near_ref)
    far_sum = [jnp.zeros((1, BLK), jnp.float32) for h in range(2)]
    for block in range(blocks):
        rows = pl.ds(block * BLK, BLK)
        key_count = (block + 1) * BLK
        query = proj_ref[0, rows, here] * jnp.bfloat16(0.125)
        grad = dout_ref[rows, here]
        dq_parts = []
        dk_sum = None
        dv_sum = None
        for h in range(2):
            own = (lane // depth) == h
            query_h = jnp.where(own, query, jnp.bfloat16(0))
            grad_h = jnp.where(own, grad, jnp.bfloat16(0))
            scores = dot_nt(keys[:key_count], query_h)
            grad_p = dot_nt(values[:key_count], grad_h)
            lse = lse_ref[pair, h:h + 1, rows]
            far = tile_ref[2 * pair + h, 1, 0:1, BLK - 1:BLK].astype(jnp.float32)
            probs = []
            delta = None
            for kb in range(block + 1):
                d = block - kb
                part = scores[kb * BLK:(kb + 1) * BLK]
                bias = tile_ref[2 * pair + h, d].astype(jnp.float32) if d < 2 else far
                part = jnp.exp(part + (bias - lse))
                probs.append(part)
                term = jnp.sum(part * grad_p[kb * BLK:(kb + 1) * BLK], axis=0, keepdims=True)
                delta = term if delta is None else delta + term
            ds = []
            for kb in range(block + 1):
                d = block - kb
                part = probs[kb] * (grad_p[kb * BLK:(kb + 1) * BLK] - delta)
                if d < 2:
                    near_ref[h, d] += part
                else:
                    far_sum[h] = far_sum[h] + jnp.sum(part, axis=0, keepdims=True)
                ds.append(part.astype(jnp.bfloat16))
            ds = jnp.concatenate(ds, axis=0)
            weights = jnp.concatenate([p.astype(jnp.bfloat16) for p in probs], axis=0)
            dv_h = dot_nn(weights, grad_h)
            dk_h = dot_nn(ds, query_h)
            dv_sum = dv_h if dv_sum is None else dv_sum + dv_h
            dk_sum = dk_h if dk_sum is None else dk_sum + dk_h
            dq_parts.append(dot_nn(keys_t[h * depth:(h + 1) * depth, :key_count], ds))
        dk_ref[:key_count] += dk_sum
        dv_ref[:key_count] += dv_sum
        dproj_ref[0, rows, here] = (jnp.concatenate(dq_parts, axis=0).T * 0.125).astype(jnp.bfloat16)
    dproj_ref[1, :, here] = dk_ref[...].astype(jnp.bfloat16)
    dproj_ref[2, :, here] = dv_ref[...].astype(jnp.bfloat16)
    flip = (
        lax.broadcasted_iota(jnp.int32, (BLK, BLK), 0) + lax.broadcasted_iota(jnp.int32, (BLK, BLK), 1) == BLK - 1
    ).astype(jnp.bfloat16)
    lanes = lax.broadcasted_iota(jnp.int32, (1, 2 * BLK), 1)
    for h in range(2):
        for d in range(2):
            near = near_ref[h, d]
            near_high = near.astype(jnp.bfloat16)
            near_low = (near - near_high.astype(jnp.float32)).astype(jnp.bfloat16)
            flipped = dot_nn(flip, near_high) + dot_nn(flip, near_low)
            spread = jnp.concatenate([flipped, jnp.zeros((BLK, BLK), jnp.float32)], axis=1)
            turned = pltpu.roll(spread, 1, 1, stride=1, stride_axis=0)
            along = jnp.sum(turned, axis=0, keepdims=True)
            if d == 1:
                along = along + jnp.where(lanes == 2 * BLK - 1, jnp.sum(far_sum[h], axis=1, keepdims=True), 0.0)
            span_ref[2 * pair + h, d:d + 1, :] = along


def combine_kernel(
    returned_hbm, copies_hbm, hidden_hbm, cot_hbm, cols_hbm, wo_hbm, att_hbm, router_ref, gains_ref, counts_ref,
    mixed_ref, ghidden_ref, own_ref, other_ref, gout_ref, sums_ref,
    returned_ref, copies_ref, hidden_ref, cot_ref, cols_ref, wo_ref, att_ref, gp_ref, load_sem,
):
    f32, bf16 = jnp.float32, jnp.bfloat16
    rows, width = ghidden_ref.shape
    shard = width // 8
    experts = returned_ref.shape[0] // CAP
    loads = {}
    for name, source, target in (
        ("cols", cols_hbm, cols_ref), ("returned", returned_hbm, returned_ref), ("hidden", hidden_hbm, hidden_ref),
        ("cot", cot_hbm, cot_ref), ("copies", copies_hbm, copies_ref), ("wo", wo_hbm, wo_ref),
        ("att", att_hbm, att_ref),
    ):
        loads[name] = pltpu.make_async_copy(source, target, load_sem.at[len(loads)])
        loads[name].start()
    gain_second = gains_ref[1:2, :]
    router_t = router_ref[...]
    step = rows // 2
    counts = counts_ref[...]
    tokens = 32 * rows
    pairs_in_all = 2 * tokens
    push = loss_weight * experts * (counts / pairs_in_all) / tokens
    slot_lane = lax.broadcasted_iota(jnp.int32, (1, returned_ref.shape[0]), 1).astype(f32)
    expert_lane = lax.broadcasted_iota(jnp.int32, (1, shard), 1).astype(f32)
    gain2_sum = jnp.zeros((1, width), f32)
    route_sum = jnp.zeros((1, shard), f32)
    grad_router = jnp.zeros((shard, width), f32)
    for name in ("cols", "returned", "hidden", "cot"):
        loads[name].wait()
    for i in range(2):
        here = slice(i * step, (i + 1) * step)
        cols = cols_ref[here, :]
        route = jnp.where(expert_lane < experts, cols, 0.0)
        marks = [(slot_lane == cols[:, experts + 2 + c:experts + 3 + c]).astype(bf16) for c in range(2)]
        picked = [dot_nn(mark, returned_ref[...]) for mark in marks]
        hidden = hidden_ref[here, :]
        grad_mixed = cot_ref[here, :].astype(f32)
        mixed_ref[here, :] = (
            hidden + picked[0] * cols[:, experts:experts + 1] + picked[1] * cols[:, experts + 1:experts + 2]
        ).astype(bf16)
        grad_route = push
        for c in range(2):
            hit = expert_lane == cols[:, experts + 4 + c:experts + 5 + c]
            grad_route = grad_route + jnp.where(hit, jnp.sum(grad_mixed * picked[c], axis=1, keepdims=True), 0.0)
        grad_logits = route * (grad_route - jnp.sum(route * grad_route, axis=1, keepdims=True))
        route_sum = route_sum + jnp.sum(route, axis=0, keepdims=True)
        if i == 0:
            loads["copies"].wait()
        grad_second = dot_nn(marks[0] + marks[1], copies_ref[...]) + dot_nn(grad_logits.astype(bf16), router_t)
        normed, scale = normalize(hidden)
        second_norm = (normed * gain_second).astype(bf16)
        grad_router = grad_router + dot_nn(grad_logits.T.astype(bf16), second_norm)
        gain2_sum = gain2_sum + jnp.sum(grad_second * normed, axis=0, keepdims=True)
        grad_normed = grad_second * gain_second
        grad_hidden = grad_mixed + scale * (
            grad_normed - normed * jnp.mean(grad_normed * normed, axis=-1, keepdims=True)
        )
        ghidden_ref[here, :] = grad_hidden
        gp_ref[here, :] = grad_hidden.astype(bf16)


    loads["wo"].wait()
    own_width = own_ref.shape[1]
    other_ref[...] = dot_nt(gp_ref[...], wo_ref[own_width:, :]).astype(bf16)
    own_ref[...] = dot_nt(gp_ref[...], wo_ref[:own_width, :]).astype(bf16)
    loads["att"].wait()
    gout_ref[...] = dot_nn(att_ref[...].T, gp_ref[...]).astype(bf16)
    for owner in range(8):
        here = slice(owner * shard, (owner + 1) * shard)
        target = sums_ref.at[owner // 2, owner % 2]
        target[0:1, :] = jnp.zeros((1, shard), f32)
        target[1:2, :] = gain2_sum[:, here]
        target[2:2 + experts, :] = grad_router[:experts, here]
        target[18:22, :] = jnp.zeros((4, shard), f32)
        target[22:23, :] = route_sum
        target[23:24, :] = jnp.zeros((1, shard), f32)


def combine(returned, copies, hidden, cot, cols, wo, att, router_t, gains, counts):
    rows, width = hidden.shape
    shard = width // 8
    f32, bf16 = jnp.float32, jnp.bfloat16
    anywhere = pl.BlockSpec(memory_space=pl.ANY)
    inside = pl.BlockSpec(memory_space=pltpu.VMEM)
    held = (returned, copies, hidden, cot, cols, wo, att)
    return pl.pallas_call(
        combine_kernel,
        out_shape=(
            jax.ShapeDtypeStruct((rows, width), bf16),
            jax.ShapeDtypeStruct((rows, width), f32),
            jax.ShapeDtypeStruct((rows, width // 2), bf16),
            jax.ShapeDtypeStruct((rows, width // 2), bf16),
            jax.ShapeDtypeStruct((width, width), bf16),
            jax.ShapeDtypeStruct((4, 2, 24, shard), f32),
        ),
        in_specs=[anywhere] * 7 + [inside] * 3,
        out_specs=(inside,) * 6,
        scratch_shapes=[pltpu.VMEM(array.shape, array.dtype) for array in held]
        + [pltpu.VMEM((rows, width), bf16), pltpu.SemaphoreType.DMA((7,))],
        compiler_params=pltpu.CompilerParams(vmem_limit_bytes=48 * 2**20),
        cost_estimate=pl.CostEstimate(flops=8 * 10**9, bytes_accessed=20 * 2**20, transcendentals=0),
        name="combine",
    )(*held, router_t, gains, counts)


def back_kernel(
    own_hbm, other_hbm, gout_hbm, sums_hbm, ghidden_hbm, gains_ref, picks_ref, proj_hbm, lse_hbm, tile_hbm, wq_hbm,
    seq_hbm,
    gtok_ref, gqkv_ref, gwo_ref, sums_ref,
    ghidden_ref, proj_ref, lse_ref, tile_ref, wq_ref, seq_ref, dout_ref, dproj_ref, span_ref, dk_ref, dv_ref,
    near_ref, turned_ref, first_send_ref, first_in_ref,
    q_stage_ref, q_in_ref, q_own_ref, q_across_ref, q_z_ref, q_z_in_ref,
    gout_ref, o_in_ref, o_sum_ref, o_across_ref, o_z_ref, o_z_in_ref,
    s_own_ref, s_in_ref, s_sum_ref, s_across_ref, s_z_ref, s_z_in_ref,
    send_sem, recv_sem, load_sem,
):
    x, z, along_z, across, sibling = places()
    core = x % 2
    chip = x // 2
    half = z % 2
    f32, bf16 = jnp.float32, jnp.bfloat16
    rows, width = gtok_ref.shape
    shard = width // 8
    step = rows // 2
    group = gqkv_ref.shape[2]
    pair = (sibling, z)
    chips = [(device, z) for device in across]
    lines = [(x, other) for other in along_z]
    barrier = pltpu.get_barrier_semaphore()
    for peer in chips + lines + [pair]:
        pl.semaphore_signal(barrier, inc=1, device_id=peer, device_id_type=MESH_ID)
    loads = {}
    for name, source, target in (
        ("gout", gout_hbm, gout_ref), ("proj", proj_hbm, proj_ref),
        ("own", own_hbm, dout_ref.at[pl.ds(pl.multiple_of(half * rows, rows), rows), :]),
        ("other", other_hbm, dout_ref.at[pl.ds(pl.multiple_of((1 - half) * rows, rows), rows), :]),
        ("lse", lse_hbm, lse_ref), ("tile", tile_hbm, tile_ref), ("seq", seq_hbm, seq_ref), ("wq", wq_hbm, wq_ref),
        ("sums", sums_hbm, s_own_ref), ("ghidden", ghidden_hbm, ghidden_ref),
    ):
        loads[name] = pltpu.make_async_copy(source, target, load_sem.at[len(loads)])
        loads[name].start()
    pl.semaphore_wait(barrier, 7)
    started = []

    def send(source, target, device):
        index = len(started)
        copy = pltpu.make_async_remote_copy(
            src_ref=source, dst_ref=target, send_sem=send_sem.at[index], recv_sem=recv_sem.at[index],
            device_id=device, device_id_type=MESH_ID,
        )
        copy.start()
        started.append(copy)
        return copy

    def lanes_of(owner):
        return pl.ds(pl.multiple_of(owner * shard, shard), shard)

    loads["gout"].wait()
    o_pair = [send(gout_ref.at[:, lanes_of(2 * j + 1 - core)], o_in_ref.at[j], pair) for j in range(4)]

    gain_first = gains_ref[0:1, :]
    loads["seq"].wait()
    for i in range(4):
        normed, _ = normalize(seq_ref[i // 2, (i % 2) * step:(i % 2 + 1) * step, :].astype(f32))
        turned_ref[:, :, :, i * step:(i + 1) * step] = (
            (normed * gain_first).astype(bf16).T.reshape(4, 2, shard, step)
        )

    for name in ("proj", "lse", "tile", "own", "other"):
        loads[name].wait()

    def attend(number):
        attend_back(
            number, proj_ref, dout_ref, lse_ref, tile_ref, dproj_ref, span_ref, dk_ref, dv_ref, near_ref
        )

    def weigh_other(slot):
        here = pl.ds(slot * group, group)
        other = turned_ref[:, 1 - core].reshape(width // 2, 2 * rows)
        for c in range(3):
            q_stage_ref[slot, c] = dot_nn(other, dproj_ref[c, :, here]).astype(bf16).reshape(4, shard, group)
        return send(q_stage_ref.at[slot], q_in_ref.at[slot], pair)

    def weigh_own(slot):
        here = pl.ds(slot * group, group)
        own = turned_ref[:, core].reshape(width // 2, 2 * rows)
        for c in range(3):
            q_own_ref[slot, c] = dot_nn(own, dproj_ref[c, :, here]).astype(bf16).reshape(4, shard, group)

    def to_chips(slot, copy):
        copy.wait_recv()
        q_own_ref[slot] = (q_own_ref[slot].astype(f32) + q_in_ref[slot].astype(f32)).astype(bf16)
        return [
            send(q_own_ref.at[slot, :, device // 2], q_across_ref.at[slot, j], chips[j])
            for j, device in enumerate(across)
        ]

    def chip_total(slot, copies):
        for copy in copies:
            copy.wait_recv()
        total = q_own_ref[slot, :, chip].astype(f32)
        for j in range(3):
            total = total + q_across_ref[slot, j].astype(f32)
        return total

    attend(2)
    attend(3)
    q_pair_1 = weigh_other(1)
    for copy in o_pair:
        copy.wait_recv()
    for j in range(4):
        o_sum_ref[j] = (gout_ref[:, lanes_of(2 * j + core)].astype(f32) + o_in_ref[j].astype(f32)).astype(bf16)
    o_chips = [send(o_sum_ref.at[device // 2], o_across_ref.at[j], chips[j]) for j, device in enumerate(across)]
    weigh_own(1)
    q_chips_1 = to_chips(1, q_pair_1)
    attend(0)
    attend(1)

    loads["wq"].wait()
    gain1_sum = jnp.zeros((1, width), f32)
    for turn, side in enumerate((1 - half, half)):
        for i in range(2):
            here = pl.ds(pl.multiple_of(side * rows + i * step, step), step)
            part = (
                dot_nt(dproj_ref[0, here, :], wq_ref[0])
                + dot_nt(dproj_ref[1, here, :], wq_ref[1])
                + dot_nt(dproj_ref[2, here, :], wq_ref[2])
            )
            normed, _ = normalize(seq_ref[side, i * step:(i + 1) * step, :].astype(f32))
            gain1_sum = gain1_sum + jnp.sum(part * normed, axis=0, keepdims=True)
            if turn:
                gtok_ref[i * step:(i + 1) * step, :] = part
            else:
                first_send_ref[i * step:(i + 1) * step, :] = part.astype(bf16)
        if not turn:
            first_copy = send(first_send_ref, first_in_ref, lines[0])
            q_pair_0 = weigh_other(0)

    loads["sums"].wait()
    table = None
    for d in range(2):
        along = span_ref[:, d, :]
        high = along.astype(bf16)
        low = (along - high.astype(f32)).astype(bf16)
        part = dot_nn(high, picks_ref[d]) + dot_nn(low, picks_ref[d])
        table = part if table is None else table + part
    heads = table.shape[0] // 2
    table = table.T[:32, :]
    blank = jnp.zeros((table.shape[0], shard - heads), f32)
    placed = pltpu.roll(jnp.concatenate([table[:, :heads], blank], axis=1), heads * z, 1) + pltpu.roll(
        jnp.concatenate([table[:, heads:], blank], axis=1), heads * ((z + 2) % 4), 1
    )
    for owner in range(8):
        here = slice(owner * shard, (owner + 1) * shard)
        target = s_own_ref.at[owner // 2, owner % 2]
        target[0:1, :] = gain1_sum[:, here]
        target[18:22, :] = placed[4 * owner:4 * owner + 4, :]
    s_pair = send(s_own_ref.at[:, 1 - core], s_in_ref, pair)
    weigh_own(0)

    q_chips_0 = to_chips(0, q_pair_0)
    s_pair.wait_recv()
    s_sum_ref[...] = s_own_ref[:, core] + s_in_ref[...]
    s_chips = [send(s_sum_ref.at[device // 2], s_across_ref.at[j], chips[j]) for j, device in enumerate(across)]
    q_z_ref[...] = chip_total(1, q_chips_1).astype(bf16)
    q_line = send(q_z_ref, q_z_in_ref, lines[1])
    for copy in o_chips:
        copy.wait_recv()
    o_total = o_sum_ref[chip].astype(f32)
    for j in range(3):
        o_total = o_total + o_across_ref[j].astype(f32)
    rows_out = gwo_ref.shape[0]
    gwo_ref[...] = o_total[:rows_out]
    o_z_ref[...] = o_total[rows_out:].astype(bf16).reshape(o_z_ref.shape)
    out_slots = (2, 1, 3)
    o_lines = [send(o_z_ref.at[out_slots[j] - 1], o_z_in_ref.at[j], lines[j]) for j in range(3)]
    for copy in s_chips:
        copy.wait_recv()
    s_z_ref[...] = s_sum_ref[chip] + s_across_ref[0] + s_across_ref[1] + s_across_ref[2]
    s_lines = [send(s_z_ref, s_z_in_ref.at[j], lines[j]) for j in range(3)]
    gqkv_ref[...] = chip_total(0, q_chips_0)

    first_copy.wait_recv()
    loads["ghidden"].wait()
    for i in range(2):
        here = slice(i * step, (i + 1) * step)
        grad = (gtok_ref[here, :] + first_in_ref[here, :].astype(f32)) * gain_first
        normed, scale = normalize(seq_ref[half, here, :].astype(f32))
        gtok_ref[here, :] = ghidden_ref[here, :] + scale * (
            grad - normed * jnp.mean(grad * normed, axis=-1, keepdims=True)
        )
    q_line.wait_recv()
    gqkv_ref[...] += q_z_in_ref[...].astype(f32)
    for copy in s_lines + o_lines:
        copy.wait_recv()
    gwo_ref[...] += o_z_in_ref[0].astype(f32) + o_z_in_ref[1].astype(f32) + o_z_in_ref[2].astype(f32)
    sums = s_z_ref[...] + s_z_in_ref[0] + s_z_in_ref[1] + s_z_in_ref[2]
    sums_ref[...] = sums
    for copy in started:
        copy.wait_send()


def run_back(own, other, gout, sums, ghidden, gains, picks, proj, lse, tiles, wq, seq):
    rows, width = ghidden.shape
    length = 2 * rows
    shard = width // 8
    group = wq.shape[2] // 2
    rows_out = width // 4
    heads = tiles.shape[0]
    f32, bf16 = jnp.float32, jnp.bfloat16
    anywhere = pl.BlockSpec(memory_space=pl.ANY)
    inside = pl.BlockSpec(memory_space=pltpu.VMEM)
    copies_count = 4 + 2 + 3 + 3 + 3 + 1 + 1 + 3 + 1 + 3 + 3
    return pl.pallas_call(
        back_kernel,
        out_shape=(
            jax.ShapeDtypeStruct((rows, width), f32),
            jax.ShapeDtypeStruct((3, shard, group), f32),
            jax.ShapeDtypeStruct((rows_out, shard), f32),
            jax.ShapeDtypeStruct((24, shard), f32),
        ),
        in_specs=[anywhere] * 5 + [inside] * 2 + [anywhere] * 5,
        out_specs=(inside,) * 4,
        scratch_shapes=[
            pltpu.VMEM(ghidden.shape, f32),
            pltpu.VMEM(proj.shape, bf16),
            pltpu.VMEM(lse.shape, f32),
            pltpu.VMEM(tiles.shape, bf16),
            pltpu.VMEM(wq.shape, bf16),
            pltpu.VMEM(seq.shape, bf16),
            pltpu.VMEM((length, 2 * group), bf16),
            pltpu.VMEM(proj.shape, bf16),
            pltpu.VMEM((heads, 2, 2 * BLK), f32),
            pltpu.VMEM((length, 128), f32),
            pltpu.VMEM((length, 128), f32),
            pltpu.VMEM((2, 2, BLK, BLK), f32),
            pltpu.VMEM((4, 2, shard, length), bf16),
            pltpu.VMEM((rows, width), bf16),
            pltpu.VMEM((rows, width), bf16),
            pltpu.VMEM((2, 3, 4, shard, group), bf16),
            pltpu.VMEM((2, 3, 4, shard, group), bf16),
            pltpu.VMEM((2, 3, 4, shard, group), bf16),
            pltpu.VMEM((2, 3, 3, shard, group), bf16),
            pltpu.VMEM((3, shard, group), bf16),
            pltpu.VMEM((3, shard, group), bf16),
            pltpu.VMEM((width, width), bf16),
            pltpu.VMEM((4, width, shard), bf16),
            pltpu.VMEM((4, width, shard), bf16),
            pltpu.VMEM((3, width, shard), bf16),
            pltpu.VMEM((3, rows_out, shard), bf16),
            pltpu.VMEM((3, rows_out, shard), bf16),
            pltpu.VMEM((4, 2, 24, shard), f32),
            pltpu.VMEM((4, 24, shard), f32),
            pltpu.VMEM((4, 24, shard), f32),
            pltpu.VMEM((3, 24, shard), f32),
            pltpu.VMEM((24, shard), f32),
            pltpu.VMEM((3, 24, shard), f32),
            pltpu.SemaphoreType.DMA((copies_count,)),
            pltpu.SemaphoreType.DMA((copies_count,)),
            pltpu.SemaphoreType.DMA((10,)),
        ],
        compiler_params=pltpu.CompilerParams(
            collective_id=2, has_side_effects=True, vmem_limit_bytes=60 * 2**20
        ),
        cost_estimate=pl.CostEstimate(flops=60 * 10**9, bytes_accessed=60 * 2**20, transcendentals=0),
        name="run_back",
    )(own, other, gout, sums, ghidden, gains, picks, proj, lse, tiles, wq, seq)


def final_kernel(
    ginner_hbm, gtok_hbm, gqkv_hbm, gwo_hbm, sums_ref, counts_ref,
    inner_hbm, tok_hbm, qkv_hbm, wo_hbm, gain1_ref, gain2_ref, grouter_ref, gbias_ref, load_ref, loss_ref,
    in_ref, out_ref, in_sem, out_sem, copy_sem,
):
    z = lax.axis_index("gy")
    f32 = jnp.float32
    copies = [
        pltpu.make_async_copy(source, target, copy_sem.at[n])
        for n, (source, target) in enumerate(((gtok_hbm, tok_hbm), (gqkv_hbm, qkv_hbm), (gwo_hbm, wo_hbm)))
    ]
    depth, _, wide = in_ref.shape
    blocks = [
        (n, pl.ds(part * wide, wide)) for n in range(ginner_hbm.shape[0]) for part in range(ginner_hbm.shape[2] // wide)
    ]
    loads = [
        pltpu.make_async_copy(ginner_hbm.at[n, :, here], in_ref.at[i % depth], in_sem.at[i % depth])
        for i, (n, here) in enumerate(blocks)
    ]
    stores = [
        pltpu.make_async_copy(out_ref.at[i % depth], inner_hbm.at[n, :, here], out_sem.at[i % depth])
        for i, (n, here) in enumerate(blocks)
    ]
    for i in range(depth - 1):
        loads[i].start()
    for copy in copies:
        copy.start()
    experts = load_ref.shape[1]
    heads = gbias_ref.shape[1]
    shard = sums_ref.shape[1]
    sums = sums_ref[...]
    gain1_ref[...] = sums[0:1, :]
    gain2_ref[...] = sums[1:2, :]
    grouter_ref[...] = sums[2:2 + experts, :].T
    gbias_ref[...] = pltpu.roll(sums[16:24, :], (shard - heads * z) % shard, 1)[2:6, :heads]
    tokens = 32 * gtok_hbm.shape[0]
    counts = counts_ref[:, :experts]
    pairs_in_all = 2 * tokens
    prob_sums = sums[22:23, :experts]
    load_ref[...] = jnp.concatenate([experts * counts / pairs_in_all, experts * prob_sums / tokens], axis=0)
    loss_ref[...] = experts * jnp.sum(counts / pairs_in_all * (prob_sums / tokens), axis=1, keepdims=True)
    for i in range(len(blocks)):
        if i + depth - 1 < len(blocks):
            loads[i + depth - 1].start()
        loads[i].wait()
        if i >= depth:
            stores[i - depth].wait()
        out_ref[i % depth] = in_ref[i % depth].astype(f32)
        stores[i].start()
    for store in stores[-depth:]:
        store.wait()
    for copy in copies:
        copy.wait()


def finish(ginner, gtok, gqkv, gwo, sums, counts, experts, heads):
    f32, bf16 = jnp.float32, jnp.bfloat16
    local, shard, inner_width = ginner.shape
    wide = inner_width // 4
    anywhere = pl.BlockSpec(memory_space=pl.ANY)
    inside = pl.BlockSpec(memory_space=pltpu.VMEM)
    return pl.pallas_call(
        final_kernel,
        out_shape=(
            jax.ShapeDtypeStruct(ginner.shape, f32),
            jax.ShapeDtypeStruct(gtok.shape, f32),
            jax.ShapeDtypeStruct(gqkv.shape, f32),
            jax.ShapeDtypeStruct(gwo.shape, f32),
            jax.ShapeDtypeStruct((1, shard), f32),
            jax.ShapeDtypeStruct((1, shard), f32),
            jax.ShapeDtypeStruct((shard, experts), f32),
            jax.ShapeDtypeStruct((4, heads), f32),
            jax.ShapeDtypeStruct((2, experts), f32),
            jax.ShapeDtypeStruct((1, 1), f32),
        ),
        in_specs=[anywhere] * 4 + [inside] * 2,
        out_specs=(anywhere,) * 4 + (inside,) * 6,
        scratch_shapes=[
            pltpu.VMEM((4, shard, wide), bf16),
            pltpu.VMEM((4, shard, wide), f32),
            pltpu.SemaphoreType.DMA((4,)),
            pltpu.SemaphoreType.DMA((4,)),
            pltpu.SemaphoreType.DMA((3,)),
        ],
        compiler_params=pltpu.CompilerParams(vmem_limit_bytes=32 * 2**20),
        cost_estimate=pl.CostEstimate(flops=0, bytes_accessed=24 * 2**20, transcendentals=0),
        name="finish",
    )(ginner, gtok, gqkv, gwo, sums, counts)


def fast_device(
    tokens, expert_ids, gain_attn, w_qkv, w_out, rel_bias, gain_ffn, router, w_in, w_down, cotangent
):
    f32, bf16 = jnp.float32, jnp.bfloat16
    tok_dev, model_width = tokens.shape
    expert_count = router.shape[1]
    top_count = expert_ids.shape[1]
    shard = model_width // 8
    group_heads = rel_bias.shape[1]

    expert_row = jnp.arange(expert_count, dtype=jnp.int32)
    hits = [(expert_ids[:, c][:, None] == expert_row[None]) for c in range(top_count)]
    both = sum(hit.astype(bf16) for hit in hits)
    steps = jnp.arange(tok_dev, dtype=jnp.int32)
    lower = (steps[None, :] < steps[:, None]).astype(bf16)
    before = jnp.dot(lower, both, preferred_element_type=f32)
    slots = [jnp.sum(jnp.where(hit, before, 0.0), axis=1).astype(jnp.int32) for hit in hits]
    kept = [slot < CAP for slot in slots]
    local_counts = jnp.sum(both.astype(f32), axis=0)
    count_high = jnp.floor(local_counts / 32.0)
    count_low = local_counts - 32.0 * count_high

    def lanes(rows):
        return jnp.pad(rows.astype(bf16), ((0, 0), (0, shard - rows.shape[1])))

    small = jnp.concatenate(
        [
            router.T,
            gain_attn[None],
            gain_ffn[None],
            lanes(rel_bias),
            lanes(count_high[None]),
            lanes(count_low[None]),
            jnp.zeros((8, shard), bf16),
        ],
        axis=0,
    )
    spots = [
        jnp.where(keep, ((expert_ids[:, c] % 4) * 4 + expert_ids[:, c] // 4) * CAP + slots[c], -1)
        for c, keep in enumerate(kept)
    ]
    buffer_rows = jnp.arange(expert_count * CAP, dtype=jnp.int32)
    marks = [buffer_rows[:, None] == spot[None] for spot in spots]
    dispatch = (marks[0] | marks[1]).astype(bf16)
    grad_rows = jnp.dot(dispatch, cotangent, preferred_element_type=f32).astype(bf16)
    grad_rows = grad_rows.reshape(expert_count, CAP, model_width)

    buckets = span_buckets()[:, :, None] == jnp.arange(128, dtype=jnp.int32)
    picks = buckets.astype(bf16)
    (
        seq_tokens, qkv_weight, out_weight, smalls, projected, attended, log_totals, bias_tiles, inner_a, inner_b,
        grads_far,
    ) = run_front(tokens, w_qkv, w_out, small, w_in, grad_rows, picks)

    own_small = smalls[0]
    router_t = own_small[:, :16].transpose(1, 0, 2).reshape(expert_count, model_width)
    gain_first = own_small[:, 16].reshape(model_width).astype(f32)
    gain_second = own_small[:, 17].reshape(model_width).astype(f32)
    all_counts = smalls[:, :, 22:24, :expert_count].astype(f32).sum(axis=(0, 1))
    counts = 32.0 * all_counts[0] + all_counts[1]

    hidden_state = tokens.astype(f32) + jnp.dot(attended, out_weight, preferred_element_type=f32)
    normed_two, _ = normalize(hidden_state)
    second_norm = (normed_two * gain_second).astype(bf16)
    logits = lax.dot_general(second_norm, router_t, (((1,), (1,)), ((), ())), preferred_element_type=f32)
    route = jax.nn.softmax(logits, axis=-1)

    gates = [
        jnp.where(keep, jnp.sum(jnp.where(hit, route, 0.0), axis=1), 0.0) for hit, keep in zip(hits, kept)
    ]
    gate_rows = jnp.sum(
        jnp.where(marks[0], gates[0][None], 0.0) + jnp.where(marks[1], gates[1][None], 0.0), axis=1
    )
    send_rows = jnp.dot(dispatch, second_norm, preferred_element_type=f32).astype(bf16)
    gate_rows = jnp.pad(gate_rows.reshape(expert_count, 1, CAP), ((0, 0), (0, 7), (0, 128 - CAP)))
    returned, grad_copies, grad_inner, grad_outer = run_experts(
        send_rows.reshape(expert_count, CAP, model_width),
        gate_rows,
        grad_rows,
        grads_far,
        w_in,
        (inner_a, inner_b),
        w_down,
    )
    grad_inner = exchange_chips(grad_inner)
    columns = jnp.concatenate(
        [route] + [column.astype(f32)[:, None] for column in gates + spots + [expert_ids[:, 0], expert_ids[:, 1]]],
        axis=1,
    )
    gains = jnp.stack([gain_first, gain_second])
    count_row = jnp.pad(counts, (0, 128 - expert_count))[None]
    mixed, grad_hidden, grad_own, grad_other, grad_out_weight, sums = combine(
        returned.reshape(-1, model_width),
        grad_copies.reshape(-1, model_width),
        hidden_state,
        cotangent,
        jnp.pad(columns, ((0, 0), (0, 128 - columns.shape[1]))),
        out_weight,
        attended,
        jnp.pad(router_t, ((0, 128 - expert_count), (0, 0))),
        gains,
        count_row,
    )
    grad_other, grad_outer = lax.optimization_barrier((swap_z(grad_other, 1), grad_outer.astype(f32)))
    grad_tokens, grad_qkv, grad_out_weight, sums = run_back(
        grad_own,
        grad_other,
        grad_out_weight,
        sums,
        grad_hidden,
        gains,
        picks,
        projected,
        log_totals,
        bias_tiles,
        qkv_weight,
        seq_tokens,
    )
    (
        grad_inner, grad_tokens, grad_qkv, grad_out_weight, gain_one, gain_two, grad_router, grad_rel_bias, router_load,
        loss,
    ) = finish(
        grad_inner, grad_tokens, grad_qkv, grad_out_weight, sums, count_row, expert_count, group_heads
    )
    return (
        mixed,
        loss[0, 0],
        router_load,
        grad_tokens,
        gain_one[0],
        grad_qkv,
        grad_out_weight,
        grad_rel_bias,
        gain_two[0],
        grad_router,
        grad_inner,
        grad_outer,
    )


def solution(mesh):
    in_specs = (
        P(("gx", "gy"), None),
        P(("gx", "gy"), None),
        P("gx"),
        P(None, "gx", "gy"),
        P("gy", "gx"),
        P("gx", "gy"),
        P("gx"),
        P("gx", None),
        P("gy", "gx", None),
        P("gy", None, "gx"),
        P(("gx", "gy"), None),
    )
    out_specs = (
        P(("gx", "gy"), None),
        P(),
        P(),
        P(("gx", "gy"), None),
        P("gx"),
        P(None, "gx", "gy"),
        P("gy", "gx"),
        P("gx", "gy"),
        P("gx"),
        P("gx", None),
        P("gy", "gx", None),
        P("gy", None, "gx"),
    )
    return jax.shard_map(
        fast_device if fits_fast(mesh) else general_device, mesh=mesh, in_specs=in_specs, out_specs=out_specs, check_vma=False
    )
```

```python
import functools
import math

import jax
import jax.numpy as jnp
from jax import lax
from jax.experimental import pallas as pl
from jax.experimental.pallas import tpu as pltpu
from jax.sharding import PartitionSpec as P

LEN = 1024
BLK = 256
CAP = 80


bucket_edges = (12, 16, 23, 32, 46, 64, 91)
epsilon = 1e-06
loss_weight = 0.01
masked_score = -1e30


def bucket_of(offset):
    magnitude = jnp.abs(offset)
    far_bucket = 8 + sum(
        ((magnitude >= edge_value).astype(jnp.int32) for edge_value in bucket_edges)
    )
    return jnp.where(magnitude < 8, magnitude, far_bucket) + 16 * (offset > 0).astype(jnp.int32)


def normalize(values):
    row_scale = lax.rsqrt(jnp.mean(values * values, axis=-1, keepdims=True) + epsilon)
    return (values * row_scale, row_scale)


def norm_back(grad_out, normed, row_scale, gain_vector):
    grad_normed = grad_out * gain_vector
    grad_gain = jnp.sum(grad_out * normed, axis=0)
    grad_input = row_scale * (
        grad_normed - normed * jnp.mean(grad_normed * normed, axis=-1, keepdims=True)
    )
    return (grad_input, grad_gain)


def spread_offsets(along_offsets, row_count):
    head_count, span_width = along_offsets.shape
    key_count = span_width - row_count + 1
    tiled_rows = jnp.broadcast_to(
        along_offsets[:, None, :], (head_count, row_count, span_width)
    ).reshape(head_count, row_count * span_width)
    padded = jnp.pad(tiled_rows, ((0, 0), (0, row_count)))
    shaped = padded.reshape(head_count, row_count, span_width + 1)[:, :, :key_count]
    return shaped[:, :, ::-1]


def gather_offsets(score_grid, row_count):
    head_count = score_grid.shape[0]
    key_count = score_grid.shape[2]
    span_width = key_count + row_count - 1
    padded = jnp.pad(score_grid[:, :, ::-1], ((0, 0), (0, 0), (0, row_count)))
    flat_rows = padded.reshape(head_count, row_count * (key_count + row_count))[
        :, : row_count * span_width
    ]
    return jnp.sum(flat_rows.reshape(head_count, row_count, span_width), axis=1)


def offset_table(q_start, row_count, key_count, bucket_count):
    spot_index = jnp.arange(key_count + row_count - 1, dtype=jnp.int32)
    offsets = key_count - 1 - spot_index - q_start
    return (
        bucket_of(offsets)[:, None] == jnp.arange(bucket_count, dtype=jnp.int32)[None, :]
    ).astype(jnp.float32)


def block_scores(query_rows, key_rows, table_float, q_start):
    row_count = query_rows.shape[0]
    depth = query_rows.shape[2]
    key_count = key_rows.shape[0]
    picks_table = offset_table(q_start, row_count, key_count, table_float.shape[0])
    along_offsets = jnp.dot(picks_table, table_float, precision=lax.Precision.HIGHEST).T
    bias_grid = spread_offsets(along_offsets, row_count)
    scores = (
        jnp.einsum("qhd,khd->hqk", query_rows, key_rows, preferred_element_type=jnp.float32)
        / math.sqrt(depth)
        + bias_grid
    )
    query_pos = q_start + jnp.arange(row_count, dtype=jnp.int32)
    key_pos = jnp.arange(key_count, dtype=jnp.int32)
    allowed = key_pos[None, :] // BLK <= query_pos[:, None] // BLK
    return (jnp.where(allowed[None], scores, masked_score), picks_table)


def general_device(
    tokens, expert_ids, gain_attn, w_qkv, w_out, rel_bias, gain_ffn, router, w_in, w_down, cotangent
):
    shard_list = (gain_attn, w_qkv, w_out, rel_bias, gain_ffn, router, w_in, w_down)
    (
        gain_first,
        qkv_weight,
        out_weight,
        bias_table,
        gain_second,
        route_weight,
        inner_weight,
        outer_weight,
    ) = (
        lax.all_gather(shard_list[0], "gx", axis=0, tiled=True),
        lax.all_gather(shard_list[1], "gx", axis=1, tiled=True),
        lax.all_gather(shard_list[2], "gx", axis=1, tiled=True),
        lax.all_gather(shard_list[3], "gx", axis=0, tiled=True),
        lax.all_gather(shard_list[4], "gx", axis=0, tiled=True),
        lax.all_gather(shard_list[5], "gx", axis=0, tiled=True),
        lax.all_gather(shard_list[6], "gx", axis=1, tiled=True),
        lax.all_gather(shard_list[7], "gx", axis=2, tiled=True),
    )
    tok_dev = tokens.shape[0]
    count_x = lax.axis_size("gx")
    count_y = lax.axis_size("gy")
    total_tokens = tok_dev * count_x * count_y
    model_width = tokens.shape[1]
    expert_count = route_weight.shape[1]
    top_count = expert_ids.shape[1]
    local_experts = inner_weight.shape[0]
    head_count = bias_table.shape[1]
    head_width = qkv_weight.shape[2]
    depth = head_width // head_count
    q_rows = min(512, LEN)
    per_seq = LEN // q_rows
    inputs_float = tokens.astype(jnp.float32)
    normed_one, scale_one = normalize(inputs_float)
    first_norm = (normed_one * gain_first.astype(jnp.float32)).astype(jnp.bfloat16)
    group_rows = lax.all_gather(first_norm, "gy", axis=0, tiled=True)
    tok_group = group_rows.shape[0]
    seq_count = tok_group // LEN
    projected = jnp.einsum(
        "td,cdf->tcf", group_rows, qkv_weight, preferred_element_type=jnp.float32
    ).astype(jnp.bfloat16)
    projected = projected.reshape(tok_group, 3, head_count, depth)
    table_float = bias_table.astype(jnp.float32)

    def forward_block(item_index):
        seq_index = item_index // per_seq
        q_start = item_index % per_seq * q_rows
        query_rows = lax.dynamic_slice_in_dim(projected, seq_index * LEN + q_start, q_rows, 0)[:, 0]
        seq_rows = lax.dynamic_slice_in_dim(projected, seq_index * LEN, LEN, 0)
        scores, unused_picks = block_scores(query_rows, seq_rows[:, 1], table_float, q_start)
        row_max = jnp.max(scores, axis=-1, keepdims=True)
        expo_scores = jnp.exp(scores - row_max)
        row_total = jnp.sum(expo_scores, axis=-1, keepdims=True)
        soft_weights = (expo_scores / row_total).astype(jnp.bfloat16)
        block_out = jnp.einsum(
            "hqk,khd->qhd", soft_weights, seq_rows[:, 2], preferred_element_type=jnp.float32
        ).astype(jnp.bfloat16)
        return (block_out.reshape(q_rows, head_width), (row_max + jnp.log(row_total))[:, :, 0])

    attended, log_totals = lax.map(forward_block, jnp.arange(seq_count * per_seq, dtype=jnp.int32))
    attended = attended.reshape(tok_group, head_width)
    attn_sum = lax.psum_scatter(
        jnp.dot(attended, out_weight, preferred_element_type=jnp.float32).astype(jnp.bfloat16),
        "gy",
        scatter_dimension=0,
        tiled=True,
    ).astype(jnp.float32)
    hidden_state = inputs_float + attn_sum
    normed_two, scale_two = normalize(hidden_state)
    second_norm = (normed_two * gain_second.astype(jnp.float32)).astype(jnp.bfloat16)
    logits = jnp.dot(second_norm, route_weight, preferred_element_type=jnp.float32)
    route = jax.nn.softmax(logits, axis=-1)
    chosen = (
        expert_ids.reshape(-1)[:, None] == jnp.arange(expert_count, dtype=jnp.int32)[None, :]
    ).astype(jnp.int32)
    earlier = jnp.cumsum(chosen, axis=0) - chosen
    slot = jnp.sum(earlier * chosen, axis=-1).reshape(tok_dev, top_count)
    kept = (slot < CAP).astype(jnp.float32)
    counts, prob_sums = lax.psum(
        (jnp.sum(chosen, axis=0).astype(jnp.float32), jnp.sum(route, axis=0)), ("gx", "gy")
    )
    loss = expert_count * jnp.sum(counts / (total_tokens * top_count) * (prob_sums / total_tokens))
    router_load = jnp.stack(
        [
            expert_count * counts / (total_tokens * top_count),
            expert_count * prob_sums / total_tokens,
        ],
        axis=0,
    )
    slot_place = expert_ids * CAP + jnp.minimum(slot, CAP - 1)
    buffer_index = jnp.arange(expert_count * CAP, dtype=jnp.int32)[:, None, None]
    hit_table = (buffer_index == slot_place[None]).astype(jnp.float32) * kept[None]
    dispatch_matrix = jnp.sum(hit_table, axis=-1).astype(jnp.bfloat16)
    send_rows = jnp.dot(dispatch_matrix, second_norm, preferred_element_type=jnp.float32).astype(
        jnp.bfloat16
    )
    send_rows = send_rows.reshape(count_y, local_experts, CAP, model_width)
    received = lax.all_to_all(send_rows, "gy", split_axis=0, concat_axis=0, tiled=True)
    upper = jnp.einsum("slcd,ldf->slcf", received, inner_weight, preferred_element_type=jnp.float32)
    half_width = upper.shape[-1] // 2
    hidden_rows = (
        jax.nn.gelu(upper[..., :half_width], approximate=True) * upper[..., half_width:]
    ).astype(jnp.bfloat16)
    expert_out = jnp.einsum(
        "slcf,lfd->slcd", hidden_rows, outer_weight, preferred_element_type=jnp.float32
    ).astype(jnp.bfloat16)
    expert_out, upper, received = (expert_out, upper, received)
    returned = lax.all_to_all(expert_out, "gy", split_axis=0, concat_axis=0, tiled=True).reshape(
        expert_count * CAP, model_width
    )
    picked_rows = jnp.take(returned, slot_place, axis=0).astype(jnp.float32)
    gate_value = jnp.take_along_axis(route, expert_ids, axis=1) * kept
    mixed = hidden_state + jnp.sum(picked_rows * gate_value[:, :, None], axis=1)
    (
        gain_first,
        qkv_weight,
        out_weight,
        bias_table,
        gain_second,
        route_weight,
        inner_weight,
        outer_weight,
    ) = (
        lax.all_gather(shard_list[0], "gx", axis=0, tiled=True),
        lax.all_gather(shard_list[1], "gx", axis=1, tiled=True),
        lax.all_gather(shard_list[2], "gx", axis=1, tiled=True),
        lax.all_gather(shard_list[3], "gx", axis=0, tiled=True),
        lax.all_gather(shard_list[4], "gx", axis=0, tiled=True),
        lax.all_gather(shard_list[5], "gx", axis=0, tiled=True),
        lax.all_gather(shard_list[6], "gx", axis=1, tiled=True),
        lax.all_gather(shard_list[7], "gx", axis=2, tiled=True),
    )
    table_float = bias_table.astype(jnp.float32)
    grad_mixed = cotangent.astype(jnp.float32)
    grad_gate = kept * jnp.sum(grad_mixed[:, None, :] * picked_rows, axis=-1)
    gate_matrix = jnp.sum(hit_table * gate_value[None], axis=-1)
    grad_buffer = jnp.dot(gate_matrix, grad_mixed, precision=lax.Precision.HIGHEST).astype(
        jnp.bfloat16
    )
    grad_expert = lax.all_to_all(
        grad_buffer.reshape(count_y, local_experts, CAP, model_width),
        "gy",
        split_axis=0,
        concat_axis=0,
        tiled=True,
    )
    half_width = upper.shape[-1] // 2
    activated, pull_gelu = jax.vjp(
        lambda gate_part, up_part: jax.nn.gelu(gate_part, approximate=True) * up_part,
        upper[..., :half_width],
        upper[..., half_width:],
    )
    hidden_rows = activated.astype(jnp.bfloat16)
    grad_hidden = jnp.einsum(
        "slcd,lfd->slcf", grad_expert, outer_weight, preferred_element_type=jnp.float32
    )
    grad_outer = jnp.einsum(
        "slcf,slcd->lfd", hidden_rows, grad_expert, preferred_element_type=jnp.float32
    )
    grad_gate_part, grad_up_part = pull_gelu(grad_hidden)
    grad_upper = jnp.concatenate([grad_gate_part, grad_up_part], axis=-1).astype(jnp.bfloat16)
    grad_inner = jnp.einsum(
        "slcd,slcf->ldf", received, grad_upper, preferred_element_type=jnp.float32
    )
    grad_received = jnp.einsum(
        "slcf,ldf->slcd", grad_upper, inner_weight, preferred_element_type=jnp.float32
    ).astype(jnp.bfloat16)
    grad_copies = lax.all_to_all(
        grad_received, "gy", split_axis=0, concat_axis=0, tiled=True
    ).reshape(expert_count * CAP, model_width)
    grad_second = jnp.sum(
        jnp.take(grad_copies, slot_place, axis=0).astype(jnp.float32) * kept[:, :, None], axis=1
    )
    expert_hits = (expert_ids[:, :, None] == jnp.arange(expert_count, dtype=jnp.int32)).astype(
        jnp.float32
    )
    grad_route = (
        jnp.sum(grad_gate[:, :, None] * expert_hits, axis=1)
        + loss_weight * expert_count * (counts / (total_tokens * top_count)) / total_tokens
    )
    grad_logits = (
        route * (grad_route - jnp.sum(route * grad_route, axis=-1, keepdims=True))
    ).astype(jnp.bfloat16)
    grad_router = jnp.dot(second_norm.T, grad_logits, preferred_element_type=jnp.float32)
    grad_second = grad_second + jnp.dot(
        grad_logits, route_weight.T, preferred_element_type=jnp.float32
    )
    grad_hidden_state, grad_gain_second = norm_back(
        grad_second, normed_two, scale_two, gain_second.astype(jnp.float32)
    )
    grad_hidden_state = grad_mixed + grad_hidden_state
    piece_rows = lax.all_gather(grad_hidden_state.astype(jnp.bfloat16), "gy", axis=0, tiled=True)
    grad_out_weight = jnp.einsum(
        "tf,td->fd", attended, piece_rows, preferred_element_type=jnp.float32
    )
    update_rows = jnp.dot(piece_rows, out_weight.T, preferred_element_type=jnp.float32).astype(
        jnp.bfloat16
    )
    grad_out_weight, grad_attended = (grad_out_weight, update_rows)

    def backward_sequence(seq_index):
        seq_rows = lax.dynamic_slice_in_dim(projected, seq_index * LEN, LEN, 0)
        key_rows = seq_rows[:, 1]
        value_rows = seq_rows[:, 2]
        grad_keys = jnp.zeros((LEN, head_count, depth), jnp.float32)
        grad_values = jnp.zeros((LEN, head_count, depth), jnp.float32)
        grad_table = jnp.zeros(table_float.shape, jnp.float32)
        grad_queries = []
        for block_index in range(per_seq):
            q_start = block_index * q_rows
            query_rows = seq_rows[q_start : q_start + q_rows, 0]
            grad_out = lax.dynamic_slice_in_dim(
                grad_attended, seq_index * LEN + q_start, q_rows, 0
            ).reshape(q_rows, head_count, depth)
            scores, picks_table = block_scores(query_rows, key_rows, table_float, q_start)
            block_lse = log_totals[seq_index * per_seq + block_index]
            soft_probs = jnp.exp(scores - block_lse[:, :, None])
            grad_probs = jnp.einsum(
                "qhd,khd->hqk", grad_out, value_rows, preferred_element_type=jnp.float32
            )
            grad_scores = (
                soft_probs * (grad_probs - jnp.sum(soft_probs * grad_probs, axis=-1, keepdims=True))
            ).astype(jnp.bfloat16)
            grad_queries.append(
                jnp.einsum(
                    "hqk,khd->qhd", grad_scores, key_rows, preferred_element_type=jnp.float32
                )
                / math.sqrt(depth)
            )
            grad_keys = grad_keys + jnp.einsum(
                "hqk,qhd->khd", grad_scores, query_rows, preferred_element_type=jnp.float32
            ) / math.sqrt(depth)
            grad_values = grad_values + jnp.einsum(
                "hqk,qhd->khd",
                soft_probs.astype(jnp.bfloat16),
                grad_out,
                preferred_element_type=jnp.float32,
            )
            along_grads = gather_offsets(grad_scores.astype(jnp.float32), q_rows)
            grad_table = grad_table + jnp.dot(
                picks_table.T, along_grads.T, precision=lax.Precision.HIGHEST
            )
        stacked = jnp.stack(
            [jnp.concatenate(grad_queries, axis=0), grad_keys, grad_values], axis=1
        ).astype(jnp.bfloat16)
        return (stacked, grad_table)

    grad_projected, table_parts = lax.map(backward_sequence, jnp.arange(seq_count, dtype=jnp.int32))
    grad_projected = grad_projected.reshape(tok_group, 3, head_width)
    grad_bias_table = jnp.sum(table_parts, axis=0)
    grad_qkv_weight = jnp.einsum(
        "td,tcf->cdf", group_rows, grad_projected, preferred_element_type=jnp.float32
    )
    grad_slice = lax.slice_in_dim(grad_projected, 0, tok_dev * lax.axis_size("gy"), axis=0)
    grad_first = lax.psum_scatter(
        jnp.einsum(
            "tcf,cdf->td", grad_slice, qkv_weight, preferred_element_type=jnp.float32
        ).astype(jnp.bfloat16),
        "gy",
        scatter_dimension=0,
        tiled=True,
    ).astype(jnp.float32)
    grad_inputs, grad_gain_first = norm_back(
        grad_first, normed_one, scale_one, gain_first.astype(jnp.float32)
    )
    grad_tokens = grad_hidden_state + grad_inputs
    grad_gain_first, grad_gain_second, grad_router = (
        lax.psum(grad_gain_first.astype(jnp.bfloat16), "gy").astype(jnp.float32),
        lax.psum(grad_gain_second.astype(jnp.bfloat16), "gy").astype(jnp.float32),
        lax.psum(grad_router.astype(jnp.bfloat16), "gy").astype(jnp.float32),
    )
    summed_grads = (
        lax.psum_scatter(
            grad_gain_first.astype(jnp.bfloat16), "gx", scatter_dimension=0, tiled=True
        ).astype(jnp.float32),
        lax.psum_scatter(
            grad_qkv_weight.astype(jnp.bfloat16), "gx", scatter_dimension=1, tiled=True
        ).astype(jnp.float32),
        lax.psum_scatter(
            grad_out_weight.astype(jnp.bfloat16), "gx", scatter_dimension=1, tiled=True
        ).astype(jnp.float32),
        lax.psum_scatter(
            grad_bias_table.astype(jnp.bfloat16), "gx", scatter_dimension=0, tiled=True
        ).astype(jnp.float32),
        lax.psum_scatter(
            grad_gain_second.astype(jnp.bfloat16), "gx", scatter_dimension=0, tiled=True
        ).astype(jnp.float32),
        lax.psum_scatter(
            grad_router.astype(jnp.bfloat16), "gx", scatter_dimension=0, tiled=True
        ).astype(jnp.float32),
        lax.psum_scatter(
            grad_inner.astype(jnp.bfloat16), "gx", scatter_dimension=1, tiled=True
        ).astype(jnp.float32),
        lax.psum_scatter(
            grad_outer.astype(jnp.bfloat16), "gx", scatter_dimension=2, tiled=True
        ).astype(jnp.float32),
    )
    return (
        mixed.astype(jnp.bfloat16),
        loss,
        router_load,
        grad_tokens,
        summed_grads[0],
        summed_grads[1],
        summed_grads[2],
        summed_grads[3],
        summed_grads[4],
        summed_grads[5],
        summed_grads[6],
        summed_grads[7],
    )


def dot_nn(a, b):
    return lax.dot_general(a, b, (((1,), (0,)), ((), ())), preferred_element_type=jnp.float32)

def dot_nt(a, b):
    return lax.dot_general(a, b, (((1,), (1,)), ((), ())), preferred_element_type=jnp.float32)

def span_buckets():
    k = jnp.arange(2 * BLK, dtype=jnp.int32)
    return jnp.stack([bucket_of(BLK - k - BLK * d) for d in range(2)])

AXES = ("gx", "gy")
MESH_ID = pl.DeviceIdType.MESH


def fits_fast(mesh):
    return mesh.shape["gx"] == 8 and mesh.shape["gy"] == 4


def places():
    x = lax.axis_index("gx")
    z = lax.axis_index("gy")
    core = x % 2
    chip = x // 2
    along_z = (z + 1 - 2 * (z % 2), (z + 2) % 4, 3 - z)
    chips = (chip + 1 - 2 * (chip % 2), (chip + 2) % 4, 3 - chip)
    return x, z, along_z, tuple(2 * other + core for other in chips), x + 1 - 2 * core


def attend_front(pair, proj_ref, span_ref, tile_ref, attended_ref, lse_ref, kept_ref):
    length = proj_ref.shape[1]
    blocks = length // BLK
    depth = 64
    wide = 2 * depth
    here = slice(pair * wide, (pair + 1) * wide)
    lane = lax.broadcasted_iota(jnp.int32, (1, wide), 1)
    for h in range(2):
        for d in range(2):
            row = span_ref[d, 2 * pair + h:2 * pair + h + 1, :]
            spread = jnp.broadcast_to(row, (BLK, 2 * BLK))
            turned = pltpu.roll(spread, 0, 1, stride=1, stride_axis=0)
            tile_ref[h, d] = turned[:, BLK:]
            kept_ref[2 * pair + h, d] = turned[:, BLK:].astype(jnp.bfloat16)
    far = [span_ref[1, 2 * pair + h:2 * pair + h + 1, 2 * BLK - 1:2 * BLK] for h in range(2)]
    keys = proj_ref[1, :, here]
    values_t = proj_ref[2, :, here].T
    for block in range(blocks):
        rows = pl.ds(block * BLK, BLK)
        query = proj_ref[0, rows, here] * jnp.bfloat16(0.125)
        key_count = (block + 1) * BLK
        outs = []
        for h in range(2):
            picked = jnp.where((lane // depth) == h, query, jnp.bfloat16(0))
            scores = dot_nt(keys[:key_count], picked)
            parts = []
            for kb in range(block + 1):
                part = scores[kb * BLK:(kb + 1) * BLK]
                d = block - kb
                parts.append(part + (tile_ref[h, d] if d < 2 else far[h]))
            top = functools.reduce(jnp.maximum, [jnp.max(p, axis=0, keepdims=True) for p in parts])
            parts = [jnp.exp(p - top) for p in parts]
            total = functools.reduce(jnp.add, [jnp.sum(p, axis=0, keepdims=True) for p in parts])
            scale = 1.0 / total
            weights = jnp.concatenate([(p * scale).astype(jnp.bfloat16) for p in parts], axis=0)
            outs.append(dot_nn(values_t[h * depth:(h + 1) * depth, :key_count], weights))
            lse_ref[pair, h:h + 1, rows] = top + jnp.log(total)
        attended_ref[rows, here] = jnp.concatenate(outs, axis=0).T.astype(jnp.bfloat16)


def front_kernel(
    tok_ref, wq_ref, wo_ref, small_ref, inner_ref, cot_hbm, picks_ref, ids_ref, spots_ref,
    seq_out, wqs_out, wos_out, smalls_out, proj_ref, att_ref, lse_ref, kept_ref, hidden_ref, cols_ref, gates_ref, rows_hbm, grads_hbm, inner_a_ref, inner_b_ref, inner_c_ref, far_ref,
    seq_ref, wqs_ref, wos_ref, wos_in_ref, smalls_ref, normed_ref, attended_ref, got_ref, span_ref, tile_ref, cot_ref, grads_ref, rows_ref, second_ref, gate_parts_ref,
    send_sem, recv_sem, local_sem, out_sem,
):
    x, z, along_z, across, sibling = places()
    half = z % 2
    f32, bf16 = jnp.float32, jnp.bfloat16
    peers = [(x, other) for other in along_z] + [(other, z) for other in across] + [(sibling, z)]
    far_peers = [(device, plane) for plane in along_z[1:] for device in (x,) + across]
    peers += [peer for n, peer in enumerate(far_peers) if n % 4]
    barrier = pltpu.get_barrier_semaphore()
    for peer in peers:
        pl.semaphore_signal(barrier, inc=1, device_id=peer, device_id_type=MESH_ID)
    depth = wq_ref.shape[1]
    group = wq_ref.shape[2]
    rows_out = wo_ref.shape[0]
    rows, width = tok_ref.shape

    def qkv_part(owner, slot):
        return wqs_ref.at[slot, owner]

    def out_part(owner, slot, slots):
        return wos_in_ref.at[owner, pl.ds(slot * rows_out, slots * rows_out), :]

    keeps = [
        pltpu.make_async_copy(source, target, local_sem.at[n])
        for n, (source, target) in enumerate(
            ((small_ref, smalls_ref.at[0, x]), (wo_ref, out_part(x, 0, 1)), (wq_ref, qkv_part(x, 0)),
             (tok_ref, seq_ref.at[half]), (cot_hbm, cot_ref))
        )
    ]
    for copy in keeps:
        copy.start()
    pl.semaphore_wait(barrier, len(peers))
    started = []

    def send(source, target, device):
        index = len(started)
        copy = pltpu.make_async_remote_copy(
            src_ref=source, dst_ref=target, send_sem=send_sem.at[index], recv_sem=recv_sem.at[index],
            device_id=device, device_id_type=MESH_ID,
        )
        copy.start()
        started.append(copy)
        return copy

    out_slots = (2, 1, 3)
    near = across + (sibling,)
    small_z = [send(small_ref, smalls_ref.at[j + 1, x], (x, along_z[j])) for j in range(3)]
    wq_z = send(wq_ref, qkv_part(x, 1), (x, along_z[1]))
    wq_first = [send(wq_ref, qkv_part(x, 0), (other, z)) for other in near]
    tok_z = send(tok_ref, seq_ref.at[half], (x, along_z[0]))
    wo_z = [send(wo_ref, out_part(x, out_slots[j], 1), (x, along_z[j])) for j in range(3)]
    blocks = rows_ref.shape[0] // 4
    slots = rows_ref.shape[1]
    chunk = blocks * slots
    slot_row = lax.broadcasted_iota(jnp.int32, (chunk, 1), 0).astype(f32)

    def marks(i):
        return [(slot_row + i * chunk == spots_ref[c:c + 1, :]).astype(bf16) for c in range(2)]

    keeps[4].wait()
    for i in range(4):
        first, second = marks(i)
        grads_ref[i * blocks:(i + 1) * blocks] = (
            dot_nn(first + second, cot_ref[...]).astype(bf16).reshape(blocks, slots, width)
        )
    keeps[0].wait()
    for copy in small_z:
        copy.wait_recv()
    small_x = [send(smalls_ref.at[:, x], smalls_ref.at[:, x], (other, z)) for other in near]
    wq_z.wait_recv()
    wq_second = [send(qkv_part(x, 1), qkv_part(x, 1), (other, z)) for other in near]
    far_copies = [
        send(grads_ref.at[(device // 2) * 4 + plane], far_ref.at[n // 4, x // 2], (device, plane))
        for n, (device, plane) in enumerate(far_peers)
    ]
    small_on = []
    first_on = []
    for j in range(3):
        owner = across[j]
        small_x[j].wait_recv()
        small_on.append(send(smalls_ref.at[:, owner], smalls_ref.at[:, owner], (sibling, z)))
        wq_first[j].wait_recv()
        first_on.append(send(qkv_part(owner, 0), qkv_part(owner, 0), (sibling, z)))
    for copy in [small_x[3], wq_first[3]] + small_on + first_on:
        copy.wait_recv()
    for copy in keeps[1:4]:
        copy.wait()
    inner_copies = [
        send(inner_ref.at[device // 2], target, (device, z))
        for device, target in zip(across, (inner_a_ref, inner_b_ref, inner_c_ref))
    ]

    own_smalls = [smalls_ref[0, g].astype(f32) for g in range(8)]
    gain = jnp.concatenate([part[16:17, :] for part in own_smalls], axis=1)
    heads = span_ref.shape[1] // 2
    lanes = lax.broadcasted_iota(jnp.int32, (1, depth), 1)
    table = jnp.concatenate([part[18:22, :] for part in own_smalls], axis=0)
    other_table = jnp.concatenate([smalls_ref[2, g].astype(f32)[18:22, :] for g in range(8)], axis=0)
    table = jnp.where(lanes < heads, table, pltpu.roll(other_table, heads, 1))
    table = jnp.where(lanes < 2 * heads, table, 0.0)
    table = jnp.concatenate([table, jnp.zeros((depth - table.shape[0], depth), f32)], axis=0)
    table = table.T[:2 * heads, :].astype(bf16)
    for d in range(2):
        span_ref[d] = dot_nt(table, picks_ref[d])
    step = rows // 2

    def norm(side, i):
        normed, _ = normalize(seq_ref[side, i * step:(i + 1) * step, :].astype(f32))
        here = pl.ds(pl.multiple_of(side * rows + i * step, step), step)
        normed_ref[here, :] = (normed * gain).astype(bf16)

    for i in range(2):
        norm(half, i)
    tok_z.wait_recv()
    for i in range(2):
        norm(1 - half, i)

    def project(slot):
        here = slice(slot * group, (slot + 1) * group)
        for c in range(3):
            proj_ref[c, :, here] = dot_nn(normed_ref[...], wqs_ref[slot, :, c].reshape(width, group)).astype(bf16)

    def attend(pair):
        attend_front(pair, proj_ref, span_ref, tile_ref, attended_ref, lse_ref, kept_ref)

    def exchange(slot):
        here = pl.ds(slot * group, group)
        there = pl.ds(pl.multiple_of((1 - half) * rows, rows), rows)
        return send(attended_ref.at[there, here], got_ref.at[:, here], (x, along_z[0]))

    project(0)
    for copy in wo_z:
        copy.wait_recv()
    wo_x = [send(out_part(x, 0, 4), out_part(x, 0, 4), (other, z)) for other in near]
    attend(0)
    second_on = []
    for j in range(3):
        owner = across[j]
        wq_second[j].wait_recv()
        second_on.append(send(qkv_part(owner, 1), qkv_part(owner, 1), (sibling, z)))
    attend(1)
    got_0 = exchange(0)
    for copy in [wq_second[3]] + second_on:
        copy.wait_recv()
    project(1)
    outs = [
        pltpu.make_async_copy(source, target, out_sem.at[n])
        for n, (source, target) in enumerate(((seq_ref, seq_out), (smalls_ref, smalls_out), (wqs_ref, wqs_out)))
    ]
    for copy in outs:
        copy.start()
    attend(2)
    attend(3)
    got_1 = exchange(1)
    wo_on = []
    for j in range(3):
        owner = across[j]
        wo_x[j].wait_recv()
        wo_on.append(send(out_part(owner, 0, 4), out_part(owner, 0, 4), (sibling, z)))
    for copy in [wo_x[3]] + wo_on:
        copy.wait_recv()
    for owner in range(8):
        wos_ref[:, owner * depth:(owner + 1) * depth] = wos_in_ref[owner]
    outs.append(pltpu.make_async_copy(wos_ref, wos_out, out_sem.at[3]))
    outs[3].start()
    own = pl.ds(pl.multiple_of(half * rows, rows), rows)
    att_ref[:, :2 * group] = attended_ref[own, :]
    for copy in (got_0, got_1):
        copy.wait_recv()
    att_ref[:, 2 * group:] = got_ref[...]

    gain_second = jnp.concatenate([part[17:18, :] for part in own_smalls], axis=1)
    experts = rows_ref.shape[0]
    router = jnp.concatenate([part[:experts, :] for part in own_smalls], axis=1)
    router = jnp.concatenate([router, jnp.zeros((depth - experts, width), f32)], axis=0).astype(bf16)
    lanes_f = lanes.astype(f32)
    for i in range(2):
        here = slice(i * step, (i + 1) * step)
        hidden = seq_ref[half, here, :].astype(f32) + dot_nn(att_ref[here, :], wos_ref[...])
        hidden_ref[here, :] = hidden
        normed, _ = normalize(hidden)
        second = (normed * gain_second).astype(bf16)
        second_ref[here, :] = second
        logits = jnp.where(lanes < experts, dot_nt(second, router), -1e30)
        route = jnp.exp(logits - jnp.max(logits, axis=1, keepdims=True))
        route = route / jnp.sum(route, axis=1, keepdims=True)
        ids = ids_ref[here, :]
        gates = []
        for c in range(2):
            gate = jnp.sum(jnp.where(lanes_f == ids[:, experts + 4 + c:experts + 5 + c], route, 0.0), axis=1, keepdims=True)
            gates.append(jnp.where(ids[:, experts + 2 + c:experts + 3 + c] >= 0.0, gate, 0.0))
            high = gates[c].astype(bf16).astype(f32)
            gate_parts_ref[c, here, :] = jnp.where(
                lanes == 0, high, jnp.where(lanes == 1, gates[c] - high, 0.0)
            ).astype(bf16)
        cols_ref[here, :] = jnp.where(
            lanes < experts, route, jnp.where(lanes == experts, gates[0], jnp.where(lanes == experts + 1, gates[1], ids))
        )
    for i in range(4):
        first, second = marks(i)
        rows_ref[i * blocks:(i + 1) * blocks] = (
            dot_nn(first + second, second_ref[...]).astype(bf16).reshape(blocks, slots, width)
        )
        parts = dot_nn(first, gate_parts_ref[0]) + dot_nn(second, gate_parts_ref[1])
        for n in range(blocks):
            turned = parts[n * slots:(n + 1) * slots, :].T
            line = jnp.concatenate([turned[0:1, :] + turned[1:2, :], jnp.zeros((1, depth - slots), f32)], axis=1)
            gates_ref[i * blocks + n] = jnp.broadcast_to(line, (8, depth))
    outs.append(pltpu.make_async_copy(rows_ref, rows_hbm, out_sem.at[4]))
    outs.append(pltpu.make_async_copy(grads_ref, grads_hbm, out_sem.at[5]))
    for copy in outs[4:]:
        copy.start()
    for copy in inner_copies + far_copies:
        copy.wait_recv()
    for copy in started:
        copy.wait_send()
    for copy in outs:
        copy.wait()


def run_front(tokens, w_qkv, w_out, small, w_in, cotangent, picks, ids, spots, experts):
    rows, width = tokens.shape
    group = w_qkv.shape[2]
    f32, bf16 = jnp.float32, jnp.bfloat16
    heads = 2 * group // 64
    anywhere = pl.BlockSpec(memory_space=pl.ANY)
    inside = pl.BlockSpec(memory_space=pltpu.VMEM)
    seq = (2, rows, width)
    wqs = (2, 8) + w_qkv.shape
    wos = (width, width)
    smalls = (4, 8) + small.shape
    copies_count = 3 + 1 + 4 + 1 + 3 + 4 + 4 + 3 + 3 + 4 + 3 + 3 + 3 + 2 + 8
    return pl.pallas_call(
        front_kernel,
        out_shape=(
            jax.ShapeDtypeStruct(seq, bf16),
            jax.ShapeDtypeStruct(wqs, bf16),
            jax.ShapeDtypeStruct(wos, bf16),
            jax.ShapeDtypeStruct(smalls, bf16),
            jax.ShapeDtypeStruct((3, 2 * rows, 2 * group), bf16),
            jax.ShapeDtypeStruct((rows, width), bf16),
            jax.ShapeDtypeStruct((heads // 2, 2, 2 * rows), f32),
            jax.ShapeDtypeStruct((heads, 2, BLK, BLK), bf16),
            jax.ShapeDtypeStruct((rows, width), f32),
            jax.ShapeDtypeStruct((rows, 128), f32),
            jax.ShapeDtypeStruct((experts, 8, 128), f32),
            jax.ShapeDtypeStruct((experts, CAP, width), bf16),
            jax.ShapeDtypeStruct((experts, CAP, width), bf16),
            jax.ShapeDtypeStruct(w_in.shape[1:], bf16),
            jax.ShapeDtypeStruct(w_in.shape[1:], bf16),
            jax.ShapeDtypeStruct(w_in.shape[1:], bf16),
            jax.ShapeDtypeStruct((2, 4, CAP, width), bf16),
        ),
        in_specs=[anywhere] * 6 + [inside] * 3,
        out_specs=(anywhere,) * 4 + (inside,) * 7 + (anywhere,) * 6,
        scratch_shapes=[
            pltpu.VMEM(seq, bf16),
            pltpu.VMEM(wqs, bf16),
            pltpu.VMEM(wos, bf16),
            pltpu.VMEM((8, width, width // 8), bf16),
            pltpu.VMEM(smalls, bf16),
            pltpu.VMEM((2 * rows, width), bf16),
            pltpu.VMEM((2 * rows, 2 * group), bf16),
            pltpu.VMEM((rows, 2 * group), bf16),
            pltpu.VMEM((2, heads, 2 * BLK), f32),
            pltpu.VMEM((2, 2, BLK, BLK), f32),
            pltpu.VMEM((rows, width), bf16),
            pltpu.VMEM((experts, CAP, width), bf16),
            pltpu.VMEM((experts, CAP, width), bf16),
            pltpu.VMEM((rows, width), bf16),
            pltpu.VMEM((2, rows, 128), bf16),
            pltpu.SemaphoreType.DMA((copies_count,)),
            pltpu.SemaphoreType.DMA((copies_count,)),
            pltpu.SemaphoreType.DMA((5,)),
            pltpu.SemaphoreType.DMA((6,)),
        ],
        compiler_params=pltpu.CompilerParams(
            collective_id=0, has_side_effects=True, vmem_limit_bytes=56 * 2**20
        ),
        cost_estimate=pl.CostEstimate(flops=60 * 10**9, bytes_accessed=30 * 2**20, transcendentals=0),
        name="run_front",
    )(tokens, w_qkv, w_out, small, w_in, cotangent, picks, ids, spots)


def expert_kernel(
    rows_ref, gates_ref, grads_ref, far_ref, inner_ref, inner_a_ref, inner_b_ref, inner_c_ref, outer_ref,
    returned_ref, copies_ref, ginner_ref, ginner_sent_ref, gouter_ref, inner_in_ref, outer_land_ref,
    x_ref, x_t_ref, dy_ref, gates_in_ref, win_ref, wout_ref, upper_ref, hid_ref, out_ref, back_ref,
    stage_in_ref, stage_out_ref, add_in_ref, outer_in_ref,
    row_send, row_recv, gate_send, gate_recv, out_send, out_recv, copy_send, copy_recv,
    grad_send, grad_recv, w_send, w_recv, part_send, part_recv, gout_send, gout_recv, local_sem, join_sem, load_sem,
):
    x, z, along_z, across, sibling = places()
    core = x % 2
    chip = x // 2
    me = chip * 4 + z
    _, _, slots, width = x_ref.shape
    chunk = 4 * slots
    tokens = 4 * chunk
    hidden = hid_ref.shape[1]
    half = stage_out_ref.shape[2]
    tiles = hidden // half
    shard = width // 8
    f32, bf16 = jnp.float32, jnp.bfloat16
    planes = (z,) + along_z
    chips = (chip,) + tuple(device // 2 for device in across)
    pair = (sibling, z)

    peers = [(m, k) for m in range(4) for k in range(4) if m or k]
    barrier = pltpu.get_barrier_semaphore()
    for m, k in peers:
        pl.semaphore_signal(
            barrier, inc=1, device_id=(2 * chips[k] + core, planes[m]), device_id_type=MESH_ID
        )
    pl.semaphore_signal(barrier, inc=1, device_id=pair, device_id_type=MESH_ID)
    pl.semaphore_wait(barrier, len(peers) + 1)

    def remote(source, target, sems, index, device):
        return pltpu.make_async_remote_copy(
            src_ref=source, dst_ref=target, send_sem=sems[0].at[index], recv_sem=sems[1].at[index],
            device_id=device, device_id_type=MESH_ID,
        )

    def to_plane(m, source_of, target_of, sems):
        return [
            remote(
                source_of(m, chips[k]), target_of(m), sems, 4 * m + k, (2 * chips[k] + core, planes[m])
            )
            for k in range(4)
            if m or k
        ]

    def lanes_of(owner):
        return pl.ds(pl.multiple_of(owner * shard, shard), shard)

    row_copies = [
        to_plane(
            m, lambda m, c: rows_ref.at[c * 4 + planes[m]], lambda m: x_ref.at[m, chip], (row_send, row_recv)
        )
        for m in range(4)
    ]
    gate_copies = [
        to_plane(
            m, lambda m, c: gates_ref.at[c * 4 + planes[m]], lambda m: gates_in_ref.at[m, chip],
            (gate_send, gate_recv),
        )
        for m in range(4)
    ]
    keeps = [
        pltpu.make_async_copy(inner_ref.at[chip], win_ref.at[chip, core], local_sem.at[0]),
        pltpu.make_async_copy(inner_a_ref, win_ref.at[chips[1], core], local_sem.at[1]),
        pltpu.make_async_copy(inner_b_ref, win_ref.at[chips[2], core], local_sem.at[2]),
        pltpu.make_async_copy(grads_ref.at[me], dy_ref.at[0, chip], local_sem.at[3]),
        pltpu.make_async_copy(inner_c_ref, win_ref.at[chips[3], core], local_sem.at[10]),
        pltpu.make_async_copy(rows_ref.at[me], x_ref.at[0, chip], local_sem.at[4]),
        pltpu.make_async_copy(gates_ref.at[me], gates_in_ref.at[0, chip], local_sem.at[5]),
        pltpu.make_async_copy(outer_ref.at[chip], wout_ref.at[:, lanes_of(x)], local_sem.at[6]),
    ]
    pair_inner = [
        remote(source, win_ref.at[chips[k], core], (w_send, w_recv), k, pair)
        for k, source in enumerate((inner_ref.at[chip], inner_a_ref, inner_b_ref, inner_c_ref))
    ]
    outer_copies = [
        remote(outer_ref.at[device // 2], outer_land_ref.at[x], (w_send, w_recv), 4 + j, (device, z))
        for j, device in enumerate(across)
    ]
    pair_outer = [remote(outer_ref.at[chip], outer_land_ref.at[x], (w_send, w_recv), 7, pair)] + [
        remote(outer_land_ref.at[device], outer_land_ref.at[device], (w_send, w_recv), 8 + j, pair)
        for j, device in enumerate(across)
    ]
    owners = across + (sibling,) + tuple(device + 1 - 2 * core for device in across)
    outer_loads = [
        pltpu.make_async_copy(outer_land_ref.at[owner], wout_ref.at[:, lanes_of(owner)], load_sem.at[n])
        for n, owner in enumerate(owners)
    ]
    for m in ROW_ORDER:
        for copy in row_copies[m]:
            copy.start()
    for copy in keeps + pair_inner + outer_copies + pair_outer[:1]:
        copy.start()
    for m in range(4):
        for copy in gate_copies[m]:
            copy.start()
    grad_copies = [
        to_plane(
            m, lambda m, c: grads_ref.at[c * 4 + planes[m]], lambda m: dy_ref.at[m, chip], (grad_send, grad_recv)
        )
        for m in range(2)
    ]
    far_grads = pltpu.make_async_copy(far_ref, dy_ref.at[pl.ds(2, 2)], local_sem.at[9])
    far_grads.start()
    for copy in keeps:
        copy.wait()
    for copy in pair_inner:
        copy.wait()

    def cols(tile, part):
        return pl.ds(pl.multiple_of(part * hidden + tile * half, half), half)

    def weight(tile, part):
        return win_ref[:, :, :, cols(tile, part)].reshape(width, half)

    def block(m):
        return pl.ds(m * chunk, chunk)

    def widen(m):
        for copy in row_copies[m]:
            copy.wait_recv()
        rows = x_ref.at[m]

        def step(tile, carry):
            values = rows[...].reshape(chunk, width)
            gate = dot_nn(values, weight(tile, 0))
            up = dot_nn(values, weight(tile, 1))
            square = gate * gate
            bent = jnp.tanh(gate * (0.7978845608028654 + 0.03567740813636141 * square))
            lifted = 0.5 + 0.5 * bent
            slope = lifted + (0.5 * gate) * (1.0 - bent * bent) * (
                0.7978845608028654 + 0.10703222440908423 * square
            )
            active = gate * lifted
            upper_ref[block(m), cols(tile, 0)] = (up * slope).astype(bf16)
            upper_ref[block(m), cols(tile, 1)] = active.astype(bf16)
            hid_ref[block(m), cols(tile, 0)] = (active * up).astype(bf16)
            return carry

        lax.fori_loop(0, tiles, step, 0)

    def narrow(m):
        def step(part, carry):
            here = pl.ds(pl.multiple_of(part * 256, 256), 256)
            values = dot_nn(hid_ref[block(m), :], wout_ref[:, here])
            out_ref[m, :, :, here] = values.astype(bf16).reshape(4, slots, 256)
            return carry

        lax.fori_loop(0, width // 256, step, 0)

    out_copies = [
        to_plane(m, lambda m, c: out_ref.at[m, c], lambda m: returned_ref.at[me], (out_send, out_recv))
        for m in range(4)
    ]
    own_out = pltpu.make_async_copy(out_ref.at[0, chip], returned_ref.at[me], local_sem.at[7])
    widen(0)
    widen(1)
    for m in range(4):
        for copy in row_copies[m]:
            copy.wait_send()
    for m in range(2):
        for copy in grad_copies[m]:
            copy.start()
    for j, copy in enumerate(outer_copies):
        copy.wait_recv()
        pair_outer[1 + j].start()
        outer_loads[j].start()
    for j, copy in enumerate(pair_outer):
        copy.wait_recv()
        outer_loads[3 + j].start()
    for copy in outer_copies + pair_outer:
        copy.wait_send()
    for copy in outer_loads:
        copy.wait()
    for m in range(4):
        if m >= 2:
            widen(m)
        narrow(m)
        for copy in out_copies[m]:
            copy.start()
    own_out.start()
    x_t_ref[...] = x_ref[...].reshape(tokens, width).T.reshape(x_t_ref.shape)

    far_grads.wait()
    for m in range(4):
        for copy in gate_copies[m] + (grad_copies[m] if m < 2 else []):
            copy.wait_recv()
        for j in range(4):
            gates = gates_in_ref[m, j].T[:slots, 0:1]
            dy_ref[m, j] = (dy_ref[m, j].astype(f32) * gates).astype(bf16)

    def outer_part(tile):
        slot = lax.rem(tile, STAGES)
        return remote(stage_out_ref.at[slot], outer_in_ref.at[tile], (part_send, part_recv), tiles + tile, pair)

    def weigh_outer(tile, carry):
        slot = lax.rem(tile, STAGES)

        @pl.when(tile >= STAGES)
        def _():
            outer_part(tile - STAGES).wait_send()

        grad_down = dot_nn(hid_ref[:, cols(tile, 0)].T, dy_ref[...].reshape(tokens, width))
        for j in range(4):
            low = grad_down[:, (2 * j) * shard:(2 * j + 1) * shard].astype(bf16)
            high = grad_down[:, (2 * j + 1) * shard:(2 * j + 2) * shard].astype(bf16)
            stage_out_ref[slot, j] = jnp.where(core == 0, high, low)
            hid_ref[pl.ds((j // 2) * half, half), pl.ds(pl.multiple_of(tile * half + (j % 2) * shard, shard), shard)] = (
                jnp.where(core == 0, low, high)
            )
        outer_part(tile).start()
        return carry

    lax.fori_loop(0, tiles, weigh_outer, 0)
    for tile in range(tiles - STAGES, tiles):
        outer_part(tile).wait_send()

    def join_outer(tile, carry):
        outer_part(tile).wait_recv()
        for j in range(4):
            own = hid_ref[pl.ds((j // 2) * half, half), pl.ds(pl.multiple_of(tile * half + (j % 2) * shard, shard), shard)]
            outer_in_ref[tile, j] = (own.astype(f32) + outer_in_ref[tile, j].astype(f32)).astype(bf16)
        return carry

    lax.fori_loop(0, tiles, join_outer, 0)
    own_gout = pltpu.make_async_copy(outer_in_ref.at[:, chip], gouter_ref.at[chip], local_sem.at[3])
    own_gout.start()
    gout_copies = [
        remote(outer_in_ref.at[:, device // 2], gouter_ref.at[chip], (gout_send, gout_recv), j, (device, z))
        for j, device in enumerate(across)
    ]
    for copy in gout_copies:
        copy.start()

    def back(first, count):
        here_rows = pl.ds(first * chunk, count * chunk)

        def step(tile, carry):
            down = wout_ref[pl.ds(pl.multiple_of(tile * half, half), half), :]
            grads = dy_ref[first:first + count].reshape(count * chunk, width)
            grad_hidden = dot_nt(grads, down)
            for part in range(2):
                slope = upper_ref[here_rows, cols(tile, part)].astype(f32)
                upper_ref[here_rows, cols(tile, part)] = (grad_hidden * slope).astype(bf16)
            return carry

        lax.fori_loop(0, tiles, step, 0)

        def gather(j, carry):
            here = pl.ds(pl.multiple_of(j * 256, 256), 256)
            weights = win_ref[j].reshape(2 * shard, 2 * hidden)
            values = dot_nt(upper_ref[here_rows, :], weights)
            back_ref[first:first + count, :, :, here] = values.astype(bf16).reshape(count, 4, slots, 256)
            return carry

        lax.fori_loop(0, 4, gather, 0)

    copy_copies = [
        to_plane(m, lambda m, c: back_ref.at[m, c], lambda m: copies_ref.at[me], (copy_send, copy_recv))
        for m in range(4)
    ]
    own_copy = pltpu.make_async_copy(back_ref.at[0, chip], copies_ref.at[me], local_sem.at[8])
    for first in range(0, 4, BACK_COUNT):
        back(first, BACK_COUNT)
        for m in range(first, first + BACK_COUNT):
            for copy in copy_copies[m]:
                copy.start()
    own_copy.start()

    def inner_part(tile):
        slot = lax.rem(tile, STAGES)
        return remote(stage_in_ref.at[slot], inner_in_ref.at[tile], (part_send, part_recv), tile, pair)

    def inner_load(tile):
        slot = lax.rem(tile, 2)
        return pltpu.make_async_copy(inner_in_ref.at[tile], add_in_ref.at[slot], join_sem.at[slot])

    def inner_stores(tile):
        slot = lax.rem(tile, 2)
        return [
            pltpu.make_async_copy(
                add_in_ref.at[slot, part], ginner_ref.at[:, :, cols(tile, part)], join_sem.at[2 + 2 * slot + part]
            )
            for part in range(2)
        ]

    def join_begin(tile):
        inner_part(tile).wait_recv()

        @pl.when(tile >= 2)
        def _():
            for copy in inner_stores(tile - 2):
                copy.wait()

        inner_load(tile).start()

    def join_end(tile):
        slot = lax.rem(tile, 2)
        inner_load(tile).wait()
        for part in range(2):
            own = upper_ref[pl.ds(0, width // 2), cols(tile, part)].astype(f32)
            other = add_in_ref[slot, part].reshape(width // 2, half).astype(f32)
            add_in_ref[slot, part] = (own + other).astype(bf16).reshape(4, shard, half)
        for copy in inner_stores(tile):
            copy.start()

    def weigh_inner(tile, carry):
        slot = lax.rem(tile, STAGES)

        @pl.when(tile >= LAG)
        def _():
            join_begin(tile - LAG)

        @pl.when(tile >= STAGES)
        def _():
            inner_part(tile - STAGES).wait_send()

        for part in range(2):
            grad_upper = upper_ref[:, cols(tile, part)]
            other = x_t_ref[:, 1 - core].reshape(width // 2, tokens)
            stage_in_ref[slot, part] = dot_nn(other, grad_upper).astype(bf16).reshape(4, shard, half)
        inner_part(tile).start()
        for part in range(2):
            grad_upper = upper_ref[:, cols(tile, part)]
            own = x_t_ref[:, core].reshape(width // 2, tokens)
            upper_ref[pl.ds(0, width // 2), cols(tile, part)] = dot_nn(own, grad_upper).astype(bf16)

        @pl.when(tile >= LAG)
        def _():
            join_end(tile - LAG)

        return carry

    lax.fori_loop(0, tiles, weigh_inner, 0)
    for tile in range(tiles - LAG, tiles):
        join_begin(tile)
        join_end(tile)
    for tile in range(tiles - STAGES, tiles):
        inner_part(tile).wait_send()
    for tile in (tiles - 2, tiles - 1):
        for copy in inner_stores(tile):
            copy.wait()
    sent = ginner_sent_ref.shape[2]
    sent_copies = [
        remote(
            ginner_ref.at[device // 2, :, pl.ds(0, sent)], ginner_sent_ref.at[j], (gout_send, gout_recv), 3 + j,
            (device, z),
        )
        for j, device in enumerate(across)
    ]
    for copy in sent_copies:
        copy.start()
    own_out.wait()
    own_copy.wait()
    own_gout.wait()
    for m in range(4):
        for copy in (grad_copies[m] if m < 2 else []) + gate_copies[m]:
            copy.wait_send()
        for copy in out_copies[m] + copy_copies[m]:
            copy.wait()
    for copy in gout_copies + sent_copies:
        copy.wait()


ROW_ORDER = (0, 1, 2, 3)
BACK_COUNT = 2
STAGES = 4
LAG = 2


def run_experts(rows, gates, grads, far, inner, inner_others, outer):
    count, slots, width = rows.shape
    tokens = count * slots
    hidden = outer.shape[1]
    half = 256
    tiles = hidden // half
    shard = width // 8
    bf16 = jnp.bfloat16
    anywhere = pl.BlockSpec(memory_space=pl.ANY)
    sems = [pltpu.SemaphoreType.DMA((count,))] * 10 + [
        pltpu.SemaphoreType.DMA((12,)),
        pltpu.SemaphoreType.DMA((12,)),
        pltpu.SemaphoreType.DMA((2 * tiles,)),
        pltpu.SemaphoreType.DMA((2 * tiles,)),
        pltpu.SemaphoreType.DMA((6,)),
        pltpu.SemaphoreType.DMA((6,)),
        pltpu.SemaphoreType.DMA((11,)),
        pltpu.SemaphoreType.DMA((6,)),
        pltpu.SemaphoreType.DMA((7,)),
    ]
    outs = pl.pallas_call(
        expert_kernel,
        out_shape=(
            jax.ShapeDtypeStruct(rows.shape, bf16),
            jax.ShapeDtypeStruct(rows.shape, bf16),
            jax.ShapeDtypeStruct(inner.shape, bf16),
            jax.ShapeDtypeStruct((3, shard, inner.shape[2] // 4), bf16),
            jax.ShapeDtypeStruct((4, tiles, half, shard), bf16),
            jax.ShapeDtypeStruct((tiles, 2, 4, shard, half), bf16),
            jax.ShapeDtypeStruct((8, hidden, shard), bf16),
        ),
        in_specs=[anywhere] * 9,
        out_specs=(anywhere,) * 7,
        scratch_shapes=[
            pltpu.VMEM((4, 4, slots, width), bf16),
            pltpu.VMEM((4, 2, shard, tokens), bf16),
            pltpu.VMEM((4, 4, slots, width), bf16),
            pltpu.VMEM((4, 4, 8, 128), jnp.float32),
            pltpu.VMEM((4, 2, shard, 2 * hidden), bf16),
            pltpu.VMEM((hidden, width), bf16),
            pltpu.VMEM((tokens, 2 * hidden), bf16),
            pltpu.VMEM((tokens, hidden), bf16),
            pltpu.VMEM((4, 4, slots, width), bf16),
            pltpu.VMEM((4, 4, slots, width), bf16),
            pltpu.VMEM((STAGES, 2, 4, shard, half), bf16),
            pltpu.VMEM((STAGES, 4, half, shard), bf16),
            pltpu.VMEM((2, 2, 4, shard, half), bf16),
            pltpu.VMEM((tiles, 4, half, shard), bf16),
        ] + sems,
        compiler_params=pltpu.CompilerParams(
            collective_id=1, has_side_effects=True, vmem_limit_bytes=63 * 2**20
        ),
        cost_estimate=pl.CostEstimate(
            flops=180 * 10**9, bytes_accessed=60 * 2**20, transcendentals=tokens * hidden
        ),
        name="run_experts",
    )(rows, gates, grads, far, inner, *inner_others, outer)
    return outs[0], outs[1], outs[2], outs[3], outs[4].reshape(outer.shape)


def attend_back(pair, proj_ref, dout_ref, lse_ref, tile_ref, dproj_ref, span_ref, dk_ref, dv_ref, near_ref):
    length = proj_ref.shape[1]
    blocks = length // BLK
    depth = 64
    wide = 2 * depth
    here = slice(pair * wide, (pair + 1) * wide)
    lane = lax.broadcasted_iota(jnp.int32, (1, wide), 1)
    keys = proj_ref[1, :, here]
    values = proj_ref[2, :, here]
    keys_t = keys.T
    dk_ref[...] = jnp.zeros_like(dk_ref)
    dv_ref[...] = jnp.zeros_like(dv_ref)
    near_ref[...] = jnp.zeros_like(near_ref)
    far_sum = [jnp.zeros((1, BLK), jnp.float32) for h in range(2)]
    for block in range(blocks):
        rows = pl.ds(block * BLK, BLK)
        key_count = (block + 1) * BLK
        query = proj_ref[0, rows, here] * jnp.bfloat16(0.125)
        grad = dout_ref[rows, here]
        dq_parts = []
        dk_sum = None
        dv_sum = None
        for h in range(2):
            own = (lane // depth) == h
            query_h = jnp.where(own, query, jnp.bfloat16(0))
            grad_h = jnp.where(own, grad, jnp.bfloat16(0))
            scores = dot_nt(keys[:key_count], query_h)
            grad_p = dot_nt(values[:key_count], grad_h)
            lse = lse_ref[pair, h:h + 1, rows]
            far = tile_ref[2 * pair + h, 1, 0:1, BLK - 1:BLK].astype(jnp.float32)
            probs = []
            delta = None
            for kb in range(block + 1):
                d = block - kb
                part = scores[kb * BLK:(kb + 1) * BLK]
                bias = tile_ref[2 * pair + h, d].astype(jnp.float32) if d < 2 else far
                part = jnp.exp(part + (bias - lse))
                probs.append(part)
                term = jnp.sum(part * grad_p[kb * BLK:(kb + 1) * BLK], axis=0, keepdims=True)
                delta = term if delta is None else delta + term
            ds = []
            for kb in range(block + 1):
                d = block - kb
                part = probs[kb] * (grad_p[kb * BLK:(kb + 1) * BLK] - delta)
                if d < 2:
                    near_ref[h, d] += part
                else:
                    far_sum[h] = far_sum[h] + jnp.sum(part, axis=0, keepdims=True)
                ds.append(part.astype(jnp.bfloat16))
            ds = jnp.concatenate(ds, axis=0)
            weights = jnp.concatenate([p.astype(jnp.bfloat16) for p in probs], axis=0)
            dv_h = dot_nn(weights, grad_h)
            dk_h = dot_nn(ds, query_h)
            dv_sum = dv_h if dv_sum is None else dv_sum + dv_h
            dk_sum = dk_h if dk_sum is None else dk_sum + dk_h
            dq_parts.append(dot_nn(keys_t[h * depth:(h + 1) * depth, :key_count], ds))
        dk_ref[:key_count] += dk_sum
        dv_ref[:key_count] += dv_sum
        dproj_ref[0, rows, here] = (jnp.concatenate(dq_parts, axis=0).T * 0.125).astype(jnp.bfloat16)
    dproj_ref[1, :, here] = dk_ref[...].astype(jnp.bfloat16)
    dproj_ref[2, :, here] = dv_ref[...].astype(jnp.bfloat16)
    flip = (
        lax.broadcasted_iota(jnp.int32, (BLK, BLK), 0) + lax.broadcasted_iota(jnp.int32, (BLK, BLK), 1) == BLK - 1
    ).astype(jnp.bfloat16)
    lanes = lax.broadcasted_iota(jnp.int32, (1, 2 * BLK), 1)
    for h in range(2):
        for d in range(2):
            near = near_ref[h, d]
            near_high = near.astype(jnp.bfloat16)
            near_low = (near - near_high.astype(jnp.float32)).astype(jnp.bfloat16)
            flipped = dot_nn(flip, near_high) + dot_nn(flip, near_low)
            spread = jnp.concatenate([flipped, jnp.zeros((BLK, BLK), jnp.float32)], axis=1)
            turned = pltpu.roll(spread, 1, 1, stride=1, stride_axis=0)
            along = jnp.sum(turned, axis=0, keepdims=True)
            if d == 1:
                along = along + jnp.where(lanes == 2 * BLK - 1, jnp.sum(far_sum[h], axis=1, keepdims=True), 0.0)
            span_ref[2 * pair + h, d:d + 1, :] = along


def back_kernel(
    returned_hbm, copies_hbm, hidden_hbm, cot_hbm, cols_hbm, wo_hbm, att_hbm, router_ref, gains_ref, counts_ref,
    picks_ref, proj_hbm, lse_hbm, tile_hbm, wq_hbm, seq_hbm, ginner_hbm,
    mixed_ref, gtok_ref, gqkv_ref, gwo_ref, sums_ref, inner_in_hbm,
    returned_ref, copies_ref, hidden_ref, cot_ref, cols_ref, wo_ref, att_ref, gp_ref, dout_send_ref,
    proj_ref, lse_ref, tile_ref, wq_ref, seq_ref, dout_ref, dproj_ref, span_ref, dk_ref, dv_ref,
    near_ref, turned_ref, first_send_ref, first_in_ref,
    q_stage_ref, q_in_ref, q_own_ref, q_across_ref, q_z_ref, q_z_in_ref,
    gout_ref, o_in_ref, o_sum_ref, o_across_ref, o_z_ref, o_z_in_ref,
    s_own_ref, s_in_ref, s_sum_ref, s_across_ref, s_z_ref, s_z_in_ref,
    send_sem, recv_sem, load_sem,
):
    x, z, along_z, across, sibling = places()
    core = x % 2
    chip = x // 2
    half = z % 2
    f32, bf16 = jnp.float32, jnp.bfloat16
    rows, width = gtok_ref.shape
    shard = width // 8
    step = rows // 2
    group = gqkv_ref.shape[2]
    experts = returned_ref.shape[0] // CAP
    pair = (sibling, z)
    chips = [(device, z) for device in across]
    lines = [(x, other) for other in along_z]
    barrier = pltpu.get_barrier_semaphore()
    for peer in chips + lines + [pair]:
        pl.semaphore_signal(barrier, inc=1, device_id=peer, device_id_type=MESH_ID)
    loads = {}
    for name, source, target in (
        ("cols", cols_hbm, cols_ref), ("returned", returned_hbm, returned_ref), ("hidden", hidden_hbm, hidden_ref),
        ("cot", cot_hbm, cot_ref), ("copies", copies_hbm, copies_ref), ("wo", wo_hbm, wo_ref),
        ("att", att_hbm, att_ref), ("seq", seq_hbm, seq_ref), ("proj", proj_hbm, proj_ref),
        ("lse", lse_hbm, lse_ref), ("tile", tile_hbm, tile_ref), ("wq", wq_hbm, wq_ref),
    ):
        loads[name] = pltpu.make_async_copy(source, target, load_sem.at[len(loads)])
        loads[name].start()
    pl.semaphore_wait(barrier, 7)
    started = []

    def send(source, target, device):
        index = len(started)
        copy = pltpu.make_async_remote_copy(
            src_ref=source, dst_ref=target, send_sem=send_sem.at[index], recv_sem=recv_sem.at[index],
            device_id=device, device_id_type=MESH_ID,
        )
        copy.start()
        started.append(copy)
        return copy

    inner_rest = inner_in_hbm.shape[2]
    inner_copies = [
        send(
            ginner_hbm.at[device // 2, :, pl.ds(ginner_hbm.shape[2] - inner_rest, inner_rest)], inner_in_hbm.at[j],
            (device, z),
        )
        for j, device in enumerate(across)
    ]

    gain_second = gains_ref[1:2, :]
    router_t = router_ref[...]
    step = rows // 2
    counts = counts_ref[...]
    tokens = 32 * rows
    pairs_in_all = 2 * tokens
    push = loss_weight * experts * (counts / pairs_in_all) / tokens
    slot_lane = lax.broadcasted_iota(jnp.int32, (1, returned_ref.shape[0]), 1).astype(f32)
    expert_lane = lax.broadcasted_iota(jnp.int32, (1, shard), 1).astype(f32)
    gain2_sum = jnp.zeros((1, width), f32)
    route_sum = jnp.zeros((1, shard), f32)
    grad_router = jnp.zeros((shard, width), f32)
    for name in ("cols", "returned", "hidden", "cot"):
        loads[name].wait()
    for i in range(2):
        here = slice(i * step, (i + 1) * step)
        cols = cols_ref[here, :]
        route = jnp.where(expert_lane < experts, cols, 0.0)
        marks = [(slot_lane == cols[:, experts + 2 + c:experts + 3 + c]).astype(bf16) for c in range(2)]
        picked = [dot_nn(mark, returned_ref[...]) for mark in marks]
        hidden = hidden_ref[here, :]
        grad_mixed = cot_ref[here, :].astype(f32)
        mixed_ref[here, :] = (
            hidden + picked[0] * cols[:, experts:experts + 1] + picked[1] * cols[:, experts + 1:experts + 2]
        ).astype(bf16)
        grad_route = push
        for c in range(2):
            hit = expert_lane == cols[:, experts + 4 + c:experts + 5 + c]
            grad_route = grad_route + jnp.where(hit, jnp.sum(grad_mixed * picked[c], axis=1, keepdims=True), 0.0)
        grad_logits = route * (grad_route - jnp.sum(route * grad_route, axis=1, keepdims=True))
        route_sum = route_sum + jnp.sum(route, axis=0, keepdims=True)
        if i == 0:
            loads["copies"].wait()
        grad_second = dot_nn(marks[0] + marks[1], copies_ref[...]) + dot_nn(grad_logits.astype(bf16), router_t)
        normed, scale = normalize(hidden)
        second_norm = (normed * gain_second).astype(bf16)
        grad_router = grad_router + dot_nn(grad_logits.T.astype(bf16), second_norm)
        gain2_sum = gain2_sum + jnp.sum(grad_second * normed, axis=0, keepdims=True)
        grad_normed = grad_second * gain_second
        grad_hidden = grad_mixed + scale * (
            grad_normed - normed * jnp.mean(grad_normed * normed, axis=-1, keepdims=True)
        )
        hidden_ref[here, :] = grad_hidden
        gp_ref[here, :] = grad_hidden.astype(bf16)


    loads["wo"].wait()
    own_width = dout_ref.shape[1]
    dout_send_ref[...] = dot_nt(gp_ref[...], wo_ref[own_width:, :]).astype(bf16)
    own_rows = pl.ds(pl.multiple_of(half * rows, rows), rows)
    dout_copy = send(dout_send_ref, dout_ref.at[own_rows, :], lines[0])
    dout_ref[own_rows, :] = dot_nt(gp_ref[...], wo_ref[:own_width, :]).astype(bf16)

    loads["att"].wait()
    grad_out = dot_nn(att_ref[...].T, gp_ref[...]).astype(bf16)
    for owner in range(8):
        gout_ref[owner // 2, owner % 2] = grad_out[:, owner * shard:(owner + 1) * shard]
    o_pair = [send(gout_ref.at[j, 1 - core], o_in_ref.at[j], pair) for j in range(4)]

    gain_first = gains_ref[0:1, :]
    loads["seq"].wait()
    for i in range(4):
        normed, _ = normalize(seq_ref[i // 2, (i % 2) * step:(i % 2 + 1) * step, :].astype(f32))
        turned_ref[:, :, :, i * step:(i + 1) * step] = (
            (normed * gain_first).astype(bf16).T.reshape(4, 2, shard, step)
        )

    for name in ("proj", "lse", "tile"):
        loads[name].wait()
    dout_copy.wait_recv()

    def attend(number):
        attend_back(
            number, proj_ref, dout_ref, lse_ref, tile_ref, dproj_ref, span_ref, dk_ref, dv_ref, near_ref
        )

    def weigh_other(slot):
        here = pl.ds(slot * group, group)
        other = turned_ref[:, 1 - core].reshape(width // 2, 2 * rows)
        for c in range(3):
            q_stage_ref[slot, c] = dot_nn(other, dproj_ref[c, :, here]).astype(bf16).reshape(4, shard, group)
        return send(q_stage_ref.at[slot], q_in_ref.at[slot], pair)

    def weigh_own(slot):
        here = pl.ds(slot * group, group)
        own = turned_ref[:, core].reshape(width // 2, 2 * rows)
        for c in range(3):
            q_own_ref[slot, c] = dot_nn(own, dproj_ref[c, :, here]).astype(bf16).reshape(4, shard, group)

    def to_chips(slot, copy):
        copy.wait_recv()
        q_own_ref[slot] = (q_own_ref[slot].astype(f32) + q_in_ref[slot].astype(f32)).astype(bf16)
        return [
            send(q_own_ref.at[slot, :, device // 2], q_across_ref.at[slot, j], chips[j])
            for j, device in enumerate(across)
        ]

    def chip_total(slot, copies):
        for copy in copies:
            copy.wait_recv()
        total = q_own_ref[slot, :, chip].astype(f32)
        for j in range(3):
            total = total + q_across_ref[slot, j].astype(f32)
        return total

    attend(2)
    attend(3)
    q_pair_1 = weigh_other(1)
    for copy in o_pair:
        copy.wait_recv()
    for j in range(4):
        o_sum_ref[j] = (gout_ref[j, core].astype(f32) + o_in_ref[j].astype(f32)).astype(bf16)
    o_chips = [send(o_sum_ref.at[device // 2], o_across_ref.at[j], chips[j]) for j, device in enumerate(across)]
    weigh_own(1)
    q_chips_1 = to_chips(1, q_pair_1)
    attend(0)
    attend(1)

    loads["wq"].wait()
    gain1_sum = jnp.zeros((1, width), f32)
    for turn, side in enumerate((1 - half, half)):
        for i in range(2):
            here = pl.ds(pl.multiple_of(side * rows + i * step, step), step)
            part = sum(
                dot_nt(dproj_ref[c, here, slot * group:(slot + 1) * group], wq_ref[slot, :, c].reshape(width, group))
                for slot in range(2)
                for c in range(3)
            )
            normed, _ = normalize(seq_ref[side, i * step:(i + 1) * step, :].astype(f32))
            gain1_sum = gain1_sum + jnp.sum(part * normed, axis=0, keepdims=True)
            if turn:
                gtok_ref[i * step:(i + 1) * step, :] = part
            else:
                first_send_ref[i * step:(i + 1) * step, :] = part.astype(bf16)
        if not turn:
            first_copy = send(first_send_ref, first_in_ref, lines[0])
            q_pair_0 = weigh_other(0)

    table = None
    for d in range(2):
        along = span_ref[:, d, :]
        high = along.astype(bf16)
        low = (along - high.astype(f32)).astype(bf16)
        part = dot_nn(high, picks_ref[d]) + dot_nn(low, picks_ref[d])
        table = part if table is None else table + part
    heads = table.shape[0] // 2
    table = table.T[:32, :]
    blank = jnp.zeros((table.shape[0], shard - heads), f32)
    placed = pltpu.roll(jnp.concatenate([table[:, :heads], blank], axis=1), heads * z, 1) + pltpu.roll(
        jnp.concatenate([table[:, heads:], blank], axis=1), heads * ((z + 2) % 4), 1
    )
    for owner in range(8):
        here = slice(owner * shard, (owner + 1) * shard)
        target = s_own_ref.at[owner // 2, owner % 2]
        target[0:1, :] = gain1_sum[:, here]
        target[1:2, :] = gain2_sum[:, here]
        target[2:2 + experts, :] = grad_router[:experts, here]
        target[22:23, :] = route_sum
        target[23:24, :] = jnp.zeros((1, shard), f32)
        target[18:22, :] = placed[4 * owner:4 * owner + 4, :]
    s_pair = send(s_own_ref.at[:, 1 - core], s_in_ref, pair)
    weigh_own(0)

    q_chips_0 = to_chips(0, q_pair_0)
    s_pair.wait_recv()
    s_sum_ref[...] = s_own_ref[:, core] + s_in_ref[...]
    s_chips = [send(s_sum_ref.at[device // 2], s_across_ref.at[j], chips[j]) for j, device in enumerate(across)]
    q_z_ref[...] = chip_total(1, q_chips_1).astype(bf16)
    q_line = send(q_z_ref, q_z_in_ref, lines[1])
    for copy in o_chips:
        copy.wait_recv()
    o_total = o_sum_ref[chip].astype(f32)
    for j in range(3):
        o_total = o_total + o_across_ref[j].astype(f32)
    rows_out = gwo_ref.shape[0]
    gwo_ref[...] = o_total[:rows_out]
    o_z_ref[...] = o_total[rows_out:].astype(bf16).reshape(o_z_ref.shape)
    out_slots = (2, 1, 3)
    o_lines = [send(o_z_ref.at[out_slots[j] - 1], o_z_in_ref.at[j], lines[j]) for j in range(3)]
    for copy in s_chips:
        copy.wait_recv()
    s_z_ref[...] = s_sum_ref[chip] + s_across_ref[0] + s_across_ref[1] + s_across_ref[2]
    s_lines = [send(s_z_ref, s_z_in_ref.at[j], lines[j]) for j in range(3)]
    gqkv_ref[...] = chip_total(0, q_chips_0)

    first_copy.wait_recv()
    for i in range(2):
        here = slice(i * step, (i + 1) * step)
        grad = (gtok_ref[here, :] + first_in_ref[here, :].astype(f32)) * gain_first
        normed, scale = normalize(seq_ref[half, here, :].astype(f32))
        gtok_ref[here, :] = hidden_ref[here, :] + scale * (
            grad - normed * jnp.mean(grad * normed, axis=-1, keepdims=True)
        )
    q_line.wait_recv()
    gqkv_ref[...] += q_z_in_ref[...].astype(f32)
    for copy in s_lines + o_lines:
        copy.wait_recv()
    gwo_ref[...] += o_z_in_ref[0].astype(f32) + o_z_in_ref[1].astype(f32) + o_z_in_ref[2].astype(f32)
    sums = s_z_ref[...] + s_z_in_ref[0] + s_z_in_ref[1] + s_z_in_ref[2]
    sums_ref[...] = sums
    for copy in inner_copies:
        copy.wait_recv()
    for copy in started:
        copy.wait_send()


def run_back(
    returned, copies, hidden, cot, cols, wo, att, router_t, gains, counts, picks, proj, lse, tiles, wq, seq, ginner, sent
):
    rows, width = hidden.shape
    length = 2 * rows
    shard = width // 8
    group = wq.shape[4]
    rows_out = width // 4
    heads = tiles.shape[0]
    f32, bf16 = jnp.float32, jnp.bfloat16
    anywhere = pl.BlockSpec(memory_space=pl.ANY)
    inside = pl.BlockSpec(memory_space=pltpu.VMEM)
    copies_count = 3 + 1 + 4 + 2 + 3 + 3 + 3 + 1 + 1 + 3 + 1 + 3 + 3
    return pl.pallas_call(
        back_kernel,
        out_shape=(
            jax.ShapeDtypeStruct((rows, width), bf16),
            jax.ShapeDtypeStruct((rows, width), f32),
            jax.ShapeDtypeStruct((3, shard, group), f32),
            jax.ShapeDtypeStruct((rows_out, shard), f32),
            jax.ShapeDtypeStruct((24, shard), f32),
            jax.ShapeDtypeStruct((3, shard, ginner.shape[2] - sent), bf16),
        ),
        in_specs=[anywhere] * 7 + [inside] * 4 + [anywhere] * 6,
        out_specs=(inside,) * 5 + (anywhere,),
        scratch_shapes=[
            pltpu.VMEM(returned.shape, bf16),
            pltpu.VMEM(copies.shape, bf16),
            pltpu.VMEM(hidden.shape, f32),
            pltpu.VMEM(cot.shape, bf16),
            pltpu.VMEM(cols.shape, f32),
            pltpu.VMEM(wo.shape, bf16),
            pltpu.VMEM(att.shape, bf16),
            pltpu.VMEM((rows, width), bf16),
            pltpu.VMEM((rows, 2 * group), bf16),
            pltpu.VMEM(proj.shape, bf16),
            pltpu.VMEM(lse.shape, f32),
            pltpu.VMEM(tiles.shape, bf16),
            pltpu.VMEM(wq.shape, bf16),
            pltpu.VMEM(seq.shape, bf16),
            pltpu.VMEM((length, 2 * group), bf16),
            pltpu.VMEM(proj.shape, bf16),
            pltpu.VMEM((heads, 2, 2 * BLK), f32),
            pltpu.VMEM((length, 128), f32),
            pltpu.VMEM((length, 128), f32),
            pltpu.VMEM((2, 2, BLK, BLK), f32),
            pltpu.VMEM((4, 2, shard, length), bf16),
            pltpu.VMEM((rows, width), bf16),
            pltpu.VMEM((rows, width), bf16),
            pltpu.VMEM((2, 3, 4, shard, group), bf16),
            pltpu.VMEM((2, 3, 4, shard, group), bf16),
            pltpu.VMEM((2, 3, 4, shard, group), bf16),
            pltpu.VMEM((2, 3, 3, shard, group), bf16),
            pltpu.VMEM((3, shard, group), bf16),
            pltpu.VMEM((3, shard, group), bf16),
            pltpu.VMEM((4, 2, width, shard), bf16),
            pltpu.VMEM((4, width, shard), bf16),
            pltpu.VMEM((4, width, shard), bf16),
            pltpu.VMEM((3, width, shard), bf16),
            pltpu.VMEM((3, rows_out, shard), bf16),
            pltpu.VMEM((3, rows_out, shard), bf16),
            pltpu.VMEM((4, 2, 24, shard), f32),
            pltpu.VMEM((4, 24, shard), f32),
            pltpu.VMEM((4, 24, shard), f32),
            pltpu.VMEM((3, 24, shard), f32),
            pltpu.VMEM((24, shard), f32),
            pltpu.VMEM((3, 24, shard), f32),
            pltpu.SemaphoreType.DMA((copies_count,)),
            pltpu.SemaphoreType.DMA((copies_count,)),
            pltpu.SemaphoreType.DMA((12,)),
        ],
        compiler_params=pltpu.CompilerParams(
            collective_id=2, has_side_effects=True, vmem_limit_bytes=62 * 2**20
        ),
        cost_estimate=pl.CostEstimate(flops=60 * 10**9, bytes_accessed=60 * 2**20, transcendentals=0),
        name="run_back",
    )(
        returned, copies, hidden, cot, cols, wo, att, router_t, gains, counts, picks, proj, lse, tiles, wq, seq, ginner
    )


def final_kernel(
    ginner_hbm, sent_hbm, rest_hbm, gouter_hbm, mixed_hbm, gtok_hbm, gqkv_hbm, gwo_hbm, sums_ref, counts_ref,
    inner_hbm, outer_hbm, mixed_out, tok_hbm, qkv_hbm, wo_hbm, gain1_ref, gain2_ref, grouter_ref, gbias_ref, load_ref,
    loss_ref,
    in_ref, out_ref, slim_in_ref, slim_out_ref, mixed_ref, tok_ref, qkv_ref, wo_ref, in_sem, out_sem, copy_sem,
):
    x, z, _, across, _ = places()
    chip = x // 2
    f32 = jnp.float32
    passed = (
        (mixed_hbm, mixed_ref, mixed_out), (gtok_hbm, tok_ref, tok_hbm), (gqkv_hbm, qkv_ref, qkv_hbm),
        (gwo_hbm, wo_ref, wo_hbm),
    )
    copies_in = [pltpu.make_async_copy(a, b, copy_sem.at[n]) for n, (a, b, _) in enumerate(passed)]
    copies = [pltpu.make_async_copy(b, c, copy_sem.at[4 + n]) for n, (_, b, c) in enumerate(passed)]
    depth, _, wide = in_ref.shape
    slim = slim_in_ref.shape[1]
    sent = sent_hbm.shape[2]
    jobs = []
    for part in range(ginner_hbm.shape[2] // wide):
        here = pl.ds(part * wide, wide)
        jobs.append((ginner_hbm.at[chip, :, here], inner_hbm.at[chip, :, here], in_ref, out_ref))
        for j, device in enumerate(across):
            source = sent_hbm.at[j, :, here] if part * wide < sent else rest_hbm.at[j, :, pl.ds(part * wide - sent, wide)]
            jobs.append((source, inner_hbm.at[device // 2, :, here], in_ref, out_ref))
    for n in range(gouter_hbm.shape[0]):
        for i in range(gouter_hbm.shape[1] // slim):
            here = pl.ds(i * slim, slim)
            jobs.append((gouter_hbm.at[n, here], outer_hbm.at[n, here], slim_in_ref, slim_out_ref))
    loads = [
        pltpu.make_async_copy(source, held.at[i % depth], in_sem.at[i % depth])
        for i, (source, _, held, _) in enumerate(jobs)
    ]
    stores = [
        pltpu.make_async_copy(held.at[i % depth], target, out_sem.at[i % depth])
        for i, (_, target, _, held) in enumerate(jobs)
    ]
    for i in range(depth - 1):
        loads[i].start()
    for copy in copies_in:
        copy.start()
    experts = load_ref.shape[1]
    heads = gbias_ref.shape[1]
    shard = sums_ref.shape[1]
    sums = sums_ref[...]
    gain1_ref[...] = sums[0:1, :]
    gain2_ref[...] = sums[1:2, :]
    grouter_ref[...] = sums[2:2 + experts, :].T
    gbias_ref[...] = pltpu.roll(sums[16:24, :], (shard - heads * z) % shard, 1)[2:6, :heads]
    tokens = 32 * gtok_hbm.shape[0]
    counts = counts_ref[:, :experts]
    pairs_in_all = 2 * tokens
    prob_sums = sums[22:23, :experts]
    load_ref[...] = jnp.concatenate([experts * counts / pairs_in_all, experts * prob_sums / tokens], axis=0)
    loss_ref[...] = experts * jnp.sum(counts / pairs_in_all * (prob_sums / tokens), axis=1, keepdims=True)
    for copy_in, copy in zip(copies_in, copies):
        copy_in.wait()
        copy.start()
    for i, (_, _, held_in, held_out) in enumerate(jobs):
        if i + depth - 1 < len(jobs):
            loads[i + depth - 1].start()
        loads[i].wait()
        if i >= depth:
            stores[i - depth].wait()
        held_out[i % depth] = held_in[i % depth].astype(f32)
        stores[i].start()
    for store in stores[-depth:]:
        store.wait()
    for copy in copies:
        copy.wait()


def finish(ginner, sent, rest, gouter, mixed, gtok, gqkv, gwo, sums, counts, experts, heads):
    f32, bf16 = jnp.float32, jnp.bfloat16
    local, shard, inner_width = ginner.shape
    wide = inner_width // 4
    slim = gouter.shape[1] // 2
    anywhere = pl.BlockSpec(memory_space=pl.ANY)
    inside = pl.BlockSpec(memory_space=pltpu.VMEM)
    return pl.pallas_call(
        final_kernel,
        out_shape=(
            jax.ShapeDtypeStruct(ginner.shape, f32),
            jax.ShapeDtypeStruct(gouter.shape, f32),
            jax.ShapeDtypeStruct(mixed.shape, bf16),
            jax.ShapeDtypeStruct(gtok.shape, f32),
            jax.ShapeDtypeStruct(gqkv.shape, f32),
            jax.ShapeDtypeStruct(gwo.shape, f32),
            jax.ShapeDtypeStruct((1, shard), f32),
            jax.ShapeDtypeStruct((1, shard), f32),
            jax.ShapeDtypeStruct((shard, experts), f32),
            jax.ShapeDtypeStruct((4, heads), f32),
            jax.ShapeDtypeStruct((2, experts), f32),
            jax.ShapeDtypeStruct((1, 1), f32),
        ),
        in_specs=[anywhere] * 8 + [inside] * 2,
        out_specs=(anywhere,) * 6 + (inside,) * 6,
        scratch_shapes=[
            pltpu.VMEM((4, shard, wide), bf16),
            pltpu.VMEM((4, shard, wide), f32),
            pltpu.VMEM((4, slim, shard), bf16),
            pltpu.VMEM((4, slim, shard), f32),
            pltpu.VMEM(mixed.shape, bf16),
            pltpu.VMEM(gtok.shape, f32),
            pltpu.VMEM(gqkv.shape, f32),
            pltpu.VMEM(gwo.shape, f32),
            pltpu.SemaphoreType.DMA((4,)),
            pltpu.SemaphoreType.DMA((4,)),
            pltpu.SemaphoreType.DMA((8,)),
        ],
        compiler_params=pltpu.CompilerParams(vmem_limit_bytes=62 * 2**20),
        cost_estimate=pl.CostEstimate(flops=0, bytes_accessed=32 * 2**20, transcendentals=0),
        name="finish",
    )(ginner, sent, rest, gouter, mixed, gtok, gqkv, gwo, sums, counts)


def fast_device(
    tokens, expert_ids, gain_attn, w_qkv, w_out, rel_bias, gain_ffn, router, w_in, w_down, cotangent
):
    f32, bf16 = jnp.float32, jnp.bfloat16
    tok_dev, model_width = tokens.shape
    expert_count = router.shape[1]
    top_count = expert_ids.shape[1]
    shard = model_width // 8
    group_heads = rel_bias.shape[1]

    expert_row = jnp.arange(expert_count, dtype=jnp.int32)
    hits = [(expert_ids[:, c][:, None] == expert_row[None]) for c in range(top_count)]
    both = sum(hit.astype(bf16) for hit in hits)
    steps = jnp.arange(tok_dev, dtype=jnp.int32)
    lower = (steps[None, :] < steps[:, None]).astype(bf16)
    before = jnp.dot(lower, both, preferred_element_type=f32)
    slots = [jnp.sum(jnp.where(hit, before, 0.0), axis=1).astype(jnp.int32) for hit in hits]
    kept = [slot < CAP for slot in slots]
    local_counts = jnp.sum(both.astype(f32), axis=0)
    count_high = jnp.floor(local_counts / 32.0)
    count_low = local_counts - 32.0 * count_high

    def lanes(rows):
        return jnp.pad(rows.astype(bf16), ((0, 0), (0, shard - rows.shape[1])))

    small = jnp.concatenate(
        [
            router.T,
            gain_attn[None],
            gain_ffn[None],
            lanes(rel_bias),
            lanes(count_high[None]),
            lanes(count_low[None]),
            jnp.zeros((8, shard), bf16),
        ],
        axis=0,
    )
    spots = [
        jnp.where(keep, ((expert_ids[:, c] % 4) * 4 + expert_ids[:, c] // 4) * CAP + slots[c], -1)
        for c, keep in enumerate(kept)
    ]
    spots_float = [spot.astype(f32) for spot in spots]
    ids = jnp.stack(spots_float + [expert_ids[:, c].astype(f32) for c in range(top_count)], axis=1)
    ids = jnp.pad(ids, ((0, 0), (expert_count + 2, 128 - expert_count - 6)))
    spot_rows = jnp.pad(jnp.stack(spots_float), ((0, 8 - top_count), (0, 0)))
    buckets = span_buckets()[:, :, None] == jnp.arange(128, dtype=jnp.int32)
    picks = buckets.astype(bf16)
    (
        seq_tokens, qkv_weight, out_weight, smalls, projected, attended, log_totals, bias_tiles, hidden_state, columns,
        gate_rows, send_rows, grad_rows, inner_a, inner_b, inner_c,
        grads_far,
    ) = run_front(tokens, w_qkv, w_out, small, w_in, cotangent, picks, ids, spot_rows, expert_count)

    own_small = smalls[0]
    router_t = own_small[:, :16].transpose(1, 0, 2).reshape(expert_count, model_width)
    gain_first = own_small[:, 16].reshape(model_width).astype(f32)
    gain_second = own_small[:, 17].reshape(model_width).astype(f32)
    all_counts = smalls[:, :, 22:24, :expert_count].astype(f32).sum(axis=(0, 1))
    counts = 32.0 * all_counts[0] + all_counts[1]

    returned, grad_copies, grad_inner, grad_sent, grad_outer = run_experts(
        send_rows,
        gate_rows,
        grad_rows,
        grads_far,
        w_in,
        (inner_a, inner_b, inner_c),
        w_down,
    )
    count_row = jnp.pad(counts, (0, 128 - expert_count))[None]
    mixed, grad_tokens, grad_qkv, grad_out_weight, sums, grad_rest = run_back(
        returned.reshape(-1, model_width),
        grad_copies.reshape(-1, model_width),
        hidden_state,
        cotangent,
        columns,
        out_weight,
        attended,
        jnp.pad(router_t, ((0, 128 - expert_count), (0, 0))),
        jnp.stack([gain_first, gain_second]),
        count_row,
        picks,
        projected,
        log_totals,
        bias_tiles,
        qkv_weight,
        seq_tokens,
        grad_inner,
        grad_sent.shape[2],
    )
    (
        grad_inner, grad_outer, mixed, grad_tokens, grad_qkv, grad_out_weight, gain_one, gain_two, grad_router,
        grad_rel_bias, router_load, loss,
    ) = finish(
        grad_inner,
        grad_sent,
        grad_rest,
        grad_outer,
        mixed,
        grad_tokens,
        grad_qkv,
        grad_out_weight,
        sums,
        count_row,
        expert_count,
        group_heads,
    )
    return (
        mixed,
        loss[0, 0],
        router_load,
        grad_tokens,
        gain_one[0],
        grad_qkv,
        grad_out_weight,
        grad_rel_bias,
        gain_two[0],
        grad_router,
        grad_inner,
        grad_outer,
    )


def solution(mesh):
    in_specs = (
        P(("gx", "gy"), None),
        P(("gx", "gy"), None),
        P("gx"),
        P(None, "gx", "gy"),
        P("gy", "gx"),
        P("gx", "gy"),
        P("gx"),
        P("gx", None),
        P("gy", "gx", None),
        P("gy", None, "gx"),
        P(("gx", "gy"), None),
    )
    out_specs = (
        P(("gx", "gy"), None),
        P(),
        P(),
        P(("gx", "gy"), None),
        P("gx"),
        P(None, "gx", "gy"),
        P("gy", "gx"),
        P("gx", "gy"),
        P("gx"),
        P("gx", None),
        P("gy", "gx", None),
        P("gy", None, "gx"),
    )
    return jax.shard_map(
        fast_device if fits_fast(mesh) else general_device, mesh=mesh, in_specs=in_specs, out_specs=out_specs, check_vma=False
    )
```

```python
import functools
import math

import jax
import jax.numpy as jnp
from jax import lax
from jax.experimental import pallas as pl
from jax.experimental.pallas import tpu as pltpu
from jax.sharding import PartitionSpec as P

LEN = 1024
BLK = 256
CAP = 80


bucket_edges = (12, 16, 23, 32, 46, 64, 91)
epsilon = 1e-06
loss_weight = 0.01
masked_score = -1e30


def bucket_of(offset):
    magnitude = jnp.abs(offset)
    far_bucket = 8 + sum(
        ((magnitude >= edge_value).astype(jnp.int32) for edge_value in bucket_edges)
    )
    return jnp.where(magnitude < 8, magnitude, far_bucket) + 16 * (offset > 0).astype(jnp.int32)


def normalize(values):
    row_scale = lax.rsqrt(jnp.mean(values * values, axis=-1, keepdims=True) + epsilon)
    return (values * row_scale, row_scale)


def norm_back(grad_out, normed, row_scale, gain_vector):
    grad_normed = grad_out * gain_vector
    grad_gain = jnp.sum(grad_out * normed, axis=0)
    grad_input = row_scale * (
        grad_normed - normed * jnp.mean(grad_normed * normed, axis=-1, keepdims=True)
    )
    return (grad_input, grad_gain)


def spread_offsets(along_offsets, row_count):
    head_count, span_width = along_offsets.shape
    key_count = span_width - row_count + 1
    tiled_rows = jnp.broadcast_to(
        along_offsets[:, None, :], (head_count, row_count, span_width)
    ).reshape(head_count, row_count * span_width)
    padded = jnp.pad(tiled_rows, ((0, 0), (0, row_count)))
    shaped = padded.reshape(head_count, row_count, span_width + 1)[:, :, :key_count]
    return shaped[:, :, ::-1]


def gather_offsets(score_grid, row_count):
    head_count = score_grid.shape[0]
    key_count = score_grid.shape[2]
    span_width = key_count + row_count - 1
    padded = jnp.pad(score_grid[:, :, ::-1], ((0, 0), (0, 0), (0, row_count)))
    flat_rows = padded.reshape(head_count, row_count * (key_count + row_count))[
        :, : row_count * span_width
    ]
    return jnp.sum(flat_rows.reshape(head_count, row_count, span_width), axis=1)


def offset_table(q_start, row_count, key_count, bucket_count):
    spot_index = jnp.arange(key_count + row_count - 1, dtype=jnp.int32)
    offsets = key_count - 1 - spot_index - q_start
    return (
        bucket_of(offsets)[:, None] == jnp.arange(bucket_count, dtype=jnp.int32)[None, :]
    ).astype(jnp.float32)


def block_scores(query_rows, key_rows, table_float, q_start):
    row_count = query_rows.shape[0]
    depth = query_rows.shape[2]
    key_count = key_rows.shape[0]
    picks_table = offset_table(q_start, row_count, key_count, table_float.shape[0])
    along_offsets = jnp.dot(picks_table, table_float, precision=lax.Precision.HIGHEST).T
    bias_grid = spread_offsets(along_offsets, row_count)
    scores = (
        jnp.einsum("qhd,khd->hqk", query_rows, key_rows, preferred_element_type=jnp.float32)
        / math.sqrt(depth)
        + bias_grid
    )
    query_pos = q_start + jnp.arange(row_count, dtype=jnp.int32)
    key_pos = jnp.arange(key_count, dtype=jnp.int32)
    allowed = key_pos[None, :] // BLK <= query_pos[:, None] // BLK
    return (jnp.where(allowed[None], scores, masked_score), picks_table)


def general_device(
    tokens, expert_ids, gain_attn, w_qkv, w_out, rel_bias, gain_ffn, router, w_in, w_down, cotangent
):
    shard_list = (gain_attn, w_qkv, w_out, rel_bias, gain_ffn, router, w_in, w_down)
    (
        gain_first,
        qkv_weight,
        out_weight,
        bias_table,
        gain_second,
        route_weight,
        inner_weight,
        outer_weight,
    ) = (
        lax.all_gather(shard_list[0], "gx", axis=0, tiled=True),
        lax.all_gather(shard_list[1], "gx", axis=1, tiled=True),
        lax.all_gather(shard_list[2], "gx", axis=1, tiled=True),
        lax.all_gather(shard_list[3], "gx", axis=0, tiled=True),
        lax.all_gather(shard_list[4], "gx", axis=0, tiled=True),
        lax.all_gather(shard_list[5], "gx", axis=0, tiled=True),
        lax.all_gather(shard_list[6], "gx", axis=1, tiled=True),
        lax.all_gather(shard_list[7], "gx", axis=2, tiled=True),
    )
    tok_dev = tokens.shape[0]
    count_x = lax.axis_size("gx")
    count_y = lax.axis_size("gy")
    total_tokens = tok_dev * count_x * count_y
    model_width = tokens.shape[1]
    expert_count = route_weight.shape[1]
    top_count = expert_ids.shape[1]
    local_experts = inner_weight.shape[0]
    head_count = bias_table.shape[1]
    head_width = qkv_weight.shape[2]
    depth = head_width // head_count
    q_rows = min(512, LEN)
    per_seq = LEN // q_rows
    inputs_float = tokens.astype(jnp.float32)
    normed_one, scale_one = normalize(inputs_float)
    first_norm = (normed_one * gain_first.astype(jnp.float32)).astype(jnp.bfloat16)
    group_rows = lax.all_gather(first_norm, "gy", axis=0, tiled=True)
    tok_group = group_rows.shape[0]
    seq_count = tok_group // LEN
    projected = jnp.einsum(
        "td,cdf->tcf", group_rows, qkv_weight, preferred_element_type=jnp.float32
    ).astype(jnp.bfloat16)
    projected = projected.reshape(tok_group, 3, head_count, depth)
    table_float = bias_table.astype(jnp.float32)

    def forward_block(item_index):
        seq_index = item_index // per_seq
        q_start = item_index % per_seq * q_rows
        query_rows = lax.dynamic_slice_in_dim(projected, seq_index * LEN + q_start, q_rows, 0)[:, 0]
        seq_rows = lax.dynamic_slice_in_dim(projected, seq_index * LEN, LEN, 0)
        scores, unused_picks = block_scores(query_rows, seq_rows[:, 1], table_float, q_start)
        row_max = jnp.max(scores, axis=-1, keepdims=True)
        expo_scores = jnp.exp(scores - row_max)
        row_total = jnp.sum(expo_scores, axis=-1, keepdims=True)
        soft_weights = (expo_scores / row_total).astype(jnp.bfloat16)
        block_out = jnp.einsum(
            "hqk,khd->qhd", soft_weights, seq_rows[:, 2], preferred_element_type=jnp.float32
        ).astype(jnp.bfloat16)
        return (block_out.reshape(q_rows, head_width), (row_max + jnp.log(row_total))[:, :, 0])

    attended, log_totals = lax.map(forward_block, jnp.arange(seq_count * per_seq, dtype=jnp.int32))
    attended = attended.reshape(tok_group, head_width)
    attn_sum = lax.psum_scatter(
        jnp.dot(attended, out_weight, preferred_element_type=jnp.float32).astype(jnp.bfloat16),
        "gy",
        scatter_dimension=0,
        tiled=True,
    ).astype(jnp.float32)
    hidden_state = inputs_float + attn_sum
    normed_two, scale_two = normalize(hidden_state)
    second_norm = (normed_two * gain_second.astype(jnp.float32)).astype(jnp.bfloat16)
    logits = jnp.dot(second_norm, route_weight, preferred_element_type=jnp.float32)
    route = jax.nn.softmax(logits, axis=-1)
    chosen = (
        expert_ids.reshape(-1)[:, None] == jnp.arange(expert_count, dtype=jnp.int32)[None, :]
    ).astype(jnp.int32)
    earlier = jnp.cumsum(chosen, axis=0) - chosen
    slot = jnp.sum(earlier * chosen, axis=-1).reshape(tok_dev, top_count)
    kept = (slot < CAP).astype(jnp.float32)
    counts, prob_sums = lax.psum(
        (jnp.sum(chosen, axis=0).astype(jnp.float32), jnp.sum(route, axis=0)), ("gx", "gy")
    )
    loss = expert_count * jnp.sum(counts / (total_tokens * top_count) * (prob_sums / total_tokens))
    router_load = jnp.stack(
        [
            expert_count * counts / (total_tokens * top_count),
            expert_count * prob_sums / total_tokens,
        ],
        axis=0,
    )
    slot_place = expert_ids * CAP + jnp.minimum(slot, CAP - 1)
    buffer_index = jnp.arange(expert_count * CAP, dtype=jnp.int32)[:, None, None]
    hit_table = (buffer_index == slot_place[None]).astype(jnp.float32) * kept[None]
    dispatch_matrix = jnp.sum(hit_table, axis=-1).astype(jnp.bfloat16)
    send_rows = jnp.dot(dispatch_matrix, second_norm, preferred_element_type=jnp.float32).astype(
        jnp.bfloat16
    )
    send_rows = send_rows.reshape(count_y, local_experts, CAP, model_width)
    received = lax.all_to_all(send_rows, "gy", split_axis=0, concat_axis=0, tiled=True)
    upper = jnp.einsum("slcd,ldf->slcf", received, inner_weight, preferred_element_type=jnp.float32)
    half_width = upper.shape[-1] // 2
    hidden_rows = (
        jax.nn.gelu(upper[..., :half_width], approximate=True) * upper[..., half_width:]
    ).astype(jnp.bfloat16)
    expert_out = jnp.einsum(
        "slcf,lfd->slcd", hidden_rows, outer_weight, preferred_element_type=jnp.float32
    ).astype(jnp.bfloat16)
    expert_out, upper, received = (expert_out, upper, received)
    returned = lax.all_to_all(expert_out, "gy", split_axis=0, concat_axis=0, tiled=True).reshape(
        expert_count * CAP, model_width
    )
    picked_rows = jnp.take(returned, slot_place, axis=0).astype(jnp.float32)
    gate_value = jnp.take_along_axis(route, expert_ids, axis=1) * kept
    mixed = hidden_state + jnp.sum(picked_rows * gate_value[:, :, None], axis=1)
    (
        gain_first,
        qkv_weight,
        out_weight,
        bias_table,
        gain_second,
        route_weight,
        inner_weight,
        outer_weight,
    ) = (
        lax.all_gather(shard_list[0], "gx", axis=0, tiled=True),
        lax.all_gather(shard_list[1], "gx", axis=1, tiled=True),
        lax.all_gather(shard_list[2], "gx", axis=1, tiled=True),
        lax.all_gather(shard_list[3], "gx", axis=0, tiled=True),
        lax.all_gather(shard_list[4], "gx", axis=0, tiled=True),
        lax.all_gather(shard_list[5], "gx", axis=0, tiled=True),
        lax.all_gather(shard_list[6], "gx", axis=1, tiled=True),
        lax.all_gather(shard_list[7], "gx", axis=2, tiled=True),
    )
    table_float = bias_table.astype(jnp.float32)
    grad_mixed = cotangent.astype(jnp.float32)
    grad_gate = kept * jnp.sum(grad_mixed[:, None, :] * picked_rows, axis=-1)
    gate_matrix = jnp.sum(hit_table * gate_value[None], axis=-1)
    grad_buffer = jnp.dot(gate_matrix, grad_mixed, precision=lax.Precision.HIGHEST).astype(
        jnp.bfloat16
    )
    grad_expert = lax.all_to_all(
        grad_buffer.reshape(count_y, local_experts, CAP, model_width),
        "gy",
        split_axis=0,
        concat_axis=0,
        tiled=True,
    )
    half_width = upper.shape[-1] // 2
    activated, pull_gelu = jax.vjp(
        lambda gate_part, up_part: jax.nn.gelu(gate_part, approximate=True) * up_part,
        upper[..., :half_width],
        upper[..., half_width:],
    )
    hidden_rows = activated.astype(jnp.bfloat16)
    grad_hidden = jnp.einsum(
        "slcd,lfd->slcf", grad_expert, outer_weight, preferred_element_type=jnp.float32
    )
    grad_outer = jnp.einsum(
        "slcf,slcd->lfd", hidden_rows, grad_expert, preferred_element_type=jnp.float32
    )
    grad_gate_part, grad_up_part = pull_gelu(grad_hidden)
    grad_upper = jnp.concatenate([grad_gate_part, grad_up_part], axis=-1).astype(jnp.bfloat16)
    grad_inner = jnp.einsum(
        "slcd,slcf->ldf", received, grad_upper, preferred_element_type=jnp.float32
    )
    grad_received = jnp.einsum(
        "slcf,ldf->slcd", grad_upper, inner_weight, preferred_element_type=jnp.float32
    ).astype(jnp.bfloat16)
    grad_copies = lax.all_to_all(
        grad_received, "gy", split_axis=0, concat_axis=0, tiled=True
    ).reshape(expert_count * CAP, model_width)
    grad_second = jnp.sum(
        jnp.take(grad_copies, slot_place, axis=0).astype(jnp.float32) * kept[:, :, None], axis=1
    )
    expert_hits = (expert_ids[:, :, None] == jnp.arange(expert_count, dtype=jnp.int32)).astype(
        jnp.float32
    )
    grad_route = (
        jnp.sum(grad_gate[:, :, None] * expert_hits, axis=1)
        + loss_weight * expert_count * (counts / (total_tokens * top_count)) / total_tokens
    )
    grad_logits = (
        route * (grad_route - jnp.sum(route * grad_route, axis=-1, keepdims=True))
    ).astype(jnp.bfloat16)
    grad_router = jnp.dot(second_norm.T, grad_logits, preferred_element_type=jnp.float32)
    grad_second = grad_second + jnp.dot(
        grad_logits, route_weight.T, preferred_element_type=jnp.float32
    )
    grad_hidden_state, grad_gain_second = norm_back(
        grad_second, normed_two, scale_two, gain_second.astype(jnp.float32)
    )
    grad_hidden_state = grad_mixed + grad_hidden_state
    piece_rows = lax.all_gather(grad_hidden_state.astype(jnp.bfloat16), "gy", axis=0, tiled=True)
    grad_out_weight = jnp.einsum(
        "tf,td->fd", attended, piece_rows, preferred_element_type=jnp.float32
    )
    update_rows = jnp.dot(piece_rows, out_weight.T, preferred_element_type=jnp.float32).astype(
        jnp.bfloat16
    )
    grad_out_weight, grad_attended = (grad_out_weight, update_rows)

    def backward_sequence(seq_index):
        seq_rows = lax.dynamic_slice_in_dim(projected, seq_index * LEN, LEN, 0)
        key_rows = seq_rows[:, 1]
        value_rows = seq_rows[:, 2]
        grad_keys = jnp.zeros((LEN, head_count, depth), jnp.float32)
        grad_values = jnp.zeros((LEN, head_count, depth), jnp.float32)
        grad_table = jnp.zeros(table_float.shape, jnp.float32)
        grad_queries = []
        for block_index in range(per_seq):
            q_start = block_index * q_rows
            query_rows = seq_rows[q_start : q_start + q_rows, 0]
            grad_out = lax.dynamic_slice_in_dim(
                grad_attended, seq_index * LEN + q_start, q_rows, 0
            ).reshape(q_rows, head_count, depth)
            scores, picks_table = block_scores(query_rows, key_rows, table_float, q_start)
            block_lse = log_totals[seq_index * per_seq + block_index]
            soft_probs = jnp.exp(scores - block_lse[:, :, None])
            grad_probs = jnp.einsum(
                "qhd,khd->hqk", grad_out, value_rows, preferred_element_type=jnp.float32
            )
            grad_scores = (
                soft_probs * (grad_probs - jnp.sum(soft_probs * grad_probs, axis=-1, keepdims=True))
            ).astype(jnp.bfloat16)
            grad_queries.append(
                jnp.einsum(
                    "hqk,khd->qhd", grad_scores, key_rows, preferred_element_type=jnp.float32
                )
                / math.sqrt(depth)
            )
            grad_keys = grad_keys + jnp.einsum(
                "hqk,qhd->khd", grad_scores, query_rows, preferred_element_type=jnp.float32
            ) / math.sqrt(depth)
            grad_values = grad_values + jnp.einsum(
                "hqk,qhd->khd",
                soft_probs.astype(jnp.bfloat16),
                grad_out,
                preferred_element_type=jnp.float32,
            )
            along_grads = gather_offsets(grad_scores.astype(jnp.float32), q_rows)
            grad_table = grad_table + jnp.dot(
                picks_table.T, along_grads.T, precision=lax.Precision.HIGHEST
            )
        stacked = jnp.stack(
            [jnp.concatenate(grad_queries, axis=0), grad_keys, grad_values], axis=1
        ).astype(jnp.bfloat16)
        return (stacked, grad_table)

    grad_projected, table_parts = lax.map(backward_sequence, jnp.arange(seq_count, dtype=jnp.int32))
    grad_projected = grad_projected.reshape(tok_group, 3, head_width)
    grad_bias_table = jnp.sum(table_parts, axis=0)
    grad_qkv_weight = jnp.einsum(
        "td,tcf->cdf", group_rows, grad_projected, preferred_element_type=jnp.float32
    )
    grad_slice = lax.slice_in_dim(grad_projected, 0, tok_dev * lax.axis_size("gy"), axis=0)
    grad_first = lax.psum_scatter(
        jnp.einsum(
            "tcf,cdf->td", grad_slice, qkv_weight, preferred_element_type=jnp.float32
        ).astype(jnp.bfloat16),
        "gy",
        scatter_dimension=0,
        tiled=True,
    ).astype(jnp.float32)
    grad_inputs, grad_gain_first = norm_back(
        grad_first, normed_one, scale_one, gain_first.astype(jnp.float32)
    )
    grad_tokens = grad_hidden_state + grad_inputs
    grad_gain_first, grad_gain_second, grad_router = (
        lax.psum(grad_gain_first.astype(jnp.bfloat16), "gy").astype(jnp.float32),
        lax.psum(grad_gain_second.astype(jnp.bfloat16), "gy").astype(jnp.float32),
        lax.psum(grad_router.astype(jnp.bfloat16), "gy").astype(jnp.float32),
    )
    summed_grads = (
        lax.psum_scatter(
            grad_gain_first.astype(jnp.bfloat16), "gx", scatter_dimension=0, tiled=True
        ).astype(jnp.float32),
        lax.psum_scatter(
            grad_qkv_weight.astype(jnp.bfloat16), "gx", scatter_dimension=1, tiled=True
        ).astype(jnp.float32),
        lax.psum_scatter(
            grad_out_weight.astype(jnp.bfloat16), "gx", scatter_dimension=1, tiled=True
        ).astype(jnp.float32),
        lax.psum_scatter(
            grad_bias_table.astype(jnp.bfloat16), "gx", scatter_dimension=0, tiled=True
        ).astype(jnp.float32),
        lax.psum_scatter(
            grad_gain_second.astype(jnp.bfloat16), "gx", scatter_dimension=0, tiled=True
        ).astype(jnp.float32),
        lax.psum_scatter(
            grad_router.astype(jnp.bfloat16), "gx", scatter_dimension=0, tiled=True
        ).astype(jnp.float32),
        lax.psum_scatter(
            grad_inner.astype(jnp.bfloat16), "gx", scatter_dimension=1, tiled=True
        ).astype(jnp.float32),
        lax.psum_scatter(
            grad_outer.astype(jnp.bfloat16), "gx", scatter_dimension=2, tiled=True
        ).astype(jnp.float32),
    )
    return (
        mixed.astype(jnp.bfloat16),
        loss,
        router_load,
        grad_tokens,
        summed_grads[0],
        summed_grads[1],
        summed_grads[2],
        summed_grads[3],
        summed_grads[4],
        summed_grads[5],
        summed_grads[6],
        summed_grads[7],
    )


def dot_nn(a, b):
    return lax.dot_general(a, b, (((1,), (0,)), ((), ())), preferred_element_type=jnp.float32)

def dot_nt(a, b):
    return lax.dot_general(a, b, (((1,), (1,)), ((), ())), preferred_element_type=jnp.float32)

def span_buckets():
    k = jnp.arange(2 * BLK, dtype=jnp.int32)
    return jnp.stack([bucket_of(BLK - k - BLK * d) for d in range(2)])

AXES = ("gx", "gy")
MESH_ID = pl.DeviceIdType.MESH


def fits_fast(mesh):
    return mesh.shape["gx"] == 8 and mesh.shape["gy"] == 4


def places():
    x = lax.axis_index("gx")
    z = lax.axis_index("gy")
    core = x % 2
    chip = x // 2
    along_z = (z + 1 - 2 * (z % 2), (z + 2) % 4, 3 - z)
    chips = (chip + 1 - 2 * (chip % 2), (chip + 2) % 4, 3 - chip)
    return x, z, along_z, tuple(2 * other + core for other in chips), x + 1 - 2 * core


def attend_front(pair, proj_ref, span_ref, tile_ref, attended_ref, lse_ref, kept_ref):
    length = proj_ref.shape[1]
    blocks = length // BLK
    depth = 64
    wide = 2 * depth
    here = slice(pair * wide, (pair + 1) * wide)
    lane = lax.broadcasted_iota(jnp.int32, (1, wide), 1)
    for h in range(2):
        for d in range(2):
            row = span_ref[d, 2 * pair + h:2 * pair + h + 1, :]
            spread = jnp.broadcast_to(row, (BLK, 2 * BLK))
            turned = pltpu.roll(spread, 0, 1, stride=1, stride_axis=0)
            tile_ref[h, d] = turned[:, BLK:]
            kept_ref[2 * pair + h, d] = turned[:, BLK:].astype(jnp.bfloat16)
    far = [span_ref[1, 2 * pair + h:2 * pair + h + 1, 2 * BLK - 1:2 * BLK] for h in range(2)]
    keys = proj_ref[1, :, here]
    values_t = proj_ref[2, :, here].T
    for block in range(blocks):
        rows = pl.ds(block * BLK, BLK)
        query = proj_ref[0, rows, here] * jnp.bfloat16(0.125)
        key_count = (block + 1) * BLK
        outs = []
        for h in range(2):
            picked = jnp.where((lane // depth) == h, query, jnp.bfloat16(0))
            scores = dot_nt(keys[:key_count], picked)
            parts = []
            for kb in range(block + 1):
                part = scores[kb * BLK:(kb + 1) * BLK]
                d = block - kb
                parts.append(part + (tile_ref[h, d] if d < 2 else far[h]))
            top = functools.reduce(jnp.maximum, [jnp.max(p, axis=0, keepdims=True) for p in parts])
            parts = [jnp.exp(p - top) for p in parts]
            total = functools.reduce(jnp.add, [jnp.sum(p, axis=0, keepdims=True) for p in parts])
            scale = 1.0 / total
            weights = jnp.concatenate([(p * scale).astype(jnp.bfloat16) for p in parts], axis=0)
            outs.append(dot_nn(values_t[h * depth:(h + 1) * depth, :key_count], weights))
            lse_ref[pair, h:h + 1, rows] = top + jnp.log(total)
        attended_ref[rows, here] = jnp.concatenate(outs, axis=0).T.astype(jnp.bfloat16)


def front_kernel(
    tok_ref, wq_ref, wo_ref, small_ref, inner_ref, cot_hbm, picks_ref, ids_ref, spots_ref,
    seq_out, wqs_out, wos_out, router_ref, gains_ref, counts_ref, proj_ref, att_ref, lse_ref, kept_ref, hidden_ref, cols_ref, gates_ref, rows_hbm, grads_hbm, inner_a_ref, inner_b_ref, inner_c_ref, far_ref,
    seq_ref, wqs_ref, wos_ref, wos_in_ref, smalls_ref, normed_ref, attended_ref, got_ref, span_ref, tile_ref, cot_ref, grads_ref, rows_ref, second_ref, gate_parts_ref,
    send_sem, recv_sem, local_sem, out_sem,
):
    x, z, along_z, across, sibling = places()
    half = z % 2
    f32, bf16 = jnp.float32, jnp.bfloat16
    peers = [(x, other) for other in along_z] + [(other, z) for other in across] + [(sibling, z)]
    far_peers = [(device, plane) for plane in along_z[1:] for device in (x,) + across]
    peers += [peer for n, peer in enumerate(far_peers) if n % 4]
    barrier = pltpu.get_barrier_semaphore()
    for peer in peers:
        pl.semaphore_signal(barrier, inc=1, device_id=peer, device_id_type=MESH_ID)
    depth = wq_ref.shape[1]
    group = wq_ref.shape[2]
    rows_out = wo_ref.shape[0]
    rows, width = tok_ref.shape

    def qkv_part(owner, slot):
        return wqs_ref.at[slot, owner]

    def out_part(owner, slot, slots):
        return wos_in_ref.at[owner, pl.ds(slot * rows_out, slots * rows_out), :]

    keeps = [
        pltpu.make_async_copy(source, target, local_sem.at[n])
        for n, (source, target) in enumerate(
            ((small_ref, smalls_ref.at[0, x]), (wo_ref, out_part(x, 0, 1)), (wq_ref, qkv_part(x, 0)),
             (tok_ref, seq_ref.at[half]), (cot_hbm, cot_ref))
        )
    ]
    for copy in keeps:
        copy.start()
    pl.semaphore_wait(barrier, len(peers))
    started = []

    def send(source, target, device):
        index = len(started)
        copy = pltpu.make_async_remote_copy(
            src_ref=source, dst_ref=target, send_sem=send_sem.at[index], recv_sem=recv_sem.at[index],
            device_id=device, device_id_type=MESH_ID,
        )
        copy.start()
        started.append(copy)
        return copy

    out_slots = (2, 1, 3)
    near = across + (sibling,)
    small_z = [send(small_ref, smalls_ref.at[j + 1, x], (x, along_z[j])) for j in range(3)]
    wq_z = send(wq_ref, qkv_part(x, 1), (x, along_z[1]))
    wq_first = [send(wq_ref, qkv_part(x, 0), (other, z)) for other in near]
    tok_z = send(tok_ref, seq_ref.at[half], (x, along_z[0]))
    wo_z = [send(wo_ref, out_part(x, out_slots[j], 1), (x, along_z[j])) for j in range(3)]
    blocks = rows_ref.shape[0] // 4
    slots = rows_ref.shape[1]
    chunk = blocks * slots
    slot_row = lax.broadcasted_iota(jnp.int32, (chunk, 1), 0).astype(f32)

    def marks(i):
        return [(slot_row + i * chunk == spots_ref[c:c + 1, :]).astype(bf16) for c in range(2)]

    keeps[4].wait()
    for i in range(4):
        first, second = marks(i)
        grads_ref[i * blocks:(i + 1) * blocks] = (
            dot_nn(first + second, cot_ref[...]).astype(bf16).reshape(blocks, slots, width)
        )
    keeps[0].wait()
    for copy in small_z:
        copy.wait_recv()
    small_x = [send(smalls_ref.at[:, x], smalls_ref.at[:, x], (other, z)) for other in near]
    wq_z.wait_recv()
    wq_second = [send(qkv_part(x, 1), qkv_part(x, 1), (other, z)) for other in near]
    far_copies = [
        send(grads_ref.at[(device // 2) * 4 + plane], far_ref.at[n // 4, x // 2], (device, plane))
        for n, (device, plane) in enumerate(far_peers)
    ]
    small_on = []
    first_on = []
    for j in range(3):
        owner = across[j]
        small_x[j].wait_recv()
        small_on.append(send(smalls_ref.at[:, owner], smalls_ref.at[:, owner], (sibling, z)))
        wq_first[j].wait_recv()
        first_on.append(send(qkv_part(owner, 0), qkv_part(owner, 0), (sibling, z)))
    for copy in [small_x[3], wq_first[3]] + small_on + first_on:
        copy.wait_recv()
    for copy in keeps[1:4]:
        copy.wait()
    inner_copies = [
        send(inner_ref.at[device // 2], target, (device, z))
        for device, target in zip(across, (inner_a_ref, inner_b_ref, inner_c_ref))
    ]

    own_smalls = [smalls_ref[0, g].astype(f32) for g in range(8)]
    gain = jnp.concatenate([part[16:17, :] for part in own_smalls], axis=1)
    heads = span_ref.shape[1] // 2
    lanes = lax.broadcasted_iota(jnp.int32, (1, depth), 1)
    table = jnp.concatenate([part[18:22, :] for part in own_smalls], axis=0)
    other_table = jnp.concatenate([smalls_ref[2, g].astype(f32)[18:22, :] for g in range(8)], axis=0)
    table = jnp.where(lanes < heads, table, pltpu.roll(other_table, heads, 1))
    table = jnp.where(lanes < 2 * heads, table, 0.0)
    table = jnp.concatenate([table, jnp.zeros((depth - table.shape[0], depth), f32)], axis=0)
    table = table.T[:2 * heads, :].astype(bf16)
    for d in range(2):
        span_ref[d] = dot_nt(table, picks_ref[d])
    step = rows // 2

    def norm(side, i):
        normed, _ = normalize(seq_ref[side, i * step:(i + 1) * step, :].astype(f32))
        here = pl.ds(pl.multiple_of(side * rows + i * step, step), step)
        normed_ref[here, :] = (normed * gain).astype(bf16)

    for i in range(2):
        norm(half, i)
    tok_z.wait_recv()
    for i in range(2):
        norm(1 - half, i)

    def project(slot):
        here = slice(slot * group, (slot + 1) * group)
        for c in range(3):
            proj_ref[c, :, here] = dot_nn(normed_ref[...], wqs_ref[slot, :, c].reshape(width, group)).astype(bf16)

    def attend(pair):
        attend_front(pair, proj_ref, span_ref, tile_ref, attended_ref, lse_ref, kept_ref)

    def exchange(slot):
        here = pl.ds(slot * group, group)
        there = pl.ds(pl.multiple_of((1 - half) * rows, rows), rows)
        return send(attended_ref.at[there, here], got_ref.at[:, here], (x, along_z[0]))

    project(0)
    for copy in wo_z:
        copy.wait_recv()
    wo_x = [send(out_part(x, 0, 4), out_part(x, 0, 4), (other, z)) for other in near]
    attend(0)
    second_on = []
    for j in range(3):
        owner = across[j]
        wq_second[j].wait_recv()
        second_on.append(send(qkv_part(owner, 1), qkv_part(owner, 1), (sibling, z)))
    attend(1)
    got_0 = exchange(0)
    for copy in [wq_second[3]] + second_on:
        copy.wait_recv()
    project(1)
    outs = [
        pltpu.make_async_copy(source, target, out_sem.at[n])
        for n, (source, target) in enumerate(((seq_ref, seq_out), (wqs_ref, wqs_out)))
    ]
    for copy in outs:
        copy.start()
    attend(2)
    attend(3)
    got_1 = exchange(1)
    wo_on = []
    for j in range(3):
        owner = across[j]
        wo_x[j].wait_recv()
        wo_on.append(send(out_part(owner, 0, 4), out_part(owner, 0, 4), (sibling, z)))
    for copy in [wo_x[3]] + wo_on:
        copy.wait_recv()
    for owner in range(8):
        wos_ref[:, owner * depth:(owner + 1) * depth] = wos_in_ref[owner]
    outs.append(pltpu.make_async_copy(wos_ref, wos_out, out_sem.at[2]))
    outs[2].start()
    own = pl.ds(pl.multiple_of(half * rows, rows), rows)
    att_ref[:, :2 * group] = attended_ref[own, :]
    for copy in (got_0, got_1):
        copy.wait_recv()
    att_ref[:, 2 * group:] = got_ref[...]

    gain_second = jnp.concatenate([part[17:18, :] for part in own_smalls], axis=1)
    experts = rows_ref.shape[0]
    router = jnp.concatenate([part[:experts, :] for part in own_smalls], axis=1)
    router = jnp.concatenate([router, jnp.zeros((depth - experts, width), f32)], axis=0).astype(bf16)
    router_ref[...] = router
    gains_ref[...] = jnp.concatenate([gain, gain_second], axis=0)
    counted = sum(smalls_ref[j, g].astype(f32) for j in range(4) for g in range(8))
    counts_ref[...] = 32.0 * counted[22:23, :] + counted[23:24, :]
    lanes_f = lanes.astype(f32)
    for i in range(2):
        here = slice(i * step, (i + 1) * step)
        hidden = seq_ref[half, here, :].astype(f32) + dot_nn(att_ref[here, :], wos_ref[...])
        hidden_ref[here, :] = hidden
        normed, _ = normalize(hidden)
        second = (normed * gain_second).astype(bf16)
        second_ref[here, :] = second
        logits = jnp.where(lanes < experts, dot_nt(second, router), -1e30)
        route = jnp.exp(logits - jnp.max(logits, axis=1, keepdims=True))
        route = route / jnp.sum(route, axis=1, keepdims=True)
        ids = ids_ref[here, :]
        gates = []
        for c in range(2):
            gate = jnp.sum(jnp.where(lanes_f == ids[:, experts + 4 + c:experts + 5 + c], route, 0.0), axis=1, keepdims=True)
            gates.append(jnp.where(ids[:, experts + 2 + c:experts + 3 + c] >= 0.0, gate, 0.0))
            high = gates[c].astype(bf16).astype(f32)
            gate_parts_ref[c, here, :] = jnp.where(
                lanes == 0, high, jnp.where(lanes == 1, gates[c] - high, 0.0)
            ).astype(bf16)
        cols_ref[here, :] = jnp.where(
            lanes < experts, route, jnp.where(lanes == experts, gates[0], jnp.where(lanes == experts + 1, gates[1], ids))
        )
    for i in range(4):
        first, second = marks(i)
        rows_ref[i * blocks:(i + 1) * blocks] = (
            dot_nn(first + second, second_ref[...]).astype(bf16).reshape(blocks, slots, width)
        )
        parts = dot_nn(first, gate_parts_ref[0]) + dot_nn(second, gate_parts_ref[1])
        for n in range(blocks):
            turned = parts[n * slots:(n + 1) * slots, :].T
            line = jnp.concatenate([turned[0:1, :] + turned[1:2, :], jnp.zeros((1, depth - slots), f32)], axis=1)
            gates_ref[i * blocks + n] = jnp.broadcast_to(line, (8, depth))
    outs.append(pltpu.make_async_copy(rows_ref, rows_hbm, out_sem.at[3]))
    outs.append(pltpu.make_async_copy(grads_ref, grads_hbm, out_sem.at[4]))
    for copy in outs[3:]:
        copy.start()
    for copy in inner_copies + far_copies:
        copy.wait_recv()
    for copy in started:
        copy.wait_send()
    for copy in outs:
        copy.wait()


def run_front(tokens, w_qkv, w_out, small, w_in, cotangent, picks, ids, spots, experts):
    rows, width = tokens.shape
    group = w_qkv.shape[2]
    f32, bf16 = jnp.float32, jnp.bfloat16
    heads = 2 * group // 64
    anywhere = pl.BlockSpec(memory_space=pl.ANY)
    inside = pl.BlockSpec(memory_space=pltpu.VMEM)
    seq = (2, rows, width)
    wqs = (2, 8) + w_qkv.shape
    wos = (width, width)
    smalls = (4, 8) + small.shape
    copies_count = 3 + 1 + 4 + 1 + 3 + 4 + 4 + 3 + 3 + 4 + 3 + 3 + 3 + 2 + 8
    return pl.pallas_call(
        front_kernel,
        out_shape=(
            jax.ShapeDtypeStruct(seq, bf16),
            jax.ShapeDtypeStruct(wqs, bf16),
            jax.ShapeDtypeStruct(wos, bf16),
            jax.ShapeDtypeStruct((128, width), bf16),
            jax.ShapeDtypeStruct((2, width), f32),
            jax.ShapeDtypeStruct((1, 128), f32),
            jax.ShapeDtypeStruct((3, 2 * rows, 2 * group), bf16),
            jax.ShapeDtypeStruct((rows, width), bf16),
            jax.ShapeDtypeStruct((heads // 2, 2, 2 * rows), f32),
            jax.ShapeDtypeStruct((heads, 2, BLK, BLK), bf16),
            jax.ShapeDtypeStruct((rows, width), f32),
            jax.ShapeDtypeStruct((rows, 128), f32),
            jax.ShapeDtypeStruct((experts, 8, 128), f32),
            jax.ShapeDtypeStruct((experts, CAP, width), bf16),
            jax.ShapeDtypeStruct((experts, CAP, width), bf16),
            jax.ShapeDtypeStruct(w_in.shape[1:], bf16),
            jax.ShapeDtypeStruct(w_in.shape[1:], bf16),
            jax.ShapeDtypeStruct(w_in.shape[1:], bf16),
            jax.ShapeDtypeStruct((2, 4, CAP, width), bf16),
        ),
        in_specs=[anywhere] * 6 + [inside] * 3,
        out_specs=(anywhere,) * 3 + (inside,) * 10 + (anywhere,) * 6,
        scratch_shapes=[
            pltpu.VMEM(seq, bf16),
            pltpu.VMEM(wqs, bf16),
            pltpu.VMEM(wos, bf16),
            pltpu.VMEM((8, width, width // 8), bf16),
            pltpu.VMEM(smalls, bf16),
            pltpu.VMEM((2 * rows, width), bf16),
            pltpu.VMEM((2 * rows, 2 * group), bf16),
            pltpu.VMEM((rows, 2 * group), bf16),
            pltpu.VMEM((2, heads, 2 * BLK), f32),
            pltpu.VMEM((2, 2, BLK, BLK), f32),
            pltpu.VMEM((rows, width), bf16),
            pltpu.VMEM((experts, CAP, width), bf16),
            pltpu.VMEM((experts, CAP, width), bf16),
            pltpu.VMEM((rows, width), bf16),
            pltpu.VMEM((2, rows, 128), bf16),
            pltpu.SemaphoreType.DMA((copies_count,)),
            pltpu.SemaphoreType.DMA((copies_count,)),
            pltpu.SemaphoreType.DMA((5,)),
            pltpu.SemaphoreType.DMA((6,)),
        ],
        compiler_params=pltpu.CompilerParams(
            collective_id=0, has_side_effects=True, vmem_limit_bytes=56 * 2**20
        ),
        cost_estimate=pl.CostEstimate(flops=60 * 10**9, bytes_accessed=30 * 2**20, transcendentals=0),
        name="run_front",
    )(tokens, w_qkv, w_out, small, w_in, cotangent, picks, ids, spots)


def expert_kernel(
    rows_ref, gates_ref, grads_ref, far_ref, inner_ref, inner_a_ref, inner_b_ref, inner_c_ref, outer_ref,
    returned_ref, copies_ref, ginner_ref, ginner_sent_ref, gouter_ref, inner_in_ref, outer_land_ref,
    x_ref, x_t_ref, dy_ref, gates_in_ref, win_ref, wout_ref, upper_ref, hid_ref, out_ref, back_ref,
    stage_in_ref, stage_out_ref, add_in_ref, outer_in_ref,
    row_send, row_recv, gate_send, gate_recv, out_send, out_recv, copy_send, copy_recv,
    grad_send, grad_recv, w_send, w_recv, part_send, part_recv, gout_send, gout_recv, local_sem, join_sem, load_sem,
):
    x, z, along_z, across, sibling = places()
    core = x % 2
    chip = x // 2
    me = chip * 4 + z
    _, _, slots, width = x_ref.shape
    chunk = 4 * slots
    tokens = 4 * chunk
    hidden = hid_ref.shape[1]
    half = stage_out_ref.shape[2]
    tiles = hidden // half
    shard = width // 8
    f32, bf16 = jnp.float32, jnp.bfloat16
    planes = (z,) + along_z
    chips = (chip,) + tuple(device // 2 for device in across)
    pair = (sibling, z)

    peers = [(m, k) for m in range(4) for k in range(4) if m or k]
    barrier = pltpu.get_barrier_semaphore()
    for m, k in peers:
        pl.semaphore_signal(
            barrier, inc=1, device_id=(2 * chips[k] + core, planes[m]), device_id_type=MESH_ID
        )
    pl.semaphore_signal(barrier, inc=1, device_id=pair, device_id_type=MESH_ID)
    pl.semaphore_wait(barrier, len(peers) + 1)

    def remote(source, target, sems, index, device):
        return pltpu.make_async_remote_copy(
            src_ref=source, dst_ref=target, send_sem=sems[0].at[index], recv_sem=sems[1].at[index],
            device_id=device, device_id_type=MESH_ID,
        )

    def to_plane(m, source_of, target_of, sems):
        return [
            remote(
                source_of(m, chips[k]), target_of(m), sems, 4 * m + k, (2 * chips[k] + core, planes[m])
            )
            for k in range(4)
            if m or k
        ]

    def lanes_of(owner):
        return pl.ds(pl.multiple_of(owner * shard, shard), shard)

    row_copies = [
        to_plane(
            m, lambda m, c: rows_ref.at[c * 4 + planes[m]], lambda m: x_ref.at[m, chip], (row_send, row_recv)
        )
        for m in range(4)
    ]
    gate_copies = [
        to_plane(
            m, lambda m, c: gates_ref.at[c * 4 + planes[m]], lambda m: gates_in_ref.at[m, chip],
            (gate_send, gate_recv),
        )
        for m in range(4)
    ]
    keeps = [
        pltpu.make_async_copy(inner_ref.at[chip], win_ref.at[chip, core], local_sem.at[0]),
        pltpu.make_async_copy(inner_a_ref, win_ref.at[chips[1], core], local_sem.at[1]),
        pltpu.make_async_copy(inner_b_ref, win_ref.at[chips[2], core], local_sem.at[2]),
        pltpu.make_async_copy(grads_ref.at[me], dy_ref.at[0, chip], local_sem.at[3]),
        pltpu.make_async_copy(inner_c_ref, win_ref.at[chips[3], core], local_sem.at[10]),
        pltpu.make_async_copy(rows_ref.at[me], x_ref.at[0, chip], local_sem.at[4]),
        pltpu.make_async_copy(gates_ref.at[me], gates_in_ref.at[0, chip], local_sem.at[5]),
        pltpu.make_async_copy(outer_ref.at[chip], wout_ref.at[:, lanes_of(x)], local_sem.at[6]),
    ]
    pair_inner = [
        remote(source, win_ref.at[chips[k], core], (w_send, w_recv), k, pair)
        for k, source in enumerate((inner_ref.at[chip], inner_a_ref, inner_b_ref, inner_c_ref))
    ]
    outer_copies = [
        remote(outer_ref.at[device // 2], outer_land_ref.at[x], (w_send, w_recv), 4 + j, (device, z))
        for j, device in enumerate(across)
    ]
    pair_outer = [remote(outer_ref.at[chip], outer_land_ref.at[x], (w_send, w_recv), 7, pair)] + [
        remote(outer_land_ref.at[device], outer_land_ref.at[device], (w_send, w_recv), 8 + j, pair)
        for j, device in enumerate(across)
    ]
    owners = across + (sibling,) + tuple(device + 1 - 2 * core for device in across)
    outer_loads = [
        pltpu.make_async_copy(outer_land_ref.at[owner], wout_ref.at[:, lanes_of(owner)], load_sem.at[n])
        for n, owner in enumerate(owners)
    ]
    for m in ROW_ORDER:
        for copy in row_copies[m]:
            copy.start()
    for copy in keeps + pair_inner + outer_copies + pair_outer[:1]:
        copy.start()
    for m in range(4):
        for copy in gate_copies[m]:
            copy.start()
    grad_copies = [
        to_plane(
            m, lambda m, c: grads_ref.at[c * 4 + planes[m]], lambda m: dy_ref.at[m, chip], (grad_send, grad_recv)
        )
        for m in range(2)
    ]
    far_grads = pltpu.make_async_copy(far_ref, dy_ref.at[pl.ds(2, 2)], local_sem.at[9])
    far_grads.start()
    for copy in keeps:
        copy.wait()
    for copy in pair_inner:
        copy.wait()

    def cols(tile, part):
        return pl.ds(pl.multiple_of(part * hidden + tile * half, half), half)

    def weight(tile, part):
        return win_ref[:, :, :, cols(tile, part)].reshape(width, half)

    def block(m):
        return pl.ds(m * chunk, chunk)

    def widen(m):
        for copy in row_copies[m]:
            copy.wait_recv()
        rows = x_ref.at[m]

        def step(tile, carry):
            values = rows[...].reshape(chunk, width)
            gate = dot_nn(values, weight(tile, 0))
            up = dot_nn(values, weight(tile, 1))
            square = gate * gate
            bent = jnp.tanh(gate * (0.7978845608028654 + 0.03567740813636141 * square))
            lifted = 0.5 + 0.5 * bent
            slope = lifted + (0.5 * gate) * (1.0 - bent * bent) * (
                0.7978845608028654 + 0.10703222440908423 * square
            )
            active = gate * lifted
            upper_ref[block(m), cols(tile, 0)] = (up * slope).astype(bf16)
            upper_ref[block(m), cols(tile, 1)] = active.astype(bf16)
            hid_ref[block(m), cols(tile, 0)] = (active * up).astype(bf16)
            return carry

        lax.fori_loop(0, tiles, step, 0)

    def narrow(m):
        def step(part, carry):
            here = pl.ds(pl.multiple_of(part * 256, 256), 256)
            values = dot_nn(hid_ref[block(m), :], wout_ref[:, here])
            out_ref[m, :, :, here] = values.astype(bf16).reshape(4, slots, 256)
            return carry

        lax.fori_loop(0, width // 256, step, 0)

    out_copies = [
        to_plane(m, lambda m, c: out_ref.at[m, c], lambda m: returned_ref.at[me], (out_send, out_recv))
        for m in range(4)
    ]
    own_out = pltpu.make_async_copy(out_ref.at[0, chip], returned_ref.at[me], local_sem.at[7])
    widen(0)
    widen(1)
    widen(2)
    for m in range(4):
        for copy in row_copies[m]:
            copy.wait_send()
    for m in range(2):
        for copy in grad_copies[m]:
            copy.start()
    for j, copy in enumerate(outer_copies):
        copy.wait_recv()
        pair_outer[1 + j].start()
        outer_loads[j].start()
    for j, copy in enumerate(pair_outer):
        copy.wait_recv()
        outer_loads[3 + j].start()
    for copy in outer_copies + pair_outer:
        copy.wait_send()
    for copy in outer_loads:
        copy.wait()
    for m in (2, 3, 1, 0):
        if m == 3:
            widen(m)
        narrow(m)
        for copy in out_copies[m]:
            copy.start()
    own_out.start()
    x_t_ref[...] = x_ref[...].reshape(tokens, width).T.reshape(x_t_ref.shape)

    far_grads.wait()
    for m in range(4):
        for copy in gate_copies[m] + (grad_copies[m] if m < 2 else []):
            copy.wait_recv()
        for j in range(4):
            gates = gates_in_ref[m, j].T[:slots, 0:1]
            dy_ref[m, j] = (dy_ref[m, j].astype(f32) * gates).astype(bf16)

    def outer_part(tile):
        slot = lax.rem(tile, STAGES)
        return remote(stage_out_ref.at[slot], outer_in_ref.at[tile], (part_send, part_recv), tiles + tile, pair)

    def weigh_outer(tile, carry):
        slot = lax.rem(tile, STAGES)

        @pl.when(tile >= STAGES)
        def _():
            outer_part(tile - STAGES).wait_send()

        grad_down = dot_nn(hid_ref[:, cols(tile, 0)].T, dy_ref[...].reshape(tokens, width))
        for j in range(4):
            low = grad_down[:, (2 * j) * shard:(2 * j + 1) * shard].astype(bf16)
            high = grad_down[:, (2 * j + 1) * shard:(2 * j + 2) * shard].astype(bf16)
            stage_out_ref[slot, j] = jnp.where(core == 0, high, low)
            hid_ref[pl.ds((j // 2) * half, half), pl.ds(pl.multiple_of(tile * half + (j % 2) * shard, shard), shard)] = (
                jnp.where(core == 0, low, high)
            )
        outer_part(tile).start()
        return carry

    lax.fori_loop(0, tiles, weigh_outer, 0)
    for tile in range(tiles - STAGES, tiles):
        outer_part(tile).wait_send()

    def join_outer(tile, carry):
        outer_part(tile).wait_recv()
        for j in range(4):
            own = hid_ref[pl.ds((j // 2) * half, half), pl.ds(pl.multiple_of(tile * half + (j % 2) * shard, shard), shard)]
            outer_in_ref[tile, j] = (own.astype(f32) + outer_in_ref[tile, j].astype(f32)).astype(bf16)
        return carry

    lax.fori_loop(0, tiles, join_outer, 0)
    own_gout = pltpu.make_async_copy(outer_in_ref.at[:, chip], gouter_ref.at[chip], local_sem.at[3])
    own_gout.start()
    gout_copies = [
        remote(outer_in_ref.at[:, device // 2], gouter_ref.at[chip], (gout_send, gout_recv), j, (device, z))
        for j, device in enumerate(across)
    ]
    for copy in gout_copies:
        copy.start()

    def back(first, count):
        here_rows = pl.ds(first * chunk, count * chunk)

        def step(tile, carry):
            down = wout_ref[pl.ds(pl.multiple_of(tile * half, half), half), :]
            grads = dy_ref[first:first + count].reshape(count * chunk, width)
            grad_hidden = dot_nt(grads, down)
            for part in range(2):
                slope = upper_ref[here_rows, cols(tile, part)].astype(f32)
                upper_ref[here_rows, cols(tile, part)] = (grad_hidden * slope).astype(bf16)
            return carry

        lax.fori_loop(0, tiles, step, 0)

        def gather(j, carry):
            here = pl.ds(pl.multiple_of(j * 256, 256), 256)
            weights = win_ref[j].reshape(2 * shard, 2 * hidden)
            values = dot_nt(upper_ref[here_rows, :], weights)
            back_ref[first:first + count, :, :, here] = values.astype(bf16).reshape(count, 4, slots, 256)
            return carry

        lax.fori_loop(0, 4, gather, 0)

    copy_copies = [
        to_plane(m, lambda m, c: back_ref.at[m, c], lambda m: copies_ref.at[me], (copy_send, copy_recv))
        for m in range(4)
    ]
    own_copy = pltpu.make_async_copy(back_ref.at[0, chip], copies_ref.at[me], local_sem.at[8])
    for first in range(4 - BACK_COUNT, -1, -BACK_COUNT):
        back(first, BACK_COUNT)
        for m in range(first, first + BACK_COUNT):
            for copy in copy_copies[m]:
                copy.start()
    own_copy.start()

    def inner_part(tile):
        slot = lax.rem(tile, STAGES)
        return remote(stage_in_ref.at[slot], inner_in_ref.at[tile], (part_send, part_recv), tile, pair)

    def inner_load(tile):
        slot = lax.rem(tile, 2)
        return pltpu.make_async_copy(inner_in_ref.at[tile], add_in_ref.at[slot], join_sem.at[slot])

    def inner_stores(tile):
        slot = lax.rem(tile, 2)
        return [
            pltpu.make_async_copy(
                add_in_ref.at[slot, part], ginner_ref.at[:, :, cols(tile, part)], join_sem.at[2 + 2 * slot + part]
            )
            for part in range(2)
        ]

    def join_begin(tile):
        inner_part(tile).wait_recv()

        @pl.when(tile >= 2)
        def _():
            for copy in inner_stores(tile - 2):
                copy.wait()

        inner_load(tile).start()

    def join_end(tile):
        slot = lax.rem(tile, 2)
        inner_load(tile).wait()
        for part in range(2):
            own = upper_ref[pl.ds(0, width // 2), cols(tile, part)].astype(f32)
            other = add_in_ref[slot, part].reshape(width // 2, half).astype(f32)
            add_in_ref[slot, part] = (own + other).astype(bf16).reshape(4, shard, half)
        for copy in inner_stores(tile):
            copy.start()

    def weigh_inner(tile, carry):
        slot = lax.rem(tile, STAGES)

        @pl.when(tile >= LAG)
        def _():
            join_begin(tile - LAG)

        @pl.when(tile >= STAGES)
        def _():
            inner_part(tile - STAGES).wait_send()

        for part in range(2):
            grad_upper = upper_ref[:, cols(tile, part)]
            other = x_t_ref[:, 1 - core].reshape(width // 2, tokens)
            stage_in_ref[slot, part] = dot_nn(other, grad_upper).astype(bf16).reshape(4, shard, half)
        inner_part(tile).start()
        for part in range(2):
            grad_upper = upper_ref[:, cols(tile, part)]
            own = x_t_ref[:, core].reshape(width // 2, tokens)
            upper_ref[pl.ds(0, width // 2), cols(tile, part)] = dot_nn(own, grad_upper).astype(bf16)

        @pl.when(tile >= LAG)
        def _():
            join_end(tile - LAG)

        return carry

    lax.fori_loop(0, tiles, weigh_inner, 0)
    for tile in range(tiles - LAG, tiles):
        join_begin(tile)
        join_end(tile)
    for tile in range(tiles - STAGES, tiles):
        inner_part(tile).wait_send()
    for tile in (tiles - 2, tiles - 1):
        for copy in inner_stores(tile):
            copy.wait()
    sent = ginner_sent_ref.shape[2]
    sent_copies = [
        remote(
            ginner_ref.at[device // 2, :, pl.ds(0, sent)], ginner_sent_ref.at[j], (gout_send, gout_recv), 3 + j,
            (device, z),
        )
        for j, device in enumerate(across)
    ]
    for copy in sent_copies:
        copy.start()
    own_out.wait()
    own_copy.wait()
    own_gout.wait()
    for m in range(4):
        for copy in (grad_copies[m] if m < 2 else []) + gate_copies[m]:
            copy.wait_send()
        for copy in out_copies[m] + copy_copies[m]:
            copy.wait()
    for copy in gout_copies + sent_copies:
        copy.wait()


ROW_ORDER = (0, 1, 2, 3)
BACK_COUNT = 2
STAGES = 4
LAG = 2


def run_experts(rows, gates, grads, far, inner, inner_others, outer):
    count, slots, width = rows.shape
    tokens = count * slots
    hidden = outer.shape[1]
    half = 256
    tiles = hidden // half
    shard = width // 8
    bf16 = jnp.bfloat16
    anywhere = pl.BlockSpec(memory_space=pl.ANY)
    sems = [pltpu.SemaphoreType.DMA((count,))] * 10 + [
        pltpu.SemaphoreType.DMA((12,)),
        pltpu.SemaphoreType.DMA((12,)),
        pltpu.SemaphoreType.DMA((2 * tiles,)),
        pltpu.SemaphoreType.DMA((2 * tiles,)),
        pltpu.SemaphoreType.DMA((6,)),
        pltpu.SemaphoreType.DMA((6,)),
        pltpu.SemaphoreType.DMA((11,)),
        pltpu.SemaphoreType.DMA((6,)),
        pltpu.SemaphoreType.DMA((7,)),
    ]
    outs = pl.pallas_call(
        expert_kernel,
        out_shape=(
            jax.ShapeDtypeStruct(rows.shape, bf16),
            jax.ShapeDtypeStruct(rows.shape, bf16),
            jax.ShapeDtypeStruct(inner.shape, bf16),
            jax.ShapeDtypeStruct((3, shard, inner.shape[2] // 4), bf16),
            jax.ShapeDtypeStruct((4, tiles, half, shard), bf16),
            jax.ShapeDtypeStruct((tiles, 2, 4, shard, half), bf16),
            jax.ShapeDtypeStruct((8, hidden, shard), bf16),
        ),
        in_specs=[anywhere] * 9,
        out_specs=(anywhere,) * 7,
        scratch_shapes=[
            pltpu.VMEM((4, 4, slots, width), bf16),
            pltpu.VMEM((4, 2, shard, tokens), bf16),
            pltpu.VMEM((4, 4, slots, width), bf16),
            pltpu.VMEM((4, 4, 8, 128), jnp.float32),
            pltpu.VMEM((4, 2, shard, 2 * hidden), bf16),
            pltpu.VMEM((hidden, width), bf16),
            pltpu.VMEM((tokens, 2 * hidden), bf16),
            pltpu.VMEM((tokens, hidden), bf16),
            pltpu.VMEM((4, 4, slots, width), bf16),
            pltpu.VMEM((4, 4, slots, width), bf16),
            pltpu.VMEM((STAGES, 2, 4, shard, half), bf16),
            pltpu.VMEM((STAGES, 4, half, shard), bf16),
            pltpu.VMEM((2, 2, 4, shard, half), bf16),
            pltpu.VMEM((tiles, 4, half, shard), bf16),
        ] + sems,
        compiler_params=pltpu.CompilerParams(
            collective_id=1, has_side_effects=True, vmem_limit_bytes=63 * 2**20
        ),
        cost_estimate=pl.CostEstimate(
            flops=180 * 10**9, bytes_accessed=60 * 2**20, transcendentals=tokens * hidden
        ),
        name="run_experts",
    )(rows, gates, grads, far, inner, *inner_others, outer)
    return outs[0], outs[1], outs[2], outs[3], outs[4].reshape(outer.shape)


def attend_back(pair, proj_ref, dout_ref, lse_ref, tile_ref, dproj_ref, span_ref, dk_ref, dv_ref, near_ref):
    length = proj_ref.shape[1]
    blocks = length // BLK
    depth = 64
    wide = 2 * depth
    here = slice(pair * wide, (pair + 1) * wide)
    lane = lax.broadcasted_iota(jnp.int32, (1, wide), 1)
    keys = proj_ref[1, :, here]
    values = proj_ref[2, :, here]
    keys_t = keys.T
    dk_ref[...] = jnp.zeros_like(dk_ref)
    dv_ref[...] = jnp.zeros_like(dv_ref)
    near_ref[...] = jnp.zeros_like(near_ref)
    far_sum = [jnp.zeros((1, BLK), jnp.float32) for h in range(2)]
    for block in range(blocks):
        rows = pl.ds(block * BLK, BLK)
        key_count = (block + 1) * BLK
        query = proj_ref[0, rows, here] * jnp.bfloat16(0.125)
        grad = dout_ref[rows, here]
        dq_parts = []
        dk_sum = None
        dv_sum = None
        for h in range(2):
            own = (lane // depth) == h
            query_h = jnp.where(own, query, jnp.bfloat16(0))
            grad_h = jnp.where(own, grad, jnp.bfloat16(0))
            scores = dot_nt(keys[:key_count], query_h)
            grad_p = dot_nt(values[:key_count], grad_h)
            lse = lse_ref[pair, h:h + 1, rows]
            far = tile_ref[2 * pair + h, 1, 0:1, BLK - 1:BLK].astype(jnp.float32)
            probs = []
            delta = None
            for kb in range(block + 1):
                d = block - kb
                part = scores[kb * BLK:(kb + 1) * BLK]
                bias = tile_ref[2 * pair + h, d].astype(jnp.float32) if d < 2 else far
                part = jnp.exp(part + (bias - lse))
                probs.append(part)
                term = jnp.sum(part * grad_p[kb * BLK:(kb + 1) * BLK], axis=0, keepdims=True)
                delta = term if delta is None else delta + term
            ds = []
            for kb in range(block + 1):
                d = block - kb
                part = probs[kb] * (grad_p[kb * BLK:(kb + 1) * BLK] - delta)
                if d < 2:
                    near_ref[h, d] += part
                else:
                    far_sum[h] = far_sum[h] + jnp.sum(part, axis=0, keepdims=True)
                ds.append(part.astype(jnp.bfloat16))
            ds = jnp.concatenate(ds, axis=0)
            weights = jnp.concatenate([p.astype(jnp.bfloat16) for p in probs], axis=0)
            dv_h = dot_nn(weights, grad_h)
            dk_h = dot_nn(ds, query_h)
            dv_sum = dv_h if dv_sum is None else dv_sum + dv_h
            dk_sum = dk_h if dk_sum is None else dk_sum + dk_h
            dq_parts.append(dot_nn(keys_t[h * depth:(h + 1) * depth, :key_count], ds))
        dk_ref[:key_count] += dk_sum
        dv_ref[:key_count] += dv_sum
        dproj_ref[0, rows, here] = (jnp.concatenate(dq_parts, axis=0).T * 0.125).astype(jnp.bfloat16)
    dproj_ref[1, :, here] = dk_ref[...].astype(jnp.bfloat16)
    dproj_ref[2, :, here] = dv_ref[...].astype(jnp.bfloat16)
    flip = (
        lax.broadcasted_iota(jnp.int32, (BLK, BLK), 0) + lax.broadcasted_iota(jnp.int32, (BLK, BLK), 1) == BLK - 1
    ).astype(jnp.bfloat16)
    lanes = lax.broadcasted_iota(jnp.int32, (1, 2 * BLK), 1)
    for h in range(2):
        for d in range(2):
            near = near_ref[h, d]
            near_high = near.astype(jnp.bfloat16)
            near_low = (near - near_high.astype(jnp.float32)).astype(jnp.bfloat16)
            flipped = dot_nn(flip, near_high) + dot_nn(flip, near_low)
            spread = jnp.concatenate([flipped, jnp.zeros((BLK, BLK), jnp.float32)], axis=1)
            turned = pltpu.roll(spread, 1, 1, stride=1, stride_axis=0)
            along = jnp.sum(turned, axis=0, keepdims=True)
            if d == 1:
                along = along + jnp.where(lanes == 2 * BLK - 1, jnp.sum(far_sum[h], axis=1, keepdims=True), 0.0)
            span_ref[2 * pair + h, d:d + 1, :] = along


def back_kernel(
    returned_hbm, copies_hbm, hidden_hbm, cot_hbm, cols_hbm, wo_hbm, att_hbm, router_ref, gains_ref, counts_ref,
    picks_ref, proj_hbm, lse_hbm, tile_hbm, wq_hbm, seq_hbm, ginner_hbm,
    mixed_ref, gtok_ref, gqkv_ref, gwo_ref, sums_ref, inner_in_hbm,
    returned_ref, copies_ref, hidden_ref, cot_ref, cols_ref, wo_ref, att_ref, gp_ref, dout_send_ref,
    proj_ref, lse_ref, tile_ref, wq_ref, seq_ref, dout_ref, dproj_ref, span_ref, dk_ref, dv_ref,
    near_ref, turned_ref, first_send_ref, first_in_ref,
    q_stage_ref, q_in_ref, q_own_ref, q_across_ref, q_z_ref, q_z_in_ref,
    gout_ref, o_in_ref, o_sum_ref, o_across_ref, o_z_ref, o_z_in_ref,
    s_own_ref, s_in_ref, s_sum_ref, s_across_ref, s_z_ref, s_z_in_ref,
    send_sem, recv_sem, load_sem,
):
    x, z, along_z, across, sibling = places()
    core = x % 2
    chip = x // 2
    half = z % 2
    f32, bf16 = jnp.float32, jnp.bfloat16
    rows, width = gtok_ref.shape
    shard = width // 8
    step = rows // 2
    group = gqkv_ref.shape[2]
    experts = returned_ref.shape[0] // CAP
    pair = (sibling, z)
    chips = [(device, z) for device in across]
    lines = [(x, other) for other in along_z]
    barrier = pltpu.get_barrier_semaphore()
    for peer in chips + lines + [pair]:
        pl.semaphore_signal(barrier, inc=1, device_id=peer, device_id_type=MESH_ID)
    loads = {}
    for name, source, target in (
        ("cols", cols_hbm, cols_ref), ("returned", returned_hbm, returned_ref), ("hidden", hidden_hbm, hidden_ref),
        ("cot", cot_hbm, cot_ref), ("copies", copies_hbm, copies_ref), ("wo", wo_hbm, wo_ref),
        ("att", att_hbm, att_ref), ("seq", seq_hbm, seq_ref), ("proj", proj_hbm, proj_ref),
        ("lse", lse_hbm, lse_ref), ("tile", tile_hbm, tile_ref), ("wq", wq_hbm, wq_ref),
    ):
        loads[name] = pltpu.make_async_copy(source, target, load_sem.at[len(loads)])
        loads[name].start()
    pl.semaphore_wait(barrier, 7)
    started = []

    def send(source, target, device):
        index = len(started)
        copy = pltpu.make_async_remote_copy(
            src_ref=source, dst_ref=target, send_sem=send_sem.at[index], recv_sem=recv_sem.at[index],
            device_id=device, device_id_type=MESH_ID,
        )
        copy.start()
        started.append(copy)
        return copy

    inner_rest = inner_in_hbm.shape[2]
    inner_copies = [
        send(
            ginner_hbm.at[device // 2, :, pl.ds(ginner_hbm.shape[2] - inner_rest, inner_rest)], inner_in_hbm.at[j],
            (device, z),
        )
        for j, device in enumerate(across)
    ]

    gain_second = gains_ref[1:2, :]
    router_t = router_ref[...]
    step = rows // 2
    counts = counts_ref[...]
    tokens = 32 * rows
    pairs_in_all = 2 * tokens
    push = loss_weight * experts * (counts / pairs_in_all) / tokens
    slot_lane = lax.broadcasted_iota(jnp.int32, (1, returned_ref.shape[0]), 1).astype(f32)
    expert_lane = lax.broadcasted_iota(jnp.int32, (1, shard), 1).astype(f32)
    own_width = dout_ref.shape[1]
    dout_copies = []
    gain2_sum = jnp.zeros((1, width), f32)
    route_sum = jnp.zeros((1, shard), f32)
    grad_router = jnp.zeros((shard, width), f32)
    for name in ("cols", "returned", "hidden", "cot"):
        loads[name].wait()
    for i in range(2):
        here = slice(i * step, (i + 1) * step)
        cols = cols_ref[here, :]
        route = jnp.where(expert_lane < experts, cols, 0.0)
        marks = [(slot_lane == cols[:, experts + 2 + c:experts + 3 + c]).astype(bf16) for c in range(2)]
        picked = [dot_nn(mark, returned_ref[...]) for mark in marks]
        hidden = hidden_ref[here, :]
        grad_mixed = cot_ref[here, :].astype(f32)
        mixed_ref[here, :] = (
            hidden + picked[0] * cols[:, experts:experts + 1] + picked[1] * cols[:, experts + 1:experts + 2]
        ).astype(bf16)
        grad_route = push
        for c in range(2):
            hit = expert_lane == cols[:, experts + 4 + c:experts + 5 + c]
            grad_route = grad_route + jnp.where(hit, jnp.sum(grad_mixed * picked[c], axis=1, keepdims=True), 0.0)
        grad_logits = route * (grad_route - jnp.sum(route * grad_route, axis=1, keepdims=True))
        route_sum = route_sum + jnp.sum(route, axis=0, keepdims=True)
        if i == 0:
            loads["copies"].wait()
        grad_second = dot_nn(marks[0] + marks[1], copies_ref[...]) + dot_nn(grad_logits.astype(bf16), router_t)
        normed, scale = normalize(hidden)
        second_norm = (normed * gain_second).astype(bf16)
        grad_router = grad_router + dot_nn(grad_logits.T.astype(bf16), second_norm)
        gain2_sum = gain2_sum + jnp.sum(grad_second * normed, axis=0, keepdims=True)
        grad_normed = grad_second * gain_second
        grad_hidden = grad_mixed + scale * (
            grad_normed - normed * jnp.mean(grad_normed * normed, axis=-1, keepdims=True)
        )
        hidden_ref[here, :] = grad_hidden
        grad_part = grad_hidden.astype(bf16)
        gp_ref[here, :] = grad_part
        if i == 0:
            loads["wo"].wait()
        dout_send_ref[here, :] = dot_nt(grad_part, wo_ref[own_width:, :]).astype(bf16)
        for slot in (1, 0) if i == 0 else (1,):
            lanes = pl.ds(slot * group, group)
            dout_copies.append(
                send(dout_send_ref.at[here, lanes], dout_ref.at[pl.ds(half * rows + i * step, step), lanes], lines[0])
            )


    own_rows = pl.ds(pl.multiple_of(half * rows, rows), rows)
    dout_ref[own_rows, :] = dot_nt(gp_ref[...], wo_ref[:own_width, :]).astype(bf16)

    loads["att"].wait()
    grad_out = dot_nn(att_ref[...].T, gp_ref[...]).astype(bf16)
    for owner in range(8):
        gout_ref[owner // 2, owner % 2] = grad_out[:, owner * shard:(owner + 1) * shard]
    o_pair = [send(gout_ref.at[j, 1 - core], o_in_ref.at[j], pair) for j in range(4)]

    gain_first = gains_ref[0:1, :]
    loads["seq"].wait()
    for i in range(4):
        normed, _ = normalize(seq_ref[i // 2, (i % 2) * step:(i % 2 + 1) * step, :].astype(f32))
        turned_ref[:, :, :, i * step:(i + 1) * step] = (
            (normed * gain_first).astype(bf16).T.reshape(4, 2, shard, step)
        )

    dout_copies.append(
        send(
            dout_send_ref.at[pl.ds(step, step), pl.ds(0, group)],
            dout_ref.at[pl.ds(half * rows + step, step), pl.ds(0, group)],
            lines[0],
        )
    )
    for name in ("proj", "lse", "tile"):
        loads[name].wait()
    for n in (0, 2):
        dout_copies[n].wait_recv()

    def attend(number):
        attend_back(
            number, proj_ref, dout_ref, lse_ref, tile_ref, dproj_ref, span_ref, dk_ref, dv_ref, near_ref
        )

    def weigh_other(slot):
        here = pl.ds(slot * group, group)
        other = turned_ref[:, 1 - core].reshape(width // 2, 2 * rows)
        for c in range(3):
            q_stage_ref[slot, c] = dot_nn(other, dproj_ref[c, :, here]).astype(bf16).reshape(4, shard, group)
        return send(q_stage_ref.at[slot], q_in_ref.at[slot], pair)

    def weigh_own(slot):
        here = pl.ds(slot * group, group)
        own = turned_ref[:, core].reshape(width // 2, 2 * rows)
        for c in range(3):
            q_own_ref[slot, c] = dot_nn(own, dproj_ref[c, :, here]).astype(bf16).reshape(4, shard, group)

    def to_chips(slot, copy):
        copy.wait_recv()
        q_own_ref[slot] = (q_own_ref[slot].astype(f32) + q_in_ref[slot].astype(f32)).astype(bf16)
        return [
            send(q_own_ref.at[slot, :, device // 2], q_across_ref.at[slot, j], chips[j])
            for j, device in enumerate(across)
        ]

    def chip_total(slot, copies):
        for copy in copies:
            copy.wait_recv()
        total = q_own_ref[slot, :, chip].astype(f32)
        for j in range(3):
            total = total + q_across_ref[slot, j].astype(f32)
        return total

    attend(2)
    attend(3)
    q_pair_1 = weigh_other(1)
    for copy in o_pair:
        copy.wait_recv()
    for j in range(4):
        o_sum_ref[j] = (gout_ref[j, core].astype(f32) + o_in_ref[j].astype(f32)).astype(bf16)
    o_chips = [send(o_sum_ref.at[device // 2], o_across_ref.at[j], chips[j]) for j, device in enumerate(across)]
    weigh_own(1)
    q_chips_1 = to_chips(1, q_pair_1)
    for n in (1, 3):
        dout_copies[n].wait_recv()
    attend(0)
    attend(1)

    loads["wq"].wait()
    gain1_sum = jnp.zeros((1, width), f32)
    first_copies = []
    for turn, side in enumerate((1 - half, half)):
        for i in range(2):
            here = pl.ds(pl.multiple_of(side * rows + i * step, step), step)
            part = sum(
                dot_nt(dproj_ref[c, here, slot * group:(slot + 1) * group], wq_ref[slot, :, c].reshape(width, group))
                for slot in range(2)
                for c in range(3)
            )
            normed, _ = normalize(seq_ref[side, i * step:(i + 1) * step, :].astype(f32))
            gain1_sum = gain1_sum + jnp.sum(part * normed, axis=0, keepdims=True)
            if turn:
                gtok_ref[i * step:(i + 1) * step, :] = part
            else:
                first_send_ref[i * step:(i + 1) * step, :] = part.astype(bf16)
                block = pl.ds(i * step, step)
                first_copies.append(send(first_send_ref.at[block], first_in_ref.at[block], lines[0]))
        if not turn:
            q_pair_0 = weigh_other(0)

    table = None
    for d in range(2):
        along = span_ref[:, d, :]
        high = along.astype(bf16)
        low = (along - high.astype(f32)).astype(bf16)
        part = dot_nn(high, picks_ref[d]) + dot_nn(low, picks_ref[d])
        table = part if table is None else table + part
    heads = table.shape[0] // 2
    table = table.T[:32, :]
    blank = jnp.zeros((table.shape[0], shard - heads), f32)
    placed = pltpu.roll(jnp.concatenate([table[:, :heads], blank], axis=1), heads * z, 1) + pltpu.roll(
        jnp.concatenate([table[:, heads:], blank], axis=1), heads * ((z + 2) % 4), 1
    )
    for owner in range(8):
        here = slice(owner * shard, (owner + 1) * shard)
        target = s_own_ref.at[owner // 2, owner % 2]
        target[0:1, :] = gain1_sum[:, here]
        target[1:2, :] = gain2_sum[:, here]
        target[2:2 + experts, :] = grad_router[:experts, here]
        target[22:23, :] = route_sum
        target[23:24, :] = jnp.zeros((1, shard), f32)
        target[18:22, :] = placed[4 * owner:4 * owner + 4, :]
    s_pair = send(s_own_ref.at[:, 1 - core], s_in_ref, pair)
    weigh_own(0)

    q_chips_0 = to_chips(0, q_pair_0)
    s_pair.wait_recv()
    s_sum_ref[...] = s_own_ref[:, core] + s_in_ref[...]
    s_chips = [send(s_sum_ref.at[device // 2], s_across_ref.at[j], chips[j]) for j, device in enumerate(across)]
    q_z_ref[...] = chip_total(1, q_chips_1).astype(bf16)
    q_line = send(q_z_ref, q_z_in_ref, lines[1])
    for copy in o_chips:
        copy.wait_recv()
    o_total = o_sum_ref[chip].astype(f32)
    for j in range(3):
        o_total = o_total + o_across_ref[j].astype(f32)
    rows_out = gwo_ref.shape[0]
    gwo_ref[...] = o_total[:rows_out]
    o_z_ref[...] = o_total[rows_out:].astype(bf16).reshape(o_z_ref.shape)
    out_slots = (2, 1, 3)
    o_lines = [send(o_z_ref.at[out_slots[j] - 1], o_z_in_ref.at[j], lines[j]) for j in range(3)]
    for copy in s_chips:
        copy.wait_recv()
    s_z_ref[...] = s_sum_ref[chip] + s_across_ref[0] + s_across_ref[1] + s_across_ref[2]
    s_lines = [send(s_z_ref, s_z_in_ref.at[j], lines[j]) for j in range(3)]
    gqkv_ref[...] = chip_total(0, q_chips_0)

    for i in range(2):
        first_copies[i].wait_recv()
        here = slice(i * step, (i + 1) * step)
        grad = (gtok_ref[here, :] + first_in_ref[here, :].astype(f32)) * gain_first
        normed, scale = normalize(seq_ref[half, here, :].astype(f32))
        gtok_ref[here, :] = hidden_ref[here, :] + scale * (
            grad - normed * jnp.mean(grad * normed, axis=-1, keepdims=True)
        )
    q_line.wait_recv()
    gqkv_ref[...] += q_z_in_ref[...].astype(f32)
    for copy in s_lines + o_lines:
        copy.wait_recv()
    gwo_ref[...] += o_z_in_ref[0].astype(f32) + o_z_in_ref[1].astype(f32) + o_z_in_ref[2].astype(f32)
    sums = s_z_ref[...] + s_z_in_ref[0] + s_z_in_ref[1] + s_z_in_ref[2]
    sums_ref[...] = sums
    for copy in inner_copies:
        copy.wait_recv()
    for copy in started:
        copy.wait_send()


def run_back(
    returned, copies, hidden, cot, cols, wo, att, router_t, gains, counts, picks, proj, lse, tiles, wq, seq, ginner, sent
):
    rows, width = hidden.shape
    length = 2 * rows
    shard = width // 8
    group = wq.shape[4]
    rows_out = width // 4
    heads = tiles.shape[0]
    f32, bf16 = jnp.float32, jnp.bfloat16
    anywhere = pl.BlockSpec(memory_space=pl.ANY)
    inside = pl.BlockSpec(memory_space=pltpu.VMEM)
    copies_count = 3 + 4 + 4 + 2 + 3 + 3 + 3 + 2 + 1 + 3 + 1 + 3 + 3
    return pl.pallas_call(
        back_kernel,
        out_shape=(
            jax.ShapeDtypeStruct((rows, width), bf16),
            jax.ShapeDtypeStruct((rows, width), f32),
            jax.ShapeDtypeStruct((3, shard, group), f32),
            jax.ShapeDtypeStruct((rows_out, shard), f32),
            jax.ShapeDtypeStruct((24, shard), f32),
            jax.ShapeDtypeStruct((3, shard, ginner.shape[2] - sent), bf16),
        ),
        in_specs=[anywhere] * 7 + [inside] * 4 + [anywhere] * 6,
        out_specs=(inside,) * 5 + (anywhere,),
        scratch_shapes=[
            pltpu.VMEM(returned.shape, bf16),
            pltpu.VMEM(copies.shape, bf16),
            pltpu.VMEM(hidden.shape, f32),
            pltpu.VMEM(cot.shape, bf16),
            pltpu.VMEM(cols.shape, f32),
            pltpu.VMEM(wo.shape, bf16),
            pltpu.VMEM(att.shape, bf16),
            pltpu.VMEM((rows, width), bf16),
            pltpu.VMEM((rows, 2 * group), bf16),
            pltpu.VMEM(proj.shape, bf16),
            pltpu.VMEM(lse.shape, f32),
            pltpu.VMEM(tiles.shape, bf16),
            pltpu.VMEM(wq.shape, bf16),
            pltpu.VMEM(seq.shape, bf16),
            pltpu.VMEM((length, 2 * group), bf16),
            pltpu.VMEM(proj.shape, bf16),
            pltpu.VMEM((heads, 2, 2 * BLK), f32),
            pltpu.VMEM((length, 128), f32),
            pltpu.VMEM((length, 128), f32),
            pltpu.VMEM((2, 2, BLK, BLK), f32),
            pltpu.VMEM((4, 2, shard, length), bf16),
            pltpu.VMEM((rows, width), bf16),
            pltpu.VMEM((rows, width), bf16),
            pltpu.VMEM((2, 3, 4, shard, group), bf16),
            pltpu.VMEM((2, 3, 4, shard, group), bf16),
            pltpu.VMEM((2, 3, 4, shard, group), bf16),
            pltpu.VMEM((2, 3, 3, shard, group), bf16),
            pltpu.VMEM((3, shard, group), bf16),
            pltpu.VMEM((3, shard, group), bf16),
            pltpu.VMEM((4, 2, width, shard), bf16),
            pltpu.VMEM((4, width, shard), bf16),
            pltpu.VMEM((4, width, shard), bf16),
            pltpu.VMEM((3, width, shard), bf16),
            pltpu.VMEM((3, rows_out, shard), bf16),
            pltpu.VMEM((3, rows_out, shard), bf16),
            pltpu.VMEM((4, 2, 24, shard), f32),
            pltpu.VMEM((4, 24, shard), f32),
            pltpu.VMEM((4, 24, shard), f32),
            pltpu.VMEM((3, 24, shard), f32),
            pltpu.VMEM((24, shard), f32),
            pltpu.VMEM((3, 24, shard), f32),
            pltpu.SemaphoreType.DMA((copies_count,)),
            pltpu.SemaphoreType.DMA((copies_count,)),
            pltpu.SemaphoreType.DMA((12,)),
        ],
        compiler_params=pltpu.CompilerParams(
            collective_id=2, has_side_effects=True, vmem_limit_bytes=62 * 2**20
        ),
        cost_estimate=pl.CostEstimate(flops=60 * 10**9, bytes_accessed=60 * 2**20, transcendentals=0),
        name="run_back",
    )(
        returned, copies, hidden, cot, cols, wo, att, router_t, gains, counts, picks, proj, lse, tiles, wq, seq, ginner
    )


def final_kernel(
    ginner_hbm, sent_hbm, rest_hbm, gouter_hbm, mixed_hbm, gtok_hbm, gqkv_hbm, gwo_hbm, sums_ref, counts_ref,
    inner_hbm, outer_hbm, mixed_out, tok_hbm, qkv_hbm, wo_hbm, gain1_ref, gain2_ref, grouter_ref, gbias_ref, load_ref,
    loss_ref,
    in_ref, out_ref, slim_in_ref, slim_out_ref, mixed_ref, tok_ref, qkv_ref, wo_ref, in_sem, out_sem, copy_sem,
):
    x, z, _, across, _ = places()
    chip = x // 2
    f32 = jnp.float32
    passed = (
        (mixed_hbm, mixed_ref, mixed_out), (gtok_hbm, tok_ref, tok_hbm), (gqkv_hbm, qkv_ref, qkv_hbm),
        (gwo_hbm, wo_ref, wo_hbm),
    )
    copies_in = [pltpu.make_async_copy(a, b, copy_sem.at[n]) for n, (a, b, _) in enumerate(passed)]
    copies = [pltpu.make_async_copy(b, c, copy_sem.at[4 + n]) for n, (_, b, c) in enumerate(passed)]
    depth, _, wide = in_ref.shape
    slim = slim_in_ref.shape[1]
    sent = sent_hbm.shape[2]
    jobs = []
    for part in range(ginner_hbm.shape[2] // wide):
        here = pl.ds(part * wide, wide)
        jobs.append((ginner_hbm.at[chip, :, here], inner_hbm.at[chip, :, here], in_ref, out_ref))
        for j, device in enumerate(across):
            source = sent_hbm.at[j, :, here] if part * wide < sent else rest_hbm.at[j, :, pl.ds(part * wide - sent, wide)]
            jobs.append((source, inner_hbm.at[device // 2, :, here], in_ref, out_ref))
    for n in range(gouter_hbm.shape[0]):
        for i in range(gouter_hbm.shape[1] // slim):
            here = pl.ds(i * slim, slim)
            jobs.append((gouter_hbm.at[n, here], outer_hbm.at[n, here], slim_in_ref, slim_out_ref))
    loads = [
        pltpu.make_async_copy(source, held.at[i % depth], in_sem.at[i % depth])
        for i, (source, _, held, _) in enumerate(jobs)
    ]
    stores = [
        pltpu.make_async_copy(held.at[i % depth], target, out_sem.at[i % depth])
        for i, (_, target, _, held) in enumerate(jobs)
    ]
    for i in range(depth - 1):
        loads[i].start()
    for copy in copies_in:
        copy.start()
    experts = load_ref.shape[1]
    heads = gbias_ref.shape[1]
    shard = sums_ref.shape[1]
    sums = sums_ref[...]
    gain1_ref[...] = sums[0:1, :]
    gain2_ref[...] = sums[1:2, :]
    grouter_ref[...] = sums[2:2 + experts, :].T
    gbias_ref[...] = pltpu.roll(sums[16:24, :], (shard - heads * z) % shard, 1)[2:6, :heads]
    tokens = 32 * gtok_hbm.shape[0]
    counts = counts_ref[:, :experts]
    pairs_in_all = 2 * tokens
    prob_sums = sums[22:23, :experts]
    load_ref[...] = jnp.concatenate([experts * counts / pairs_in_all, experts * prob_sums / tokens], axis=0)
    loss_ref[...] = experts * jnp.sum(counts / pairs_in_all * (prob_sums / tokens), axis=1, keepdims=True)
    for copy_in, copy in zip(copies_in, copies):
        copy_in.wait()
        copy.start()
    for i, (_, _, held_in, held_out) in enumerate(jobs):
        if i + depth - 1 < len(jobs):
            loads[i + depth - 1].start()
        loads[i].wait()
        if i >= depth:
            stores[i - depth].wait()
        held_out[i % depth] = held_in[i % depth].astype(f32)
        stores[i].start()
    for store in stores[-depth:]:
        store.wait()
    for copy in copies:
        copy.wait()


def finish(ginner, sent, rest, gouter, mixed, gtok, gqkv, gwo, sums, counts, experts, heads):
    f32, bf16 = jnp.float32, jnp.bfloat16
    local, shard, inner_width = ginner.shape
    wide = inner_width // 4
    slim = gouter.shape[1] // 2
    anywhere = pl.BlockSpec(memory_space=pl.ANY)
    inside = pl.BlockSpec(memory_space=pltpu.VMEM)
    return pl.pallas_call(
        final_kernel,
        out_shape=(
            jax.ShapeDtypeStruct(ginner.shape, f32),
            jax.ShapeDtypeStruct(gouter.shape, f32),
            jax.ShapeDtypeStruct(mixed.shape, bf16),
            jax.ShapeDtypeStruct(gtok.shape, f32),
            jax.ShapeDtypeStruct(gqkv.shape, f32),
            jax.ShapeDtypeStruct(gwo.shape, f32),
            jax.ShapeDtypeStruct((1, shard), f32),
            jax.ShapeDtypeStruct((1, shard), f32),
            jax.ShapeDtypeStruct((shard, experts), f32),
            jax.ShapeDtypeStruct((4, heads), f32),
            jax.ShapeDtypeStruct((2, experts), f32),
            jax.ShapeDtypeStruct((1, 1), f32),
        ),
        in_specs=[anywhere] * 8 + [inside] * 2,
        out_specs=(anywhere,) * 6 + (inside,) * 6,
        scratch_shapes=[
            pltpu.VMEM((4, shard, wide), bf16),
            pltpu.VMEM((4, shard, wide), f32),
            pltpu.VMEM((4, slim, shard), bf16),
            pltpu.VMEM((4, slim, shard), f32),
            pltpu.VMEM(mixed.shape, bf16),
            pltpu.VMEM(gtok.shape, f32),
            pltpu.VMEM(gqkv.shape, f32),
            pltpu.VMEM(gwo.shape, f32),
            pltpu.SemaphoreType.DMA((4,)),
            pltpu.SemaphoreType.DMA((4,)),
            pltpu.SemaphoreType.DMA((8,)),
        ],
        compiler_params=pltpu.CompilerParams(vmem_limit_bytes=62 * 2**20),
        cost_estimate=pl.CostEstimate(flops=0, bytes_accessed=32 * 2**20, transcendentals=0),
        name="finish",
    )(ginner, sent, rest, gouter, mixed, gtok, gqkv, gwo, sums, counts)


def fast_device(
    tokens, expert_ids, gain_attn, w_qkv, w_out, rel_bias, gain_ffn, router, w_in, w_down, cotangent
):
    f32, bf16 = jnp.float32, jnp.bfloat16
    tok_dev, model_width = tokens.shape
    expert_count = router.shape[1]
    top_count = expert_ids.shape[1]
    shard = model_width // 8
    group_heads = rel_bias.shape[1]

    expert_row = jnp.arange(expert_count, dtype=jnp.int32)
    hits = [(expert_ids[:, c][:, None] == expert_row[None]) for c in range(top_count)]
    both = sum(hit.astype(bf16) for hit in hits)
    steps = jnp.arange(tok_dev, dtype=jnp.int32)
    lower = (steps[None, :] < steps[:, None]).astype(bf16)
    before = jnp.dot(lower, both, preferred_element_type=f32)
    slots = [jnp.sum(jnp.where(hit, before, 0.0), axis=1).astype(jnp.int32) for hit in hits]
    kept = [slot < CAP for slot in slots]
    local_counts = jnp.sum(both.astype(f32), axis=0)
    count_high = jnp.floor(local_counts / 32.0)
    count_low = local_counts - 32.0 * count_high

    def lanes(rows):
        return jnp.pad(rows.astype(bf16), ((0, 0), (0, shard - rows.shape[1])))

    small = jnp.concatenate(
        [
            router.T,
            gain_attn[None],
            gain_ffn[None],
            lanes(rel_bias),
            lanes(count_high[None]),
            lanes(count_low[None]),
            jnp.zeros((8, shard), bf16),
        ],
        axis=0,
    )
    spots = [
        jnp.where(keep, ((expert_ids[:, c] % 4) * 4 + expert_ids[:, c] // 4) * CAP + slots[c], -1)
        for c, keep in enumerate(kept)
    ]
    spots_float = [spot.astype(f32) for spot in spots]
    ids = jnp.stack(spots_float + [expert_ids[:, c].astype(f32) for c in range(top_count)], axis=1)
    ids = jnp.pad(ids, ((0, 0), (expert_count + 2, 128 - expert_count - 6)))
    spot_rows = jnp.pad(jnp.stack(spots_float), ((0, 8 - top_count), (0, 0)))
    buckets = span_buckets()[:, :, None] == jnp.arange(128, dtype=jnp.int32)
    picks = buckets.astype(bf16)
    (
        seq_tokens, qkv_weight, out_weight, router_t, gains, count_row, projected, attended, log_totals, bias_tiles, hidden_state, columns,
        gate_rows, send_rows, grad_rows, inner_a, inner_b, inner_c,
        grads_far,
    ) = run_front(tokens, w_qkv, w_out, small, w_in, cotangent, picks, ids, spot_rows, expert_count)

    returned, grad_copies, grad_inner, grad_sent, grad_outer = run_experts(
        send_rows,
        gate_rows,
        grad_rows,
        grads_far,
        w_in,
        (inner_a, inner_b, inner_c),
        w_down,
    )
    mixed, grad_tokens, grad_qkv, grad_out_weight, sums, grad_rest = run_back(
        returned.reshape(-1, model_width),
        grad_copies.reshape(-1, model_width),
        hidden_state,
        cotangent,
        columns,
        out_weight,
        attended,
        router_t,
        gains,
        count_row,
        picks,
        projected,
        log_totals,
        bias_tiles,
        qkv_weight,
        seq_tokens,
        grad_inner,
        grad_sent.shape[2],
    )
    (
        grad_inner, grad_outer, mixed, grad_tokens, grad_qkv, grad_out_weight, gain_one, gain_two, grad_router,
        grad_rel_bias, router_load, loss,
    ) = finish(
        grad_inner,
        grad_sent,
        grad_rest,
        grad_outer,
        mixed,
        grad_tokens,
        grad_qkv,
        grad_out_weight,
        sums,
        count_row,
        expert_count,
        group_heads,
    )
    return (
        mixed,
        loss[0, 0],
        router_load,
        grad_tokens,
        gain_one[0],
        grad_qkv,
        grad_out_weight,
        grad_rel_bias,
        gain_two[0],
        grad_router,
        grad_inner,
        grad_outer,
    )


def solution(mesh):
    in_specs = (
        P(("gx", "gy"), None),
        P(("gx", "gy"), None),
        P("gx"),
        P(None, "gx", "gy"),
        P("gy", "gx"),
        P("gx", "gy"),
        P("gx"),
        P("gx", None),
        P("gy", "gx", None),
        P("gy", None, "gx"),
        P(("gx", "gy"), None),
    )
    out_specs = (
        P(("gx", "gy"), None),
        P(),
        P(),
        P(("gx", "gy"), None),
        P("gx"),
        P(None, "gx", "gy"),
        P("gy", "gx"),
        P("gx", "gy"),
        P("gx"),
        P("gx", None),
        P("gy", "gx", None),
        P("gy", None, "gx"),
    )
    return jax.shard_map(
        fast_device if fits_fast(mesh) else general_device, mesh=mesh, in_specs=in_specs, out_specs=out_specs, check_vma=False
    )
```

```python
import functools
import math

import jax
import jax.numpy as jnp
from jax import lax
from jax.experimental import pallas as pl
from jax.experimental.pallas import tpu as pltpu
from jax.sharding import PartitionSpec as P

LEN = 1024
BLK = 256
CAP = 80


bucket_edges = (12, 16, 23, 32, 46, 64, 91)
epsilon = 1e-06
loss_weight = 0.01
masked_score = -1e30


def bucket_of(offset):
    magnitude = jnp.abs(offset)
    far_bucket = 8 + sum(
        ((magnitude >= edge_value).astype(jnp.int32) for edge_value in bucket_edges)
    )
    return jnp.where(magnitude < 8, magnitude, far_bucket) + 16 * (offset > 0).astype(jnp.int32)


def normalize(values):
    row_scale = lax.rsqrt(jnp.mean(values * values, axis=-1, keepdims=True) + epsilon)
    return (values * row_scale, row_scale)


def norm_back(grad_out, normed, row_scale, gain_vector):
    grad_normed = grad_out * gain_vector
    grad_gain = jnp.sum(grad_out * normed, axis=0)
    grad_input = row_scale * (
        grad_normed - normed * jnp.mean(grad_normed * normed, axis=-1, keepdims=True)
    )
    return (grad_input, grad_gain)


def spread_offsets(along_offsets, row_count):
    head_count, span_width = along_offsets.shape
    key_count = span_width - row_count + 1
    tiled_rows = jnp.broadcast_to(
        along_offsets[:, None, :], (head_count, row_count, span_width)
    ).reshape(head_count, row_count * span_width)
    padded = jnp.pad(tiled_rows, ((0, 0), (0, row_count)))
    shaped = padded.reshape(head_count, row_count, span_width + 1)[:, :, :key_count]
    return shaped[:, :, ::-1]


def gather_offsets(score_grid, row_count):
    head_count = score_grid.shape[0]
    key_count = score_grid.shape[2]
    span_width = key_count + row_count - 1
    padded = jnp.pad(score_grid[:, :, ::-1], ((0, 0), (0, 0), (0, row_count)))
    flat_rows = padded.reshape(head_count, row_count * (key_count + row_count))[
        :, : row_count * span_width
    ]
    return jnp.sum(flat_rows.reshape(head_count, row_count, span_width), axis=1)


def offset_table(q_start, row_count, key_count, bucket_count):
    spot_index = jnp.arange(key_count + row_count - 1, dtype=jnp.int32)
    offsets = key_count - 1 - spot_index - q_start
    return (
        bucket_of(offsets)[:, None] == jnp.arange(bucket_count, dtype=jnp.int32)[None, :]
    ).astype(jnp.float32)


def block_scores(query_rows, key_rows, table_float, q_start):
    row_count = query_rows.shape[0]
    depth = query_rows.shape[2]
    key_count = key_rows.shape[0]
    picks_table = offset_table(q_start, row_count, key_count, table_float.shape[0])
    along_offsets = jnp.dot(picks_table, table_float, precision=lax.Precision.HIGHEST).T
    bias_grid = spread_offsets(along_offsets, row_count)
    scores = (
        jnp.einsum("qhd,khd->hqk", query_rows, key_rows, preferred_element_type=jnp.float32)
        / math.sqrt(depth)
        + bias_grid
    )
    query_pos = q_start + jnp.arange(row_count, dtype=jnp.int32)
    key_pos = jnp.arange(key_count, dtype=jnp.int32)
    allowed = key_pos[None, :] // BLK <= query_pos[:, None] // BLK
    return (jnp.where(allowed[None], scores, masked_score), picks_table)


def general_device(
    tokens, expert_ids, gain_attn, w_qkv, w_out, rel_bias, gain_ffn, router, w_in, w_down, cotangent
):
    shard_list = (gain_attn, w_qkv, w_out, rel_bias, gain_ffn, router, w_in, w_down)
    (
        gain_first,
        qkv_weight,
        out_weight,
        bias_table,
        gain_second,
        route_weight,
        inner_weight,
        outer_weight,
    ) = (
        lax.all_gather(shard_list[0], "gx", axis=0, tiled=True),
        lax.all_gather(shard_list[1], "gx", axis=1, tiled=True),
        lax.all_gather(shard_list[2], "gx", axis=1, tiled=True),
        lax.all_gather(shard_list[3], "gx", axis=0, tiled=True),
        lax.all_gather(shard_list[4], "gx", axis=0, tiled=True),
        lax.all_gather(shard_list[5], "gx", axis=0, tiled=True),
        lax.all_gather(shard_list[6], "gx", axis=1, tiled=True),
        lax.all_gather(shard_list[7], "gx", axis=2, tiled=True),
    )
    tok_dev = tokens.shape[0]
    count_x = lax.axis_size("gx")
    count_y = lax.axis_size("gy")
    total_tokens = tok_dev * count_x * count_y
    model_width = tokens.shape[1]
    expert_count = route_weight.shape[1]
    top_count = expert_ids.shape[1]
    local_experts = inner_weight.shape[0]
    head_count = bias_table.shape[1]
    head_width = qkv_weight.shape[2]
    depth = head_width // head_count
    q_rows = min(512, LEN)
    per_seq = LEN // q_rows
    inputs_float = tokens.astype(jnp.float32)
    normed_one, scale_one = normalize(inputs_float)
    first_norm = (normed_one * gain_first.astype(jnp.float32)).astype(jnp.bfloat16)
    group_rows = lax.all_gather(first_norm, "gy", axis=0, tiled=True)
    tok_group = group_rows.shape[0]
    seq_count = tok_group // LEN
    projected = jnp.einsum(
        "td,cdf->tcf", group_rows, qkv_weight, preferred_element_type=jnp.float32
    ).astype(jnp.bfloat16)
    projected = projected.reshape(tok_group, 3, head_count, depth)
    table_float = bias_table.astype(jnp.float32)

    def forward_block(item_index):
        seq_index = item_index // per_seq
        q_start = item_index % per_seq * q_rows
        query_rows = lax.dynamic_slice_in_dim(projected, seq_index * LEN + q_start, q_rows, 0)[:, 0]
        seq_rows = lax.dynamic_slice_in_dim(projected, seq_index * LEN, LEN, 0)
        scores, unused_picks = block_scores(query_rows, seq_rows[:, 1], table_float, q_start)
        row_max = jnp.max(scores, axis=-1, keepdims=True)
        expo_scores = jnp.exp(scores - row_max)
        row_total = jnp.sum(expo_scores, axis=-1, keepdims=True)
        soft_weights = (expo_scores / row_total).astype(jnp.bfloat16)
        block_out = jnp.einsum(
            "hqk,khd->qhd", soft_weights, seq_rows[:, 2], preferred_element_type=jnp.float32
        ).astype(jnp.bfloat16)
        return (block_out.reshape(q_rows, head_width), (row_max + jnp.log(row_total))[:, :, 0])

    attended, log_totals = lax.map(forward_block, jnp.arange(seq_count * per_seq, dtype=jnp.int32))
    attended = attended.reshape(tok_group, head_width)
    attn_sum = lax.psum_scatter(
        jnp.dot(attended, out_weight, preferred_element_type=jnp.float32).astype(jnp.bfloat16),
        "gy",
        scatter_dimension=0,
        tiled=True,
    ).astype(jnp.float32)
    hidden_state = inputs_float + attn_sum
    normed_two, scale_two = normalize(hidden_state)
    second_norm = (normed_two * gain_second.astype(jnp.float32)).astype(jnp.bfloat16)
    logits = jnp.dot(second_norm, route_weight, preferred_element_type=jnp.float32)
    route = jax.nn.softmax(logits, axis=-1)
    chosen = (
        expert_ids.reshape(-1)[:, None] == jnp.arange(expert_count, dtype=jnp.int32)[None, :]
    ).astype(jnp.int32)
    earlier = jnp.cumsum(chosen, axis=0) - chosen
    slot = jnp.sum(earlier * chosen, axis=-1).reshape(tok_dev, top_count)
    kept = (slot < CAP).astype(jnp.float32)
    counts, prob_sums = lax.psum(
        (jnp.sum(chosen, axis=0).astype(jnp.float32), jnp.sum(route, axis=0)), ("gx", "gy")
    )
    loss = expert_count * jnp.sum(counts / (total_tokens * top_count) * (prob_sums / total_tokens))
    router_load = jnp.stack(
        [
            expert_count * counts / (total_tokens * top_count),
            expert_count * prob_sums / total_tokens,
        ],
        axis=0,
    )
    slot_place = expert_ids * CAP + jnp.minimum(slot, CAP - 1)
    buffer_index = jnp.arange(expert_count * CAP, dtype=jnp.int32)[:, None, None]
    hit_table = (buffer_index == slot_place[None]).astype(jnp.float32) * kept[None]
    dispatch_matrix = jnp.sum(hit_table, axis=-1).astype(jnp.bfloat16)
    send_rows = jnp.dot(dispatch_matrix, second_norm, preferred_element_type=jnp.float32).astype(
        jnp.bfloat16
    )
    send_rows = send_rows.reshape(count_y, local_experts, CAP, model_width)
    received = lax.all_to_all(send_rows, "gy", split_axis=0, concat_axis=0, tiled=True)
    upper = jnp.einsum("slcd,ldf->slcf", received, inner_weight, preferred_element_type=jnp.float32)
    half_width = upper.shape[-1] // 2
    hidden_rows = (
        jax.nn.gelu(upper[..., :half_width], approximate=True) * upper[..., half_width:]
    ).astype(jnp.bfloat16)
    expert_out = jnp.einsum(
        "slcf,lfd->slcd", hidden_rows, outer_weight, preferred_element_type=jnp.float32
    ).astype(jnp.bfloat16)
    expert_out, upper, received = (expert_out, upper, received)
    returned = lax.all_to_all(expert_out, "gy", split_axis=0, concat_axis=0, tiled=True).reshape(
        expert_count * CAP, model_width
    )
    picked_rows = jnp.take(returned, slot_place, axis=0).astype(jnp.float32)
    gate_value = jnp.take_along_axis(route, expert_ids, axis=1) * kept
    mixed = hidden_state + jnp.sum(picked_rows * gate_value[:, :, None], axis=1)
    (
        gain_first,
        qkv_weight,
        out_weight,
        bias_table,
        gain_second,
        route_weight,
        inner_weight,
        outer_weight,
    ) = (
        lax.all_gather(shard_list[0], "gx", axis=0, tiled=True),
        lax.all_gather(shard_list[1], "gx", axis=1, tiled=True),
        lax.all_gather(shard_list[2], "gx", axis=1, tiled=True),
        lax.all_gather(shard_list[3], "gx", axis=0, tiled=True),
        lax.all_gather(shard_list[4], "gx", axis=0, tiled=True),
        lax.all_gather(shard_list[5], "gx", axis=0, tiled=True),
        lax.all_gather(shard_list[6], "gx", axis=1, tiled=True),
        lax.all_gather(shard_list[7], "gx", axis=2, tiled=True),
    )
    table_float = bias_table.astype(jnp.float32)
    grad_mixed = cotangent.astype(jnp.float32)
    grad_gate = kept * jnp.sum(grad_mixed[:, None, :] * picked_rows, axis=-1)
    gate_matrix = jnp.sum(hit_table * gate_value[None], axis=-1)
    grad_buffer = jnp.dot(gate_matrix, grad_mixed, precision=lax.Precision.HIGHEST).astype(
        jnp.bfloat16
    )
    grad_expert = lax.all_to_all(
        grad_buffer.reshape(count_y, local_experts, CAP, model_width),
        "gy",
        split_axis=0,
        concat_axis=0,
        tiled=True,
    )
    half_width = upper.shape[-1] // 2
    activated, pull_gelu = jax.vjp(
        lambda gate_part, up_part: jax.nn.gelu(gate_part, approximate=True) * up_part,
        upper[..., :half_width],
        upper[..., half_width:],
    )
    hidden_rows = activated.astype(jnp.bfloat16)
    grad_hidden = jnp.einsum(
        "slcd,lfd->slcf", grad_expert, outer_weight, preferred_element_type=jnp.float32
    )
    grad_outer = jnp.einsum(
        "slcf,slcd->lfd", hidden_rows, grad_expert, preferred_element_type=jnp.float32
    )
    grad_gate_part, grad_up_part = pull_gelu(grad_hidden)
    grad_upper = jnp.concatenate([grad_gate_part, grad_up_part], axis=-1).astype(jnp.bfloat16)
    grad_inner = jnp.einsum(
        "slcd,slcf->ldf", received, grad_upper, preferred_element_type=jnp.float32
    )
    grad_received = jnp.einsum(
        "slcf,ldf->slcd", grad_upper, inner_weight, preferred_element_type=jnp.float32
    ).astype(jnp.bfloat16)
    grad_copies = lax.all_to_all(
        grad_received, "gy", split_axis=0, concat_axis=0, tiled=True
    ).reshape(expert_count * CAP, model_width)
    grad_second = jnp.sum(
        jnp.take(grad_copies, slot_place, axis=0).astype(jnp.float32) * kept[:, :, None], axis=1
    )
    expert_hits = (expert_ids[:, :, None] == jnp.arange(expert_count, dtype=jnp.int32)).astype(
        jnp.float32
    )
    grad_route = (
        jnp.sum(grad_gate[:, :, None] * expert_hits, axis=1)
        + loss_weight * expert_count * (counts / (total_tokens * top_count)) / total_tokens
    )
    grad_logits = (
        route * (grad_route - jnp.sum(route * grad_route, axis=-1, keepdims=True))
    ).astype(jnp.bfloat16)
    grad_router = jnp.dot(second_norm.T, grad_logits, preferred_element_type=jnp.float32)
    grad_second = grad_second + jnp.dot(
        grad_logits, route_weight.T, preferred_element_type=jnp.float32
    )
    grad_hidden_state, grad_gain_second = norm_back(
        grad_second, normed_two, scale_two, gain_second.astype(jnp.float32)
    )
    grad_hidden_state = grad_mixed + grad_hidden_state
    piece_rows = lax.all_gather(grad_hidden_state.astype(jnp.bfloat16), "gy", axis=0, tiled=True)
    grad_out_weight = jnp.einsum(
        "tf,td->fd", attended, piece_rows, preferred_element_type=jnp.float32
    )
    update_rows = jnp.dot(piece_rows, out_weight.T, preferred_element_type=jnp.float32).astype(
        jnp.bfloat16
    )
    grad_out_weight, grad_attended = (grad_out_weight, update_rows)

    def backward_sequence(seq_index):
        seq_rows = lax.dynamic_slice_in_dim(projected, seq_index * LEN, LEN, 0)
        key_rows = seq_rows[:, 1]
        value_rows = seq_rows[:, 2]
        grad_keys = jnp.zeros((LEN, head_count, depth), jnp.float32)
        grad_values = jnp.zeros((LEN, head_count, depth), jnp.float32)
        grad_table = jnp.zeros(table_float.shape, jnp.float32)
        grad_queries = []
        for block_index in range(per_seq):
            q_start = block_index * q_rows
            query_rows = seq_rows[q_start : q_start + q_rows, 0]
            grad_out = lax.dynamic_slice_in_dim(
                grad_attended, seq_index * LEN + q_start, q_rows, 0
            ).reshape(q_rows, head_count, depth)
            scores, picks_table = block_scores(query_rows, key_rows, table_float, q_start)
            block_lse = log_totals[seq_index * per_seq + block_index]
            soft_probs = jnp.exp(scores - block_lse[:, :, None])
            grad_probs = jnp.einsum(
                "qhd,khd->hqk", grad_out, value_rows, preferred_element_type=jnp.float32
            )
            grad_scores = (
                soft_probs * (grad_probs - jnp.sum(soft_probs * grad_probs, axis=-1, keepdims=True))
            ).astype(jnp.bfloat16)
            grad_queries.append(
                jnp.einsum(
                    "hqk,khd->qhd", grad_scores, key_rows, preferred_element_type=jnp.float32
                )
                / math.sqrt(depth)
            )
            grad_keys = grad_keys + jnp.einsum(
                "hqk,qhd->khd", grad_scores, query_rows, preferred_element_type=jnp.float32
            ) / math.sqrt(depth)
            grad_values = grad_values + jnp.einsum(
                "hqk,qhd->khd",
                soft_probs.astype(jnp.bfloat16),
                grad_out,
                preferred_element_type=jnp.float32,
            )
            along_grads = gather_offsets(grad_scores.astype(jnp.float32), q_rows)
            grad_table = grad_table + jnp.dot(
                picks_table.T, along_grads.T, precision=lax.Precision.HIGHEST
            )
        stacked = jnp.stack(
            [jnp.concatenate(grad_queries, axis=0), grad_keys, grad_values], axis=1
        ).astype(jnp.bfloat16)
        return (stacked, grad_table)

    grad_projected, table_parts = lax.map(backward_sequence, jnp.arange(seq_count, dtype=jnp.int32))
    grad_projected = grad_projected.reshape(tok_group, 3, head_width)
    grad_bias_table = jnp.sum(table_parts, axis=0)
    grad_qkv_weight = jnp.einsum(
        "td,tcf->cdf", group_rows, grad_projected, preferred_element_type=jnp.float32
    )
    grad_slice = lax.slice_in_dim(grad_projected, 0, tok_dev * lax.axis_size("gy"), axis=0)
    grad_first = lax.psum_scatter(
        jnp.einsum(
            "tcf,cdf->td", grad_slice, qkv_weight, preferred_element_type=jnp.float32
        ).astype(jnp.bfloat16),
        "gy",
        scatter_dimension=0,
        tiled=True,
    ).astype(jnp.float32)
    grad_inputs, grad_gain_first = norm_back(
        grad_first, normed_one, scale_one, gain_first.astype(jnp.float32)
    )
    grad_tokens = grad_hidden_state + grad_inputs
    grad_gain_first, grad_gain_second, grad_router = (
        lax.psum(grad_gain_first.astype(jnp.bfloat16), "gy").astype(jnp.float32),
        lax.psum(grad_gain_second.astype(jnp.bfloat16), "gy").astype(jnp.float32),
        lax.psum(grad_router.astype(jnp.bfloat16), "gy").astype(jnp.float32),
    )
    summed_grads = (
        lax.psum_scatter(
            grad_gain_first.astype(jnp.bfloat16), "gx", scatter_dimension=0, tiled=True
        ).astype(jnp.float32),
        lax.psum_scatter(
            grad_qkv_weight.astype(jnp.bfloat16), "gx", scatter_dimension=1, tiled=True
        ).astype(jnp.float32),
        lax.psum_scatter(
            grad_out_weight.astype(jnp.bfloat16), "gx", scatter_dimension=1, tiled=True
        ).astype(jnp.float32),
        lax.psum_scatter(
            grad_bias_table.astype(jnp.bfloat16), "gx", scatter_dimension=0, tiled=True
        ).astype(jnp.float32),
        lax.psum_scatter(
            grad_gain_second.astype(jnp.bfloat16), "gx", scatter_dimension=0, tiled=True
        ).astype(jnp.float32),
        lax.psum_scatter(
            grad_router.astype(jnp.bfloat16), "gx", scatter_dimension=0, tiled=True
        ).astype(jnp.float32),
        lax.psum_scatter(
            grad_inner.astype(jnp.bfloat16), "gx", scatter_dimension=1, tiled=True
        ).astype(jnp.float32),
        lax.psum_scatter(
            grad_outer.astype(jnp.bfloat16), "gx", scatter_dimension=2, tiled=True
        ).astype(jnp.float32),
    )
    return (
        mixed.astype(jnp.bfloat16),
        loss,
        router_load,
        grad_tokens,
        summed_grads[0],
        summed_grads[1],
        summed_grads[2],
        summed_grads[3],
        summed_grads[4],
        summed_grads[5],
        summed_grads[6],
        summed_grads[7],
    )


def dot_nn(a, b):
    return lax.dot_general(a, b, (((1,), (0,)), ((), ())), preferred_element_type=jnp.float32)

def dot_nt(a, b):
    return lax.dot_general(a, b, (((1,), (1,)), ((), ())), preferred_element_type=jnp.float32)

def span_buckets():
    k = jnp.arange(2 * BLK, dtype=jnp.int32)
    return jnp.stack([bucket_of(BLK - k - BLK * d) for d in range(2)])

AXES = ("gx", "gy")
MESH_ID = pl.DeviceIdType.MESH


def fits_fast(mesh):
    return mesh.shape["gx"] == 8 and mesh.shape["gy"] == 4


def places():
    x = lax.axis_index("gx")
    z = lax.axis_index("gy")
    core = x % 2
    chip = x // 2
    along_z = (z + 1 - 2 * (z % 2), (z + 2) % 4, 3 - z)
    chips = (chip + 1 - 2 * (chip % 2), (chip + 2) % 4, 3 - chip)
    return x, z, along_z, tuple(2 * other + core for other in chips), x + 1 - 2 * core


def attend_front(pair, proj_ref, span_ref, tile_ref, attended_ref, lse_ref, kept_ref):
    length = proj_ref.shape[1]
    blocks = length // BLK
    depth = 64
    wide = 2 * depth
    here = slice(pair * wide, (pair + 1) * wide)
    lane = lax.broadcasted_iota(jnp.int32, (1, wide), 1)
    for h in range(2):
        for d in range(2):
            row = span_ref[d, 2 * pair + h:2 * pair + h + 1, :]
            spread = jnp.broadcast_to(row, (BLK, 2 * BLK))
            turned = pltpu.roll(spread, 0, 1, stride=1, stride_axis=0)
            tile_ref[h, d] = turned[:, BLK:]
            kept_ref[2 * pair + h, d] = turned[:, BLK:].astype(jnp.bfloat16)
    far = [span_ref[1, 2 * pair + h:2 * pair + h + 1, 2 * BLK - 1:2 * BLK] for h in range(2)]
    keys = proj_ref[1, :, here]
    values_t = proj_ref[2, :, here].T
    for block in range(blocks):
        rows = pl.ds(block * BLK, BLK)
        query = proj_ref[0, rows, here] * jnp.bfloat16(0.125)
        key_count = (block + 1) * BLK
        outs = []
        for h in range(2):
            picked = jnp.where((lane // depth) == h, query, jnp.bfloat16(0))
            scores = dot_nt(keys[:key_count], picked)
            parts = []
            for kb in range(block + 1):
                part = scores[kb * BLK:(kb + 1) * BLK]
                d = block - kb
                parts.append(part + (tile_ref[h, d] if d < 2 else far[h]))
            top = functools.reduce(jnp.maximum, [jnp.max(p, axis=0, keepdims=True) for p in parts])
            parts = [jnp.exp(p - top) for p in parts]
            total = functools.reduce(jnp.add, [jnp.sum(p, axis=0, keepdims=True) for p in parts])
            scale = 1.0 / total
            weights = jnp.concatenate([(p * scale).astype(jnp.bfloat16) for p in parts], axis=0)
            outs.append(dot_nn(values_t[h * depth:(h + 1) * depth, :key_count], weights))
            lse_ref[pair, h:h + 1, rows] = top + jnp.log(total)
        attended_ref[rows, here] = jnp.concatenate(outs, axis=0).T.astype(jnp.bfloat16)


def front_kernel(
    tok_ref, wq_ref, wo_ref, inner_ref, cot_hbm, picks_ref, eid_ref, router_in_ref, gain1_ref, gain2_ref, bias_ref,
    seq_out, wqs_out, wos_out, router_ref, gains_ref, counts_ref, proj_ref, att_ref, lse_ref, kept_ref, hidden_ref, cols_ref, gates_ref, rows_hbm, grads_hbm, inner_a_ref, inner_b_ref, inner_c_ref, far_ref,
    seq_ref, wqs_ref, wos_ref, wos_in_ref, smalls_ref, normed_ref, attended_ref, got_ref, span_ref, tile_ref, cot_ref, grads_ref, rows_ref, second_ref, gate_parts_ref,
    small_ref, ids_ref, spots_ref,
    send_sem, recv_sem, local_sem, out_sem,
):
    x, z, along_z, across, sibling = places()
    half = z % 2
    f32, bf16 = jnp.float32, jnp.bfloat16
    peers = [(x, other) for other in along_z] + [(other, z) for other in across] + [(sibling, z)]
    far_peers = [(device, plane) for plane in along_z[1:] for device in (x,) + across]
    peers += [peer for n, peer in enumerate(far_peers) if n % 4]
    barrier = pltpu.get_barrier_semaphore()
    for peer in peers:
        pl.semaphore_signal(barrier, inc=1, device_id=peer, device_id_type=MESH_ID)
    depth = wq_ref.shape[1]
    group = wq_ref.shape[2]
    rows_out = wo_ref.shape[0]
    rows, width = tok_ref.shape

    def qkv_part(owner, slot):
        return wqs_ref.at[slot, owner]

    def out_part(owner, slot, slots):
        return wos_in_ref.at[owner, pl.ds(slot * rows_out, slots * rows_out), :]

    keeps = [
        pltpu.make_async_copy(source, target, local_sem.at[n])
        for n, (source, target) in enumerate(
            ((small_ref, smalls_ref.at[0, x]), (wo_ref, out_part(x, 0, 1)), (wq_ref, qkv_part(x, 0)),
             (tok_ref, seq_ref.at[half]), (cot_hbm, cot_ref))
        )
    ]
    for copy in keeps[1:]:
        copy.start()

    experts = rows_ref.shape[0]
    lanes = lax.broadcasted_iota(jnp.int32, (1, depth), 1)
    lanes_f = lanes.astype(f32)
    named = jnp.concatenate([eid_ref[...].astype(f32), jnp.zeros((6, rows), f32)], axis=0).T
    named = [named[:, c:c + 1] for c in range(2)]
    hits = [(lanes_f == name).astype(f32) for name in named]
    both = hits[0] + hits[1]
    earlier = lax.broadcasted_iota(jnp.int32, (rows, rows), 1) < lax.broadcasted_iota(jnp.int32, (rows, rows), 0)
    before = dot_nn(earlier.astype(bf16), both.astype(bf16))
    spots = []
    for name, hit in zip(named, hits):
        slot = jnp.sum(hit * before, axis=1, keepdims=True)
        plane = jnp.floor(name * 0.25)
        spot = (4.0 * (name - 4.0 * plane) + plane) * CAP + slot
        spots.append(jnp.where(slot < CAP, spot, -1.0))
    ids = jnp.zeros((rows, depth), f32)
    for n, column in enumerate(spots + named):
        ids = jnp.where(lanes == experts + 2 + n, column, ids)
    ids_ref[...] = ids
    spots_ref[...] = jnp.where(lanes == 0, spots[0], jnp.where(lanes == 1, spots[1], 0.0)).T[:8, :]
    counted = jnp.sum(both, axis=0, keepdims=True)
    high = jnp.floor(counted / 32.0)
    router_rows = router_in_ref[...].astype(f32)
    bias = bias_ref[...].astype(f32)
    bias = jnp.concatenate([bias, jnp.zeros((bias.shape[0], depth - bias.shape[1]), f32)], axis=1)
    small_ref[...] = jnp.concatenate(
        [
            router_rows, gain1_ref[...].astype(f32), gain2_ref[...].astype(f32), bias, high, counted - 32.0 * high,
            jnp.zeros((8, depth), f32),
        ],
        axis=0,
    ).astype(bf16)
    keeps[0].start()
    pl.semaphore_wait(barrier, len(peers))
    started = []

    def send(source, target, device):
        index = len(started)
        copy = pltpu.make_async_remote_copy(
            src_ref=source, dst_ref=target, send_sem=send_sem.at[index], recv_sem=recv_sem.at[index],
            device_id=device, device_id_type=MESH_ID,
        )
        copy.start()
        started.append(copy)
        return copy

    out_slots = (2, 1, 3)
    near = across + (sibling,)
    small_z = [send(small_ref, smalls_ref.at[j + 1, x], (x, along_z[j])) for j in range(3)]
    wq_z = send(wq_ref, qkv_part(x, 1), (x, along_z[1]))
    wq_first = [send(wq_ref, qkv_part(x, 0), (other, z)) for other in near]
    tok_z = send(tok_ref, seq_ref.at[half], (x, along_z[0]))
    wo_z = [send(wo_ref, out_part(x, out_slots[j], 1), (x, along_z[j])) for j in range(3)]
    blocks = rows_ref.shape[0] // 4
    slots = rows_ref.shape[1]
    chunk = blocks * slots
    slot_row = lax.broadcasted_iota(jnp.int32, (chunk, 1), 0).astype(f32)

    def marks(i):
        return [(slot_row + i * chunk == spots_ref[c:c + 1, :]).astype(bf16) for c in range(2)]

    keeps[4].wait()
    for i in range(4):
        first, second = marks(i)
        grads_ref[i * blocks:(i + 1) * blocks] = (
            dot_nn(first + second, cot_ref[...]).astype(bf16).reshape(blocks, slots, width)
        )
    keeps[0].wait()
    for copy in small_z:
        copy.wait_recv()
    small_x = [send(smalls_ref.at[:, x], smalls_ref.at[:, x], (other, z)) for other in near]
    wq_z.wait_recv()
    wq_second = [send(qkv_part(x, 1), qkv_part(x, 1), (other, z)) for other in near]
    far_copies = [
        send(grads_ref.at[(device // 2) * 4 + plane], far_ref.at[n // 4, x // 2], (device, plane))
        for n, (device, plane) in enumerate(far_peers)
    ]
    small_on = []
    first_on = []
    for j in range(3):
        owner = across[j]
        small_x[j].wait_recv()
        small_on.append(send(smalls_ref.at[:, owner], smalls_ref.at[:, owner], (sibling, z)))
        wq_first[j].wait_recv()
        first_on.append(send(qkv_part(owner, 0), qkv_part(owner, 0), (sibling, z)))
    for copy in [small_x[3], wq_first[3]] + small_on + first_on:
        copy.wait_recv()
    for copy in keeps[1:4]:
        copy.wait()
    inner_copies = [
        send(inner_ref.at[device // 2], target, (device, z))
        for device, target in zip(across, (inner_a_ref, inner_b_ref, inner_c_ref))
    ]

    own_smalls = [smalls_ref[0, g].astype(f32) for g in range(8)]
    gain = jnp.concatenate([part[16:17, :] for part in own_smalls], axis=1)
    heads = span_ref.shape[1] // 2
    table = jnp.concatenate([part[18:22, :] for part in own_smalls], axis=0)
    other_table = jnp.concatenate([smalls_ref[2, g].astype(f32)[18:22, :] for g in range(8)], axis=0)
    table = jnp.where(lanes < heads, table, pltpu.roll(other_table, heads, 1))
    table = jnp.where(lanes < 2 * heads, table, 0.0)
    table = jnp.concatenate([table, jnp.zeros((depth - table.shape[0], depth), f32)], axis=0)
    table = table.T[:2 * heads, :].astype(bf16)
    for d in range(2):
        span_ref[d] = dot_nt(table, picks_ref[d])
    step = rows // 2

    def norm(side, i):
        normed, _ = normalize(seq_ref[side, i * step:(i + 1) * step, :].astype(f32))
        here = pl.ds(pl.multiple_of(side * rows + i * step, step), step)
        normed_ref[here, :] = (normed * gain).astype(bf16)

    for i in range(2):
        norm(half, i)
    tok_z.wait_recv()
    for i in range(2):
        norm(1 - half, i)

    def project(slot):
        here = slice(slot * group, (slot + 1) * group)
        for c in range(3):
            proj_ref[c, :, here] = dot_nn(normed_ref[...], wqs_ref[slot, :, c].reshape(width, group)).astype(bf16)

    def attend(pair):
        attend_front(pair, proj_ref, span_ref, tile_ref, attended_ref, lse_ref, kept_ref)

    def exchange(slot):
        here = pl.ds(slot * group, group)
        there = pl.ds(pl.multiple_of((1 - half) * rows, rows), rows)
        return send(attended_ref.at[there, here], got_ref.at[:, here], (x, along_z[0]))

    project(0)
    for copy in wo_z:
        copy.wait_recv()
    wo_x = [send(out_part(x, 0, 4), out_part(x, 0, 4), (other, z)) for other in near]
    attend(0)
    second_on = []
    for j in range(3):
        owner = across[j]
        wq_second[j].wait_recv()
        second_on.append(send(qkv_part(owner, 1), qkv_part(owner, 1), (sibling, z)))
    attend(1)
    got_0 = exchange(0)
    for copy in [wq_second[3]] + second_on:
        copy.wait_recv()
    project(1)
    outs = [
        pltpu.make_async_copy(source, target, out_sem.at[n])
        for n, (source, target) in enumerate(((seq_ref, seq_out), (wqs_ref, wqs_out)))
    ]
    for copy in outs:
        copy.start()
    attend(2)
    attend(3)
    got_1 = exchange(1)
    wo_on = []
    for j in range(3):
        owner = across[j]
        wo_x[j].wait_recv()
        wo_on.append(send(out_part(owner, 0, 4), out_part(owner, 0, 4), (sibling, z)))
    for copy in [wo_x[3]] + wo_on:
        copy.wait_recv()
    for owner in range(8):
        wos_ref[:, owner * depth:(owner + 1) * depth] = wos_in_ref[owner]
    outs.append(pltpu.make_async_copy(wos_ref, wos_out, out_sem.at[2]))
    outs[2].start()
    own = pl.ds(pl.multiple_of(half * rows, rows), rows)
    att_ref[:, :2 * group] = attended_ref[own, :]
    for copy in (got_0, got_1):
        copy.wait_recv()
    att_ref[:, 2 * group:] = got_ref[...]

    gain_second = jnp.concatenate([part[17:18, :] for part in own_smalls], axis=1)
    router = jnp.concatenate([part[:experts, :] for part in own_smalls], axis=1)
    router = jnp.concatenate([router, jnp.zeros((depth - experts, width), f32)], axis=0).astype(bf16)
    router_ref[...] = router
    gains_ref[...] = jnp.concatenate([gain, gain_second], axis=0)
    counted = sum(smalls_ref[j, g].astype(f32) for j in range(4) for g in range(8))
    counts_ref[...] = 32.0 * counted[22:23, :] + counted[23:24, :]
    for i in range(2):
        here = slice(i * step, (i + 1) * step)
        hidden = seq_ref[half, here, :].astype(f32) + dot_nn(att_ref[here, :], wos_ref[...])
        hidden_ref[here, :] = hidden
        normed, _ = normalize(hidden)
        second = (normed * gain_second).astype(bf16)
        second_ref[here, :] = second
        logits = jnp.where(lanes < experts, dot_nt(second, router), -1e30)
        route = jnp.exp(logits - jnp.max(logits, axis=1, keepdims=True))
        route = route / jnp.sum(route, axis=1, keepdims=True)
        ids = ids_ref[here, :]
        gates = []
        for c in range(2):
            gate = jnp.sum(jnp.where(lanes_f == ids[:, experts + 4 + c:experts + 5 + c], route, 0.0), axis=1, keepdims=True)
            gates.append(jnp.where(ids[:, experts + 2 + c:experts + 3 + c] >= 0.0, gate, 0.0))
            high = gates[c].astype(bf16).astype(f32)
            gate_parts_ref[c, here, :] = jnp.where(
                lanes == 0, high, jnp.where(lanes == 1, gates[c] - high, 0.0)
            ).astype(bf16)
        cols_ref[here, :] = jnp.where(
            lanes < experts, route, jnp.where(lanes == experts, gates[0], jnp.where(lanes == experts + 1, gates[1], ids))
        )
    for i in range(4):
        first, second = marks(i)
        rows_ref[i * blocks:(i + 1) * blocks] = (
            dot_nn(first + second, second_ref[...]).astype(bf16).reshape(blocks, slots, width)
        )
        parts = dot_nn(first, gate_parts_ref[0]) + dot_nn(second, gate_parts_ref[1])
        for n in range(blocks):
            turned = parts[n * slots:(n + 1) * slots, :].T
            line = jnp.concatenate([turned[0:1, :] + turned[1:2, :], jnp.zeros((1, depth - slots), f32)], axis=1)
            gates_ref[i * blocks + n] = jnp.broadcast_to(line, (8, depth))
    outs.append(pltpu.make_async_copy(rows_ref, rows_hbm, out_sem.at[3]))
    outs.append(pltpu.make_async_copy(grads_ref, grads_hbm, out_sem.at[4]))
    for copy in outs[3:]:
        copy.start()
    for copy in inner_copies + far_copies:
        copy.wait_recv()
    for copy in started:
        copy.wait_send()
    for copy in outs:
        copy.wait()


def run_front(tokens, w_qkv, w_out, w_in, cotangent, picks, ids, router, gain_first, gain_second, bias):
    rows, width = tokens.shape
    group = w_qkv.shape[2]
    f32, bf16 = jnp.float32, jnp.bfloat16
    heads = 2 * group // 64
    anywhere = pl.BlockSpec(memory_space=pl.ANY)
    inside = pl.BlockSpec(memory_space=pltpu.VMEM)
    seq = (2, rows, width)
    wqs = (2, 8) + w_qkv.shape
    wos = (width, width)
    experts = router.shape[0]
    small = (32, 128)
    smalls = (4, 8) + small
    copies_count = 3 + 1 + 4 + 1 + 3 + 4 + 4 + 3 + 3 + 4 + 3 + 3 + 3 + 2 + 8
    return pl.pallas_call(
        front_kernel,
        out_shape=(
            jax.ShapeDtypeStruct(seq, bf16),
            jax.ShapeDtypeStruct(wqs, bf16),
            jax.ShapeDtypeStruct(wos, bf16),
            jax.ShapeDtypeStruct((128, width), bf16),
            jax.ShapeDtypeStruct((2, width), f32),
            jax.ShapeDtypeStruct((1, 128), f32),
            jax.ShapeDtypeStruct((3, 2 * rows, 2 * group), bf16),
            jax.ShapeDtypeStruct((rows, width), bf16),
            jax.ShapeDtypeStruct((heads // 2, 2, 2 * rows), f32),
            jax.ShapeDtypeStruct((heads, 2, BLK, BLK), bf16),
            jax.ShapeDtypeStruct((rows, width), f32),
            jax.ShapeDtypeStruct((rows, 128), f32),
            jax.ShapeDtypeStruct((experts, 8, 128), f32),
            jax.ShapeDtypeStruct((experts, CAP, width), bf16),
            jax.ShapeDtypeStruct((experts, CAP, width), bf16),
            jax.ShapeDtypeStruct(w_in.shape[1:], bf16),
            jax.ShapeDtypeStruct(w_in.shape[1:], bf16),
            jax.ShapeDtypeStruct(w_in.shape[1:], bf16),
            jax.ShapeDtypeStruct((2, 4, CAP, width), bf16),
        ),
        in_specs=[anywhere] * 5 + [inside] * 6,
        out_specs=(anywhere,) * 3 + (inside,) * 10 + (anywhere,) * 6,
        scratch_shapes=[
            pltpu.VMEM(seq, bf16),
            pltpu.VMEM(wqs, bf16),
            pltpu.VMEM(wos, bf16),
            pltpu.VMEM((8, width, width // 8), bf16),
            pltpu.VMEM(smalls, bf16),
            pltpu.VMEM((2 * rows, width), bf16),
            pltpu.VMEM((2 * rows, 2 * group), bf16),
            pltpu.VMEM((rows, 2 * group), bf16),
            pltpu.VMEM((2, heads, 2 * BLK), f32),
            pltpu.VMEM((2, 2, BLK, BLK), f32),
            pltpu.VMEM((rows, width), bf16),
            pltpu.VMEM((experts, CAP, width), bf16),
            pltpu.VMEM((experts, CAP, width), bf16),
            pltpu.VMEM((rows, width), bf16),
            pltpu.VMEM((2, rows, 128), bf16),
            pltpu.VMEM(small, bf16),
            pltpu.VMEM((rows, 128), f32),
            pltpu.VMEM((8, rows), f32),
            pltpu.SemaphoreType.DMA((copies_count,)),
            pltpu.SemaphoreType.DMA((copies_count,)),
            pltpu.SemaphoreType.DMA((5,)),
            pltpu.SemaphoreType.DMA((6,)),
        ],
        compiler_params=pltpu.CompilerParams(
            collective_id=0, has_side_effects=True, vmem_limit_bytes=56 * 2**20
        ),
        cost_estimate=pl.CostEstimate(flops=60 * 10**9, bytes_accessed=30 * 2**20, transcendentals=0),
        name="run_front",
    )(tokens, w_qkv, w_out, w_in, cotangent, picks, ids, router, gain_first, gain_second, bias)


def expert_kernel(
    rows_ref, gates_ref, grads_ref, far_ref, inner_ref, inner_a_ref, inner_b_ref, inner_c_ref, outer_ref,
    returned_ref, copies_ref, ginner_ref, ginner_sent_ref, gouter_ref, inner_in_ref, outer_land_ref,
    x_ref, x_t_ref, dy_ref, gates_in_ref, win_ref, wout_ref, upper_ref, hid_ref, out_ref, back_ref,
    stage_in_ref, stage_out_ref, add_in_ref, outer_in_ref,
    row_send, row_recv, gate_send, gate_recv, out_send, out_recv, copy_send, copy_recv,
    grad_send, grad_recv, w_send, w_recv, part_send, part_recv, gout_send, gout_recv, local_sem, join_sem, load_sem,
):
    x, z, along_z, across, sibling = places()
    core = x % 2
    chip = x // 2
    me = chip * 4 + z
    _, _, slots, width = x_ref.shape
    chunk = 4 * slots
    tokens = 4 * chunk
    hidden = hid_ref.shape[1]
    half = stage_out_ref.shape[2]
    tiles = hidden // half
    shard = width // 8
    f32, bf16 = jnp.float32, jnp.bfloat16
    planes = (z,) + along_z
    chips = (chip,) + tuple(device // 2 for device in across)
    pair = (sibling, z)

    peers = [(m, k) for m in range(4) for k in range(4) if m or k]
    barrier = pltpu.get_barrier_semaphore()
    for m, k in peers:
        pl.semaphore_signal(
            barrier, inc=1, device_id=(2 * chips[k] + core, planes[m]), device_id_type=MESH_ID
        )
    pl.semaphore_signal(barrier, inc=1, device_id=pair, device_id_type=MESH_ID)
    pl.semaphore_wait(barrier, len(peers) + 1)

    def remote(source, target, sems, index, device):
        return pltpu.make_async_remote_copy(
            src_ref=source, dst_ref=target, send_sem=sems[0].at[index], recv_sem=sems[1].at[index],
            device_id=device, device_id_type=MESH_ID,
        )

    def to_plane(m, source_of, target_of, sems):
        return [
            remote(
                source_of(m, chips[k]), target_of(m), sems, 4 * m + k, (2 * chips[k] + core, planes[m])
            )
            for k in range(4)
            if m or k
        ]

    def lanes_of(owner):
        return pl.ds(pl.multiple_of(owner * shard, shard), shard)

    row_copies = [
        to_plane(
            m, lambda m, c: rows_ref.at[c * 4 + planes[m]], lambda m: x_ref.at[m, chip], (row_send, row_recv)
        )
        for m in range(4)
    ]
    gate_copies = [
        to_plane(
            m, lambda m, c: gates_ref.at[c * 4 + planes[m]], lambda m: gates_in_ref.at[m, chip],
            (gate_send, gate_recv),
        )
        for m in range(4)
    ]
    keeps = [
        pltpu.make_async_copy(inner_ref.at[chip], win_ref.at[chip, core], local_sem.at[0]),
        pltpu.make_async_copy(inner_a_ref, win_ref.at[chips[1], core], local_sem.at[1]),
        pltpu.make_async_copy(inner_b_ref, win_ref.at[chips[2], core], local_sem.at[2]),
        pltpu.make_async_copy(grads_ref.at[me], dy_ref.at[0, chip], local_sem.at[3]),
        pltpu.make_async_copy(inner_c_ref, win_ref.at[chips[3], core], local_sem.at[10]),
        pltpu.make_async_copy(rows_ref.at[me], x_ref.at[0, chip], local_sem.at[4]),
        pltpu.make_async_copy(gates_ref.at[me], gates_in_ref.at[0, chip], local_sem.at[5]),
        pltpu.make_async_copy(outer_ref.at[chip], wout_ref.at[:, lanes_of(x)], local_sem.at[6]),
    ]
    pair_inner = [
        remote(source, win_ref.at[chips[k], core], (w_send, w_recv), k, pair)
        for k, source in enumerate((inner_ref.at[chip], inner_a_ref, inner_b_ref, inner_c_ref))
    ]
    outer_copies = [
        remote(outer_ref.at[device // 2], outer_land_ref.at[x], (w_send, w_recv), 4 + j, (device, z))
        for j, device in enumerate(across)
    ]
    pair_outer = [remote(outer_ref.at[chip], outer_land_ref.at[x], (w_send, w_recv), 7, pair)] + [
        remote(outer_land_ref.at[device], outer_land_ref.at[device], (w_send, w_recv), 8 + j, pair)
        for j, device in enumerate(across)
    ]
    owners = across + (sibling,) + tuple(device + 1 - 2 * core for device in across)
    outer_loads = [
        pltpu.make_async_copy(outer_land_ref.at[owner], wout_ref.at[:, lanes_of(owner)], load_sem.at[n])
        for n, owner in enumerate(owners)
    ]
    for m in ROW_ORDER:
        for copy in row_copies[m]:
            copy.start()
    for copy in keeps + pair_inner + outer_copies + pair_outer[:1]:
        copy.start()
    for m in range(4):
        for copy in gate_copies[m]:
            copy.start()
    grad_copies = [
        to_plane(
            m, lambda m, c: grads_ref.at[c * 4 + planes[m]], lambda m: dy_ref.at[m, chip], (grad_send, grad_recv)
        )
        for m in range(2)
    ]
    far_grads = pltpu.make_async_copy(far_ref, dy_ref.at[pl.ds(2, 2)], local_sem.at[9])
    far_grads.start()
    for copy in keeps:
        copy.wait()
    for copy in pair_inner:
        copy.wait()

    def cols(tile, part):
        return pl.ds(pl.multiple_of(part * hidden + tile * half, half), half)

    def weight(tile, part):
        return win_ref[:, :, :, cols(tile, part)].reshape(width, half)

    def block(m):
        return pl.ds(m * chunk, chunk)

    def widen(m):
        for copy in row_copies[m]:
            copy.wait_recv()
        rows = x_ref.at[m]

        def step(tile, carry):
            values = rows[...].reshape(chunk, width)
            gate = dot_nn(values, weight(tile, 0))
            up = dot_nn(values, weight(tile, 1))
            square = gate * gate
            bent = jnp.tanh(gate * (0.7978845608028654 + 0.03567740813636141 * square))
            lifted = 0.5 + 0.5 * bent
            slope = lifted + (0.5 * gate) * (1.0 - bent * bent) * (
                0.7978845608028654 + 0.10703222440908423 * square
            )
            active = gate * lifted
            upper_ref[block(m), cols(tile, 0)] = (up * slope).astype(bf16)
            upper_ref[block(m), cols(tile, 1)] = active.astype(bf16)
            hid_ref[block(m), cols(tile, 0)] = (active * up).astype(bf16)
            return carry

        lax.fori_loop(0, tiles, step, 0)

    def narrow(m):
        def step(part, carry):
            here = pl.ds(pl.multiple_of(part * 256, 256), 256)
            values = dot_nn(hid_ref[block(m), :], wout_ref[:, here])
            out_ref[m, :, :, here] = values.astype(bf16).reshape(4, slots, 256)
            return carry

        lax.fori_loop(0, width // 256, step, 0)

    out_copies = [
        to_plane(m, lambda m, c: out_ref.at[m, c], lambda m: returned_ref.at[me], (out_send, out_recv))
        for m in range(4)
    ]
    own_out = pltpu.make_async_copy(out_ref.at[0, chip], returned_ref.at[me], local_sem.at[7])
    widen(0)
    widen(1)
    widen(2)
    for m in range(4):
        for copy in row_copies[m]:
            copy.wait_send()
    for m in range(2):
        for copy in grad_copies[m]:
            copy.start()
    for j, copy in enumerate(outer_copies):
        copy.wait_recv()
        pair_outer[1 + j].start()
        outer_loads[j].start()
    for j, copy in enumerate(pair_outer):
        copy.wait_recv()
        outer_loads[3 + j].start()
    for copy in outer_copies + pair_outer:
        copy.wait_send()
    for copy in outer_loads:
        copy.wait()
    for m in (2, 3, 1, 0):
        if m == 3:
            widen(m)
        narrow(m)
        for copy in out_copies[m]:
            copy.start()
    own_out.start()
    x_t_ref[...] = x_ref[...].reshape(tokens, width).T.reshape(x_t_ref.shape)

    far_grads.wait()
    for m in range(4):
        for copy in gate_copies[m] + (grad_copies[m] if m < 2 else []):
            copy.wait_recv()
        for j in range(4):
            gates = gates_in_ref[m, j].T[:slots, 0:1]
            dy_ref[m, j] = (dy_ref[m, j].astype(f32) * gates).astype(bf16)

    def outer_part(tile):
        slot = lax.rem(tile, STAGES)
        return remote(stage_out_ref.at[slot], outer_in_ref.at[tile], (part_send, part_recv), tiles + tile, pair)

    def weigh_outer(tile, carry):
        slot = lax.rem(tile, STAGES)

        @pl.when(tile >= STAGES)
        def _():
            outer_part(tile - STAGES).wait_send()

        grad_down = dot_nn(hid_ref[:, cols(tile, 0)].T, dy_ref[...].reshape(tokens, width))
        for j in range(4):
            low = grad_down[:, (2 * j) * shard:(2 * j + 1) * shard].astype(bf16)
            high = grad_down[:, (2 * j + 1) * shard:(2 * j + 2) * shard].astype(bf16)
            stage_out_ref[slot, j] = jnp.where(core == 0, high, low)
            hid_ref[pl.ds((j // 2) * half, half), pl.ds(pl.multiple_of(tile * half + (j % 2) * shard, shard), shard)] = (
                jnp.where(core == 0, low, high)
            )
        outer_part(tile).start()
        return carry

    lax.fori_loop(0, tiles, weigh_outer, 0)
    for tile in range(tiles - STAGES, tiles):
        outer_part(tile).wait_send()

    def join_outer(tile, carry):
        outer_part(tile).wait_recv()
        for j in range(4):
            own = hid_ref[pl.ds((j // 2) * half, half), pl.ds(pl.multiple_of(tile * half + (j % 2) * shard, shard), shard)]
            outer_in_ref[tile, j] = (own.astype(f32) + outer_in_ref[tile, j].astype(f32)).astype(bf16)
        return carry

    lax.fori_loop(0, tiles, join_outer, 0)
    own_gout = pltpu.make_async_copy(outer_in_ref.at[:, chip], gouter_ref.at[chip], local_sem.at[3])
    own_gout.start()
    gout_copies = [
        remote(outer_in_ref.at[:, device // 2], gouter_ref.at[chip], (gout_send, gout_recv), j, (device, z))
        for j, device in enumerate(across)
    ]
    for copy in gout_copies:
        copy.start()

    def back(first, count):
        here_rows = pl.ds(first * chunk, count * chunk)

        def step(tile, carry):
            down = wout_ref[pl.ds(pl.multiple_of(tile * half, half), half), :]
            grads = dy_ref[first:first + count].reshape(count * chunk, width)
            grad_hidden = dot_nt(grads, down)
            for part in range(2):
                slope = upper_ref[here_rows, cols(tile, part)].astype(f32)
                upper_ref[here_rows, cols(tile, part)] = (grad_hidden * slope).astype(bf16)
            return carry

        lax.fori_loop(0, tiles, step, 0)

        def gather(j, carry):
            here = pl.ds(pl.multiple_of(j * 256, 256), 256)
            weights = win_ref[j].reshape(2 * shard, 2 * hidden)
            values = dot_nt(upper_ref[here_rows, :], weights)
            back_ref[first:first + count, :, :, here] = values.astype(bf16).reshape(count, 4, slots, 256)
            return carry

        lax.fori_loop(0, 4, gather, 0)

    copy_copies = [
        to_plane(m, lambda m, c: back_ref.at[m, c], lambda m: copies_ref.at[me], (copy_send, copy_recv))
        for m in range(4)
    ]
    own_copy = pltpu.make_async_copy(back_ref.at[0, chip], copies_ref.at[me], local_sem.at[8])
    for first in range(4 - BACK_COUNT, -1, -BACK_COUNT):
        back(first, BACK_COUNT)
        for m in range(first, first + BACK_COUNT):
            for copy in copy_copies[m]:
                copy.start()
    own_copy.start()

    def inner_part(tile):
        slot = lax.rem(tile, STAGES)
        return remote(stage_in_ref.at[slot], inner_in_ref.at[tile], (part_send, part_recv), tile, pair)

    def inner_load(tile):
        slot = lax.rem(tile, 2)
        return pltpu.make_async_copy(inner_in_ref.at[tile], add_in_ref.at[slot], join_sem.at[slot])

    def inner_stores(tile):
        slot = lax.rem(tile, 2)
        return [
            pltpu.make_async_copy(
                add_in_ref.at[slot, part], ginner_ref.at[:, :, cols(tile, part)], join_sem.at[2 + 2 * slot + part]
            )
            for part in range(2)
        ]

    def join_begin(tile):
        inner_part(tile).wait_recv()

        @pl.when(tile >= 2)
        def _():
            for copy in inner_stores(tile - 2):
                copy.wait()

        inner_load(tile).start()

    def join_end(tile):
        slot = lax.rem(tile, 2)
        inner_load(tile).wait()
        for part in range(2):
            own = upper_ref[pl.ds(0, width // 2), cols(tile, part)].astype(f32)
            other = add_in_ref[slot, part].reshape(width // 2, half).astype(f32)
            add_in_ref[slot, part] = (own + other).astype(bf16).reshape(4, shard, half)
        for copy in inner_stores(tile):
            copy.start()

    def weigh_inner(tile, carry):
        slot = lax.rem(tile, STAGES)

        @pl.when(tile >= LAG)
        def _():
            join_begin(tile - LAG)

        @pl.when(tile >= STAGES)
        def _():
            inner_part(tile - STAGES).wait_send()

        for part in range(2):
            grad_upper = upper_ref[:, cols(tile, part)]
            other = x_t_ref[:, 1 - core].reshape(width // 2, tokens)
            stage_in_ref[slot, part] = dot_nn(other, grad_upper).astype(bf16).reshape(4, shard, half)
        inner_part(tile).start()
        for part in range(2):
            grad_upper = upper_ref[:, cols(tile, part)]
            own = x_t_ref[:, core].reshape(width // 2, tokens)
            upper_ref[pl.ds(0, width // 2), cols(tile, part)] = dot_nn(own, grad_upper).astype(bf16)

        @pl.when(tile >= LAG)
        def _():
            join_end(tile - LAG)

        return carry

    lax.fori_loop(0, tiles, weigh_inner, 0)
    for tile in range(tiles - LAG, tiles):
        join_begin(tile)
        join_end(tile)
    for tile in range(tiles - STAGES, tiles):
        inner_part(tile).wait_send()
    for tile in (tiles - 2, tiles - 1):
        for copy in inner_stores(tile):
            copy.wait()
    sent = ginner_sent_ref.shape[2]
    sent_copies = [
        remote(
            ginner_ref.at[device // 2, :, pl.ds(0, sent)], ginner_sent_ref.at[j], (gout_send, gout_recv), 3 + j,
            (device, z),
        )
        for j, device in enumerate(across)
    ]
    for copy in sent_copies:
        copy.start()
    own_out.wait()
    own_copy.wait()
    own_gout.wait()
    for m in range(4):
        for copy in (grad_copies[m] if m < 2 else []) + gate_copies[m]:
            copy.wait_send()
        for copy in out_copies[m] + copy_copies[m]:
            copy.wait()
    for copy in gout_copies + sent_copies:
        copy.wait()


ROW_ORDER = (0, 1, 2, 3)
BACK_COUNT = 2
STAGES = 4
LAG = 2


def run_experts(rows, gates, grads, far, inner, inner_others, outer):
    count, slots, width = rows.shape
    tokens = count * slots
    hidden = outer.shape[1]
    half = 256
    tiles = hidden // half
    shard = width // 8
    bf16 = jnp.bfloat16
    anywhere = pl.BlockSpec(memory_space=pl.ANY)
    sems = [pltpu.SemaphoreType.DMA((count,))] * 10 + [
        pltpu.SemaphoreType.DMA((12,)),
        pltpu.SemaphoreType.DMA((12,)),
        pltpu.SemaphoreType.DMA((2 * tiles,)),
        pltpu.SemaphoreType.DMA((2 * tiles,)),
        pltpu.SemaphoreType.DMA((6,)),
        pltpu.SemaphoreType.DMA((6,)),
        pltpu.SemaphoreType.DMA((11,)),
        pltpu.SemaphoreType.DMA((6,)),
        pltpu.SemaphoreType.DMA((7,)),
    ]
    outs = pl.pallas_call(
        expert_kernel,
        out_shape=(
            jax.ShapeDtypeStruct(rows.shape, bf16),
            jax.ShapeDtypeStruct(rows.shape, bf16),
            jax.ShapeDtypeStruct(inner.shape, bf16),
            jax.ShapeDtypeStruct((3, shard, inner.shape[2] // 4), bf16),
            jax.ShapeDtypeStruct((4, tiles, half, shard), bf16),
            jax.ShapeDtypeStruct((tiles, 2, 4, shard, half), bf16),
            jax.ShapeDtypeStruct((8, hidden, shard), bf16),
        ),
        in_specs=[anywhere] * 9,
        out_specs=(anywhere,) * 7,
        scratch_shapes=[
            pltpu.VMEM((4, 4, slots, width), bf16),
            pltpu.VMEM((4, 2, shard, tokens), bf16),
            pltpu.VMEM((4, 4, slots, width), bf16),
            pltpu.VMEM((4, 4, 8, 128), jnp.float32),
            pltpu.VMEM((4, 2, shard, 2 * hidden), bf16),
            pltpu.VMEM((hidden, width), bf16),
            pltpu.VMEM((tokens, 2 * hidden), bf16),
            pltpu.VMEM((tokens, hidden), bf16),
            pltpu.VMEM((4, 4, slots, width), bf16),
            pltpu.VMEM((4, 4, slots, width), bf16),
            pltpu.VMEM((STAGES, 2, 4, shard, half), bf16),
            pltpu.VMEM((STAGES, 4, half, shard), bf16),
            pltpu.VMEM((2, 2, 4, shard, half), bf16),
            pltpu.VMEM((tiles, 4, half, shard), bf16),
        ] + sems,
        compiler_params=pltpu.CompilerParams(
            collective_id=1, has_side_effects=True, vmem_limit_bytes=63 * 2**20
        ),
        cost_estimate=pl.CostEstimate(
            flops=180 * 10**9, bytes_accessed=60 * 2**20, transcendentals=tokens * hidden
        ),
        name="run_experts",
    )(rows, gates, grads, far, inner, *inner_others, outer)
    return outs[0], outs[1], outs[2], outs[3], outs[4].reshape(outer.shape)


def attend_back(pair, proj_ref, dout_ref, lse_ref, tile_ref, dproj_ref, span_ref, dk_ref, dv_ref, near_ref):
    length = proj_ref.shape[1]
    blocks = length // BLK
    depth = 64
    wide = 2 * depth
    here = slice(pair * wide, (pair + 1) * wide)
    lane = lax.broadcasted_iota(jnp.int32, (1, wide), 1)
    keys = proj_ref[1, :, here]
    values = proj_ref[2, :, here]
    keys_t = keys.T
    dk_ref[...] = jnp.zeros_like(dk_ref)
    dv_ref[...] = jnp.zeros_like(dv_ref)
    near_ref[...] = jnp.zeros_like(near_ref)
    far_sum = [jnp.zeros((1, BLK), jnp.float32) for h in range(2)]
    for block in range(blocks):
        rows = pl.ds(block * BLK, BLK)
        key_count = (block + 1) * BLK
        query = proj_ref[0, rows, here] * jnp.bfloat16(0.125)
        grad = dout_ref[rows, here]
        dq_parts = []
        dk_sum = None
        dv_sum = None
        for h in range(2):
            own = (lane // depth) == h
            query_h = jnp.where(own, query, jnp.bfloat16(0))
            grad_h = jnp.where(own, grad, jnp.bfloat16(0))
            scores = dot_nt(keys[:key_count], query_h)
            grad_p = dot_nt(values[:key_count], grad_h)
            lse = lse_ref[pair, h:h + 1, rows]
            far = tile_ref[2 * pair + h, 1, 0:1, BLK - 1:BLK].astype(jnp.float32)
            probs = []
            delta = None
            for kb in range(block + 1):
                d = block - kb
                part = scores[kb * BLK:(kb + 1) * BLK]
                bias = tile_ref[2 * pair + h, d].astype(jnp.float32) if d < 2 else far
                part = jnp.exp(part + (bias - lse))
                probs.append(part)
                term = jnp.sum(part * grad_p[kb * BLK:(kb + 1) * BLK], axis=0, keepdims=True)
                delta = term if delta is None else delta + term
            ds = []
            for kb in range(block + 1):
                d = block - kb
                part = probs[kb] * (grad_p[kb * BLK:(kb + 1) * BLK] - delta)
                if d < 2:
                    near_ref[h, d] += part
                else:
                    far_sum[h] = far_sum[h] + jnp.sum(part, axis=0, keepdims=True)
                ds.append(part.astype(jnp.bfloat16))
            ds = jnp.concatenate(ds, axis=0)
            weights = jnp.concatenate([p.astype(jnp.bfloat16) for p in probs], axis=0)
            dv_h = dot_nn(weights, grad_h)
            dk_h = dot_nn(ds, query_h)
            dv_sum = dv_h if dv_sum is None else dv_sum + dv_h
            dk_sum = dk_h if dk_sum is None else dk_sum + dk_h
            dq_parts.append(dot_nn(keys_t[h * depth:(h + 1) * depth, :key_count], ds))
        dk_ref[:key_count] += dk_sum
        dv_ref[:key_count] += dv_sum
        dproj_ref[0, rows, here] = (jnp.concatenate(dq_parts, axis=0).T * 0.125).astype(jnp.bfloat16)
    dproj_ref[1, :, here] = dk_ref[...].astype(jnp.bfloat16)
    dproj_ref[2, :, here] = dv_ref[...].astype(jnp.bfloat16)
    flip = (
        lax.broadcasted_iota(jnp.int32, (BLK, BLK), 0) + lax.broadcasted_iota(jnp.int32, (BLK, BLK), 1) == BLK - 1
    ).astype(jnp.bfloat16)
    lanes = lax.broadcasted_iota(jnp.int32, (1, 2 * BLK), 1)
    for h in range(2):
        for d in range(2):
            near = near_ref[h, d]
            near_high = near.astype(jnp.bfloat16)
            near_low = (near - near_high.astype(jnp.float32)).astype(jnp.bfloat16)
            flipped = dot_nn(flip, near_high) + dot_nn(flip, near_low)
            spread = jnp.concatenate([flipped, jnp.zeros((BLK, BLK), jnp.float32)], axis=1)
            turned = pltpu.roll(spread, 1, 1, stride=1, stride_axis=0)
            along = jnp.sum(turned, axis=0, keepdims=True)
            if d == 1:
                along = along + jnp.where(lanes == 2 * BLK - 1, jnp.sum(far_sum[h], axis=1, keepdims=True), 0.0)
            span_ref[2 * pair + h, d:d + 1, :] = along


def back_kernel(
    returned_hbm, copies_hbm, hidden_hbm, cot_hbm, cols_hbm, wo_hbm, att_hbm, router_ref, gains_ref, counts_ref,
    picks_ref, proj_hbm, lse_hbm, tile_hbm, wq_hbm, seq_hbm, ginner_hbm,
    mixed_ref, gtok_ref, gqkv_ref, gwo_ref, sums_ref, inner_in_hbm,
    returned_ref, copies_ref, hidden_ref, cot_ref, cols_ref, wo_ref, att_ref, gp_ref, dout_send_ref,
    proj_ref, lse_ref, tile_ref, wq_ref, seq_ref, dout_ref, dproj_ref, span_ref, dk_ref, dv_ref,
    near_ref, turned_ref, first_send_ref, first_in_ref,
    q_stage_ref, q_in_ref, q_own_ref, q_across_ref, q_z_ref, q_z_in_ref,
    gout_ref, o_in_ref, o_sum_ref, o_across_ref, o_z_ref, o_z_in_ref,
    s_own_ref, s_in_ref, s_sum_ref, s_across_ref, s_z_ref, s_z_in_ref,
    send_sem, recv_sem, load_sem,
):
    x, z, along_z, across, sibling = places()
    core = x % 2
    chip = x // 2
    half = z % 2
    f32, bf16 = jnp.float32, jnp.bfloat16
    rows, width = gtok_ref.shape
    shard = width // 8
    step = rows // 2
    group = gqkv_ref.shape[2]
    experts = returned_ref.shape[0] // CAP
    pair = (sibling, z)
    chips = [(device, z) for device in across]
    lines = [(x, other) for other in along_z]
    barrier = pltpu.get_barrier_semaphore()
    for peer in chips + lines + [pair]:
        pl.semaphore_signal(barrier, inc=1, device_id=peer, device_id_type=MESH_ID)
    loads = {}
    for name, source, target in (
        ("cols", cols_hbm, cols_ref), ("returned", returned_hbm, returned_ref), ("hidden", hidden_hbm, hidden_ref),
        ("cot", cot_hbm, cot_ref), ("copies", copies_hbm, copies_ref), ("wo", wo_hbm, wo_ref),
        ("att", att_hbm, att_ref), ("seq", seq_hbm, seq_ref), ("proj", proj_hbm, proj_ref),
        ("lse", lse_hbm, lse_ref), ("tile", tile_hbm, tile_ref), ("wq", wq_hbm, wq_ref),
    ):
        loads[name] = pltpu.make_async_copy(source, target, load_sem.at[len(loads)])
        loads[name].start()
    pl.semaphore_wait(barrier, 7)
    started = []

    def send(source, target, device):
        index = len(started)
        copy = pltpu.make_async_remote_copy(
            src_ref=source, dst_ref=target, send_sem=send_sem.at[index], recv_sem=recv_sem.at[index],
            device_id=device, device_id_type=MESH_ID,
        )
        copy.start()
        started.append(copy)
        return copy

    inner_rest = inner_in_hbm.shape[2]
    inner_copies = [
        send(
            ginner_hbm.at[device // 2, :, pl.ds(ginner_hbm.shape[2] - inner_rest, inner_rest)], inner_in_hbm.at[j],
            (device, z),
        )
        for j, device in enumerate(across)
    ]

    gain_second = gains_ref[1:2, :]
    router_t = router_ref[...]
    step = rows // 2
    counts = counts_ref[...]
    tokens = 32 * rows
    pairs_in_all = 2 * tokens
    push = loss_weight * experts * (counts / pairs_in_all) / tokens
    slot_lane = lax.broadcasted_iota(jnp.int32, (1, returned_ref.shape[0]), 1).astype(f32)
    expert_lane = lax.broadcasted_iota(jnp.int32, (1, shard), 1).astype(f32)
    own_width = dout_ref.shape[1]
    dout_copies = []
    gain2_sum = jnp.zeros((1, width), f32)
    route_sum = jnp.zeros((1, shard), f32)
    grad_router = jnp.zeros((shard, width), f32)
    for name in ("cols", "returned", "hidden", "cot"):
        loads[name].wait()
    for i in range(2):
        here = slice(i * step, (i + 1) * step)
        cols = cols_ref[here, :]
        route = jnp.where(expert_lane < experts, cols, 0.0)
        marks = [(slot_lane == cols[:, experts + 2 + c:experts + 3 + c]).astype(bf16) for c in range(2)]
        picked = [dot_nn(mark, returned_ref[...]) for mark in marks]
        hidden = hidden_ref[here, :]
        grad_mixed = cot_ref[here, :].astype(f32)
        mixed_ref[here, :] = (
            hidden + picked[0] * cols[:, experts:experts + 1] + picked[1] * cols[:, experts + 1:experts + 2]
        ).astype(bf16)
        grad_route = push
        for c in range(2):
            hit = expert_lane == cols[:, experts + 4 + c:experts + 5 + c]
            grad_route = grad_route + jnp.where(hit, jnp.sum(grad_mixed * picked[c], axis=1, keepdims=True), 0.0)
        grad_logits = route * (grad_route - jnp.sum(route * grad_route, axis=1, keepdims=True))
        route_sum = route_sum + jnp.sum(route, axis=0, keepdims=True)
        if i == 0:
            loads["copies"].wait()
        grad_second = dot_nn(marks[0] + marks[1], copies_ref[...]) + dot_nn(grad_logits.astype(bf16), router_t)
        normed, scale = normalize(hidden)
        second_norm = (normed * gain_second).astype(bf16)
        grad_router = grad_router + dot_nn(grad_logits.T.astype(bf16), second_norm)
        gain2_sum = gain2_sum + jnp.sum(grad_second * normed, axis=0, keepdims=True)
        grad_normed = grad_second * gain_second
        grad_hidden = grad_mixed + scale * (
            grad_normed - normed * jnp.mean(grad_normed * normed, axis=-1, keepdims=True)
        )
        hidden_ref[here, :] = grad_hidden
        grad_part = grad_hidden.astype(bf16)
        gp_ref[here, :] = grad_part
        if i == 0:
            loads["wo"].wait()
        dout_send_ref[here, :] = dot_nt(grad_part, wo_ref[own_width:, :]).astype(bf16)
        for slot in (1, 0) if i == 0 else (1,):
            lanes = pl.ds(slot * group, group)
            dout_copies.append(
                send(dout_send_ref.at[here, lanes], dout_ref.at[pl.ds(half * rows + i * step, step), lanes], lines[0])
            )


    own_rows = pl.ds(pl.multiple_of(half * rows, rows), rows)
    dout_ref[own_rows, :] = dot_nt(gp_ref[...], wo_ref[:own_width, :]).astype(bf16)

    loads["att"].wait()
    grad_out = dot_nn(att_ref[...].T, gp_ref[...]).astype(bf16)
    for owner in range(8):
        gout_ref[owner // 2, owner % 2] = grad_out[:, owner * shard:(owner + 1) * shard]
    o_pair = [send(gout_ref.at[j, 1 - core], o_in_ref.at[j], pair) for j in range(4)]

    gain_first = gains_ref[0:1, :]
    loads["seq"].wait()
    for i in range(4):
        normed, _ = normalize(seq_ref[i // 2, (i % 2) * step:(i % 2 + 1) * step, :].astype(f32))
        turned_ref[:, :, :, i * step:(i + 1) * step] = (
            (normed * gain_first).astype(bf16).T.reshape(4, 2, shard, step)
        )

    dout_copies.append(
        send(
            dout_send_ref.at[pl.ds(step, step), pl.ds(0, group)],
            dout_ref.at[pl.ds(half * rows + step, step), pl.ds(0, group)],
            lines[0],
        )
    )
    for name in ("proj", "lse", "tile"):
        loads[name].wait()
    for n in (0, 2):
        dout_copies[n].wait_recv()

    def attend(number):
        attend_back(
            number, proj_ref, dout_ref, lse_ref, tile_ref, dproj_ref, span_ref, dk_ref, dv_ref, near_ref
        )

    def weigh_other(slot):
        here = pl.ds(slot * group, group)
        other = turned_ref[:, 1 - core].reshape(width // 2, 2 * rows)
        for c in range(3):
            q_stage_ref[slot, c] = dot_nn(other, dproj_ref[c, :, here]).astype(bf16).reshape(4, shard, group)
        return send(q_stage_ref.at[slot], q_in_ref.at[slot], pair)

    def weigh_own(slot):
        here = pl.ds(slot * group, group)
        own = turned_ref[:, core].reshape(width // 2, 2 * rows)
        for c in range(3):
            q_own_ref[slot, c] = dot_nn(own, dproj_ref[c, :, here]).astype(bf16).reshape(4, shard, group)

    def to_chips(slot, copy):
        copy.wait_recv()
        q_own_ref[slot] = (q_own_ref[slot].astype(f32) + q_in_ref[slot].astype(f32)).astype(bf16)
        return [
            send(q_own_ref.at[slot, :, device // 2], q_across_ref.at[slot, j], chips[j])
            for j, device in enumerate(across)
        ]

    def chip_total(slot, copies):
        for copy in copies:
            copy.wait_recv()
        total = q_own_ref[slot, :, chip].astype(f32)
        for j in range(3):
            total = total + q_across_ref[slot, j].astype(f32)
        return total

    attend(2)
    attend(3)
    q_pair_1 = weigh_other(1)
    for copy in o_pair:
        copy.wait_recv()
    for j in range(4):
        o_sum_ref[j] = (gout_ref[j, core].astype(f32) + o_in_ref[j].astype(f32)).astype(bf16)
    o_chips = [send(o_sum_ref.at[device // 2], o_across_ref.at[j], chips[j]) for j, device in enumerate(across)]
    weigh_own(1)
    q_chips_1 = to_chips(1, q_pair_1)
    for n in (1, 3):
        dout_copies[n].wait_recv()
    attend(0)
    attend(1)

    loads["wq"].wait()
    gain1_sum = jnp.zeros((1, width), f32)
    first_copies = []
    for turn, side in enumerate((1 - half, half)):
        for i in range(2):
            here = pl.ds(pl.multiple_of(side * rows + i * step, step), step)
            part = sum(
                dot_nt(dproj_ref[c, here, slot * group:(slot + 1) * group], wq_ref[slot, :, c].reshape(width, group))
                for slot in range(2)
                for c in range(3)
            )
            normed, _ = normalize(seq_ref[side, i * step:(i + 1) * step, :].astype(f32))
            gain1_sum = gain1_sum + jnp.sum(part * normed, axis=0, keepdims=True)
            if turn:
                gtok_ref[i * step:(i + 1) * step, :] = part
            else:
                first_send_ref[i * step:(i + 1) * step, :] = part.astype(bf16)
                block = pl.ds(i * step, step)
                first_copies.append(send(first_send_ref.at[block], first_in_ref.at[block], lines[0]))
        if not turn:
            q_pair_0 = weigh_other(0)

    table = None
    for d in range(2):
        along = span_ref[:, d, :]
        high = along.astype(bf16)
        low = (along - high.astype(f32)).astype(bf16)
        part = dot_nn(high, picks_ref[d]) + dot_nn(low, picks_ref[d])
        table = part if table is None else table + part
    heads = table.shape[0] // 2
    table = table.T[:32, :]
    blank = jnp.zeros((table.shape[0], shard - heads), f32)
    placed = pltpu.roll(jnp.concatenate([table[:, :heads], blank], axis=1), heads * z, 1) + pltpu.roll(
        jnp.concatenate([table[:, heads:], blank], axis=1), heads * ((z + 2) % 4), 1
    )
    for owner in range(8):
        here = slice(owner * shard, (owner + 1) * shard)
        target = s_own_ref.at[owner // 2, owner % 2]
        target[0:1, :] = gain1_sum[:, here]
        target[1:2, :] = gain2_sum[:, here]
        target[2:2 + experts, :] = grad_router[:experts, here]
        target[22:23, :] = route_sum
        target[23:24, :] = jnp.zeros((1, shard), f32)
        target[18:22, :] = placed[4 * owner:4 * owner + 4, :]
    s_pair = send(s_own_ref.at[:, 1 - core], s_in_ref, pair)
    weigh_own(0)

    q_chips_0 = to_chips(0, q_pair_0)
    s_pair.wait_recv()
    s_sum_ref[...] = s_own_ref[:, core] + s_in_ref[...]
    s_chips = [send(s_sum_ref.at[device // 2], s_across_ref.at[j], chips[j]) for j, device in enumerate(across)]
    q_z_ref[...] = chip_total(1, q_chips_1).astype(bf16)
    q_line = send(q_z_ref, q_z_in_ref, lines[1])
    for copy in o_chips:
        copy.wait_recv()
    o_total = o_sum_ref[chip].astype(f32)
    for j in range(3):
        o_total = o_total + o_across_ref[j].astype(f32)
    rows_out = gwo_ref.shape[0]
    gwo_ref[...] = o_total[:rows_out]
    o_z_ref[...] = o_total[rows_out:].astype(bf16).reshape(o_z_ref.shape)
    out_slots = (2, 1, 3)
    o_lines = [send(o_z_ref.at[out_slots[j] - 1], o_z_in_ref.at[j], lines[j]) for j in range(3)]
    for copy in s_chips:
        copy.wait_recv()
    s_z_ref[...] = s_sum_ref[chip] + s_across_ref[0] + s_across_ref[1] + s_across_ref[2]
    s_lines = [send(s_z_ref, s_z_in_ref.at[j], lines[j]) for j in range(3)]
    gqkv_ref[...] = chip_total(0, q_chips_0)

    for i in range(2):
        first_copies[i].wait_recv()
        here = slice(i * step, (i + 1) * step)
        grad = (gtok_ref[here, :] + first_in_ref[here, :].astype(f32)) * gain_first
        normed, scale = normalize(seq_ref[half, here, :].astype(f32))
        gtok_ref[here, :] = hidden_ref[here, :] + scale * (
            grad - normed * jnp.mean(grad * normed, axis=-1, keepdims=True)
        )
    q_line.wait_recv()
    gqkv_ref[...] += q_z_in_ref[...].astype(f32)
    for copy in s_lines + o_lines:
        copy.wait_recv()
    gwo_ref[...] += o_z_in_ref[0].astype(f32) + o_z_in_ref[1].astype(f32) + o_z_in_ref[2].astype(f32)
    sums = s_z_ref[...] + s_z_in_ref[0] + s_z_in_ref[1] + s_z_in_ref[2]
    sums_ref[...] = sums
    for copy in inner_copies:
        copy.wait_recv()
    for copy in started:
        copy.wait_send()


def run_back(
    returned, copies, hidden, cot, cols, wo, att, router_t, gains, counts, picks, proj, lse, tiles, wq, seq, ginner, sent
):
    rows, width = hidden.shape
    length = 2 * rows
    shard = width // 8
    group = wq.shape[4]
    rows_out = width // 4
    heads = tiles.shape[0]
    f32, bf16 = jnp.float32, jnp.bfloat16
    anywhere = pl.BlockSpec(memory_space=pl.ANY)
    inside = pl.BlockSpec(memory_space=pltpu.VMEM)
    copies_count = 3 + 4 + 4 + 2 + 3 + 3 + 3 + 2 + 1 + 3 + 1 + 3 + 3
    return pl.pallas_call(
        back_kernel,
        out_shape=(
            jax.ShapeDtypeStruct((rows, width), bf16),
            jax.ShapeDtypeStruct((rows, width), f32),
            jax.ShapeDtypeStruct((3, shard, group), f32),
            jax.ShapeDtypeStruct((rows_out, shard), f32),
            jax.ShapeDtypeStruct((24, shard), f32),
            jax.ShapeDtypeStruct((3, shard, ginner.shape[2] - sent), bf16),
        ),
        in_specs=[anywhere] * 7 + [inside] * 4 + [anywhere] * 6,
        out_specs=(inside,) * 5 + (anywhere,),
        scratch_shapes=[
            pltpu.VMEM(returned.shape, bf16),
            pltpu.VMEM(copies.shape, bf16),
            pltpu.VMEM(hidden.shape, f32),
            pltpu.VMEM(cot.shape, bf16),
            pltpu.VMEM(cols.shape, f32),
            pltpu.VMEM(wo.shape, bf16),
            pltpu.VMEM(att.shape, bf16),
            pltpu.VMEM((rows, width), bf16),
            pltpu.VMEM((rows, 2 * group), bf16),
            pltpu.VMEM(proj.shape, bf16),
            pltpu.VMEM(lse.shape, f32),
            pltpu.VMEM(tiles.shape, bf16),
            pltpu.VMEM(wq.shape, bf16),
            pltpu.VMEM(seq.shape, bf16),
            pltpu.VMEM((length, 2 * group), bf16),
            pltpu.VMEM(proj.shape, bf16),
            pltpu.VMEM((heads, 2, 2 * BLK), f32),
            pltpu.VMEM((length, 128), f32),
            pltpu.VMEM((length, 128), f32),
            pltpu.VMEM((2, 2, BLK, BLK), f32),
            pltpu.VMEM((4, 2, shard, length), bf16),
            pltpu.VMEM((rows, width), bf16),
            pltpu.VMEM((rows, width), bf16),
            pltpu.VMEM((2, 3, 4, shard, group), bf16),
            pltpu.VMEM((2, 3, 4, shard, group), bf16),
            pltpu.VMEM((2, 3, 4, shard, group), bf16),
            pltpu.VMEM((2, 3, 3, shard, group), bf16),
            pltpu.VMEM((3, shard, group), bf16),
            pltpu.VMEM((3, shard, group), bf16),
            pltpu.VMEM((4, 2, width, shard), bf16),
            pltpu.VMEM((4, width, shard), bf16),
            pltpu.VMEM((4, width, shard), bf16),
            pltpu.VMEM((3, width, shard), bf16),
            pltpu.VMEM((3, rows_out, shard), bf16),
            pltpu.VMEM((3, rows_out, shard), bf16),
            pltpu.VMEM((4, 2, 24, shard), f32),
            pltpu.VMEM((4, 24, shard), f32),
            pltpu.VMEM((4, 24, shard), f32),
            pltpu.VMEM((3, 24, shard), f32),
            pltpu.VMEM((24, shard), f32),
            pltpu.VMEM((3, 24, shard), f32),
            pltpu.SemaphoreType.DMA((copies_count,)),
            pltpu.SemaphoreType.DMA((copies_count,)),
            pltpu.SemaphoreType.DMA((12,)),
        ],
        compiler_params=pltpu.CompilerParams(
            collective_id=2, has_side_effects=True, vmem_limit_bytes=62 * 2**20
        ),
        cost_estimate=pl.CostEstimate(flops=60 * 10**9, bytes_accessed=60 * 2**20, transcendentals=0),
        name="run_back",
    )(
        returned, copies, hidden, cot, cols, wo, att, router_t, gains, counts, picks, proj, lse, tiles, wq, seq, ginner
    )


def final_kernel(
    ginner_hbm, sent_hbm, rest_hbm, gouter_hbm, mixed_hbm, gtok_hbm, gqkv_hbm, gwo_hbm, sums_ref, counts_ref,
    inner_hbm, outer_hbm, mixed_out, tok_hbm, qkv_hbm, wo_hbm, gain1_ref, gain2_ref, grouter_ref, gbias_ref, load_ref,
    loss_ref,
    in_ref, out_ref, slim_in_ref, slim_out_ref, mixed_ref, tok_ref, qkv_ref, wo_ref, in_sem, out_sem, copy_sem,
):
    x, z, _, across, _ = places()
    chip = x // 2
    f32 = jnp.float32
    passed = (
        (mixed_hbm, mixed_ref, mixed_out), (gtok_hbm, tok_ref, tok_hbm), (gqkv_hbm, qkv_ref, qkv_hbm),
        (gwo_hbm, wo_ref, wo_hbm),
    )
    copies_in = [pltpu.make_async_copy(a, b, copy_sem.at[n]) for n, (a, b, _) in enumerate(passed)]
    copies = [pltpu.make_async_copy(b, c, copy_sem.at[4 + n]) for n, (_, b, c) in enumerate(passed)]
    depth, _, wide = in_ref.shape
    slim = slim_in_ref.shape[1]
    sent = sent_hbm.shape[2]
    jobs = []
    for part in range(ginner_hbm.shape[2] // wide):
        here = pl.ds(part * wide, wide)
        jobs.append((ginner_hbm.at[chip, :, here], inner_hbm.at[chip, :, here], in_ref, out_ref))
        for j, device in enumerate(across):
            source = sent_hbm.at[j, :, here] if part * wide < sent else rest_hbm.at[j, :, pl.ds(part * wide - sent, wide)]
            jobs.append((source, inner_hbm.at[device // 2, :, here], in_ref, out_ref))
    for n in range(gouter_hbm.shape[0]):
        for i in range(gouter_hbm.shape[1] // slim):
            here = pl.ds(i * slim, slim)
            jobs.append((gouter_hbm.at[n, here], outer_hbm.at[n, here], slim_in_ref, slim_out_ref))
    loads = [
        pltpu.make_async_copy(source, held.at[i % depth], in_sem.at[i % depth])
        for i, (source, _, held, _) in enumerate(jobs)
    ]
    stores = [
        pltpu.make_async_copy(held.at[i % depth], target, out_sem.at[i % depth])
        for i, (_, target, _, held) in enumerate(jobs)
    ]
    for i in range(depth - 1):
        loads[i].start()
    for copy in copies_in:
        copy.start()
    experts = load_ref.shape[1]
    heads = gbias_ref.shape[1]
    shard = sums_ref.shape[1]
    sums = sums_ref[...]
    gain1_ref[...] = sums[0:1, :]
    gain2_ref[...] = sums[1:2, :]
    grouter_ref[...] = sums[2:2 + experts, :]
    gbias_ref[...] = pltpu.roll(sums[16:24, :], (shard - heads * z) % shard, 1)[2:6, :heads]
    tokens = 32 * gtok_hbm.shape[0]
    counts = counts_ref[:, :experts]
    pairs_in_all = 2 * tokens
    prob_sums = sums[22:23, :experts]
    load_ref[...] = jnp.concatenate([experts * counts / pairs_in_all, experts * prob_sums / tokens], axis=0)
    loss_ref[...] = experts * jnp.sum(counts / pairs_in_all * (prob_sums / tokens), axis=1, keepdims=True)
    for copy_in, copy in zip(copies_in, copies):
        copy_in.wait()
        copy.start()
    for i, (_, _, held_in, held_out) in enumerate(jobs):
        if i + depth - 1 < len(jobs):
            loads[i + depth - 1].start()
        loads[i].wait()
        if i >= depth:
            stores[i - depth].wait()
        held_out[i % depth] = held_in[i % depth].astype(f32)
        stores[i].start()
    for store in stores[-depth:]:
        store.wait()
    for copy in copies:
        copy.wait()


def finish(ginner, sent, rest, gouter, mixed, gtok, gqkv, gwo, sums, counts, experts, heads):
    f32, bf16 = jnp.float32, jnp.bfloat16
    local, shard, inner_width = ginner.shape
    wide = inner_width // 4
    slim = gouter.shape[1] // 2
    anywhere = pl.BlockSpec(memory_space=pl.ANY)
    inside = pl.BlockSpec(memory_space=pltpu.VMEM)
    return pl.pallas_call(
        final_kernel,
        out_shape=(
            jax.ShapeDtypeStruct(ginner.shape, f32),
            jax.ShapeDtypeStruct(gouter.shape, f32),
            jax.ShapeDtypeStruct(mixed.shape, bf16),
            jax.ShapeDtypeStruct(gtok.shape, f32),
            jax.ShapeDtypeStruct(gqkv.shape, f32),
            jax.ShapeDtypeStruct(gwo.shape, f32),
            jax.ShapeDtypeStruct((1, shard), f32),
            jax.ShapeDtypeStruct((1, shard), f32),
            jax.ShapeDtypeStruct((experts, shard), f32),
            jax.ShapeDtypeStruct((4, heads), f32),
            jax.ShapeDtypeStruct((2, experts), f32),
            jax.ShapeDtypeStruct((1, 1), f32),
        ),
        in_specs=[anywhere] * 8 + [inside] * 2,
        out_specs=(anywhere,) * 6 + (inside,) * 6,
        scratch_shapes=[
            pltpu.VMEM((8, shard, wide), bf16),
            pltpu.VMEM((8, shard, wide), f32),
            pltpu.VMEM((8, slim, shard), bf16),
            pltpu.VMEM((8, slim, shard), f32),
            pltpu.VMEM(mixed.shape, bf16),
            pltpu.VMEM(gtok.shape, f32),
            pltpu.VMEM(gqkv.shape, f32),
            pltpu.VMEM(gwo.shape, f32),
            pltpu.SemaphoreType.DMA((8,)),
            pltpu.SemaphoreType.DMA((8,)),
            pltpu.SemaphoreType.DMA((8,)),
        ],
        compiler_params=pltpu.CompilerParams(vmem_limit_bytes=62 * 2**20),
        cost_estimate=pl.CostEstimate(flops=0, bytes_accessed=32 * 2**20, transcendentals=0),
        name="finish",
    )(ginner, sent, rest, gouter, mixed, gtok, gqkv, gwo, sums, counts)


def fast_device(
    tokens, expert_ids, gain_attn, w_qkv, w_out, rel_bias, gain_ffn, router, w_in, w_down, cotangent
):
    model_width = tokens.shape[1]
    expert_count = router.shape[1]
    group_heads = rel_bias.shape[1]

    buckets = span_buckets()[:, :, None] == jnp.arange(128, dtype=jnp.int32)
    picks = buckets.astype(jnp.bfloat16)
    (
        seq_tokens, qkv_weight, out_weight, router_t, gains, count_row, projected, attended, log_totals, bias_tiles, hidden_state, columns,
        gate_rows, send_rows, grad_rows, inner_a, inner_b, inner_c,
        grads_far,
    ) = run_front(
        tokens, w_qkv, w_out, w_in, cotangent, picks, expert_ids.T, router.T, gain_attn[None], gain_ffn[None], rel_bias
    )

    returned, grad_copies, grad_inner, grad_sent, grad_outer = run_experts(
        send_rows,
        gate_rows,
        grad_rows,
        grads_far,
        w_in,
        (inner_a, inner_b, inner_c),
        w_down,
    )
    mixed, grad_tokens, grad_qkv, grad_out_weight, sums, grad_rest = run_back(
        returned.reshape(-1, model_width),
        grad_copies.reshape(-1, model_width),
        hidden_state,
        cotangent,
        columns,
        out_weight,
        attended,
        router_t,
        gains,
        count_row,
        picks,
        projected,
        log_totals,
        bias_tiles,
        qkv_weight,
        seq_tokens,
        grad_inner,
        grad_sent.shape[2],
    )
    (
        grad_inner, grad_outer, mixed, grad_tokens, grad_qkv, grad_out_weight, gain_one, gain_two, grad_router,
        grad_rel_bias, router_load, loss,
    ) = finish(
        grad_inner,
        grad_sent,
        grad_rest,
        grad_outer,
        mixed,
        grad_tokens,
        grad_qkv,
        grad_out_weight,
        sums,
        count_row,
        expert_count,
        group_heads,
    )
    return (
        mixed,
        loss[0, 0],
        router_load,
        grad_tokens,
        gain_one[0],
        grad_qkv,
        grad_out_weight,
        grad_rel_bias,
        gain_two[0],
        grad_router.T,
        grad_inner,
        grad_outer,
    )


def solution(mesh):
    in_specs = (
        P(("gx", "gy"), None),
        P(("gx", "gy"), None),
        P("gx"),
        P(None, "gx", "gy"),
        P("gy", "gx"),
        P("gx", "gy"),
        P("gx"),
        P("gx", None),
        P("gy", "gx", None),
        P("gy", None, "gx"),
        P(("gx", "gy"), None),
    )
    out_specs = (
        P(("gx", "gy"), None),
        P(),
        P(),
        P(("gx", "gy"), None),
        P("gx"),
        P(None, "gx", "gy"),
        P("gy", "gx"),
        P("gx", "gy"),
        P("gx"),
        P("gx", None),
        P("gy", "gx", None),
        P("gy", None, "gx"),
    )
    return jax.shard_map(
        fast_device if fits_fast(mesh) else general_device, mesh=mesh, in_specs=in_specs, out_specs=out_specs, check_vma=False
    )
```

```python
import functools
import math

import jax
import jax.numpy as jnp
from jax import lax
from jax.experimental import pallas as pl
from jax.experimental.pallas import tpu as pltpu
from jax.sharding import PartitionSpec as P

LEN = 1024
BLK = 256
CAP = 80


bucket_edges = (12, 16, 23, 32, 46, 64, 91)
epsilon = 1e-06
loss_weight = 0.01
masked_score = -1e30


def bucket_of(offset):
    magnitude = jnp.abs(offset)
    far_bucket = 8 + sum(
        ((magnitude >= edge_value).astype(jnp.int32) for edge_value in bucket_edges)
    )
    return jnp.where(magnitude < 8, magnitude, far_bucket) + 16 * (offset > 0).astype(jnp.int32)


def normalize(values):
    row_scale = lax.rsqrt(jnp.mean(values * values, axis=-1, keepdims=True) + epsilon)
    return (values * row_scale, row_scale)


def norm_back(grad_out, normed, row_scale, gain_vector):
    grad_normed = grad_out * gain_vector
    grad_gain = jnp.sum(grad_out * normed, axis=0)
    grad_input = row_scale * (
        grad_normed - normed * jnp.mean(grad_normed * normed, axis=-1, keepdims=True)
    )
    return (grad_input, grad_gain)


def spread_offsets(along_offsets, row_count):
    head_count, span_width = along_offsets.shape
    key_count = span_width - row_count + 1
    tiled_rows = jnp.broadcast_to(
        along_offsets[:, None, :], (head_count, row_count, span_width)
    ).reshape(head_count, row_count * span_width)
    padded = jnp.pad(tiled_rows, ((0, 0), (0, row_count)))
    shaped = padded.reshape(head_count, row_count, span_width + 1)[:, :, :key_count]
    return shaped[:, :, ::-1]


def gather_offsets(score_grid, row_count):
    head_count = score_grid.shape[0]
    key_count = score_grid.shape[2]
    span_width = key_count + row_count - 1
    padded = jnp.pad(score_grid[:, :, ::-1], ((0, 0), (0, 0), (0, row_count)))
    flat_rows = padded.reshape(head_count, row_count * (key_count + row_count))[
        :, : row_count * span_width
    ]
    return jnp.sum(flat_rows.reshape(head_count, row_count, span_width), axis=1)


def offset_table(q_start, row_count, key_count, bucket_count):
    spot_index = jnp.arange(key_count + row_count - 1, dtype=jnp.int32)
    offsets = key_count - 1 - spot_index - q_start
    return (
        bucket_of(offsets)[:, None] == jnp.arange(bucket_count, dtype=jnp.int32)[None, :]
    ).astype(jnp.float32)


def block_scores(query_rows, key_rows, table_float, q_start):
    row_count = query_rows.shape[0]
    depth = query_rows.shape[2]
    key_count = key_rows.shape[0]
    picks_table = offset_table(q_start, row_count, key_count, table_float.shape[0])
    along_offsets = jnp.dot(picks_table, table_float, precision=lax.Precision.HIGHEST).T
    bias_grid = spread_offsets(along_offsets, row_count)
    scores = (
        jnp.einsum("qhd,khd->hqk", query_rows, key_rows, preferred_element_type=jnp.float32)
        / math.sqrt(depth)
        + bias_grid
    )
    query_pos = q_start + jnp.arange(row_count, dtype=jnp.int32)
    key_pos = jnp.arange(key_count, dtype=jnp.int32)
    allowed = key_pos[None, :] // BLK <= query_pos[:, None] // BLK
    return (jnp.where(allowed[None], scores, masked_score), picks_table)


def general_device(
    tokens, expert_ids, gain_attn, w_qkv, w_out, rel_bias, gain_ffn, router, w_in, w_down, cotangent
):
    shard_list = (gain_attn, w_qkv, w_out, rel_bias, gain_ffn, router, w_in, w_down)
    (
        gain_first,
        qkv_weight,
        out_weight,
        bias_table,
        gain_second,
        route_weight,
        inner_weight,
        outer_weight,
    ) = (
        lax.all_gather(shard_list[0], "gx", axis=0, tiled=True),
        lax.all_gather(shard_list[1], "gx", axis=1, tiled=True),
        lax.all_gather(shard_list[2], "gx", axis=1, tiled=True),
        lax.all_gather(shard_list[3], "gx", axis=0, tiled=True),
        lax.all_gather(shard_list[4], "gx", axis=0, tiled=True),
        lax.all_gather(shard_list[5], "gx", axis=0, tiled=True),
        lax.all_gather(shard_list[6], "gx", axis=1, tiled=True),
        lax.all_gather(shard_list[7], "gx", axis=2, tiled=True),
    )
    tok_dev = tokens.shape[0]
    count_x = lax.axis_size("gx")
    count_y = lax.axis_size("gy")
    total_tokens = tok_dev * count_x * count_y
    model_width = tokens.shape[1]
    expert_count = route_weight.shape[1]
    top_count = expert_ids.shape[1]
    local_experts = inner_weight.shape[0]
    head_count = bias_table.shape[1]
    head_width = qkv_weight.shape[2]
    depth = head_width // head_count
    q_rows = min(512, LEN)
    per_seq = LEN // q_rows
    inputs_float = tokens.astype(jnp.float32)
    normed_one, scale_one = normalize(inputs_float)
    first_norm = (normed_one * gain_first.astype(jnp.float32)).astype(jnp.bfloat16)
    group_rows = lax.all_gather(first_norm, "gy", axis=0, tiled=True)
    tok_group = group_rows.shape[0]
    seq_count = tok_group // LEN
    projected = jnp.einsum(
        "td,cdf->tcf", group_rows, qkv_weight, preferred_element_type=jnp.float32
    ).astype(jnp.bfloat16)
    projected = projected.reshape(tok_group, 3, head_count, depth)
    table_float = bias_table.astype(jnp.float32)

    def forward_block(item_index):
        seq_index = item_index // per_seq
        q_start = item_index % per_seq * q_rows
        query_rows = lax.dynamic_slice_in_dim(projected, seq_index * LEN + q_start, q_rows, 0)[:, 0]
        seq_rows = lax.dynamic_slice_in_dim(projected, seq_index * LEN, LEN, 0)
        scores, unused_picks = block_scores(query_rows, seq_rows[:, 1], table_float, q_start)
        row_max = jnp.max(scores, axis=-1, keepdims=True)
        expo_scores = jnp.exp(scores - row_max)
        row_total = jnp.sum(expo_scores, axis=-1, keepdims=True)
        soft_weights = (expo_scores / row_total).astype(jnp.bfloat16)
        block_out = jnp.einsum(
            "hqk,khd->qhd", soft_weights, seq_rows[:, 2], preferred_element_type=jnp.float32
        ).astype(jnp.bfloat16)
        return (block_out.reshape(q_rows, head_width), (row_max + jnp.log(row_total))[:, :, 0])

    attended, log_totals = lax.map(forward_block, jnp.arange(seq_count * per_seq, dtype=jnp.int32))
    attended = attended.reshape(tok_group, head_width)
    attn_sum = lax.psum_scatter(
        jnp.dot(attended, out_weight, preferred_element_type=jnp.float32).astype(jnp.bfloat16),
        "gy",
        scatter_dimension=0,
        tiled=True,
    ).astype(jnp.float32)
    hidden_state = inputs_float + attn_sum
    normed_two, scale_two = normalize(hidden_state)
    second_norm = (normed_two * gain_second.astype(jnp.float32)).astype(jnp.bfloat16)
    logits = jnp.dot(second_norm, route_weight, preferred_element_type=jnp.float32)
    route = jax.nn.softmax(logits, axis=-1)
    chosen = (
        expert_ids.reshape(-1)[:, None] == jnp.arange(expert_count, dtype=jnp.int32)[None, :]
    ).astype(jnp.int32)
    earlier = jnp.cumsum(chosen, axis=0) - chosen
    slot = jnp.sum(earlier * chosen, axis=-1).reshape(tok_dev, top_count)
    kept = (slot < CAP).astype(jnp.float32)
    counts, prob_sums = lax.psum(
        (jnp.sum(chosen, axis=0).astype(jnp.float32), jnp.sum(route, axis=0)), ("gx", "gy")
    )
    loss = expert_count * jnp.sum(counts / (total_tokens * top_count) * (prob_sums / total_tokens))
    router_load = jnp.stack(
        [
            expert_count * counts / (total_tokens * top_count),
            expert_count * prob_sums / total_tokens,
        ],
        axis=0,
    )
    slot_place = expert_ids * CAP + jnp.minimum(slot, CAP - 1)
    buffer_index = jnp.arange(expert_count * CAP, dtype=jnp.int32)[:, None, None]
    hit_table = (buffer_index == slot_place[None]).astype(jnp.float32) * kept[None]
    dispatch_matrix = jnp.sum(hit_table, axis=-1).astype(jnp.bfloat16)
    send_rows = jnp.dot(dispatch_matrix, second_norm, preferred_element_type=jnp.float32).astype(
        jnp.bfloat16
    )
    send_rows = send_rows.reshape(count_y, local_experts, CAP, model_width)
    received = lax.all_to_all(send_rows, "gy", split_axis=0, concat_axis=0, tiled=True)
    upper = jnp.einsum("slcd,ldf->slcf", received, inner_weight, preferred_element_type=jnp.float32)
    half_width = upper.shape[-1] // 2
    hidden_rows = (
        jax.nn.gelu(upper[..., :half_width], approximate=True) * upper[..., half_width:]
    ).astype(jnp.bfloat16)
    expert_out = jnp.einsum(
        "slcf,lfd->slcd", hidden_rows, outer_weight, preferred_element_type=jnp.float32
    ).astype(jnp.bfloat16)
    expert_out, upper, received = (expert_out, upper, received)
    returned = lax.all_to_all(expert_out, "gy", split_axis=0, concat_axis=0, tiled=True).reshape(
        expert_count * CAP, model_width
    )
    picked_rows = jnp.take(returned, slot_place, axis=0).astype(jnp.float32)
    gate_value = jnp.take_along_axis(route, expert_ids, axis=1) * kept
    mixed = hidden_state + jnp.sum(picked_rows * gate_value[:, :, None], axis=1)
    (
        gain_first,
        qkv_weight,
        out_weight,
        bias_table,
        gain_second,
        route_weight,
        inner_weight,
        outer_weight,
    ) = (
        lax.all_gather(shard_list[0], "gx", axis=0, tiled=True),
        lax.all_gather(shard_list[1], "gx", axis=1, tiled=True),
        lax.all_gather(shard_list[2], "gx", axis=1, tiled=True),
        lax.all_gather(shard_list[3], "gx", axis=0, tiled=True),
        lax.all_gather(shard_list[4], "gx", axis=0, tiled=True),
        lax.all_gather(shard_list[5], "gx", axis=0, tiled=True),
        lax.all_gather(shard_list[6], "gx", axis=1, tiled=True),
        lax.all_gather(shard_list[7], "gx", axis=2, tiled=True),
    )
    table_float = bias_table.astype(jnp.float32)
    grad_mixed = cotangent.astype(jnp.float32)
    grad_gate = kept * jnp.sum(grad_mixed[:, None, :] * picked_rows, axis=-1)
    gate_matrix = jnp.sum(hit_table * gate_value[None], axis=-1)
    grad_buffer = jnp.dot(gate_matrix, grad_mixed, precision=lax.Precision.HIGHEST).astype(
        jnp.bfloat16
    )
    grad_expert = lax.all_to_all(
        grad_buffer.reshape(count_y, local_experts, CAP, model_width),
        "gy",
        split_axis=0,
        concat_axis=0,
        tiled=True,
    )
    half_width = upper.shape[-1] // 2
    activated, pull_gelu = jax.vjp(
        lambda gate_part, up_part: jax.nn.gelu(gate_part, approximate=True) * up_part,
        upper[..., :half_width],
        upper[..., half_width:],
    )
    hidden_rows = activated.astype(jnp.bfloat16)
    grad_hidden = jnp.einsum(
        "slcd,lfd->slcf", grad_expert, outer_weight, preferred_element_type=jnp.float32
    )
    grad_outer = jnp.einsum(
        "slcf,slcd->lfd", hidden_rows, grad_expert, preferred_element_type=jnp.float32
    )
    grad_gate_part, grad_up_part = pull_gelu(grad_hidden)
    grad_upper = jnp.concatenate([grad_gate_part, grad_up_part], axis=-1).astype(jnp.bfloat16)
    grad_inner = jnp.einsum(
        "slcd,slcf->ldf", received, grad_upper, preferred_element_type=jnp.float32
    )
    grad_received = jnp.einsum(
        "slcf,ldf->slcd", grad_upper, inner_weight, preferred_element_type=jnp.float32
    ).astype(jnp.bfloat16)
    grad_copies = lax.all_to_all(
        grad_received, "gy", split_axis=0, concat_axis=0, tiled=True
    ).reshape(expert_count * CAP, model_width)
    grad_second = jnp.sum(
        jnp.take(grad_copies, slot_place, axis=0).astype(jnp.float32) * kept[:, :, None], axis=1
    )
    expert_hits = (expert_ids[:, :, None] == jnp.arange(expert_count, dtype=jnp.int32)).astype(
        jnp.float32
    )
    grad_route = (
        jnp.sum(grad_gate[:, :, None] * expert_hits, axis=1)
        + loss_weight * expert_count * (counts / (total_tokens * top_count)) / total_tokens
    )
    grad_logits = (
        route * (grad_route - jnp.sum(route * grad_route, axis=-1, keepdims=True))
    ).astype(jnp.bfloat16)
    grad_router = jnp.dot(second_norm.T, grad_logits, preferred_element_type=jnp.float32)
    grad_second = grad_second + jnp.dot(
        grad_logits, route_weight.T, preferred_element_type=jnp.float32
    )
    grad_hidden_state, grad_gain_second = norm_back(
        grad_second, normed_two, scale_two, gain_second.astype(jnp.float32)
    )
    grad_hidden_state = grad_mixed + grad_hidden_state
    piece_rows = lax.all_gather(grad_hidden_state.astype(jnp.bfloat16), "gy", axis=0, tiled=True)
    grad_out_weight = jnp.einsum(
        "tf,td->fd", attended, piece_rows, preferred_element_type=jnp.float32
    )
    update_rows = jnp.dot(piece_rows, out_weight.T, preferred_element_type=jnp.float32).astype(
        jnp.bfloat16
    )
    grad_out_weight, grad_attended = (grad_out_weight, update_rows)

    def backward_sequence(seq_index):
        seq_rows = lax.dynamic_slice_in_dim(projected, seq_index * LEN, LEN, 0)
        key_rows = seq_rows[:, 1]
        value_rows = seq_rows[:, 2]
        grad_keys = jnp.zeros((LEN, head_count, depth), jnp.float32)
        grad_values = jnp.zeros((LEN, head_count, depth), jnp.float32)
        grad_table = jnp.zeros(table_float.shape, jnp.float32)
        grad_queries = []
        for block_index in range(per_seq):
            q_start = block_index * q_rows
            query_rows = seq_rows[q_start : q_start + q_rows, 0]
            grad_out = lax.dynamic_slice_in_dim(
                grad_attended, seq_index * LEN + q_start, q_rows, 0
            ).reshape(q_rows, head_count, depth)
            scores, picks_table = block_scores(query_rows, key_rows, table_float, q_start)
            block_lse = log_totals[seq_index * per_seq + block_index]
            soft_probs = jnp.exp(scores - block_lse[:, :, None])
            grad_probs = jnp.einsum(
                "qhd,khd->hqk", grad_out, value_rows, preferred_element_type=jnp.float32
            )
            grad_scores = (
                soft_probs * (grad_probs - jnp.sum(soft_probs * grad_probs, axis=-1, keepdims=True))
            ).astype(jnp.bfloat16)
            grad_queries.append(
                jnp.einsum(
                    "hqk,khd->qhd", grad_scores, key_rows, preferred_element_type=jnp.float32
                )
                / math.sqrt(depth)
            )
            grad_keys = grad_keys + jnp.einsum(
                "hqk,qhd->khd", grad_scores, query_rows, preferred_element_type=jnp.float32
            ) / math.sqrt(depth)
            grad_values = grad_values + jnp.einsum(
                "hqk,qhd->khd",
                soft_probs.astype(jnp.bfloat16),
                grad_out,
                preferred_element_type=jnp.float32,
            )
            along_grads = gather_offsets(grad_scores.astype(jnp.float32), q_rows)
            grad_table = grad_table + jnp.dot(
                picks_table.T, along_grads.T, precision=lax.Precision.HIGHEST
            )
        stacked = jnp.stack(
            [jnp.concatenate(grad_queries, axis=0), grad_keys, grad_values], axis=1
        ).astype(jnp.bfloat16)
        return (stacked, grad_table)

    grad_projected, table_parts = lax.map(backward_sequence, jnp.arange(seq_count, dtype=jnp.int32))
    grad_projected = grad_projected.reshape(tok_group, 3, head_width)
    grad_bias_table = jnp.sum(table_parts, axis=0)
    grad_qkv_weight = jnp.einsum(
        "td,tcf->cdf", group_rows, grad_projected, preferred_element_type=jnp.float32
    )
    grad_slice = lax.slice_in_dim(grad_projected, 0, tok_dev * lax.axis_size("gy"), axis=0)
    grad_first = lax.psum_scatter(
        jnp.einsum(
            "tcf,cdf->td", grad_slice, qkv_weight, preferred_element_type=jnp.float32
        ).astype(jnp.bfloat16),
        "gy",
        scatter_dimension=0,
        tiled=True,
    ).astype(jnp.float32)
    grad_inputs, grad_gain_first = norm_back(
        grad_first, normed_one, scale_one, gain_first.astype(jnp.float32)
    )
    grad_tokens = grad_hidden_state + grad_inputs
    grad_gain_first, grad_gain_second, grad_router = (
        lax.psum(grad_gain_first.astype(jnp.bfloat16), "gy").astype(jnp.float32),
        lax.psum(grad_gain_second.astype(jnp.bfloat16), "gy").astype(jnp.float32),
        lax.psum(grad_router.astype(jnp.bfloat16), "gy").astype(jnp.float32),
    )
    summed_grads = (
        lax.psum_scatter(
            grad_gain_first.astype(jnp.bfloat16), "gx", scatter_dimension=0, tiled=True
        ).astype(jnp.float32),
        lax.psum_scatter(
            grad_qkv_weight.astype(jnp.bfloat16), "gx", scatter_dimension=1, tiled=True
        ).astype(jnp.float32),
        lax.psum_scatter(
            grad_out_weight.astype(jnp.bfloat16), "gx", scatter_dimension=1, tiled=True
        ).astype(jnp.float32),
        lax.psum_scatter(
            grad_bias_table.astype(jnp.bfloat16), "gx", scatter_dimension=0, tiled=True
        ).astype(jnp.float32),
        lax.psum_scatter(
            grad_gain_second.astype(jnp.bfloat16), "gx", scatter_dimension=0, tiled=True
        ).astype(jnp.float32),
        lax.psum_scatter(
            grad_router.astype(jnp.bfloat16), "gx", scatter_dimension=0, tiled=True
        ).astype(jnp.float32),
        lax.psum_scatter(
            grad_inner.astype(jnp.bfloat16), "gx", scatter_dimension=1, tiled=True
        ).astype(jnp.float32),
        lax.psum_scatter(
            grad_outer.astype(jnp.bfloat16), "gx", scatter_dimension=2, tiled=True
        ).astype(jnp.float32),
    )
    return (
        mixed.astype(jnp.bfloat16),
        loss,
        router_load,
        grad_tokens,
        summed_grads[0],
        summed_grads[1],
        summed_grads[2],
        summed_grads[3],
        summed_grads[4],
        summed_grads[5],
        summed_grads[6],
        summed_grads[7],
    )


def dot_nn(a, b):
    return lax.dot_general(a, b, (((1,), (0,)), ((), ())), preferred_element_type=jnp.float32)

def dot_nt(a, b):
    return lax.dot_general(a, b, (((1,), (1,)), ((), ())), preferred_element_type=jnp.float32)

def pick_buckets(d):
    k = lax.broadcasted_iota(jnp.int32, (2 * BLK, 1), 0)
    lanes = lax.broadcasted_iota(jnp.int32, (1, 128), 1)
    return (bucket_of(BLK - k - BLK * d) == lanes).astype(jnp.bfloat16)


MESH_ID = pl.DeviceIdType.MESH


def fits_fast(mesh):
    return mesh.shape["gx"] == 8 and mesh.shape["gy"] == 4


def places():
    x = lax.axis_index("gx")
    z = lax.axis_index("gy")
    core = x % 2
    chip = x // 2
    along_z = (z + 1 - 2 * (z % 2), (z + 2) % 4, 3 - z)
    chips = (chip + 1 - 2 * (chip % 2), (chip + 2) % 4, 3 - chip)
    return x, z, along_z, tuple(2 * other + core for other in chips), x + 1 - 2 * core


def attend_front(pair, proj_ref, span_ref, tile_ref, attended_ref, lse_ref, kept_ref):
    length = proj_ref.shape[1]
    blocks = length // BLK
    depth = 64
    wide = 2 * depth
    here = slice(pair * wide, (pair + 1) * wide)
    lane = lax.broadcasted_iota(jnp.int32, (1, wide), 1)
    for h in range(2):
        for d in range(2):
            row = span_ref[d, 2 * pair + h:2 * pair + h + 1, :]
            spread = jnp.broadcast_to(row, (BLK, 2 * BLK))
            turned = pltpu.roll(spread, 0, 1, stride=1, stride_axis=0)
            tile_ref[h, d] = turned[:, BLK:]
            kept_ref[2 * pair + h, d] = turned[:, BLK:].astype(jnp.bfloat16)
    far = [span_ref[1, 2 * pair + h:2 * pair + h + 1, 2 * BLK - 1:2 * BLK] for h in range(2)]
    keys = proj_ref[1, :, here]
    values_t = proj_ref[2, :, here].T
    for block in range(blocks):
        rows = pl.ds(block * BLK, BLK)
        query = proj_ref[0, rows, here] * jnp.bfloat16(0.125)
        key_count = (block + 1) * BLK
        outs = []
        for h in range(2):
            picked = jnp.where((lane // depth) == h, query, jnp.bfloat16(0))
            scores = dot_nt(keys[:key_count], picked)
            parts = []
            for kb in range(block + 1):
                part = scores[kb * BLK:(kb + 1) * BLK]
                d = block - kb
                parts.append(part + (tile_ref[h, d] if d < 2 else far[h]))
            top = functools.reduce(jnp.maximum, [jnp.max(p, axis=0, keepdims=True) for p in parts])
            parts = [jnp.exp(p - top) for p in parts]
            total = functools.reduce(jnp.add, [jnp.sum(p, axis=0, keepdims=True) for p in parts])
            scale = 1.0 / total
            weights = jnp.concatenate([(p * scale).astype(jnp.bfloat16) for p in parts], axis=0)
            outs.append(dot_nn(values_t[h * depth:(h + 1) * depth, :key_count], weights))
            lse_ref[pair, h:h + 1, rows] = top + jnp.log(total)
        attended_ref[rows, here] = jnp.concatenate(outs, axis=0).T.astype(jnp.bfloat16)


def front_kernel(
    tok_ref, wq_ref, wo_ref, inner_ref, cot_hbm, eid_ref, router_in_ref, gain1_ref, gain2_ref, bias_ref,
    seq_out, wqs_out, wos_out, router_ref, gains_ref, counts_ref, proj_ref, att_ref, lse_ref, kept_ref, hidden_ref, cols_ref, gates_ref, rows_hbm, grads_hbm, inner_a_ref, inner_b_ref, inner_c_ref, far_ref,
    seq_ref, wqs_ref, wos_ref, wos_in_ref, smalls_ref, normed_ref, attended_ref, got_ref, span_ref, tile_ref, cot_ref, grads_ref, rows_ref, second_ref, gate_parts_ref,
    small_ref, ids_ref, spots_ref,
    send_sem, recv_sem, local_sem, out_sem,
):
    x, z, along_z, across, sibling = places()
    half = z % 2
    f32, bf16 = jnp.float32, jnp.bfloat16
    peers = [(x, other) for other in along_z] + [(other, z) for other in across] + [(sibling, z)]
    far_peers = [(device, plane) for plane in along_z[1:] for device in (x,) + across]
    peers += [peer for n, peer in enumerate(far_peers) if n % 4]
    barrier = pltpu.get_barrier_semaphore()
    for peer in peers:
        pl.semaphore_signal(barrier, inc=1, device_id=peer, device_id_type=MESH_ID)
    depth = wq_ref.shape[1]
    group = wq_ref.shape[2]
    rows_out = wo_ref.shape[0]
    rows, width = tok_ref.shape

    def qkv_part(owner, slot):
        return wqs_ref.at[slot, owner]

    def out_part(owner, slot, slots):
        return wos_in_ref.at[owner, pl.ds(slot * rows_out, slots * rows_out), :]

    keeps = [
        pltpu.make_async_copy(source, target, local_sem.at[n])
        for n, (source, target) in enumerate(
            ((small_ref, smalls_ref.at[0, x]), (wo_ref, out_part(x, 0, 1)), (wq_ref, qkv_part(x, 0)),
             (tok_ref, seq_ref.at[half]), (cot_hbm, cot_ref))
        )
    ]
    for copy in keeps[1:]:
        copy.start()

    experts = rows_ref.shape[0]
    lanes = lax.broadcasted_iota(jnp.int32, (1, depth), 1)
    lanes_f = lanes.astype(f32)
    named = jnp.concatenate([eid_ref[...].astype(f32), jnp.zeros((6, rows), f32)], axis=0).T
    named = [named[:, c:c + 1] for c in range(2)]
    hits = [(lanes_f == name).astype(f32) for name in named]
    both = hits[0] + hits[1]
    earlier = lax.broadcasted_iota(jnp.int32, (rows, rows), 1) < lax.broadcasted_iota(jnp.int32, (rows, rows), 0)
    before = dot_nn(earlier.astype(bf16), both.astype(bf16))
    spots = []
    for name, hit in zip(named, hits):
        slot = jnp.sum(hit * before, axis=1, keepdims=True)
        plane = jnp.floor(name * 0.25)
        spot = (4.0 * (name - 4.0 * plane) + plane) * CAP + slot
        spots.append(jnp.where(slot < CAP, spot, -1.0))
    ids = jnp.zeros((rows, depth), f32)
    for n, column in enumerate(spots + named):
        ids = jnp.where(lanes == experts + 2 + n, column, ids)
    ids_ref[...] = ids
    spots_ref[...] = jnp.where(lanes == 0, spots[0], jnp.where(lanes == 1, spots[1], 0.0)).T[:8, :]
    counted = jnp.sum(both, axis=0, keepdims=True)
    high = jnp.floor(counted / 32.0)
    router_rows = router_in_ref[...].astype(f32)
    bias = bias_ref[...].astype(f32)
    bias = jnp.concatenate([bias, jnp.zeros((bias.shape[0], depth - bias.shape[1]), f32)], axis=1)
    small_ref[...] = jnp.concatenate(
        [
            router_rows, gain1_ref[...].astype(f32), gain2_ref[...].astype(f32), bias, high, counted - 32.0 * high,
            jnp.zeros((8, depth), f32),
        ],
        axis=0,
    ).astype(bf16)
    keeps[0].start()
    pl.semaphore_wait(barrier, len(peers))
    started = []

    def send(source, target, device):
        index = len(started)
        copy = pltpu.make_async_remote_copy(
            src_ref=source, dst_ref=target, send_sem=send_sem.at[index], recv_sem=recv_sem.at[index],
            device_id=device, device_id_type=MESH_ID,
        )
        copy.start()
        started.append(copy)
        return copy

    out_slots = (2, 1, 3)
    near = across + (sibling,)
    small_z = [send(small_ref, smalls_ref.at[j + 1, x], (x, along_z[j])) for j in range(3)]
    wq_z = send(wq_ref, qkv_part(x, 1), (x, along_z[1]))
    wq_first = [send(wq_ref, qkv_part(x, 0), (other, z)) for other in near]
    tok_z = send(tok_ref, seq_ref.at[half], (x, along_z[0]))
    wo_z = [send(wo_ref, out_part(x, out_slots[j], 1), (x, along_z[j])) for j in range(3)]
    blocks = rows_ref.shape[0] // 4
    slots = rows_ref.shape[1]
    chunk = blocks * slots
    slot_row = lax.broadcasted_iota(jnp.int32, (chunk, 1), 0).astype(f32)

    def marks(i):
        return [(slot_row + i * chunk == spots_ref[c:c + 1, :]).astype(bf16) for c in range(2)]

    keeps[4].wait()
    for i in range(4):
        first, second = marks(i)
        grads_ref[i * blocks:(i + 1) * blocks] = (
            dot_nn(first + second, cot_ref[...]).astype(bf16).reshape(blocks, slots, width)
        )
    keeps[0].wait()
    for copy in small_z:
        copy.wait_recv()
    small_x = [send(smalls_ref.at[:, x], smalls_ref.at[:, x], (other, z)) for other in near]
    wq_z.wait_recv()
    wq_second = [send(qkv_part(x, 1), qkv_part(x, 1), (other, z)) for other in near]
    far_copies = [
        send(grads_ref.at[(device // 2) * 4 + plane], far_ref.at[n // 4, x // 2], (device, plane))
        for n, (device, plane) in enumerate(far_peers)
    ]
    small_on = []
    first_on = []
    for j in range(3):
        owner = across[j]
        small_x[j].wait_recv()
        small_on.append(send(smalls_ref.at[:, owner], smalls_ref.at[:, owner], (sibling, z)))
        wq_first[j].wait_recv()
        first_on.append(send(qkv_part(owner, 0), qkv_part(owner, 0), (sibling, z)))
    for copy in [small_x[3], wq_first[3]] + small_on + first_on:
        copy.wait_recv()
    for copy in keeps[1:4]:
        copy.wait()
    inner_copies = [
        send(inner_ref.at[device // 2], target, (device, z))
        for device, target in zip(across, (inner_a_ref, inner_b_ref, inner_c_ref))
    ]

    own_smalls = [smalls_ref[0, g].astype(f32) for g in range(8)]
    gain = jnp.concatenate([part[16:17, :] for part in own_smalls], axis=1)
    heads = span_ref.shape[1] // 2
    table = jnp.concatenate([part[18:22, :] for part in own_smalls], axis=0)
    other_table = jnp.concatenate([smalls_ref[2, g].astype(f32)[18:22, :] for g in range(8)], axis=0)
    table = jnp.where(lanes < heads, table, pltpu.roll(other_table, heads, 1))
    table = jnp.where(lanes < 2 * heads, table, 0.0)
    table = jnp.concatenate([table, jnp.zeros((depth - table.shape[0], depth), f32)], axis=0)
    table = table.T[:2 * heads, :].astype(bf16)
    for d in range(2):
        span_ref[d] = dot_nt(table, pick_buckets(d))
    step = rows // 2

    def norm(side, i):
        normed, _ = normalize(seq_ref[side, i * step:(i + 1) * step, :].astype(f32))
        here = pl.ds(pl.multiple_of(side * rows + i * step, step), step)
        normed_ref[here, :] = (normed * gain).astype(bf16)

    for i in range(2):
        norm(half, i)
    tok_z.wait_recv()
    for i in range(2):
        norm(1 - half, i)

    def project(slot):
        here = slice(slot * group, (slot + 1) * group)
        for c in range(3):
            proj_ref[c, :, here] = dot_nn(normed_ref[...], wqs_ref[slot, :, c].reshape(width, group)).astype(bf16)

    def attend(pair):
        attend_front(pair, proj_ref, span_ref, tile_ref, attended_ref, lse_ref, kept_ref)

    def exchange(slot):
        here = pl.ds(slot * group, group)
        there = pl.ds(pl.multiple_of((1 - half) * rows, rows), rows)
        return send(attended_ref.at[there, here], got_ref.at[:, here], (x, along_z[0]))

    project(0)
    for copy in wo_z:
        copy.wait_recv()
    wo_x = [send(out_part(x, 0, 4), out_part(x, 0, 4), (other, z)) for other in near]
    attend(0)
    second_on = []
    for j in range(3):
        owner = across[j]
        wq_second[j].wait_recv()
        second_on.append(send(qkv_part(owner, 1), qkv_part(owner, 1), (sibling, z)))
    attend(1)
    got_0 = exchange(0)
    for copy in [wq_second[3]] + second_on:
        copy.wait_recv()
    project(1)
    outs = [
        pltpu.make_async_copy(source, target, out_sem.at[n])
        for n, (source, target) in enumerate(((seq_ref, seq_out), (wqs_ref, wqs_out)))
    ]
    for copy in outs:
        copy.start()
    attend(2)
    attend(3)
    got_1 = exchange(1)
    wo_on = []
    for j in range(3):
        owner = across[j]
        wo_x[j].wait_recv()
        wo_on.append(send(out_part(owner, 0, 4), out_part(owner, 0, 4), (sibling, z)))
    for copy in [wo_x[3]] + wo_on:
        copy.wait_recv()
    for owner in range(8):
        wos_ref[:, owner * depth:(owner + 1) * depth] = wos_in_ref[owner]
    outs.append(pltpu.make_async_copy(wos_ref, wos_out, out_sem.at[2]))
    outs[2].start()
    own = pl.ds(pl.multiple_of(half * rows, rows), rows)
    att_ref[:, :2 * group] = attended_ref[own, :]
    for copy in (got_0, got_1):
        copy.wait_recv()
    att_ref[:, 2 * group:] = got_ref[...]

    gain_second = jnp.concatenate([part[17:18, :] for part in own_smalls], axis=1)
    router = jnp.concatenate([part[:experts, :] for part in own_smalls], axis=1)
    router = jnp.concatenate([router, jnp.zeros((depth - experts, width), f32)], axis=0).astype(bf16)
    router_ref[...] = router
    gains_ref[...] = jnp.concatenate([gain, gain_second], axis=0)
    counted = sum(smalls_ref[j, g].astype(f32) for j in range(4) for g in range(8))
    counts_ref[...] = 32.0 * counted[22:23, :] + counted[23:24, :]
    for i in range(2):
        here = slice(i * step, (i + 1) * step)
        hidden = seq_ref[half, here, :].astype(f32) + dot_nn(att_ref[here, :], wos_ref[...])
        hidden_ref[here, :] = hidden
        normed, _ = normalize(hidden)
        second = (normed * gain_second).astype(bf16)
        second_ref[here, :] = second
        logits = jnp.where(lanes < experts, dot_nt(second, router), -1e30)
        route = jnp.exp(logits - jnp.max(logits, axis=1, keepdims=True))
        route = route / jnp.sum(route, axis=1, keepdims=True)
        ids = ids_ref[here, :]
        gates = []
        for c in range(2):
            gate = jnp.sum(jnp.where(lanes_f == ids[:, experts + 4 + c:experts + 5 + c], route, 0.0), axis=1, keepdims=True)
            gates.append(jnp.where(ids[:, experts + 2 + c:experts + 3 + c] >= 0.0, gate, 0.0))
            high = gates[c].astype(bf16).astype(f32)
            gate_parts_ref[c, here, :] = jnp.where(
                lanes == 0, high, jnp.where(lanes == 1, gates[c] - high, 0.0)
            ).astype(bf16)
        cols_ref[here, :] = jnp.where(
            lanes < experts, route, jnp.where(lanes == experts, gates[0], jnp.where(lanes == experts + 1, gates[1], ids))
        )
    for i in range(4):
        first, second = marks(i)
        rows_ref[i * blocks:(i + 1) * blocks] = (
            dot_nn(first + second, second_ref[...]).astype(bf16).reshape(blocks, slots, width)
        )
        parts = dot_nn(first, gate_parts_ref[0]) + dot_nn(second, gate_parts_ref[1])
        for n in range(blocks):
            turned = parts[n * slots:(n + 1) * slots, :].T
            line = jnp.concatenate([turned[0:1, :] + turned[1:2, :], jnp.zeros((1, depth - slots), f32)], axis=1)
            gates_ref[i * blocks + n] = jnp.broadcast_to(line, (8, depth))
    outs.append(pltpu.make_async_copy(rows_ref, rows_hbm, out_sem.at[3]))
    outs.append(pltpu.make_async_copy(grads_ref, grads_hbm, out_sem.at[4]))
    for copy in outs[3:]:
        copy.start()
    for copy in inner_copies + far_copies:
        copy.wait_recv()
    for copy in started:
        copy.wait_send()
    for copy in outs:
        copy.wait()


def run_front(tokens, w_qkv, w_out, w_in, cotangent, ids, router, gain_first, gain_second, bias):
    rows, width = tokens.shape
    group = w_qkv.shape[2]
    f32, bf16 = jnp.float32, jnp.bfloat16
    heads = 2 * group // 64
    anywhere = pl.BlockSpec(memory_space=pl.ANY)
    inside = pl.BlockSpec(memory_space=pltpu.VMEM)
    seq = (2, rows, width)
    wqs = (2, 8) + w_qkv.shape
    wos = (width, width)
    experts = router.shape[0]
    small = (32, 128)
    smalls = (4, 8) + small
    copies_count = 3 + 1 + 4 + 1 + 3 + 4 + 4 + 3 + 3 + 4 + 3 + 3 + 3 + 2 + 8
    return pl.pallas_call(
        front_kernel,
        out_shape=(
            jax.ShapeDtypeStruct(seq, bf16),
            jax.ShapeDtypeStruct(wqs, bf16),
            jax.ShapeDtypeStruct(wos, bf16),
            jax.ShapeDtypeStruct((128, width), bf16),
            jax.ShapeDtypeStruct((2, width), f32),
            jax.ShapeDtypeStruct((1, 128), f32),
            jax.ShapeDtypeStruct((3, 2 * rows, 2 * group), bf16),
            jax.ShapeDtypeStruct((rows, width), bf16),
            jax.ShapeDtypeStruct((heads // 2, 2, 2 * rows), f32),
            jax.ShapeDtypeStruct((heads, 2, BLK, BLK), bf16),
            jax.ShapeDtypeStruct((rows, width), f32),
            jax.ShapeDtypeStruct((rows, 128), f32),
            jax.ShapeDtypeStruct((experts, 8, 128), f32),
            jax.ShapeDtypeStruct((experts, CAP, width), bf16),
            jax.ShapeDtypeStruct((experts, CAP, width), bf16),
            jax.ShapeDtypeStruct(w_in.shape[1:], bf16),
            jax.ShapeDtypeStruct(w_in.shape[1:], bf16),
            jax.ShapeDtypeStruct(w_in.shape[1:], bf16),
            jax.ShapeDtypeStruct((2, 4, CAP, width), bf16),
        ),
        in_specs=[anywhere] * 5 + [inside] * 5,
        out_specs=(anywhere,) * 3 + (inside,) * 10 + (anywhere,) * 6,
        scratch_shapes=[
            pltpu.VMEM(seq, bf16),
            pltpu.VMEM(wqs, bf16),
            pltpu.VMEM(wos, bf16),
            pltpu.VMEM((8, width, width // 8), bf16),
            pltpu.VMEM(smalls, bf16),
            pltpu.VMEM((2 * rows, width), bf16),
            pltpu.VMEM((2 * rows, 2 * group), bf16),
            pltpu.VMEM((rows, 2 * group), bf16),
            pltpu.VMEM((2, heads, 2 * BLK), f32),
            pltpu.VMEM((2, 2, BLK, BLK), f32),
            pltpu.VMEM((rows, width), bf16),
            pltpu.VMEM((experts, CAP, width), bf16),
            pltpu.VMEM((experts, CAP, width), bf16),
            pltpu.VMEM((rows, width), bf16),
            pltpu.VMEM((2, rows, 128), bf16),
            pltpu.VMEM(small, bf16),
            pltpu.VMEM((rows, 128), f32),
            pltpu.VMEM((8, rows), f32),
            pltpu.SemaphoreType.DMA((copies_count,)),
            pltpu.SemaphoreType.DMA((copies_count,)),
            pltpu.SemaphoreType.DMA((5,)),
            pltpu.SemaphoreType.DMA((6,)),
        ],
        compiler_params=pltpu.CompilerParams(
            collective_id=0, has_side_effects=True, vmem_limit_bytes=56 * 2**20
        ),
        cost_estimate=pl.CostEstimate(flops=60 * 10**9, bytes_accessed=30 * 2**20, transcendentals=0),
        name="run_front",
    )(tokens, w_qkv, w_out, w_in, cotangent, ids, router, gain_first, gain_second, bias)


def expert_kernel(
    rows_ref, gates_ref, grads_ref, far_ref, inner_ref, inner_a_ref, inner_b_ref, inner_c_ref, outer_ref,
    returned_ref, copies_ref, ginner_ref, ginner_sent_ref, gouter_ref, inner_in_ref, outer_land_ref,
    x_ref, x_t_ref, dy_ref, gates_in_ref, win_ref, wout_ref, upper_ref, hid_ref, out_ref, back_ref,
    stage_in_ref, stage_out_ref, add_in_ref, outer_in_ref,
    row_send, row_recv, gate_send, gate_recv, out_send, out_recv, copy_send, copy_recv,
    grad_send, grad_recv, w_send, w_recv, part_send, part_recv, gout_send, gout_recv, local_sem, join_sem, load_sem,
):
    x, z, along_z, across, sibling = places()
    core = x % 2
    chip = x // 2
    me = chip * 4 + z
    _, _, slots, width = x_ref.shape
    chunk = 4 * slots
    tokens = 4 * chunk
    hidden = hid_ref.shape[1]
    half = stage_out_ref.shape[2]
    tiles = hidden // half
    shard = width // 8
    f32, bf16 = jnp.float32, jnp.bfloat16
    planes = (z,) + along_z
    chips = (chip,) + tuple(device // 2 for device in across)
    pair = (sibling, z)

    peers = [(m, k) for m in range(4) for k in range(4) if m or k]
    barrier = pltpu.get_barrier_semaphore()
    for m, k in peers:
        pl.semaphore_signal(
            barrier, inc=1, device_id=(2 * chips[k] + core, planes[m]), device_id_type=MESH_ID
        )
    pl.semaphore_signal(barrier, inc=1, device_id=pair, device_id_type=MESH_ID)
    pl.semaphore_wait(barrier, len(peers) + 1)

    def remote(source, target, sems, index, device):
        return pltpu.make_async_remote_copy(
            src_ref=source, dst_ref=target, send_sem=sems[0].at[index], recv_sem=sems[1].at[index],
            device_id=device, device_id_type=MESH_ID,
        )

    def to_plane(m, source_of, target_of, sems):
        return [
            remote(
                source_of(m, chips[k]), target_of(m), sems, 4 * m + k, (2 * chips[k] + core, planes[m])
            )
            for k in range(4)
            if m or k
        ]

    def lanes_of(owner):
        return pl.ds(pl.multiple_of(owner * shard, shard), shard)

    row_copies = [
        to_plane(
            m, lambda m, c: rows_ref.at[c * 4 + planes[m]], lambda m: x_ref.at[m, chip], (row_send, row_recv)
        )
        for m in range(4)
    ]
    gate_copies = [
        to_plane(
            m, lambda m, c: gates_ref.at[c * 4 + planes[m]], lambda m: gates_in_ref.at[m, chip],
            (gate_send, gate_recv),
        )
        for m in range(4)
    ]
    keeps = [
        pltpu.make_async_copy(inner_ref.at[chip], win_ref.at[chip, core], local_sem.at[0]),
        pltpu.make_async_copy(inner_a_ref, win_ref.at[chips[1], core], local_sem.at[1]),
        pltpu.make_async_copy(inner_b_ref, win_ref.at[chips[2], core], local_sem.at[2]),
        pltpu.make_async_copy(grads_ref.at[me], dy_ref.at[0, chip], local_sem.at[3]),
        pltpu.make_async_copy(inner_c_ref, win_ref.at[chips[3], core], local_sem.at[10]),
        pltpu.make_async_copy(rows_ref.at[me], x_ref.at[0, chip], local_sem.at[4]),
        pltpu.make_async_copy(gates_ref.at[me], gates_in_ref.at[0, chip], local_sem.at[5]),
        pltpu.make_async_copy(outer_ref.at[chip], wout_ref.at[:, lanes_of(x)], local_sem.at[6]),
    ]
    pair_inner = [
        remote(source, win_ref.at[chips[k], core], (w_send, w_recv), k, pair)
        for k, source in enumerate((inner_ref.at[chip], inner_a_ref, inner_b_ref, inner_c_ref))
    ]
    outer_copies = [
        remote(outer_ref.at[device // 2], outer_land_ref.at[x], (w_send, w_recv), 4 + j, (device, z))
        for j, device in enumerate(across)
    ]
    pair_outer = [remote(outer_ref.at[chip], outer_land_ref.at[x], (w_send, w_recv), 7, pair)] + [
        remote(outer_land_ref.at[device], outer_land_ref.at[device], (w_send, w_recv), 8 + j, pair)
        for j, device in enumerate(across)
    ]
    owners = across + (sibling,) + tuple(device + 1 - 2 * core for device in across)
    outer_loads = [
        pltpu.make_async_copy(outer_land_ref.at[owner], wout_ref.at[:, lanes_of(owner)], load_sem.at[n])
        for n, owner in enumerate(owners)
    ]
    for m in ROW_ORDER:
        for copy in row_copies[m]:
            copy.start()
    for copy in keeps + pair_inner + outer_copies + pair_outer[:1]:
        copy.start()
    for m in range(4):
        for copy in gate_copies[m]:
            copy.start()
    grad_copies = [
        to_plane(
            m, lambda m, c: grads_ref.at[c * 4 + planes[m]], lambda m: dy_ref.at[m, chip], (grad_send, grad_recv)
        )
        for m in range(2)
    ]
    far_grads = pltpu.make_async_copy(far_ref, dy_ref.at[pl.ds(2, 2)], local_sem.at[9])
    far_grads.start()
    for copy in keeps:
        copy.wait()
    for copy in pair_inner:
        copy.wait()

    def cols(tile, part):
        return pl.ds(pl.multiple_of(part * hidden + tile * half, half), half)

    def weight(tile, part):
        return win_ref[:, :, :, cols(tile, part)].reshape(width, half)

    def block(m):
        return pl.ds(m * chunk, chunk)

    def widen(m):
        for copy in row_copies[m]:
            copy.wait_recv()
        rows = x_ref.at[m]

        def step(tile, carry):
            values = rows[...].reshape(chunk, width)
            gate = dot_nn(values, weight(tile, 0))
            up = dot_nn(values, weight(tile, 1))
            square = gate * gate
            bent = jnp.tanh(gate * (0.7978845608028654 + 0.03567740813636141 * square))
            lifted = 0.5 + 0.5 * bent
            slope = lifted + (0.5 * gate) * (1.0 - bent * bent) * (
                0.7978845608028654 + 0.10703222440908423 * square
            )
            active = gate * lifted
            upper_ref[block(m), cols(tile, 0)] = (up * slope).astype(bf16)
            upper_ref[block(m), cols(tile, 1)] = active.astype(bf16)
            hid_ref[block(m), cols(tile, 0)] = (active * up).astype(bf16)
            return carry

        lax.fori_loop(0, tiles, step, 0)

    def narrow(m):
        def step(part, carry):
            here = pl.ds(pl.multiple_of(part * 256, 256), 256)
            values = dot_nn(hid_ref[block(m), :], wout_ref[:, here])
            out_ref[m, :, :, here] = values.astype(bf16).reshape(4, slots, 256)
            return carry

        lax.fori_loop(0, width // 256, step, 0)

    out_copies = [
        to_plane(m, lambda m, c: out_ref.at[m, c], lambda m: returned_ref.at[me], (out_send, out_recv))
        for m in range(4)
    ]
    own_out = pltpu.make_async_copy(out_ref.at[0, chip], returned_ref.at[me], local_sem.at[7])
    widen(0)
    widen(1)
    widen(2)
    for m in range(4):
        for copy in row_copies[m]:
            copy.wait_send()
    for m in range(2):
        for copy in grad_copies[m]:
            copy.start()
    for j, copy in enumerate(outer_copies):
        copy.wait_recv()
        pair_outer[1 + j].start()
        outer_loads[j].start()
    for j, copy in enumerate(pair_outer):
        copy.wait_recv()
        outer_loads[3 + j].start()
    for copy in outer_copies + pair_outer:
        copy.wait_send()
    for copy in outer_loads:
        copy.wait()
    for m in (2, 3, 1, 0):
        if m == 3:
            widen(m)
        narrow(m)
        for copy in out_copies[m]:
            copy.start()
    own_out.start()
    x_t_ref[...] = x_ref[...].reshape(tokens, width).T.reshape(x_t_ref.shape)

    far_grads.wait()
    for m in range(4):
        for copy in gate_copies[m] + (grad_copies[m] if m < 2 else []):
            copy.wait_recv()
        for j in range(4):
            gates = gates_in_ref[m, j].T[:slots, 0:1]
            dy_ref[m, j] = (dy_ref[m, j].astype(f32) * gates).astype(bf16)

    def outer_part(tile):
        slot = lax.rem(tile, STAGES)
        return remote(stage_out_ref.at[slot], outer_in_ref.at[tile], (part_send, part_recv), tiles + tile, pair)

    def weigh_outer(tile, carry):
        slot = lax.rem(tile, STAGES)

        @pl.when(tile >= STAGES)
        def _():
            outer_part(tile - STAGES).wait_send()

        grad_down = dot_nn(hid_ref[:, cols(tile, 0)].T, dy_ref[...].reshape(tokens, width))
        for j in range(4):
            low = grad_down[:, (2 * j) * shard:(2 * j + 1) * shard].astype(bf16)
            high = grad_down[:, (2 * j + 1) * shard:(2 * j + 2) * shard].astype(bf16)
            stage_out_ref[slot, j] = jnp.where(core == 0, high, low)
            hid_ref[pl.ds((j // 2) * half, half), pl.ds(pl.multiple_of(tile * half + (j % 2) * shard, shard), shard)] = (
                jnp.where(core == 0, low, high)
            )
        outer_part(tile).start()
        return carry

    lax.fori_loop(0, tiles, weigh_outer, 0)
    for tile in range(tiles - STAGES, tiles):
        outer_part(tile).wait_send()

    def join_outer(tile, carry):
        outer_part(tile).wait_recv()
        for j in range(4):
            own = hid_ref[pl.ds((j // 2) * half, half), pl.ds(pl.multiple_of(tile * half + (j % 2) * shard, shard), shard)]
            outer_in_ref[tile, j] = (own.astype(f32) + outer_in_ref[tile, j].astype(f32)).astype(bf16)
        return carry

    lax.fori_loop(0, tiles, join_outer, 0)
    own_gout = pltpu.make_async_copy(outer_in_ref.at[:, chip], gouter_ref.at[chip], local_sem.at[3])
    own_gout.start()
    gout_copies = [
        remote(outer_in_ref.at[:, device // 2], gouter_ref.at[chip], (gout_send, gout_recv), j, (device, z))
        for j, device in enumerate(across)
    ]
    for copy in gout_copies:
        copy.start()

    def back(first, count):
        here_rows = pl.ds(first * chunk, count * chunk)

        def step(tile, carry):
            down = wout_ref[pl.ds(pl.multiple_of(tile * half, half), half), :]
            grads = dy_ref[first:first + count].reshape(count * chunk, width)
            grad_hidden = dot_nt(grads, down)
            for part in range(2):
                slope = upper_ref[here_rows, cols(tile, part)].astype(f32)
                upper_ref[here_rows, cols(tile, part)] = (grad_hidden * slope).astype(bf16)
            return carry

        lax.fori_loop(0, tiles, step, 0)

        def gather(j, carry):
            here = pl.ds(pl.multiple_of(j * 256, 256), 256)
            weights = win_ref[j].reshape(2 * shard, 2 * hidden)
            values = dot_nt(upper_ref[here_rows, :], weights)
            back_ref[first:first + count, :, :, here] = values.astype(bf16).reshape(count, 4, slots, 256)
            return carry

        lax.fori_loop(0, 4, gather, 0)

    copy_copies = [
        to_plane(m, lambda m, c: back_ref.at[m, c], lambda m: copies_ref.at[me], (copy_send, copy_recv))
        for m in range(4)
    ]
    own_copy = pltpu.make_async_copy(back_ref.at[0, chip], copies_ref.at[me], local_sem.at[8])
    for first in range(4 - BACK_COUNT, -1, -BACK_COUNT):
        back(first, BACK_COUNT)
        for m in range(first, first + BACK_COUNT):
            for copy in copy_copies[m]:
                copy.start()
    own_copy.start()

    def inner_part(tile):
        slot = lax.rem(tile, STAGES)
        return remote(stage_in_ref.at[slot], inner_in_ref.at[tile], (part_send, part_recv), tile, pair)

    def inner_load(tile):
        slot = lax.rem(tile, 2)
        return pltpu.make_async_copy(inner_in_ref.at[tile], add_in_ref.at[slot], join_sem.at[slot])

    def inner_stores(tile):
        slot = lax.rem(tile, 2)
        return [
            pltpu.make_async_copy(
                add_in_ref.at[slot, part], ginner_ref.at[:, :, cols(tile, part)], join_sem.at[2 + 2 * slot + part]
            )
            for part in range(2)
        ]

    def join_begin(tile):
        inner_part(tile).wait_recv()

        @pl.when(tile >= 2)
        def _():
            for copy in inner_stores(tile - 2):
                copy.wait()

        inner_load(tile).start()

    def join_end(tile):
        slot = lax.rem(tile, 2)
        inner_load(tile).wait()
        for part in range(2):
            own = upper_ref[pl.ds(0, width // 2), cols(tile, part)].astype(f32)
            other = add_in_ref[slot, part].reshape(width // 2, half).astype(f32)
            add_in_ref[slot, part] = (own + other).astype(bf16).reshape(4, shard, half)
        for copy in inner_stores(tile):
            copy.start()

    def weigh_inner(tile, carry):
        slot = lax.rem(tile, STAGES)

        @pl.when(tile >= LAG)
        def _():
            join_begin(tile - LAG)

        @pl.when(tile >= STAGES)
        def _():
            inner_part(tile - STAGES).wait_send()

        for part in range(2):
            grad_upper = upper_ref[:, cols(tile, part)]
            other = x_t_ref[:, 1 - core].reshape(width // 2, tokens)
            stage_in_ref[slot, part] = dot_nn(other, grad_upper).astype(bf16).reshape(4, shard, half)
        inner_part(tile).start()
        for part in range(2):
            grad_upper = upper_ref[:, cols(tile, part)]
            own = x_t_ref[:, core].reshape(width // 2, tokens)
            upper_ref[pl.ds(0, width // 2), cols(tile, part)] = dot_nn(own, grad_upper).astype(bf16)

        @pl.when(tile >= LAG)
        def _():
            join_end(tile - LAG)

        return carry

    lax.fori_loop(0, tiles, weigh_inner, 0)
    for tile in range(tiles - LAG, tiles):
        join_begin(tile)
        join_end(tile)
    for tile in range(tiles - STAGES, tiles):
        inner_part(tile).wait_send()
    for tile in (tiles - 2, tiles - 1):
        for copy in inner_stores(tile):
            copy.wait()
    sent = ginner_sent_ref.shape[2]
    sent_copies = [
        remote(
            ginner_ref.at[device // 2, :, pl.ds(0, sent)], ginner_sent_ref.at[j], (gout_send, gout_recv), 3 + j,
            (device, z),
        )
        for j, device in enumerate(across)
    ]
    for copy in sent_copies:
        copy.start()
    own_out.wait()
    own_copy.wait()
    own_gout.wait()
    for m in range(4):
        for copy in (grad_copies[m] if m < 2 else []) + gate_copies[m]:
            copy.wait_send()
        for copy in out_copies[m] + copy_copies[m]:
            copy.wait()
    for copy in gout_copies + sent_copies:
        copy.wait()


ROW_ORDER = (0, 1, 2, 3)
BACK_COUNT = 2
STAGES = 4
LAG = 2


def run_experts(rows, gates, grads, far, inner, inner_others, outer):
    count, slots, width = rows.shape
    tokens = count * slots
    hidden = outer.shape[1]
    half = 256
    tiles = hidden // half
    shard = width // 8
    bf16 = jnp.bfloat16
    anywhere = pl.BlockSpec(memory_space=pl.ANY)
    sems = [pltpu.SemaphoreType.DMA((count,))] * 10 + [
        pltpu.SemaphoreType.DMA((12,)),
        pltpu.SemaphoreType.DMA((12,)),
        pltpu.SemaphoreType.DMA((2 * tiles,)),
        pltpu.SemaphoreType.DMA((2 * tiles,)),
        pltpu.SemaphoreType.DMA((6,)),
        pltpu.SemaphoreType.DMA((6,)),
        pltpu.SemaphoreType.DMA((11,)),
        pltpu.SemaphoreType.DMA((6,)),
        pltpu.SemaphoreType.DMA((7,)),
    ]
    outs = pl.pallas_call(
        expert_kernel,
        out_shape=(
            jax.ShapeDtypeStruct(rows.shape, bf16),
            jax.ShapeDtypeStruct(rows.shape, bf16),
            jax.ShapeDtypeStruct(inner.shape, bf16),
            jax.ShapeDtypeStruct((3, shard, inner.shape[2] // 4), bf16),
            jax.ShapeDtypeStruct((4, tiles, half, shard), bf16),
            jax.ShapeDtypeStruct((tiles, 2, 4, shard, half), bf16),
            jax.ShapeDtypeStruct((8, hidden, shard), bf16),
        ),
        in_specs=[anywhere] * 9,
        out_specs=(anywhere,) * 7,
        scratch_shapes=[
            pltpu.VMEM((4, 4, slots, width), bf16),
            pltpu.VMEM((4, 2, shard, tokens), bf16),
            pltpu.VMEM((4, 4, slots, width), bf16),
            pltpu.VMEM((4, 4, 8, 128), jnp.float32),
            pltpu.VMEM((4, 2, shard, 2 * hidden), bf16),
            pltpu.VMEM((hidden, width), bf16),
            pltpu.VMEM((tokens, 2 * hidden), bf16),
            pltpu.VMEM((tokens, hidden), bf16),
            pltpu.VMEM((4, 4, slots, width), bf16),
            pltpu.VMEM((4, 4, slots, width), bf16),
            pltpu.VMEM((STAGES, 2, 4, shard, half), bf16),
            pltpu.VMEM((STAGES, 4, half, shard), bf16),
            pltpu.VMEM((2, 2, 4, shard, half), bf16),
            pltpu.VMEM((tiles, 4, half, shard), bf16),
        ] + sems,
        compiler_params=pltpu.CompilerParams(
            collective_id=1, has_side_effects=True, vmem_limit_bytes=63 * 2**20
        ),
        cost_estimate=pl.CostEstimate(
            flops=180 * 10**9, bytes_accessed=60 * 2**20, transcendentals=tokens * hidden
        ),
        name="run_experts",
    )(rows, gates, grads, far, inner, *inner_others, outer)
    return outs[0], outs[1], outs[2], outs[3], outs[4].reshape(outer.shape)


def attend_back(pair, proj_ref, dout_ref, lse_ref, tile_ref, dproj_ref, span_ref, dk_ref, dv_ref, near_ref):
    length = proj_ref.shape[1]
    blocks = length // BLK
    depth = 64
    wide = 2 * depth
    here = slice(pair * wide, (pair + 1) * wide)
    lane = lax.broadcasted_iota(jnp.int32, (1, wide), 1)
    keys = proj_ref[1, :, here]
    values = proj_ref[2, :, here]
    keys_t = keys.T
    dk_ref[...] = jnp.zeros_like(dk_ref)
    dv_ref[...] = jnp.zeros_like(dv_ref)
    near_ref[...] = jnp.zeros_like(near_ref)
    far_sum = [jnp.zeros((1, BLK), jnp.float32) for h in range(2)]
    for block in range(blocks):
        rows = pl.ds(block * BLK, BLK)
        key_count = (block + 1) * BLK
        query = proj_ref[0, rows, here] * jnp.bfloat16(0.125)
        grad = dout_ref[rows, here]
        dq_parts = []
        dk_sum = None
        dv_sum = None
        for h in range(2):
            own = (lane // depth) == h
            query_h = jnp.where(own, query, jnp.bfloat16(0))
            grad_h = jnp.where(own, grad, jnp.bfloat16(0))
            scores = dot_nt(keys[:key_count], query_h)
            grad_p = dot_nt(values[:key_count], grad_h)
            lse = lse_ref[pair, h:h + 1, rows]
            far = tile_ref[2 * pair + h, 1, 0:1, BLK - 1:BLK].astype(jnp.float32)
            probs = []
            delta = None
            for kb in range(block + 1):
                d = block - kb
                part = scores[kb * BLK:(kb + 1) * BLK]
                bias = tile_ref[2 * pair + h, d].astype(jnp.float32) if d < 2 else far
                part = jnp.exp(part + (bias - lse))
                probs.append(part)
                term = jnp.sum(part * grad_p[kb * BLK:(kb + 1) * BLK], axis=0, keepdims=True)
                delta = term if delta is None else delta + term
            ds = []
            for kb in range(block + 1):
                d = block - kb
                part = probs[kb] * (grad_p[kb * BLK:(kb + 1) * BLK] - delta)
                if d < 2:
                    near_ref[h, d] += part
                else:
                    far_sum[h] = far_sum[h] + jnp.sum(part, axis=0, keepdims=True)
                ds.append(part.astype(jnp.bfloat16))
            ds = jnp.concatenate(ds, axis=0)
            weights = jnp.concatenate([p.astype(jnp.bfloat16) for p in probs], axis=0)
            dv_h = dot_nn(weights, grad_h)
            dk_h = dot_nn(ds, query_h)
            dv_sum = dv_h if dv_sum is None else dv_sum + dv_h
            dk_sum = dk_h if dk_sum is None else dk_sum + dk_h
            dq_parts.append(dot_nn(keys_t[h * depth:(h + 1) * depth, :key_count], ds))
        dk_ref[:key_count] += dk_sum
        dv_ref[:key_count] += dv_sum
        dproj_ref[0, rows, here] = (jnp.concatenate(dq_parts, axis=0).T * 0.125).astype(jnp.bfloat16)
    dproj_ref[1, :, here] = dk_ref[...].astype(jnp.bfloat16)
    dproj_ref[2, :, here] = dv_ref[...].astype(jnp.bfloat16)
    flip = (
        lax.broadcasted_iota(jnp.int32, (BLK, BLK), 0) + lax.broadcasted_iota(jnp.int32, (BLK, BLK), 1) == BLK - 1
    ).astype(jnp.bfloat16)
    lanes = lax.broadcasted_iota(jnp.int32, (1, 2 * BLK), 1)
    for h in range(2):
        for d in range(2):
            near = near_ref[h, d]
            near_high = near.astype(jnp.bfloat16)
            near_low = (near - near_high.astype(jnp.float32)).astype(jnp.bfloat16)
            flipped = dot_nn(flip, near_high) + dot_nn(flip, near_low)
            spread = jnp.concatenate([flipped, jnp.zeros((BLK, BLK), jnp.float32)], axis=1)
            turned = pltpu.roll(spread, 1, 1, stride=1, stride_axis=0)
            along = jnp.sum(turned, axis=0, keepdims=True)
            if d == 1:
                along = along + jnp.where(lanes == 2 * BLK - 1, jnp.sum(far_sum[h], axis=1, keepdims=True), 0.0)
            span_ref[2 * pair + h, d:d + 1, :] = along


def back_kernel(
    returned_hbm, copies_hbm, hidden_hbm, cot_hbm, cols_hbm, wo_hbm, att_hbm, router_ref, gains_ref, counts_ref,
    proj_hbm, lse_hbm, tile_hbm, wq_hbm, seq_hbm, ginner_hbm,
    mixed_ref, gtok_ref, gqkv_ref, gwo_ref, sums_ref, inner_in_hbm,
    returned_ref, copies_ref, hidden_ref, cot_ref, cols_ref, wo_ref, att_ref, gp_ref, dout_send_ref,
    proj_ref, lse_ref, tile_ref, wq_ref, seq_ref, dout_ref, dproj_ref, span_ref, dk_ref, dv_ref,
    near_ref, turned_ref, first_send_ref, first_in_ref,
    q_stage_ref, q_in_ref, q_own_ref, q_across_ref, q_z_ref, q_z_in_ref,
    gout_ref, o_in_ref, o_sum_ref, o_across_ref, o_z_ref, o_z_in_ref,
    s_own_ref, s_in_ref, s_sum_ref, s_across_ref, s_z_ref, s_z_in_ref,
    send_sem, recv_sem, load_sem,
):
    x, z, along_z, across, sibling = places()
    core = x % 2
    chip = x // 2
    half = z % 2
    f32, bf16 = jnp.float32, jnp.bfloat16
    rows, width = gtok_ref.shape
    shard = width // 8
    step = rows // 2
    group = gqkv_ref.shape[2]
    experts = returned_ref.shape[0] // CAP
    pair = (sibling, z)
    chips = [(device, z) for device in across]
    lines = [(x, other) for other in along_z]
    barrier = pltpu.get_barrier_semaphore()
    for peer in chips + lines + [pair]:
        pl.semaphore_signal(barrier, inc=1, device_id=peer, device_id_type=MESH_ID)
    loads = {}
    for name, source, target in (
        ("cols", cols_hbm, cols_ref), ("returned", returned_hbm, returned_ref), ("hidden", hidden_hbm, hidden_ref),
        ("cot", cot_hbm, cot_ref), ("copies", copies_hbm, copies_ref), ("wo", wo_hbm, wo_ref),
        ("att", att_hbm, att_ref), ("seq", seq_hbm, seq_ref), ("proj", proj_hbm, proj_ref),
        ("lse", lse_hbm, lse_ref), ("tile", tile_hbm, tile_ref), ("wq", wq_hbm, wq_ref),
    ):
        loads[name] = pltpu.make_async_copy(source, target, load_sem.at[len(loads)])
        loads[name].start()
    pl.semaphore_wait(barrier, 7)
    started = []

    def send(source, target, device):
        index = len(started)
        copy = pltpu.make_async_remote_copy(
            src_ref=source, dst_ref=target, send_sem=send_sem.at[index], recv_sem=recv_sem.at[index],
            device_id=device, device_id_type=MESH_ID,
        )
        copy.start()
        started.append(copy)
        return copy

    inner_rest = inner_in_hbm.shape[2]
    inner_copies = [
        send(
            ginner_hbm.at[device // 2, :, pl.ds(ginner_hbm.shape[2] - inner_rest, inner_rest)], inner_in_hbm.at[j],
            (device, z),
        )
        for j, device in enumerate(across)
    ]

    gain_second = gains_ref[1:2, :]
    router_t = router_ref[...]
    step = rows // 2
    counts = counts_ref[...]
    tokens = 32 * rows
    pairs_in_all = 2 * tokens
    push = loss_weight * experts * (counts / pairs_in_all) / tokens
    slot_lane = lax.broadcasted_iota(jnp.int32, (1, returned_ref.shape[0]), 1).astype(f32)
    expert_lane = lax.broadcasted_iota(jnp.int32, (1, shard), 1).astype(f32)
    own_width = dout_ref.shape[1]
    dout_copies = []
    gain2_sum = jnp.zeros((1, width), f32)
    route_sum = jnp.zeros((1, shard), f32)
    grad_router = jnp.zeros((shard, width), f32)
    for name in ("cols", "returned", "hidden", "cot"):
        loads[name].wait()
    for i in range(2):
        here = slice(i * step, (i + 1) * step)
        cols = cols_ref[here, :]
        route = jnp.where(expert_lane < experts, cols, 0.0)
        marks = [(slot_lane == cols[:, experts + 2 + c:experts + 3 + c]).astype(bf16) for c in range(2)]
        picked = [dot_nn(mark, returned_ref[...]) for mark in marks]
        hidden = hidden_ref[here, :]
        grad_mixed = cot_ref[here, :].astype(f32)
        mixed_ref[here, :] = (
            hidden + picked[0] * cols[:, experts:experts + 1] + picked[1] * cols[:, experts + 1:experts + 2]
        ).astype(bf16)
        grad_route = push
        for c in range(2):
            hit = expert_lane == cols[:, experts + 4 + c:experts + 5 + c]
            grad_route = grad_route + jnp.where(hit, jnp.sum(grad_mixed * picked[c], axis=1, keepdims=True), 0.0)
        grad_logits = route * (grad_route - jnp.sum(route * grad_route, axis=1, keepdims=True))
        route_sum = route_sum + jnp.sum(route, axis=0, keepdims=True)
        if i == 0:
            loads["copies"].wait()
        grad_second = dot_nn(marks[0] + marks[1], copies_ref[...]) + dot_nn(grad_logits.astype(bf16), router_t)
        normed, scale = normalize(hidden)
        second_norm = (normed * gain_second).astype(bf16)
        grad_router = grad_router + dot_nn(grad_logits.T.astype(bf16), second_norm)
        gain2_sum = gain2_sum + jnp.sum(grad_second * normed, axis=0, keepdims=True)
        grad_normed = grad_second * gain_second
        grad_hidden = grad_mixed + scale * (
            grad_normed - normed * jnp.mean(grad_normed * normed, axis=-1, keepdims=True)
        )
        hidden_ref[here, :] = grad_hidden
        grad_part = grad_hidden.astype(bf16)
        gp_ref[here, :] = grad_part
        if i == 0:
            loads["wo"].wait()
        dout_send_ref[here, :] = dot_nt(grad_part, wo_ref[own_width:, :]).astype(bf16)
        for slot in (1, 0) if i == 0 else (1,):
            lanes = pl.ds(slot * group, group)
            dout_copies.append(
                send(dout_send_ref.at[here, lanes], dout_ref.at[pl.ds(half * rows + i * step, step), lanes], lines[0])
            )


    own_rows = pl.ds(pl.multiple_of(half * rows, rows), rows)
    dout_ref[own_rows, :] = dot_nt(gp_ref[...], wo_ref[:own_width, :]).astype(bf16)

    loads["att"].wait()
    grad_out = dot_nn(att_ref[...].T, gp_ref[...]).astype(bf16)
    for owner in range(8):
        gout_ref[owner // 2, owner % 2] = grad_out[:, owner * shard:(owner + 1) * shard]
    o_pair = [send(gout_ref.at[j, 1 - core], o_in_ref.at[j], pair) for j in range(4)]

    gain_first = gains_ref[0:1, :]
    loads["seq"].wait()
    for i in range(4):
        normed, _ = normalize(seq_ref[i // 2, (i % 2) * step:(i % 2 + 1) * step, :].astype(f32))
        turned_ref[:, :, :, i * step:(i + 1) * step] = (
            (normed * gain_first).astype(bf16).T.reshape(4, 2, shard, step)
        )

    dout_copies.append(
        send(
            dout_send_ref.at[pl.ds(step, step), pl.ds(0, group)],
            dout_ref.at[pl.ds(half * rows + step, step), pl.ds(0, group)],
            lines[0],
        )
    )
    for name in ("proj", "lse", "tile"):
        loads[name].wait()
    for n in (0, 2):
        dout_copies[n].wait_recv()

    def attend(number):
        attend_back(
            number, proj_ref, dout_ref, lse_ref, tile_ref, dproj_ref, span_ref, dk_ref, dv_ref, near_ref
        )

    def weigh_other(slot):
        here = pl.ds(slot * group, group)
        other = turned_ref[:, 1 - core].reshape(width // 2, 2 * rows)
        for c in range(3):
            q_stage_ref[slot, c] = dot_nn(other, dproj_ref[c, :, here]).astype(bf16).reshape(4, shard, group)
        return send(q_stage_ref.at[slot], q_in_ref.at[slot], pair)

    def weigh_own(slot):
        here = pl.ds(slot * group, group)
        own = turned_ref[:, core].reshape(width // 2, 2 * rows)
        for c in range(3):
            q_own_ref[slot, c] = dot_nn(own, dproj_ref[c, :, here]).astype(bf16).reshape(4, shard, group)

    def to_chips(slot, copy):
        copy.wait_recv()
        q_own_ref[slot] = (q_own_ref[slot].astype(f32) + q_in_ref[slot].astype(f32)).astype(bf16)
        return [
            send(q_own_ref.at[slot, :, device // 2], q_across_ref.at[slot, j], chips[j])
            for j, device in enumerate(across)
        ]

    def chip_total(slot, copies):
        for copy in copies:
            copy.wait_recv()
        total = q_own_ref[slot, :, chip].astype(f32)
        for j in range(3):
            total = total + q_across_ref[slot, j].astype(f32)
        return total

    attend(2)
    attend(3)
    q_pair_1 = weigh_other(1)
    for copy in o_pair:
        copy.wait_recv()
    for j in range(4):
        o_sum_ref[j] = (gout_ref[j, core].astype(f32) + o_in_ref[j].astype(f32)).astype(bf16)
    o_chips = [send(o_sum_ref.at[device // 2], o_across_ref.at[j], chips[j]) for j, device in enumerate(across)]
    weigh_own(1)
    q_chips_1 = to_chips(1, q_pair_1)
    for n in (1, 3):
        dout_copies[n].wait_recv()
    attend(0)
    attend(1)

    loads["wq"].wait()
    gain1_sum = jnp.zeros((1, width), f32)
    first_copies = []
    for turn, side in enumerate((1 - half, half)):
        for i in range(2):
            here = pl.ds(pl.multiple_of(side * rows + i * step, step), step)
            part = sum(
                dot_nt(dproj_ref[c, here, slot * group:(slot + 1) * group], wq_ref[slot, :, c].reshape(width, group))
                for slot in range(2)
                for c in range(3)
            )
            normed, _ = normalize(seq_ref[side, i * step:(i + 1) * step, :].astype(f32))
            gain1_sum = gain1_sum + jnp.sum(part * normed, axis=0, keepdims=True)
            if turn:
                gtok_ref[i * step:(i + 1) * step, :] = part
            else:
                first_send_ref[i * step:(i + 1) * step, :] = part.astype(bf16)
                block = pl.ds(i * step, step)
                first_copies.append(send(first_send_ref.at[block], first_in_ref.at[block], lines[0]))
        if not turn:
            q_pair_0 = weigh_other(0)

    table = None
    for d in range(2):
        along = span_ref[:, d, :]
        high = along.astype(bf16)
        low = (along - high.astype(f32)).astype(bf16)
        picks = pick_buckets(d)
        part = dot_nn(high, picks) + dot_nn(low, picks)
        table = part if table is None else table + part
    heads = table.shape[0] // 2
    table = table.T[:32, :]
    blank = jnp.zeros((table.shape[0], shard - heads), f32)
    placed = pltpu.roll(jnp.concatenate([table[:, :heads], blank], axis=1), heads * z, 1) + pltpu.roll(
        jnp.concatenate([table[:, heads:], blank], axis=1), heads * ((z + 2) % 4), 1
    )
    for owner in range(8):
        here = slice(owner * shard, (owner + 1) * shard)
        target = s_own_ref.at[owner // 2, owner % 2]
        target[0:1, :] = gain1_sum[:, here]
        target[1:2, :] = gain2_sum[:, here]
        target[2:2 + experts, :] = grad_router[:experts, here]
        target[22:23, :] = route_sum
        target[23:24, :] = jnp.zeros((1, shard), f32)
        target[18:22, :] = placed[4 * owner:4 * owner + 4, :]
    s_pair = send(s_own_ref.at[:, 1 - core], s_in_ref, pair)
    weigh_own(0)

    q_chips_0 = to_chips(0, q_pair_0)
    s_pair.wait_recv()
    s_sum_ref[...] = s_own_ref[:, core] + s_in_ref[...]
    s_chips = [send(s_sum_ref.at[device // 2], s_across_ref.at[j], chips[j]) for j, device in enumerate(across)]
    q_z_ref[...] = chip_total(1, q_chips_1).astype(bf16)
    q_line = send(q_z_ref, q_z_in_ref, lines[1])
    for copy in o_chips:
        copy.wait_recv()
    o_total = o_sum_ref[chip].astype(f32)
    for j in range(3):
        o_total = o_total + o_across_ref[j].astype(f32)
    rows_out = gwo_ref.shape[0]
    gwo_ref[...] = o_total[:rows_out]
    o_z_ref[...] = o_total[rows_out:].astype(bf16).reshape(o_z_ref.shape)
    out_slots = (2, 1, 3)
    o_lines = [send(o_z_ref.at[out_slots[j] - 1], o_z_in_ref.at[j], lines[j]) for j in range(3)]
    for copy in s_chips:
        copy.wait_recv()
    s_z_ref[...] = s_sum_ref[chip] + s_across_ref[0] + s_across_ref[1] + s_across_ref[2]
    s_lines = [send(s_z_ref, s_z_in_ref.at[j], lines[j]) for j in range(3)]
    gqkv_ref[...] = chip_total(0, q_chips_0)

    for i in range(2):
        first_copies[i].wait_recv()
        here = slice(i * step, (i + 1) * step)
        grad = (gtok_ref[here, :] + first_in_ref[here, :].astype(f32)) * gain_first
        normed, scale = normalize(seq_ref[half, here, :].astype(f32))
        gtok_ref[here, :] = hidden_ref[here, :] + scale * (
            grad - normed * jnp.mean(grad * normed, axis=-1, keepdims=True)
        )
    q_line.wait_recv()
    gqkv_ref[...] += q_z_in_ref[...].astype(f32)
    for copy in s_lines + o_lines:
        copy.wait_recv()
    gwo_ref[...] += o_z_in_ref[0].astype(f32) + o_z_in_ref[1].astype(f32) + o_z_in_ref[2].astype(f32)
    sums = s_z_ref[...] + s_z_in_ref[0] + s_z_in_ref[1] + s_z_in_ref[2]
    sums_ref[...] = sums
    for copy in inner_copies:
        copy.wait_recv()
    for copy in started:
        copy.wait_send()


def run_back(
    returned, copies, hidden, cot, cols, wo, att, router_t, gains, counts, proj, lse, tiles, wq, seq, ginner, sent
):
    rows, width = hidden.shape
    length = 2 * rows
    shard = width // 8
    group = wq.shape[4]
    rows_out = width // 4
    heads = tiles.shape[0]
    f32, bf16 = jnp.float32, jnp.bfloat16
    anywhere = pl.BlockSpec(memory_space=pl.ANY)
    inside = pl.BlockSpec(memory_space=pltpu.VMEM)
    copies_count = 3 + 4 + 4 + 2 + 3 + 3 + 3 + 2 + 1 + 3 + 1 + 3 + 3
    return pl.pallas_call(
        back_kernel,
        out_shape=(
            jax.ShapeDtypeStruct((rows, width), bf16),
            jax.ShapeDtypeStruct((rows, width), f32),
            jax.ShapeDtypeStruct((3, shard, group), f32),
            jax.ShapeDtypeStruct((rows_out, shard), f32),
            jax.ShapeDtypeStruct((24, shard), f32),
            jax.ShapeDtypeStruct((3, shard, ginner.shape[2] - sent), bf16),
        ),
        in_specs=[anywhere] * 7 + [inside] * 3 + [anywhere] * 6,
        out_specs=(inside,) * 5 + (anywhere,),
        scratch_shapes=[
            pltpu.VMEM(returned.shape, bf16),
            pltpu.VMEM(copies.shape, bf16),
            pltpu.VMEM(hidden.shape, f32),
            pltpu.VMEM(cot.shape, bf16),
            pltpu.VMEM(cols.shape, f32),
            pltpu.VMEM(wo.shape, bf16),
            pltpu.VMEM(att.shape, bf16),
            pltpu.VMEM((rows, width), bf16),
            pltpu.VMEM((rows, 2 * group), bf16),
            pltpu.VMEM(proj.shape, bf16),
            pltpu.VMEM(lse.shape, f32),
            pltpu.VMEM(tiles.shape, bf16),
            pltpu.VMEM(wq.shape, bf16),
            pltpu.VMEM(seq.shape, bf16),
            pltpu.VMEM((length, 2 * group), bf16),
            pltpu.VMEM(proj.shape, bf16),
            pltpu.VMEM((heads, 2, 2 * BLK), f32),
            pltpu.VMEM((length, 128), f32),
            pltpu.VMEM((length, 128), f32),
            pltpu.VMEM((2, 2, BLK, BLK), f32),
            pltpu.VMEM((4, 2, shard, length), bf16),
            pltpu.VMEM((rows, width), bf16),
            pltpu.VMEM((rows, width), bf16),
            pltpu.VMEM((2, 3, 4, shard, group), bf16),
            pltpu.VMEM((2, 3, 4, shard, group), bf16),
            pltpu.VMEM((2, 3, 4, shard, group), bf16),
            pltpu.VMEM((2, 3, 3, shard, group), bf16),
            pltpu.VMEM((3, shard, group), bf16),
            pltpu.VMEM((3, shard, group), bf16),
            pltpu.VMEM((4, 2, width, shard), bf16),
            pltpu.VMEM((4, width, shard), bf16),
            pltpu.VMEM((4, width, shard), bf16),
            pltpu.VMEM((3, width, shard), bf16),
            pltpu.VMEM((3, rows_out, shard), bf16),
            pltpu.VMEM((3, rows_out, shard), bf16),
            pltpu.VMEM((4, 2, 24, shard), f32),
            pltpu.VMEM((4, 24, shard), f32),
            pltpu.VMEM((4, 24, shard), f32),
            pltpu.VMEM((3, 24, shard), f32),
            pltpu.VMEM((24, shard), f32),
            pltpu.VMEM((3, 24, shard), f32),
            pltpu.SemaphoreType.DMA((copies_count,)),
            pltpu.SemaphoreType.DMA((copies_count,)),
            pltpu.SemaphoreType.DMA((12,)),
        ],
        compiler_params=pltpu.CompilerParams(
            collective_id=2, has_side_effects=True, vmem_limit_bytes=62 * 2**20
        ),
        cost_estimate=pl.CostEstimate(flops=60 * 10**9, bytes_accessed=60 * 2**20, transcendentals=0),
        name="run_back",
    )(
        returned, copies, hidden, cot, cols, wo, att, router_t, gains, counts, proj, lse, tiles, wq, seq, ginner
    )


def final_kernel(
    ginner_hbm, sent_hbm, rest_hbm, gouter_hbm, mixed_hbm, gtok_hbm, gqkv_hbm, gwo_hbm, sums_ref, counts_ref,
    inner_hbm, outer_hbm, mixed_out, tok_hbm, qkv_hbm, wo_hbm, gain1_ref, gain2_ref, grouter_ref, gbias_ref, load_ref,
    loss_ref,
    in_ref, out_ref, slim_in_ref, slim_out_ref, mixed_ref, tok_ref, qkv_ref, wo_ref, in_sem, out_sem, copy_sem,
):
    x, z, _, across, _ = places()
    chip = x // 2
    f32 = jnp.float32
    passed = (
        (mixed_hbm, mixed_ref, mixed_out), (gtok_hbm, tok_ref, tok_hbm), (gqkv_hbm, qkv_ref, qkv_hbm),
        (gwo_hbm, wo_ref, wo_hbm),
    )
    copies_in = [pltpu.make_async_copy(a, b, copy_sem.at[n]) for n, (a, b, _) in enumerate(passed)]
    copies = [pltpu.make_async_copy(b, c, copy_sem.at[4 + n]) for n, (_, b, c) in enumerate(passed)]
    depth, _, wide = in_ref.shape
    slim = slim_in_ref.shape[1]
    sent = sent_hbm.shape[2]
    jobs = []
    for part in range(ginner_hbm.shape[2] // wide):
        here = pl.ds(part * wide, wide)
        jobs.append((ginner_hbm.at[chip, :, here], inner_hbm.at[chip, :, here], in_ref, out_ref))
        for j, device in enumerate(across):
            source = sent_hbm.at[j, :, here] if part * wide < sent else rest_hbm.at[j, :, pl.ds(part * wide - sent, wide)]
            jobs.append((source, inner_hbm.at[device // 2, :, here], in_ref, out_ref))
    for n in range(gouter_hbm.shape[0]):
        for i in range(gouter_hbm.shape[1] // slim):
            here = pl.ds(i * slim, slim)
            jobs.append((gouter_hbm.at[n, here], outer_hbm.at[n, here], slim_in_ref, slim_out_ref))
    loads = [
        pltpu.make_async_copy(source, held.at[i % depth], in_sem.at[i % depth])
        for i, (source, _, held, _) in enumerate(jobs)
    ]
    stores = [
        pltpu.make_async_copy(held.at[i % depth], target, out_sem.at[i % depth])
        for i, (_, target, _, held) in enumerate(jobs)
    ]
    for i in range(depth - 1):
        loads[i].start()
    for copy in copies_in:
        copy.start()
    experts = load_ref.shape[1]
    heads = gbias_ref.shape[1]
    shard = sums_ref.shape[1]
    sums = sums_ref[...]
    gain1_ref[...] = sums[0:1, :]
    gain2_ref[...] = sums[1:2, :]
    grouter_ref[...] = sums[2:2 + experts, :]
    gbias_ref[...] = pltpu.roll(sums[16:24, :], (shard - heads * z) % shard, 1)[2:6, :heads]
    tokens = 32 * gtok_hbm.shape[0]
    counts = counts_ref[:, :experts]
    pairs_in_all = 2 * tokens
    prob_sums = sums[22:23, :experts]
    load_ref[...] = jnp.concatenate([experts * counts / pairs_in_all, experts * prob_sums / tokens], axis=0)
    loss_ref[...] = experts * jnp.sum(counts / pairs_in_all * (prob_sums / tokens), axis=1, keepdims=True)
    for copy_in, copy in zip(copies_in, copies):
        copy_in.wait()
        copy.start()
    for i, (_, _, held_in, held_out) in enumerate(jobs):
        if i + depth - 1 < len(jobs):
            loads[i + depth - 1].start()
        loads[i].wait()
        if i >= depth:
            stores[i - depth].wait()
        held_out[i % depth] = held_in[i % depth].astype(f32)
        stores[i].start()
    for store in stores[-depth:]:
        store.wait()
    for copy in copies:
        copy.wait()


def finish(ginner, sent, rest, gouter, mixed, gtok, gqkv, gwo, sums, counts, experts, heads):
    f32, bf16 = jnp.float32, jnp.bfloat16
    local, shard, inner_width = ginner.shape
    wide = inner_width // 4
    slim = gouter.shape[1] // 2
    anywhere = pl.BlockSpec(memory_space=pl.ANY)
    inside = pl.BlockSpec(memory_space=pltpu.VMEM)
    return pl.pallas_call(
        final_kernel,
        out_shape=(
            jax.ShapeDtypeStruct(ginner.shape, f32),
            jax.ShapeDtypeStruct(gouter.shape, f32),
            jax.ShapeDtypeStruct(mixed.shape, bf16),
            jax.ShapeDtypeStruct(gtok.shape, f32),
            jax.ShapeDtypeStruct(gqkv.shape, f32),
            jax.ShapeDtypeStruct(gwo.shape, f32),
            jax.ShapeDtypeStruct((1, shard), f32),
            jax.ShapeDtypeStruct((1, shard), f32),
            jax.ShapeDtypeStruct((experts, shard), f32),
            jax.ShapeDtypeStruct((4, heads), f32),
            jax.ShapeDtypeStruct((2, experts), f32),
            jax.ShapeDtypeStruct((1, 1), f32),
        ),
        in_specs=[anywhere] * 8 + [inside] * 2,
        out_specs=(anywhere,) * 6 + (inside,) * 6,
        scratch_shapes=[
            pltpu.VMEM((8, shard, wide), bf16),
            pltpu.VMEM((8, shard, wide), f32),
            pltpu.VMEM((8, slim, shard), bf16),
            pltpu.VMEM((8, slim, shard), f32),
            pltpu.VMEM(mixed.shape, bf16),
            pltpu.VMEM(gtok.shape, f32),
            pltpu.VMEM(gqkv.shape, f32),
            pltpu.VMEM(gwo.shape, f32),
            pltpu.SemaphoreType.DMA((8,)),
            pltpu.SemaphoreType.DMA((8,)),
            pltpu.SemaphoreType.DMA((8,)),
        ],
        compiler_params=pltpu.CompilerParams(vmem_limit_bytes=62 * 2**20),
        cost_estimate=pl.CostEstimate(flops=0, bytes_accessed=32 * 2**20, transcendentals=0),
        name="finish",
    )(ginner, sent, rest, gouter, mixed, gtok, gqkv, gwo, sums, counts)


def fast_device(
    tokens, expert_ids, gain_attn, w_qkv, w_out, rel_bias, gain_ffn, router, w_in, w_down, cotangent
):
    model_width = tokens.shape[1]
    expert_count = router.shape[1]
    group_heads = rel_bias.shape[1]

    (
        seq_tokens, qkv_weight, out_weight, router_t, gains, count_row, projected, attended, log_totals, bias_tiles, hidden_state, columns,
        gate_rows, send_rows, grad_rows, inner_a, inner_b, inner_c,
        grads_far,
    ) = run_front(
        tokens, w_qkv, w_out, w_in, cotangent, expert_ids.T, router.T, gain_attn[None], gain_ffn[None], rel_bias
    )

    returned, grad_copies, grad_inner, grad_sent, grad_outer = run_experts(
        send_rows,
        gate_rows,
        grad_rows,
        grads_far,
        w_in,
        (inner_a, inner_b, inner_c),
        w_down,
    )
    mixed, grad_tokens, grad_qkv, grad_out_weight, sums, grad_rest = run_back(
        returned.reshape(-1, model_width),
        grad_copies.reshape(-1, model_width),
        hidden_state,
        cotangent,
        columns,
        out_weight,
        attended,
        router_t,
        gains,
        count_row,
        projected,
        log_totals,
        bias_tiles,
        qkv_weight,
        seq_tokens,
        grad_inner,
        grad_sent.shape[2],
    )
    (
        grad_inner, grad_outer, mixed, grad_tokens, grad_qkv, grad_out_weight, gain_one, gain_two, grad_router,
        grad_rel_bias, router_load, loss,
    ) = finish(
        grad_inner,
        grad_sent,
        grad_rest,
        grad_outer,
        mixed,
        grad_tokens,
        grad_qkv,
        grad_out_weight,
        sums,
        count_row,
        expert_count,
        group_heads,
    )
    return (
        mixed,
        loss[0, 0],
        router_load,
        grad_tokens,
        gain_one[0],
        grad_qkv,
        grad_out_weight,
        grad_rel_bias,
        gain_two[0],
        grad_router.T,
        grad_inner,
        grad_outer,
    )


def solution(mesh):
    in_specs = (
        P(("gx", "gy"), None),
        P(("gx", "gy"), None),
        P("gx"),
        P(None, "gx", "gy"),
        P("gy", "gx"),
        P("gx", "gy"),
        P("gx"),
        P("gx", None),
        P("gy", "gx", None),
        P("gy", None, "gx"),
        P(("gx", "gy"), None),
    )
    out_specs = (
        P(("gx", "gy"), None),
        P(),
        P(),
        P(("gx", "gy"), None),
        P("gx"),
        P(None, "gx", "gy"),
        P("gy", "gx"),
        P("gx", "gy"),
        P("gx"),
        P("gx", None),
        P("gy", "gx", None),
        P("gy", None, "gx"),
    )
    return jax.shard_map(
        fast_device if fits_fast(mesh) else general_device, mesh=mesh, in_specs=in_specs, out_specs=out_specs, check_vma=False
    )
```
